128 devices in a mesh: dp: 8 (over y, core), row: 4 (over x), col: 4 (over z).
Axes of the slice: x: 4, y: 4, z: 4, core: 2. Of those that a mesh axis runs over, the one named last changes fastest.
Arguments:
- tokens: bfloat16 [16384, 2048], P(('dp', 'col'), 'row'), may hold values from -6 to 6
- positions: int32 [8, 2048], P('dp', 'row'), may hold values from 0 to 2047, each once within a row
- routes: int32 [16384, 4], P(('dp', 'col')), may hold values from 0 to 63, all different within a row; in each aligned block of 512 rows (0 to 511, 512 to 1023, ...) at most 36 rows name the same one
- attention_norm_gain: float32 [2048], P('row'), may hold values from 0.1 to 1.9
- experts_norm_gain: float32 [2048], P('row'), may hold values from 0.1 to 1.9
- w_qkv: bfloat16 [2048, 16, 384], P('row', 'col'), may hold values from -0.125 to 0.125
- q_gain: float32 [128], replicated, may hold values from 0.1 to 1.9
- k_gain: float32 [128], replicated, may hold values from 0.1 to 1.9
- w_out: bfloat16 [2048, 2048], P('col', 'row'), may hold values from -6 to 6
- w_router: bfloat16 [2048, 64], P('row'), may hold values from -0.0625 to 0.0625
- w_gate_up: bfloat16 [64, 2048, 2, 1024], P(('dp', 'col'), None, None, 'row'), may hold values from -0.125 to 0.125
- w_down: bfloat16 [64, 1024, 2048], P(('dp', 'col'), 'row'), may hold values from -0.75 to 0.75
- cotangent: bfloat16 [16384, 2048], P(('dp', 'col'), 'row'), may hold values from -6 to 6
Outputs:
- output: bfloat16 [16384, 2048], P(('dp', 'col'), 'row')
- grad_tokens: bfloat16 [16384, 2048], P(('dp', 'col'), 'row')
- grad_norm_attn: float32 [2048], P('row')
- grad_norm_moe: float32 [2048], P('row')
- grad_qkv: float32 [2048, 16, 384], P('row', 'col')
- grad_q_gain: float32 [128], replicated
- grad_k_gain: float32 [128], replicated
- grad_out: float32 [2048, 2048], P('col', 'row')
- grad_router: float32 [2048, 64], P('row')
- grad_gate_up: float32 [64, 2048, 2, 1024], P(('dp', 'col'), None, None, 'row')
- grad_down: float32 [64, 1024, 2048], P(('dp', 'col'), 'row')
The draws below stay inside these ranges and needn't reach their ends.
Inputs may be any that keep to these rules, and one draw needn't show every extreme that they name: `routes`: each row names 4 different experts. In each aligned block of 512 rows no expert is named by more than 36 rows, and in some block one expert is named by exactly 36. `positions`: row d is a permutation of the 2048 places of sequence d.
All inputs are finite; a program needn't handle non-finite values.
Results may differ from the reference program's by a relative error of at most 0.03.
Values may be sent and summed in bfloat16 or wider, within the bound.
A program may use at most 256 MiB of HBM per device.

```python
import math
import jax
import jax.numpy as jnp
import numpy as np
from jax import lax

MODEL_WIDTH = 2048
HEADS = 16
HEAD_DIM = 128
FF = 1024
EXPERTS = 64
TOPK = 4
TOK_G = 512
SEQ = 2048
TOKENS = 16384
CAP = 36
N_DP = 8


def level_of(stream_key, dims, shards, low, top_value):
    def one(dim, parts):
        heights = jax.random.uniform(jax.random.fold_in(jax.random.fold_in(stream_key, 6), dim), (parts,), jnp.float32, low / len(shards), top_value / len(shards))
        return jnp.repeat(jnp.exp(heights), dims[dim] // parts).reshape((-1,) + (1,) * (len(dims) - dim - 1))

    level = one(*shards[0])
    for cut in shards[1:]:
        level = level * one(*cut)
    return level


def routed_block(stream_key, own, number, rows, count, top, limit, lean):
    ranking = jax.random.permutation(stream_key, count)
    crowded, usual = portions_of(count, rows * top, limit, lean, True), portions_of(count, rows * top, limit, lean, False)
    places = jnp.arange(count)

    def named(lengths, offset_by):
        used = int((lengths > 0).sum())
        fixed = max(1, used // 4)
        moved = fixed + (places - fixed + offset_by * (used - fixed)) % max(1, count - fixed)
        return jnp.zeros((count,), jnp.int32).at[ranking[jnp.where(places < fixed, places, moved)]].set(jnp.asarray(lengths, jnp.int32))

    lengths = jnp.where(number % 4 == 0, named(crowded, number // 4), named(usual, number - number // 4 - 1))
    mixed = jax.random.permutation(jax.random.fold_in(own, 3), count)
    donor, receiver = mixed[0:count // 2 * 2:2], mixed[1:count // 2 * 2:2]
    slack = jnp.minimum(lengths[donor] - 1, limit - lengths[receiver]) // 2
    slack = jnp.where((donor == ranking[0]) | (receiver == ranking[0]) | (lengths[receiver] == 0), 0, jnp.maximum(slack, 0))
    moved = jax.random.randint(jax.random.fold_in(own, 4), (count // 2,), 0, 1 << 20) % (slack + 1)
    lengths = lengths.at[donor].add(-moved).at[receiver].add(moved)
    members = jnp.searchsorted(jnp.cumsum(lengths), jnp.arange(rows * top), side="right").astype(jnp.int32)
    table = members.reshape(top, rows).T
    table = table[jax.random.permutation(jax.random.fold_in(own, 1), rows)]
    offset_by = jax.random.randint(jax.random.fold_in(own, 2), (rows, 1), 0, top)
    return jnp.take_along_axis(table, (jnp.arange(top)[None, :] + offset_by) % top, axis=1)


def portions_of(number_of, total, limit, skew, full):
    portions = [(1 << 20) // math.isqrt(rank ** skew) + 1 for rank in range(1, number_of + 1)]
    largest = limit if full else min(limit, max(-(-total // number_of), total * portions[0] // sum(portions)))
    least = 1 if total - largest >= number_of - 1 else 0
    counts, surplus = [largest] + [least] * (number_of - 1), total - largest - least * (number_of - 1)
    while surplus > 0:
        movable = [i for i in range(1, number_of) if counts[i] < largest] or [i for i in range(1, number_of) if counts[i] < limit]
        mass, budget = sum([portions[i] for i in movable]), surplus
        for i in movable:
            addition = min(limit - counts[i], max(1, budget * portions[i] // mass), surplus)
            counts[i] = counts[i] + addition
            surplus = surplus - addition
    return np.array(counts)


def noise(stream_key, dims, scale, limit, cuts=(), held_as=jnp.bfloat16):
    loudness = level_of(stream_key, dims, cuts, -0.22, 0.18) if cuts else 1.0
    array = jax.random.normal(stream_key, dims, jnp.float32) * scale * loudness
    return jnp.minimum(jnp.maximum(array, -limit), limit).astype(held_as)


def setup_inputs(seed: int = 0) -> dict:
    key_list = jax.random.split(jax.random.key(seed), 14)
    tokens = noise(key_list[0], (TOKENS, MODEL_WIDTH), 1.0, 6.0, ((0, 32), (1, 4)))
    positions = jax.vmap(lambda own: jax.random.permutation(own, SEQ))(jax.random.split(key_list[1], N_DP)).reshape((N_DP, SEQ)).astype(jnp.int32)
    routes_keys = jax.random.split(jax.random.fold_in(key_list[2], 1), TOKENS // TOK_G)
    routes_turns = jax.random.permutation(jax.random.fold_in(key_list[2], 3), TOKENS // TOK_G)
    routes = jax.vmap(lambda own, number: routed_block(jax.random.fold_in(key_list[2], 2), own, number, TOK_G, EXPERTS, TOPK, CAP, 1))(routes_keys, routes_turns).reshape((TOKENS, TOPK))
    attention_norm_gain = jnp.clip(1.0 + 0.18 * jax.random.normal(key_list[3], (MODEL_WIDTH,), jnp.float32), 0.1, 1.9)
    experts_norm_gain = jnp.clip(1.0 + 0.18 * jax.random.normal(key_list[4], (MODEL_WIDTH,), jnp.float32), 0.1, 1.9)
    w_qkv = noise(key_list[5], (MODEL_WIDTH, HEADS, 3 * HEAD_DIM), MODEL_WIDTH ** -0.5, 0.125, ((0, 4), (1, 4)))
    q_gain = jnp.clip(1.0 + 0.18 * jax.random.normal(key_list[6], (HEAD_DIM,), jnp.float32), 0.1, 1.9)
    k_gain = jnp.clip(1.0 + 0.18 * jax.random.normal(key_list[7], (HEAD_DIM,), jnp.float32), 0.1, 1.9)
    w_out = noise(key_list[8], (HEADS * HEAD_DIM, MODEL_WIDTH), (max(1, HEADS * HEAD_DIM // SEQ)) ** -0.5, 6.0, ((0, 4), (1, 4)))
    w_router = noise(key_list[9], (MODEL_WIDTH, EXPERTS), (4 * MODEL_WIDTH) ** -0.5, 0.0625, ((0, 4),))
    w_gate_up = noise(key_list[10], (EXPERTS, MODEL_WIDTH, 2, FF), MODEL_WIDTH ** -0.5, 0.125, ((0, 32), (3, 4)))
    w_down = noise(key_list[11], (EXPERTS, FF, MODEL_WIDTH), (FF // 16) ** -0.5, 0.75, ((0, 32), (1, 4)))
    cotangent = noise(key_list[12], (TOKENS, MODEL_WIDTH), 1.0, 6.0, ((0, 32), (1, 4)))
    return {"tokens": tokens, "positions": positions, "routes": routes, "attention_norm_gain": attention_norm_gain, "experts_norm_gain": experts_norm_gain, "w_qkv": w_qkv, "q_gain": q_gain, "k_gain": k_gain, "w_out": w_out, "w_router": w_router, "w_gate_up": w_gate_up, "w_down": w_down, "cotangent": cotangent}


EPS = 1e-06
THETA = 10000.0
EXACT = lax.Precision.HIGHEST

@jax.custom_vjp
def low(v):
    return lax.optimization_barrier(v.astype(jnp.bfloat16)).astype(jnp.float32)

@jax.custom_vjp
def low_back(v):
    return v

def low_keep(v):
    return (low(v), None)

def low_pass(kept, grad):
    return (grad,)

def back_keep(v):
    return (v, None)

def back_low(kept, grad):
    return (low(grad),)
low.defvjp(low_keep, low_pass)
low_back.defvjp(back_keep, back_low)

def rms_scale(operand, gain_vec):
    return operand * lax.rsqrt(lax.optimization_barrier(jnp.mean(operand * operand, axis=-1, keepdims=True)) + EPS) * gain_vec

def rotate(operand, position):
    half_width = operand.shape[-1] // 2
    frequency = THETA ** (-2.0 * jnp.arange(half_width, dtype=jnp.float32) / operand.shape[-1])
    angles = position.astype(jnp.float32)[:, None] * frequency[None, :]
    cosine = jnp.cos(angles)[:, None, :]
    sine_part = jnp.sin(angles)[:, None, :]
    first_half = operand[..., :half_width]
    second_half = operand[..., half_width:]
    return jnp.concatenate([first_half * cosine - second_half * sine_part, second_half * cosine + first_half * sine_part], axis=-1)

def attend_sequence(seq_tokens, seq_positions, attention_norm_gain, w_qkv, q_gain, k_gain, w_out):
    length = seq_tokens.shape[0]
    normalized_rows = low(rms_scale(seq_tokens, attention_norm_gain))
    qkv_parts = low_back(jnp.dot(normalized_rows, w_qkv.reshape(MODEL_WIDTH, HEADS * 3 * HEAD_DIM), precision=EXACT))
    qkv_parts = qkv_parts.reshape(length, HEADS, 3, HEAD_DIM)
    queries = low(rotate(rms_scale(qkv_parts[:, :, 0], q_gain), seq_positions))
    keys = low(rotate(rms_scale(qkv_parts[:, :, 1], k_gain), seq_positions))
    values = low(qkv_parts[:, :, 2])
    block_rows = min(512, length)

    def one_block(query_block):
        scores = low_back(jnp.einsum('qhd,khd->hqk', query_block, keys, precision=EXACT) * HEAD_DIM ** (-0.5))
        exp_scores = jnp.exp(scores - lax.optimization_barrier(jnp.max(scores, axis=-1, keepdims=True)))
        probs = low(exp_scores / lax.optimization_barrier(jnp.sum(exp_scores, axis=-1, keepdims=True)))
        return jnp.einsum('hqk,khd->qhd', probs, values, precision=EXACT)
    attended = lax.map(jax.checkpoint(one_block), queries.reshape(length // block_rows, block_rows, HEADS, HEAD_DIM))
    attended = low_back(low(attended.reshape(length, HEADS * HEAD_DIM)))
    return seq_tokens + low_back(jnp.dot(attended, w_out, precision=EXACT))

def slot_tables(routes):
    flat_routes = routes.reshape(-1)
    choice_count = flat_routes.shape[0]
    sources = TOKENS // TOK_G
    onehot = (flat_routes[:, None] == jnp.arange(EXPERTS, dtype=jnp.int32)[None, :]).astype(jnp.int32)
    running = jnp.cumsum(onehot.reshape(sources, TOK_G * TOPK, EXPERTS), axis=1).reshape(choice_count, EXPERTS)
    slot_rank = lax.optimization_barrier(jnp.sum(running * onehot, axis=1)) - 1
    choice_id = jnp.arange(choice_count, dtype=jnp.int32)
    token_place = choice_id // (TOK_G * TOPK) * CAP + slot_rank
    filled = jnp.zeros((EXPERTS, sources * CAP), jnp.int32)
    slot_owner = filled.at[flat_routes, token_place].set(choice_id)
    slot_live = filled.at[flat_routes, token_place].set(1)
    return (slot_owner, slot_live)

def mix_experts(hidden_middle, routes, experts_norm_gain, w_router, w_gate_up, w_down, slot_owner, slot_live):
    experts_input = low(rms_scale(hidden_middle, experts_norm_gain))
    logits = jnp.dot(experts_input, w_router, precision=EXACT)
    chosen = jnp.take_along_axis(logits, routes, axis=1)
    shifted = jnp.exp(chosen - lax.optimization_barrier(jnp.max(chosen, axis=1, keepdims=True)))
    gate_probs = shifted / lax.optimization_barrier(jnp.sum(shifted, axis=1, keepdims=True))

    def one_expert(pieces):
        slot_choices, gate_up_w, down_w = pieces
        expert_in = low_back(jnp.take(experts_input, slot_choices // TOPK, axis=0))
        gate_up = low_back(jnp.dot(expert_in, gate_up_w.reshape(MODEL_WIDTH, 2 * FF), precision=EXACT))
        gate_part = gate_up[:, :FF]
        act = low(gate_part / (1.0 + jnp.exp(-gate_part)) * gate_up[:, FF:])
        return low_back(low(jnp.dot(act, down_w, precision=EXACT)))
    expert_out = lax.map(jax.checkpoint(one_expert), (slot_owner, w_gate_up, w_down))
    flat_owner = slot_owner.reshape(-1)
    slot_weight = jnp.take(gate_probs.reshape(-1), flat_owner) * slot_live.reshape(-1).astype(jnp.float32)
    combined = jnp.zeros_like(hidden_middle).at[flat_owner // TOPK].add(slot_weight[:, None] * expert_out.reshape(-1, MODEL_WIDTH))
    return hidden_middle + combined

def reference(tokens, positions, routes, attention_norm_gain, experts_norm_gain, w_qkv, q_gain, k_gain, w_out, w_router, w_gate_up, w_down, cotangent):
    slot_owner, slot_live = slot_tables(routes)

    def layer(layer_in, gain_attn, gain_moe, qkv_w, gain_q, gain_k, out_w, router_w, gate_up_w, down_w):
        sequences = layer_in.reshape(N_DP, SEQ, MODEL_WIDTH)

        def one_sequence(pieces):
            return attend_sequence(pieces[0], pieces[1], gain_attn, qkv_w, gain_q, gain_k, out_w)
        hidden_middle = lax.map(jax.checkpoint(one_sequence), (sequences, positions)).reshape(TOKENS, MODEL_WIDTH)
        return mix_experts(hidden_middle, routes, gain_moe, router_w, gate_up_w, down_w, slot_owner, slot_live)
    result, pullback = jax.vjp(layer, tokens.astype(jnp.float32), attention_norm_gain, experts_norm_gain, w_qkv.astype(jnp.float32), q_gain, k_gain, w_out.astype(jnp.float32), w_router.astype(jnp.float32), w_gate_up.astype(jnp.float32), w_down.astype(jnp.float32))
    grads = pullback(cotangent.astype(jnp.float32))
    return (result.astype(jnp.bfloat16), grads[0].astype(jnp.bfloat16), grads[1], grads[2], grads[3], grads[4], grads[5], grads[6], grads[7], grads[8], grads[9])
```

```python
import jax
import jax.numpy as jnp
from jax import lax
from jax.experimental import pallas as pl
from jax.experimental.pallas import tpu as pltpu
from jax.sharding import PartitionSpec as P

WIDTH = 2048
HEAD = 128
EXPERTS = 64
CAP = 36
MAIN = 32
TAIL = CAP - MAIN
SEQ = 2048
EPS = 1e-06
THETA = 10000.0
EXACT = lax.Precision.HIGHEST
MESH = pl.DeviceIdType.MESH
SIZES = (4, 2, 4, 4)
BF = jnp.bfloat16
F32 = jnp.float32
ROWS = [(0, 0, d, 0) for d in (2, 1, 3)]
COLS = [(0, 0, 0, d) for d in (2, 1, 3)]
SIBLING = (0, 1, 0, 0)
PLANE = [(0, 0, i, (i + s) % 4) for s in range(4) for i in range(4) if (i, s) != (0, 0)]
CUBE = [
    (i, 0, (i + s) % 4, (i + t) % 4)
    for s in range(4)
    for t in range(4)
    for i in range(4)
    if (i, s, t) != (0, 0, 0)
]
SOURCES = [(i, 0, 0, (i + s) % 4) for s in range(4) for i in range(4) if (i, s) != (0, 0)]
SIDES = [(i, 0, (i + s) % 4, 0) for s in range(4) for i in range(4) if (i, s) != (0, 0)]
LINES = [(d, 0, 0, 0) for d in (2, 1, 3)]
OTHERS = [
    (a, k, 0, d) for a in range(4) for k in range(2) for d in range(4) if (a, k, d) != (0, 0, 0)
]


def shape(dims, dtype=BF):
    return jax.ShapeDtypeStruct(dims, dtype)


def here():
    group = lax.axis_index("dp")
    return (group // 2, group % 2, lax.axis_index("row"), lax.axis_index("col"))


def moved(place, offset):
    return tuple((p + o) % n for p, o, n in zip(place, offset, SIZES))


def back(place, offset):
    return tuple((p + n - o) % n for p, o, n in zip(place, offset, SIZES))


def device(place):
    return (place[0] * 2 + place[1], place[2], place[3])


def exchange(inputs, outputs, sends, kept, call_id, micros=30, work=None, work_in=(), work_out=(), work_scratch=()):
    offsets = sorted({s[0] for s in sends})
    n_in, n_out, n_send = len(inputs), len(outputs), len(sends)
    m_in, m_out = len(work_in), len(work_out)

    def kernel(*refs):
        ins, refs = refs[:n_in], refs[n_in:]
        worked, refs = refs[:m_in], refs[m_in:]
        outs, refs = refs[:n_out], refs[n_out:]
        made, refs = refs[:m_out], refs[m_out:]
        send_sem, recv_sem, kept_sem = refs[:3]
        special = {"work": worked, "scratch": refs[3:]}
        me = here()
        barrier = pltpu.get_barrier_semaphore()
        for offset in offsets:
            pl.semaphore_signal(
                barrier, inc=1, device_id=device(moved(me, offset)), device_id_type=MESH
            )
        local = []
        for index, (i, take, o, put) in enumerate(kept):
            local.append(
                pltpu.make_async_copy(take(ins[i], me), put(outs[o], me), kept_sem.at[index])
            )
            local[-1].start()
        pl.semaphore_wait(barrier, len(offsets))
        copies, arrived = [], set()

        def arrive(index):
            if index not in arrived:
                arrived.add(index)
                copies[index].wait_recv()

        def named(group, index):
            return special[index[0]][index[1]] if isinstance(index, tuple) else group[index]

        def start(index):
            offset, i, take, o, put = sends[index][:5]
            needs = sends[index][5] if len(sends[index]) > 5 else None
            for need in needs or ():
                if need >= 0:
                    arrive(need)
                elif need not in arrived:
                    arrived.add(need)
                    for copy in local:
                        copy.wait()
            peer = moved(me, offset)
            copies.append(
                pltpu.make_async_remote_copy(
                    src_ref=take(named(ins if needs is None else outs, i), me, peer),
                    dst_ref=put(named(outs, o), me, peer),
                    send_sem=send_sem.at[index],
                    recv_sem=recv_sem.at[index],
                    device_id=device(peer),
                    device_id_type=MESH,
                )
            )
            copies[-1].start()

        for index in range(n_send):
            start(index)
        if work is not None:
            work(arrive, *worked, *made, *refs[3:])
        for index in range(n_send):
            arrive(index)
        for copy in copies:
            copy.wait_send()
        if -1 not in arrived:
            for copy in local:
                copy.wait()

    return pl.pallas_call(
        kernel,
        out_shape=list(outputs) + list(work_out),
        in_specs=[pl.BlockSpec(memory_space=pl.ANY)] * n_in
        + [pl.BlockSpec(memory_space=pltpu.VMEM)] * m_in,
        out_specs=[pl.BlockSpec(memory_space=pl.ANY)] * n_out
        + [pl.BlockSpec(memory_space=pltpu.VMEM)] * m_out,
        scratch_shapes=[
            pltpu.SemaphoreType.DMA((n_send,)),
            pltpu.SemaphoreType.DMA((n_send,)),
            pltpu.SemaphoreType.DMA((max(1, len(kept)),)),
            *work_scratch,
        ],
        compiler_params=pltpu.CompilerParams(
            collective_id=call_id,
            has_side_effects=True,
            vmem_limit_bytes=(8 if work is None else 56) * 2**20,
        ),
        cost_estimate=pl.CostEstimate(
            flops=0, bytes_accessed=micros * 3_500_000, transcendentals=0
        ),
    )(*inputs, *work_in)


def rows(start, size):
    return pl.ds(pl.multiple_of(start, size), size)


def gather_inputs(tokens, w_qkv, w_out, small_int, small_float):
    outputs = [
        shape((512, WIDTH)),
        shape((4, 512, 1536)),
        shape((4, 4, HEAD, 512)),
        shape((4, 4, HEAD), jnp.int32),
        shape((4, 4, HEAD), F32),
    ]
    sends = []

    def eighth(size):
        me = here()
        return rows((me[1] * 4 + me[0]) * size, size)

    def half(size):
        return rows(here()[1] * size, size)

    def add(group, take, o, put=None, i=None, needs=None):
        numbers = []
        for offset in group:
            numbers.append(len(sends))
            if needs is None:
                sends.append((offset, i, take, o, put))
            else:
                view = lambda ref, me, p: take(ref, me)
                sends.append((offset, o, view, o, view, needs))
        return numbers

    first = add(
        ROWS,
        lambda s, me, p: s.at[eighth(64), rows(p[2] * 384, 384)],
        1,
        lambda o, me, p: o.at[me[2], eighth(64), rows(me[3] * 384, 384)],
        1,
    )
    add(ROWS, lambda s, me, p: s, 0, lambda o, me, p: o.at[:, rows(me[2] * 512, 512)], 0)
    add(ROWS, lambda s, me, p: s, 3, lambda o, me, p: o.at[me[2]], 3)
    add(ROWS, lambda s, me, p: s, 4, lambda o, me, p: o.at[me[2]], 4)
    low, high = pl.ds(0, 2), pl.ds(2, 2)
    out_z = add(COLS, lambda o, me: o.at[low, me[3], eighth(16)], 2, needs=[-1])
    out_y = add(LINES, lambda o, me: o.at[high, me[3], eighth(16)], 2, needs=[-1])
    by_z = add(
        COLS, lambda o, me: o.at[low, eighth(64), rows(me[3] * 384, 384)], 1, needs=first
    )
    by_y = add(
        LINES, lambda o, me: o.at[high, eighth(64), rows(me[3] * 384, 384)], 1, needs=first
    )
    out_zy = add(LINES, lambda o, me: o.at[low, :, eighth(16)], 2, needs=out_z)
    out_yz = add(COLS, lambda o, me: o.at[high, me[3], half(64)], 2, needs=out_y)
    by_zy = add(LINES, lambda o, me: o.at[low, eighth(64)], 1, needs=by_z)
    by_yz = add(
        COLS, lambda o, me: o.at[high, half(256), rows(me[3] * 384, 384)], 1, needs=by_y
    )
    pair = [SIBLING]
    add(pair, lambda o, me: o.at[low, :, half(64)], 2, needs=out_zy)
    add(pair, lambda o, me: o.at[high, :, half(64)], 2, needs=out_yz)
    add(pair, lambda o, me: o.at[low, half(256)], 1, needs=by_zy)
    add(pair, lambda o, me: o.at[high, half(256)], 1, needs=by_yz)
    kept = [
        (0, lambda s, me: s, 0, lambda o, me: o.at[:, rows(me[2] * 512, 512)]),
        (
            1,
            lambda s, me: s.at[eighth(64), rows(me[2] * 384, 384)],
            1,
            lambda o, me: o.at[me[2], eighth(64), rows(me[3] * 384, 384)],
        ),
        (2, lambda s, me: s.at[:, eighth(16)], 2, lambda o, me: o.at[:, me[3], eighth(16)]),
        (3, lambda s, me: s, 3, lambda o, me: o.at[me[2]]),
        (4, lambda s, me: s, 4, lambda o, me: o.at[me[2]]),
    ]
    return exchange(
        [tokens, w_qkv.reshape(512, 1536), w_out.reshape(4, HEAD, 512), small_int, small_float],
        outputs,
        sends,
        kept,
        0,
    )


def to_heads(qkv):
    take = lambda s, me, p: s.at[:, rows(p[3] * 384, 384)]
    put = lambda o, me, p: o.at[rows(me[3] * 512, 512)]
    return exchange(
        [qkv],
        [shape((SEQ, 384))],
        [(offset, 0, take, 0, put) for offset in COLS],
        [(0, lambda s, me: take(s, me, me), 0, lambda o, me: put(o, me, me))],
        1,
    )[0]


def from_heads(grads, qkv_part):
    take = lambda s, me, p: s.at[rows(p[3] * 512, 512)]
    put = lambda o, me, p: o.at[:, rows(me[3] * 384, 384)]
    return exchange(
        [grads, qkv_part],
        [shape((512, 1536)), shape((4, 256, 384))],
        [(offset, 0, take, 0, put) for offset in COLS]
        + [(SIBLING, 1, lambda s, me, p: s.at[:, rows(p[1] * 256, 256)], 1, lambda o, me, p: o)],
        [(0, lambda s, me: take(s, me, me), 0, lambda o, me: put(o, me, me))],
        2,
    )


def gather_attended(attended):
    take = lambda s, me, p: s.at[rows(p[3] * 512, 512)]
    put = lambda o, me, p: o.at[:, rows((me[2] * 4 + me[3]) * HEAD, HEAD)]
    return exchange(
        [attended],
        [shape((512, WIDTH))],
        [(offset, 0, take, 0, put) for offset in PLANE],
        [(0, lambda s, me: take(s, me, me), 0, lambda o, me: put(o, me, me))],
        3,
    )[0]


def spread_attended_grad(partial, out_part, small_part):
    take = lambda s, me, p: s.at[:, rows((p[2] * 4 + p[3]) * HEAD, HEAD)]
    put = lambda o, me, p: o.at[me[2], rows(me[3] * 512, 512)]
    return exchange(
        [partial, out_part, small_part],
        [shape((4, SEQ, HEAD)), shape((16, 64, 512)), shape(small_part.shape, F32)],
        [(offset, 0, take, 0, put) for offset in PLANE]
        + [
            (SIBLING, 1, lambda s, me, p: s.at[:, rows(p[1] * 64, 64)], 1, lambda o, me, p: o),
            (SIBLING, 2, lambda s, me, p: s, 2, lambda o, me, p: o),
        ],
        [(0, lambda s, me: take(s, me, me), 0, lambda o, me: put(o, me, me))],
        4,
    )


def row_stack(operand, call_id):
    take = lambda s, me, p: s
    put = lambda o, me, p: o.at[me[2]]
    return exchange(
        [operand],
        [shape((4,) + operand.shape, operand.dtype)],
        [(offset, 0, take, 0, put) for offset in ROWS],
        [(0, lambda s, me: s, 0, lambda o, me: put(o, me, me))],
        call_id,
    )[0]


def spread_features(partial, stats, qkv_half, out_half, small):
    take = lambda s, me, p: s.at[:, rows(p[2] * 512, 512)]
    put = lambda o, me, p: o.at[me[2]]
    whole = lambda s, me, p: s
    take_qkv = lambda s, me, p: s.at[p[2], rows(p[0] * 64, 64)]
    put_qkv = lambda o, me, p: o.at[me[0], me[2]]
    take_out = lambda s, me, p: s.at[p[0] * 4 + p[3]]
    put_out = lambda o, me, p: o.at[me[0] * 4 + me[3]]
    keep = lambda i, take, put: (i, lambda s, me: take(s, me, me), i, lambda o, me: put(o, me, me))
    return exchange(
        [partial, stats, qkv_half, out_half, small],
        [
            shape((4, 512, 512)),
            shape((4,) + stats.shape, F32),
            shape((4, 4, 64, 384)),
            shape((16, 64, 512)),
            shape((16,) + small.shape[1:], F32),
        ],
        [(offset, 0, take, 0, put) for offset in ROWS]
        + [(offset, 1, whole, 1, put) for offset in ROWS]
        + [(offset, 2, take_qkv, 2, put_qkv) for offset in SIDES]
        + [(offset, 3, take_out, 3, put_out) for offset in SOURCES]
        + [(offset, 4, take_out, 4, put_out) for offset in SOURCES],
        [
            keep(0, take, put),
            keep(1, whole, put),
            keep(2, take_qkv, put_qkv),
            keep(3, take_out, put_out),
            keep(4, take_out, put_out),
        ],
        5,
    )


def expert_at(place):
    return place[0] * 16 + (place[2] // 2) * 8 + place[3] * 2 + place[2] % 2


def to_experts(main, tail, call_id, **work):
    take = lambda s, me, p: s.at[expert_at(p)]
    put_main = lambda o, me, p: o.at[me[0] * 4 + me[3], :, rows(me[2] * 512, 512)]
    put_tail = lambda o, me, p: o.at[me[0] * 4 + me[3], me[2]]
    sends = []
    for offset in CUBE:
        sends.append((offset, 0, take, 0, put_main))
        sends.append((offset, 1, take, 1, put_tail))
    return exchange(
        [main, tail],
        [shape((16, MAIN, WIDTH)), shape((16, 4) + tail.shape[1:])],
        sends,
        [
            (0, lambda s, me: take(s, me, me), 0, lambda o, me: put_main(o, me, me)),
            (1, lambda s, me: take(s, me, me), 1, lambda o, me: put_tail(o, me, me)),
        ],
        call_id,
        **work,
    )


def from_experts(main, tail, call_id, first_sends=(), **work):
    take_main = lambda s, me, p: s.at[p[0] * 4 + p[3], :, rows(p[2] * 512, 512)]
    take_tail = lambda s, me, p: s.at[p[0] * 4 + p[3], p[2]]
    put = lambda o, me, p: o.at[expert_at(me)]
    sends = list(first_sends)
    for offset in CUBE:
        sends.append((offset, 0, take_main, 0, put))
        sends.append((offset, 1, take_tail, 1, put))
    return exchange(
        [main, tail],
        [shape((EXPERTS, MAIN, 512)), shape((EXPERTS,) + tail.shape[2:])],
        sends,
        [
            (0, lambda s, me: take_main(s, me, me), 0, lambda o, me: put(o, me, me)),
            (1, lambda s, me: take_tail(s, me, me), 1, lambda o, me: put(o, me, me)),
        ],
        call_id,
        **work,
    )


def collect_sums(qkv_piece, out_piece, small_piece, late):
    put_qkv = lambda o, me, p: o.at[me[1], me[0]]
    put_out = lambda o, me, p: o.at[me[0], me[1]]
    put_small = lambda o, me, p: o.at[me[0] * 4 + me[3]]
    put_late = lambda o, me, p: o.at[(me[0] * 2 + me[1]) * 4 + me[3]]
    whole = lambda s, me, p: s
    sends = []
    for offset in LINES:
        sends.append((offset, 0, whole, 0, put_qkv))
        sends.append((offset, 1, whole, 1, put_out))
    sends.append((SIBLING, 0, whole, 0, put_qkv))
    sends.append((SIBLING, 1, whole, 1, put_out))
    sends += [(offset, 2, whole, 2, put_small) for offset in SOURCES]
    sends += [(offset, 3, whole, 3, put_late) for offset in OTHERS]
    for index, offset in enumerate(LINES):
        for o, view in ((0, put_qkv), (1, put_out)):
            brought = lambda ref, me, p, view=view, offset=offset: view(ref, back(me, offset), p)
            sends.append((SIBLING, o, brought, o, brought, [2 * index + o]))
    return exchange(
        [qkv_piece, out_piece, small_piece, late],
        [
            shape((2, 4, 64, 1536)),
            shape((4, 2, 64, 512)),
            shape((16,) + small_piece.shape, F32),
            shape((32,) + late.shape, F32),
        ],
        sends,
        [
            (0, lambda s, me: s, 0, lambda o, me: put_qkv(o, me, me)),
            (1, lambda s, me: s, 1, lambda o, me: put_out(o, me, me)),
            (2, lambda s, me: s, 2, lambda o, me: put_small(o, me, me)),
            (3, lambda s, me: s, 3, lambda o, me: put_late(o, me, me)),
        ],
        12,
    )


BLOCK = 256
SCALE = HEAD ** (-0.5)
LAST = (((1,), (1,)), ((), ()))
FIRST = (((0,), (0,)), ((), ()))


def swapped(operand):
    return pltpu.roll(operand, HEAD // 2, 1)


def attend_kernel(arrive, qkv_ref, cos_ref, sin_ref, gain_ref, out_ref, query_ref, key_ref, lse_ref):
    def prepare(step, carry):
        span = pl.ds(pl.multiple_of(step * BLOCK, BLOCK), BLOCK)
        for part, target in ((0, query_ref), (1, key_ref)):
            raw = qkv_ref[span, part * HEAD : (part + 1) * HEAD].astype(F32)
            scaled = (
                raw
                * lax.rsqrt(jnp.mean(raw * raw, axis=1, keepdims=True) + EPS)
                * gain_ref[part : part + 1, :]
            )
            target[span, :] = (scaled * cos_ref[span, :] + swapped(scaled) * sin_ref[span, :]).astype(
                BF
            )
        return carry

    lax.fori_loop(0, SEQ // BLOCK, prepare, 0)

    def block(step, carry):
        span = pl.ds(pl.multiple_of(step * BLOCK, BLOCK), BLOCK)
        scores = (
            lax.dot_general(query_ref[span, :], key_ref[...], LAST, preferred_element_type=F32)
            * SCALE
        )
        largest = jnp.max(scores, axis=1, keepdims=True)
        weights = jnp.exp(scores - largest)
        total = jnp.sum(weights, axis=1, keepdims=True)
        mixed = jnp.dot(
            weights.astype(BF), qkv_ref[:, 2 * HEAD :], preferred_element_type=F32
        )
        out_ref[span, :] = (mixed / total).astype(BF)
        lse_ref[span, :] = largest + jnp.log(total)
        return carry

    lax.fori_loop(0, SEQ // BLOCK, block, 0)


def attend(qkv, cosine, sine, gains, main, tail):
    return to_experts(
        main,
        tail,
        6,
        work=attend_kernel,
        work_in=[qkv, cosine, sine, gains],
        work_out=[
            shape((SEQ, HEAD)),
            shape((SEQ, HEAD)),
            shape((SEQ, HEAD)),
            shape((SEQ, 1), F32),
        ],
    )


def attend_back_kernel(
    arrive,
    qkv_ref,
    query_ref,
    key_ref,
    lse_ref,
    parts_ref,
    cos_ref,
    sin_ref,
    gain_ref,
    normed_ref,
    before_ref,
    behind_ref,
    across_ref,
    beyond_ref,
    grad_ref,
    gain_grad_ref,
    weight_grad_ref,
    query_grad,
    key_grad,
    value_grad,
):
    key_grad[...] = jnp.zeros_like(key_grad)
    value_grad[...] = jnp.zeros_like(value_grad)

    def block(step, carry):
        span = pl.ds(pl.multiple_of(step * BLOCK, BLOCK), BLOCK)
        query = query_ref[span, :]
        out_grad = parts_ref[0, span, :].astype(F32)
        for part in range(1, 4):
            out_grad = out_grad + parts_ref[part, span, :].astype(F32)
        out_grad = out_grad.astype(BF)
        scores = (
            lax.dot_general(query, key_ref[...], LAST, preferred_element_type=F32) * SCALE
        )
        soft = jnp.exp(scores - lse_ref[span, :])
        prob_grad = lax.dot_general(
            out_grad, qkv_ref[:, 2 * HEAD :], LAST, preferred_element_type=F32
        )
        inner = jnp.sum(soft * prob_grad, axis=1, keepdims=True)
        score_grad = (soft * (prob_grad - inner)).astype(BF)
        query_grad[span, :] = (
            jnp.dot(score_grad, key_ref[...], preferred_element_type=F32) * SCALE
        )
        key_grad[...] += lax.dot_general(score_grad, query, FIRST, preferred_element_type=F32)
        value_grad[...] += lax.dot_general(
            soft.astype(BF), out_grad, FIRST, preferred_element_type=F32
        )
        return carry

    lax.fori_loop(0, SEQ // BLOCK, block, 0)
    gain_grad_ref[...] = jnp.zeros_like(gain_grad_ref)

    def finish(step, carry):
        span = pl.ds(pl.multiple_of(step * BLOCK, BLOCK), BLOCK)
        for part, source, factor in ((0, query_grad, 1.0), (1, key_grad, SCALE)):
            turned = source[span, :] * factor
            grad = turned * cos_ref[span, :] + swapped(turned * sin_ref[span, :])
            raw = qkv_ref[span, part * HEAD : (part + 1) * HEAD].astype(F32)
            inverse = lax.rsqrt(jnp.mean(raw * raw, axis=1, keepdims=True) + EPS)
            unit = raw * inverse
            gain_grad_ref[part : part + 1, :] += jnp.sum(grad * unit, axis=0, keepdims=True)
            scaled = grad * gain_ref[part : part + 1, :]
            raw_grad = inverse * (scaled - unit * jnp.mean(scaled * unit, axis=1, keepdims=True))
            grad_ref[span, part * HEAD : (part + 1) * HEAD] = raw_grad.astype(BF)
        grad_ref[span, 2 * HEAD :] = value_grad[span, :].astype(BF)
        return carry

    lax.fori_loop(0, SEQ // BLOCK, finish, 0)
    col = lax.axis_index("col")

    def project(step, carry):
        span = pl.ds(pl.multiple_of(step * BLOCK, BLOCK), BLOCK)
        total = jnp.zeros((BLOCK, 3 * HEAD), F32)
        for ref, ahead, skip in (
            (normed_ref, 0, 0),
            (before_ref, 3, 0),
            (behind_ref, 1, 0),
            (across_ref, 2, 0),
            (beyond_ref, 2, 256),
        ):
            size = ref.shape[0]
            first = pl.multiple_of(lax.rem(col + ahead, 4) * 512 + skip, 256)
            total += lax.dot_general(
                ref[:, span], grad_ref[pl.ds(first, size), :], FIRST, preferred_element_type=F32
            )
        weight_grad_ref[span, :] = total.astype(BF)
        return carry

    lax.fori_loop(0, WIDTH // BLOCK, project, 0)


def attend_back(operands, main, tail):
    return from_experts(
        main,
        tail,
        13,
        work=attend_back_kernel,
        work_in=operands,
        work_out=[shape((SEQ, 3 * HEAD)), shape((8, HEAD), F32), shape((WIDTH, 3 * HEAD))],
        work_scratch=[pltpu.VMEM((SEQ, HEAD), F32)] * 3,
    )


SLOTS = 16 * CAP


def expert_kernel(*refs):
    in_main, in_tail, cot_main, cot_tail, gate_ref = refs[:5]
    weights, refs = refs[5:13], refs[13:]
    x_ref, slot_grad_ref, out_main, out_tail, back_main, back_tail = refs[:6]
    act_ref, grad_ref, gate_grad_ref, inner_ref = refs[6:10]
    cot_ref, up_ref, down_ref, out_sum, back_sum, row_sem, weight_sem = refs[10:]
    whole, first, last = pl.ds(0, SLOTS), pl.ds(0, 16 * MAIN), pl.ds(16 * MAIN, 16 * TAIL)
    loads = [
        pltpu.make_async_copy(source, target.at[span], row_sem.at[index])
        for index, (source, target, span) in enumerate(
            (
                (in_main, x_ref, first),
                (in_tail, x_ref, last),
                (cot_main, cot_ref, first),
                (cot_tail, cot_ref, last),
            )
        )
    ]
    for load in loads:
        load.start()
    weight_loads = []
    for slot in range(4):
        for part, target in ((0, up_ref), (4, down_ref)):
            weight_loads.append(
                pltpu.make_async_copy(
                    weights[part + slot], target.at[slot], weight_sem.at[part + slot]
                )
            )
            weight_loads[-1].start()
    for load in loads:
        load.wait()
    slot_grad_ref[...] = (gate_ref[...] * cot_ref[...].astype(F32)).astype(BF)
    for slot in range(4):
        weight_loads[2 * slot].wait()
        weight_loads[2 * slot + 1].wait()
        gate_up = jnp.dot(x_ref[...], up_ref[slot], preferred_element_type=F32)
        gate_part, up_part = gate_up[:, :256], gate_up[:, 256:]
        sigmoid = 1.0 / (1.0 + jnp.exp(-gate_part))
        silu = gate_part * sigmoid
        act = (silu * up_part).astype(BF)
        act_ref[slot] = act
        act_grad = lax.dot_general(
            slot_grad_ref[...], down_ref[slot], LAST, preferred_element_type=F32
        )
        slope = sigmoid * (1.0 + gate_part * (1.0 - sigmoid))
        grad_ref[slot, :, :256] = (act_grad * up_part * slope).astype(BF)
        grad_ref[slot, :, 256:] = (act_grad * silu).astype(BF)
        out = jnp.dot(act, down_ref[slot], preferred_element_type=F32)
        out_sum[...] = out if slot == 0 else out_sum[...] + out
        in_grad = lax.dot_general(
            grad_ref[slot], up_ref[slot], LAST, preferred_element_type=F32
        )
        back_sum[...] = in_grad if slot == 0 else back_sum[...] + in_grad
    out = out_sum[...].astype(BF)
    out_main[...] = out[: 16 * MAIN]
    out_tail[...] = out[16 * MAIN :]
    gate_grad_ref[...] = jnp.sum(
        cot_ref[...].astype(F32) * out.astype(F32), axis=1, keepdims=True
    )
    inner_ref[...] = jnp.sum(back_sum[...] * x_ref[...].astype(F32), axis=1, keepdims=True)
    in_grad = back_sum[...].astype(BF)
    back_main[...] = in_grad[: 16 * MAIN]
    back_tail[...] = in_grad[16 * MAIN :]


def run_expert(in_main, in_tail, cot_main, cot_tail, gate, weights):
    main, tail = shape((16 * MAIN, WIDTH)), shape((16 * TAIL, WIDTH))
    return pl.pallas_call(
        expert_kernel,
        out_shape=[
            shape((SLOTS, WIDTH)),
            shape((SLOTS, WIDTH)),
            main,
            tail,
            main,
            tail,
            shape((4, SLOTS, 256)),
            shape((4, SLOTS, 512)),
            shape((SLOTS, 1), F32),
            shape((SLOTS, 1), F32),
        ],
        in_specs=[pl.BlockSpec(memory_space=pl.ANY)] * 4
        + [pl.BlockSpec(memory_space=pltpu.VMEM)]
        + [pl.BlockSpec(memory_space=pl.ANY)] * 8,
        out_specs=[pl.BlockSpec(memory_space=pltpu.VMEM)] * 10,
        scratch_shapes=[
            pltpu.VMEM((SLOTS, WIDTH), BF),
            pltpu.VMEM((4, WIDTH, 512), BF),
            pltpu.VMEM((4, 256, WIDTH), BF),
            pltpu.VMEM((SLOTS, WIDTH), F32),
            pltpu.VMEM((SLOTS, WIDTH), F32),
            pltpu.SemaphoreType.DMA((4,)),
            pltpu.SemaphoreType.DMA((8,)),
        ],
        compiler_params=pltpu.CompilerParams(vmem_limit_bytes=60 * 2**20),
        cost_estimate=pl.CostEstimate(
            flops=2 * SLOTS * WIDTH * 1024 * 6,
            bytes_accessed=100_000_000,
            transcendentals=SLOTS * 1024,
        ),
    )(in_main, in_tail, cot_main, cot_tail, gate, *weights)


def weight_grads_kernel(
    arrive, x_ref, slot_grad_ref, grad_ref, act_ref, up_grad, down_grad, *theirs
):
    their_x, their_slot_grad, their_grad, their_act = theirs

    def own_up(step, carry):
        span = pl.ds(pl.multiple_of(step * 512, 512), 512)
        for slot in range(2):
            up_grad[slot, span, :] = lax.dot_general(
                x_ref[:, span], grad_ref[slot], FIRST, preferred_element_type=F32
            )
        return carry

    def own_down(step, carry):
        span = pl.ds(pl.multiple_of(step * 512, 512), 512)
        for slot in range(2):
            down_grad[slot, :, span] = lax.dot_general(
                act_ref[slot], slot_grad_ref[:, span], FIRST, preferred_element_type=F32
            )
        return carry

    def their_up(step, carry):
        span = pl.ds(pl.multiple_of(step * 512, 512), 512)
        for slot in range(2):
            up_grad[slot, span, :] += lax.dot_general(
                their_x[:, span], their_grad[slot], FIRST, preferred_element_type=F32
            )
        return carry

    def their_down(step, carry):
        span = pl.ds(pl.multiple_of(step * 512, 512), 512)
        for slot in range(2):
            down_grad[slot, :, span] += lax.dot_general(
                their_act[slot], their_slot_grad[:, span], FIRST, preferred_element_type=F32
            )
        return carry

    lax.fori_loop(0, 4, own_up, 0)
    lax.fori_loop(0, 4, own_down, 0)
    for index in range(4):
        arrive(index)
    lax.fori_loop(0, 4, their_up, 0)
    lax.fori_loop(0, 4, their_down, 0)


def return_rows(main, tail, x, slot_grad, grads, acts):
    whole = lambda s, me, p: s
    other = lambda s, me, p: s.at[pl.ds(2, 2)]
    return from_experts(
        main,
        tail,
        9,
        first_sends=[
            (SIBLING, ("work", 0), whole, ("scratch", 0), whole),
            (SIBLING, ("work", 1), whole, ("scratch", 1), whole),
            (SIBLING, ("work", 2), other, ("scratch", 2), whole),
            (SIBLING, ("work", 3), other, ("scratch", 3), whole),
        ],
        work=weight_grads_kernel,
        work_in=[x, slot_grad, grads, acts],
        work_out=[shape((2, WIDTH, 512), F32), shape((2, 256, WIDTH), F32)],
        work_scratch=[
            pltpu.VMEM((SLOTS, WIDTH), BF),
            pltpu.VMEM((SLOTS, WIDTH), BF),
            pltpu.VMEM((2, SLOTS, 512), BF),
            pltpu.VMEM((2, SLOTS, 256), BF),
        ],
    )


def dot(left, right):
    return jnp.dot(left, right, preferred_element_type=F32)


def dot_last(left, right):
    return lax.dot_general(left, right, LAST, preferred_element_type=F32)


def dot_first(left, right):
    return lax.dot_general(left, right, FIRST, preferred_element_type=F32)


def pieces(value):
    high = value.astype(BF)
    rest = value - high.astype(F32)
    middle = rest.astype(BF)
    low = (rest - middle.astype(F32)).astype(BF)
    return [high, middle, low]


def aux_rows(values):
    stacked = jnp.stack([piece for value in values for piece in pieces(value)], axis=1)
    return jnp.pad(stacked, ((0, 0), (0, 16 - stacked.shape[1]), (0, HEAD - CAP)))


def aux_value(rows_of, index):
    return jnp.sum(rows_of[:, 3 * index : 3 * index + 3, :CAP].astype(F32), axis=1)


def pack_tail(tail):
    return (
        tail.reshape(EXPERTS, TAIL, 4, HEAD).transpose(0, 2, 1, 3).reshape(EXPERTS, 16, HEAD)
    )


def unpack_tail(tail):
    return (
        tail.reshape(EXPERTS, 4, TAIL, HEAD).transpose(0, 2, 1, 3).reshape(EXPERTS * TAIL, 512)
    )


def join_tail(tail):
    return tail.reshape(16, 4, 4, TAIL, HEAD).transpose(0, 3, 1, 2, 4).reshape(16 * TAIL, WIDTH)


def split_tail(tail):
    return (
        tail.reshape(16, TAIL, 4, 4, HEAD).transpose(0, 2, 3, 1, 4).reshape(16, 4, 16, HEAD)
    )


def join_values(values):
    return jnp.concatenate([values[:, :MAIN].reshape(-1), values[:, MAIN:].reshape(-1)])


def split_values(values):
    return jnp.concatenate(
        [values[: 16 * MAIN].reshape(16, MAIN), values[16 * MAIN :].reshape(16, TAIL)], axis=1
    )


FIRST_HOP = [
    ((2 * y + k) * 4 + x, (2 * y + 1 - x % 2) * 4 + 2 * k + x // 2)
    for y in range(4)
    for k in range(2)
    for x in range(4)
]
SECOND_HOP = [
    ((2 * y + k) * 4 + x, (2 * y + x % 2) * 4 + 2 * k + 1 - x // 2)
    for y in range(4)
    for k in range(2)
    for x in range(4)
]
PAIR = [(d, d ^ 1) for d in range(8)]


def hop(operand, pairs):
    return lax.ppermute(operand, ("dp", "row"), pairs)


def hop_col(operand, by):
    return lax.ppermute(operand, "col", [(c, (c + by) % 4) for c in range(4)])


def after(*operands):
    return lax.optimization_barrier(operands)


def inverse_pairs(pairs):
    return [(b, a) for a, b in pairs]


def shards(
    tokens,
    positions,
    routes,
    attention_norm_gain,
    experts_norm_gain,
    w_qkv,
    q_gain,
    k_gain,
    w_out,
    w_router,
    w_gate_up,
    w_down,
    cotangent,
):
    row = lax.axis_index("row")
    upper = row // 2
    token_rows, w_group, w_all, position_rows, gain_rows = gather_inputs(
        tokens,
        w_qkv,
        w_out,
        positions.reshape(4, HEAD),
        attention_norm_gain.reshape(4, HEAD),
    )
    w_group = w_group.reshape(WIDTH, 1536)
    w_all = w_all.reshape(WIDTH, 512)
    gain_full = gain_rows.reshape(WIDTH)

    w_gate_up, w_down, token_rows = after(w_gate_up, w_down, token_rows)
    gate_up_w = w_gate_up.reshape(2, WIDTH, 512)
    own = lambda w, which: lax.dynamic_index_in_dim(w, which, 0, keepdims=False)
    gate_up_1 = hop(own(gate_up_w, upper), FIRST_HOP)
    gate_up_2 = hop(own(gate_up_w, 1 - upper), SECOND_HOP)
    down_1 = hop(own(w_down, upper), FIRST_HOP)
    down_2 = hop(own(w_down, 1 - upper), SECOND_HOP)
    sibling = lambda w: lax.ppermute(w, "dp", PAIR)
    up_ws = [gate_up_1, gate_up_2, sibling(gate_up_1), sibling(gate_up_2)]
    down_ws = [down_1, down_2, sibling(down_1), sibling(down_2)]

    frequency = THETA ** (-2.0 * jnp.arange(HEAD // 2, dtype=F32) / HEAD)
    angles = position_rows.reshape(SEQ).astype(F32)[:, None] * frequency[None, :]
    cosine = jnp.concatenate([jnp.cos(angles)] * 2, axis=1)
    sine = jnp.concatenate([-jnp.sin(angles), jnp.sin(angles)], axis=1)
    gains = jnp.concatenate([q_gain[None], k_gain[None], jnp.zeros((6, HEAD), F32)], axis=0)

    experts = jnp.arange(EXPERTS, dtype=jnp.int32)
    named = jnp.any(routes[:, :, None] == experts[None, None, :], axis=1)
    place = jnp.arange(512, dtype=jnp.int32)
    earlier = (place[None, :] < place[:, None]).astype(BF)
    rank = dot(earlier, named.astype(BF))
    rank = jnp.where(named, rank, -1.0).T
    main_pick = (
        (rank[:, None, :] == jnp.arange(MAIN, dtype=F32)[None, :, None])
        .astype(BF)
        .reshape(EXPERTS * MAIN, 512)
    )
    tail_pick = (
        (rank[:, None, :] == jnp.arange(MAIN, CAP, dtype=F32)[None, :, None])
        .astype(BF)
        .reshape(EXPERTS * TAIL, 512)
    )
    all_pick = jnp.concatenate(
        [main_pick.reshape(EXPERTS, MAIN, 512), tail_pick.reshape(EXPERTS, TAIL, 512)], axis=1
    )

    def pick_rows(operand):
        return (
            dot(main_pick, operand).astype(BF).reshape(EXPERTS, MAIN, 512),
            pack_tail(dot(tail_pick, operand).astype(BF)),
        )

    def place_rows(main, tail):
        return dot_first(main_pick, main.reshape(EXPERTS * MAIN, 512)) + dot_first(
            tail_pick, unpack_tail(tail)
        )

    token_full = token_rows.astype(F32)
    inverse_attention = lax.rsqrt(jnp.mean(token_full * token_full, axis=1) + EPS)
    normed_exact = token_full * inverse_attention[:, None] * gain_full[None, :]
    normed = normed_exact.astype(BF)
    qkv = to_heads(dot(normed, w_group).astype(BF))
    cot_main, cot_tail, attended, query, key, lse = attend(
        qkv, cosine, sine, gains, *pick_rows(cotangent)
    )
    attended_rows = gather_attended(attended)

    token_float = tokens.astype(F32)
    hidden = token_float + dot(attended_rows, w_all)
    scaled_hidden = hidden * experts_norm_gain
    partial_stats = jnp.concatenate(
        [
            lax.dot_general(
                w_router.astype(F32),
                scaled_hidden,
                (((0,), (1,)), ((), ())),
                precision=EXACT,
                preferred_element_type=F32,
            ),
            jnp.sum(hidden * hidden, axis=1)[None],
            jnp.zeros((7, 512), F32),
        ],
        axis=0,
    )
    stats = jnp.sum(row_stack(partial_stats, 7), axis=0)
    inverse_experts = lax.rsqrt(stats[EXPERTS] / WIDTH + EPS)
    logits = stats[:EXPERTS] * inverse_experts[None, :]
    unit_experts = hidden * inverse_experts[:, None]
    experts_input = (unit_experts * experts_norm_gain).astype(BF)
    named_t = rank >= 0
    largest = jnp.max(jnp.where(named_t, logits, -jnp.inf), axis=0, keepdims=True)
    shifted = jnp.where(named_t, jnp.exp(jnp.where(named_t, logits - largest, 0.0)), 0.0)
    gates = shifted / jnp.sum(shifted, axis=0, keepdims=True)
    slot_gates = jnp.sum(all_pick.astype(F32) * gates[:, None, :], axis=2)

    send_main, send_tail = pick_rows(experts_input)
    in_main, in_tail = to_experts(
        send_main, jnp.concatenate([send_tail, aux_rows([slot_gates])], axis=1), 8
    )
    in_main, in_tail, normed = after(in_main, in_tail, normed)
    before, behind = hop_col(normed, 1), hop_col(normed, 3)
    gate_of = join_values(aux_value(in_tail[:, 0, 16:], 0))[:, None]
    (
        slot_in,
        slot_grad,
        out_main,
        out_tail,
        back_main,
        back_tail,
        acts,
        gate_up_grads,
        slot_gate_grad,
        slot_inner,
    ) = run_expert(
        in_main.reshape(16 * MAIN, WIDTH),
        join_tail(in_tail[:, :, :16]),
        cot_main.reshape(16 * MAIN, WIDTH),
        join_tail(cot_tail),
        gate_of,
        up_ws + down_ws,
    )
    aux = jnp.broadcast_to(
        aux_rows([split_values(slot_gate_grad[:, 0]), split_values(slot_inner[:, 0])])[:, None],
        (16, 4, 16, HEAD),
    )
    back_main, back_tail, up_grads, down_grads = return_rows(
        back_main.reshape(16, MAIN, WIDTH),
        jnp.concatenate([split_tail(back_tail), aux], axis=2),
        slot_in,
        slot_grad,
        gate_up_grads,
        acts,
    )
    first_back, second_back = inverse_pairs(FIRST_HOP), inverse_pairs(SECOND_HOP)
    up_grads, down_grads = up_grads.astype(BF), down_grads.astype(BF)
    up_1, up_2 = hop(up_grads[0], first_back), hop(up_grads[1], second_back)
    down_1, down_2 = hop(down_grads[0], first_back), hop(down_grads[1], second_back)

    back_tail, before, behind = after(back_tail, before, behind)
    across, beyond = hop_col(before[:256], 1), hop_col(behind[256:], 3)
    back_aux = back_tail[:, 16:]
    picked = all_pick.astype(F32)
    gate_grad = jnp.sum(picked * aux_value(back_aux, 0)[:, :, None], axis=1)
    inner = jnp.sum(picked * aux_value(back_aux, 1)[:, :, None], axis=(0, 1))
    logit_grad = gates * (gate_grad - jnp.sum(gates * gate_grad, axis=0, keepdims=True))
    experts_input_grad = place_rows(back_main, back_tail[:, :16]) + lax.dot_general(
        logit_grad,
        w_router.astype(F32),
        (((0,), (1,)), ((), ())),
        precision=EXACT,
        preferred_element_type=F32,
    )
    mean_experts = (inner + jnp.sum(logit_grad * logits, axis=0)) / WIDTH
    cot_float = cotangent.astype(F32)
    middle_grad = cot_float + inverse_experts[:, None] * (
        experts_input_grad * experts_norm_gain - unit_experts * mean_experts[:, None]
    )
    router_part = lax.dot_general(
        logit_grad,
        experts_input.astype(F32),
        (((1,), (0,)), ((), ())),
        precision=EXACT,
        preferred_element_type=F32,
    )
    experts_gain_part = jnp.sum(experts_input_grad * unit_experts, axis=0)
    attended_grad = middle_grad.astype(BF)
    out_part = dot_first(attended_rows, attended_grad).astype(BF).reshape(16, HEAD, 512)
    small_part = jnp.concatenate(
        [
            router_part.reshape(256, HEAD),
            experts_gain_part.reshape(4, HEAD),
            jnp.zeros((124, HEAD), F32),
        ],
        axis=0,
    )
    core = lax.axis_index("dp") % 2
    grad_parts, out_other, small_other = spread_attended_grad(
        dot_last(attended_grad, w_all).astype(BF), out_part, small_part
    )
    out_half = (
        lax.dynamic_slice_in_dim(out_part, core * 64, 64, 1).astype(F32)
        + out_other.astype(F32)
    ).astype(BF)
    small = (small_part + small_other).reshape(16, 24, HEAD)
    out_main, out_tail, qkv_grad, head_gain_part, qkv_part = attend_back(
        [qkv, query, key, lse, grad_parts, cosine, sine, gains]
        + [normed, before, behind, across, beyond],
        out_main.reshape(16, MAIN, WIDTH),
        split_tail(out_tail),
    )
    qkv_part = qkv_part.reshape(4, 512, 384)
    qkv_grad, qkv_other = from_heads(qkv_grad, qkv_part)
    qkv_half = (
        lax.dynamic_slice_in_dim(qkv_part, core * 256, 256, 1).astype(F32)
        + qkv_other.astype(F32)
    ).astype(BF)
    normed_grad_part = dot_last(qkv_grad, w_group)
    stat_part = jnp.sum(normed_grad_part * normed_exact, axis=1)
    normed_grad, row_stats, qkv_pieces, out_pieces, small_pieces = spread_features(
        normed_grad_part.astype(BF),
        jnp.concatenate([stat_part.reshape(4, HEAD), head_gain_part[:4]], axis=0),
        qkv_half,
        out_half,
        small,
    )
    normed_grad = jnp.sum(normed_grad.astype(F32), axis=0)
    row_stats = jnp.sum(row_stats, axis=0)
    mean_attention = row_stats[:4].reshape(512) / WIDTH
    unit_attention = token_float * inverse_attention[:, None]
    token_grad = middle_grad + inverse_attention[:, None] * (
        normed_grad * attention_norm_gain - unit_attention * mean_attention[:, None]
    )
    attention_gain_part = jnp.sum(normed_grad * unit_attention, axis=0)

    qkv_piece = (
        jnp.sum(qkv_pieces.astype(F32), axis=0).transpose(1, 0, 2).reshape(64, 1536).astype(BF)
    )
    out_piece = jnp.sum(out_pieces.astype(F32), axis=0).astype(BF)
    qkv_piece, up_1, up_2, down_1, down_2 = after(qkv_piece, up_1, up_2, down_1, down_2)
    is_lower = upper == 0
    grad_gate_up = jnp.stack(
        [jnp.where(is_lower, up_1, up_2), jnp.where(is_lower, up_2, up_1)]
    ).astype(F32)
    grad_down = jnp.stack(
        [jnp.where(is_lower, down_1, down_2), jnp.where(is_lower, down_2, down_1)]
    ).astype(F32)
    qkv_total, out_total, small_total, late = collect_sums(
        qkv_piece,
        out_piece,
        jnp.sum(small_pieces, axis=0),
        jnp.concatenate([attention_gain_part.reshape(4, HEAD), row_stats[4:]], axis=0),
    )
    small_total = small_total.reshape(384, HEAD)
    late = jnp.sum(late, axis=0)
    weight = all_pick.astype(F32) * gates[:, None, :]
    weight_high = weight.astype(BF)
    weight_low = (weight - weight_high.astype(F32)).astype(BF)
    out_tail_rows = unpack_tail(out_tail)
    output = hidden
    for part in (weight_high, weight_low):
        output = (
            output
            + dot_first(
                part[:, :MAIN].reshape(EXPERTS * MAIN, 512),
                out_main.reshape(EXPERTS * MAIN, 512),
            )
            + dot_first(part[:, MAIN:].reshape(EXPERTS * TAIL, 512), out_tail_rows)
        )
    output = output.astype(BF)

    return (
        output,
        token_grad.astype(BF),
        late[:4].reshape(512),
        small_total[256:260].reshape(512),
        qkv_total.astype(F32).reshape(512, 4, 384),
        late[4],
        late[5],
        out_total.astype(F32).reshape(512, 512),
        small_total[:256].reshape(EXPERTS, 512).T,
        grad_gate_up.reshape(2, WIDTH, 2, 256),
        grad_down,
    )


def solution(mesh):
    tokens_like = P(("dp", "col"), "row")
    up_like = P(("dp", "col"), None, None, "row")
    down_like = P(("dp", "col"), "row", None)
    return jax.shard_map(
        shards,
        mesh=mesh,
        in_specs=(
            tokens_like,
            P("dp", "row"),
            P(("dp", "col"), None),
            P("row"),
            P("row"),
            P("row", "col", None),
            P(),
            P(),
            P("col", "row"),
            P("row", None),
            up_like,
            down_like,
            tokens_like,
        ),
        out_specs=(
            tokens_like,
            tokens_like,
            P("row"),
            P("row"),
            P("row", "col", None),
            P(),
            P(),
            P("col", "row"),
            P("row", None),
            up_like,
            down_like,
        ),
        check_vma=False,
    )
```

```python
import jax
import jax.numpy as jnp
from jax import lax
from jax.experimental import pallas as pl
from jax.experimental.pallas import tpu as pltpu
from jax.sharding import PartitionSpec as P

WIDTH = 2048
HEAD = 128
EXPERTS = 64
CAP = 36
MAIN = 32
TAIL = 8
USED = CAP - MAIN
SEQ = 2048
EPS = 1e-06
THETA = 10000.0
EXACT = lax.Precision.HIGHEST
MESH = pl.DeviceIdType.MESH
SIZES = (4, 2, 4, 4)
BF = jnp.bfloat16
F32 = jnp.float32
ROWS = [(0, 0, d, 0) for d in (2, 1, 3)]
COLS = [(0, 0, 0, d) for d in (2, 1, 3)]
SIBLING = (0, 1, 0, 0)
PLANE = [(0, 0, i, (i + s) % 4) for s in range(4) for i in range(4) if (i, s) != (0, 0)]
CUBE = [
    (i, 0, (i + s) % 4, (i + t) % 4)
    for s in range(4)
    for t in range(4)
    for i in range(4)
    if (i, s, t) != (0, 0, 0)
]
SOURCES = [(i, 0, 0, (i + s) % 4) for s in range(4) for i in range(4) if (i, s) != (0, 0)]
LINES = [(d, 0, 0, 0) for d in (2, 1, 3)]
OTHERS = [
    (a, k, 0, d) for a in range(4) for k in range(2) for d in range(4) if (a, k, d) != (0, 0, 0)
]


def shape(dims, dtype=BF):
    return jax.ShapeDtypeStruct(dims, dtype)


def here():
    group = lax.axis_index("dp")
    return (group // 2, group % 2, lax.axis_index("row"), lax.axis_index("col"))


class Hop:
    def __init__(self, to, origin):
        self.to, self.origin = to, origin


ONE_WAY = Hop(
    lambda p: (p[0], 1 - p[2] % 2, 2 * p[1] + p[2] // 2, p[3]),
    lambda p: (p[0], p[2] // 2, 2 * (p[2] % 2) + 1 - p[1], p[3]),
)
OTHER_WAY = Hop(
    lambda p: (p[0], p[2] % 2, 2 * p[1] + 1 - p[2] // 2, p[3]),
    lambda p: (p[0], p[2] // 2, 2 * (1 - p[2] % 2) + p[1], p[3]),
)


class Links:
    def __init__(self, send, arrive):
        self.send, self.arrive = send, arrive


def moved(place, offset):
    if isinstance(offset, Hop):
        return offset.to(place)
    return tuple((p + o) % n for p, o, n in zip(place, offset, SIZES))


def device(place):
    return (place[0] * 2 + place[1], place[2], place[3])


def exchange(
    inputs,
    outputs,
    sends,
    kept,
    call_id,
    micros=30,
    work=None,
    work_in=(),
    work_out=(),
    work_scratch=(),
    stages=(),
    deferred=(),
):
    offsets = sorted({s[0] for s in sends if not isinstance(s[0], Hop)})
    hops = {id(s[0]): s[0] for s in sends if isinstance(s[0], Hop)}.values()
    n_in, n_out, n_send = len(inputs), len(outputs), len(sends)
    m_in, m_out = len(work_in), len(work_out)

    def kernel(*refs):
        ins, refs = refs[:n_in], refs[n_in:]
        worked, refs = refs[:m_in], refs[m_in:]
        outs, refs = refs[:n_out], refs[n_out:]
        made, refs = refs[:m_out], refs[m_out:]
        send_sem, recv_sem, kept_sem = refs[:3]
        staged, refs = refs[3 : 3 + len(kept)], refs[3 + len(kept) :]
        special = {"work": worked, "made": made, "scratch": refs}
        me = here()
        barrier = pltpu.get_barrier_semaphore()
        greeted = [moved(me, offset) for offset in offsets]
        for way in hops:
            greeted += [way.to(me), way.origin(me)]
        for peer in greeted:
            pl.semaphore_signal(barrier, inc=1, device_id=device(peer), device_id_type=MESH)
        local = []
        for index, (i, take, o, put, _) in enumerate(kept):
            source, target = take(ins[i], me), put(outs[o], me)
            local.append(
                (
                    pltpu.make_async_copy(source, staged[index], kept_sem.at[index, 0]),
                    pltpu.make_async_copy(staged[index], target, kept_sem.at[index, 1]),
                )
            )
            local[-1][0].start()
        pl.semaphore_wait(barrier, len(greeted))
        copies, arrived = {}, set()

        def arrive(index):
            if index not in arrived:
                arrived.add(index)
                copies[index].wait_recv()

        def named(group, index):
            return special[index[0]][index[1]] if isinstance(index, tuple) else group[index]

        def start(index):
            offset, i, take, o, put = sends[index][:5]
            needs = sends[index][5] if len(sends[index]) > 5 else None
            for need in needs or ():
                if need >= 0:
                    arrive(need)
                elif need not in arrived:
                    arrived.add(need)
                    local[-need - 1][1].wait()
            peer = moved(me, offset)
            copies[index] = pltpu.make_async_remote_copy(
                src_ref=take(named(ins if needs is None else outs, i), me, peer),
                dst_ref=put(named(outs, o), me, peer),
                send_sem=send_sem.at[index],
                recv_sem=recv_sem.at[index],
                device_id=device(peer),
                device_id_type=MESH,
            )
            copies[index].start()

        links = Links(start, arrive)
        parts = work(links, *worked, *made, *refs) if stages else ()
        first = [i for i in range(n_send) if len(sends[i]) < 6 and i not in deferred]
        for index in first:
            start(index)
        for load, store in local:
            load.wait()
            store.start()
        for index in range(n_send):
            if index in first or index in deferred:
                continue
            for part, at in zip(parts, stages):
                if at == index:
                    part()
            start(index)
        if work is not None and not stages:
            work(links, *worked, *made, *refs)
        for index in range(n_send):
            arrive(index)
        for copy in copies.values():
            copy.wait_send()
        for index, copy in enumerate(local):
            if -index - 1 not in arrived:
                copy[1].wait()

    return pl.pallas_call(
        kernel,
        out_shape=list(outputs) + list(work_out),
        in_specs=[pl.BlockSpec(memory_space=pl.ANY)] * n_in
        + [pl.BlockSpec(memory_space=pltpu.VMEM)] * m_in,
        out_specs=[pl.BlockSpec(memory_space=pl.ANY)] * n_out
        + [pl.BlockSpec(memory_space=pltpu.VMEM)] * m_out,
        scratch_shapes=[
            pltpu.SemaphoreType.DMA((n_send,)),
            pltpu.SemaphoreType.DMA((n_send,)),
            pltpu.SemaphoreType.DMA((max(1, len(kept)), 2)),
            *[pltpu.VMEM(k[4], inputs[k[0]].dtype) for k in kept],
            *work_scratch,
        ],
        compiler_params=pltpu.CompilerParams(
            collective_id=call_id,
            has_side_effects=True,
            vmem_limit_bytes=(8 if work is None else 56) * 2**20,
        ),
        cost_estimate=pl.CostEstimate(
            flops=0, bytes_accessed=micros * 3_500_000, transcendentals=0
        ),
    )(*inputs, *work_in)


def rows(start, size):
    return pl.ds(pl.multiple_of(start, size), size)


def eighth(size):
    me = here()
    return rows((me[1] * 4 + me[0]) * size, size)


def half(size):
    return rows(here()[1] * size, size)


class Sends(list):
    def add(self, group, take, o, put=None, i=None, needs=None):
        first = len(self)
        for offset in group:
            if needs is None:
                self.append((offset, i, take, o, put))
            else:
                view = lambda ref, me, p: take(ref, me)
                self.append((offset, o, view, o, view, needs))
        return list(range(first, len(self)))


def early_kernel(links, up_ref, rank_ref, cot_ref, up_1, up_2, main_ref, tail_ref):
    upper = lax.axis_index("row") // 2

    def unpack(which, target):
        def part(step, carry):
            span = pl.ds(pl.multiple_of(step * 256, 256), 256)
            target[span, :256] = up_ref[which, span, 0, :]
            target[span, 256:] = up_ref[which, span, 1, :]
            return carry

        return lambda: lax.fori_loop(0, WIDTH // 256, part, 0)

    def pick():
        def part(step, carry):
            ranks = rank_ref[pl.ds(pl.multiple_of(step * 8, 8), 8), :]
            slots = lax.broadcasted_iota(jnp.int32, (8, MAIN + TAIL, 512), 1).astype(F32)
            chosen = (ranks[:, None, :] == slots).astype(F32).reshape(8 * (MAIN + TAIL), 512)
            rows_of = jnp.dot(chosen.astype(BF), cot_ref[...], preferred_element_type=F32)
            rows_of = rows_of.reshape(8, MAIN + TAIL, 512)
            group = pl.ds(pl.multiple_of(step * 8, 8), 8)
            main_ref[group] = rows_of[:, :MAIN].astype(BF)
            tail_ref[group] = rows_of[:, MAIN:].astype(BF)
            return carry

        lax.fori_loop(0, EXPERTS // 8, part, 0)

    return [unpack(upper, up_1), unpack(1 - upper, up_2), pick]


def gather_inputs(tokens, w_qkv, w_out, w_down, small_int, small_float, early):
    outputs = [
        shape((512, WIDTH)),
        shape((4, 512, 1536)),
        shape((4, 4, HEAD), jnp.int32),
        shape((4, 4, HEAD), F32),
        shape((4, 4, HEAD, 512)),
        shape((256, WIDTH)),
        shape((256, WIDTH)),
    ]
    sends = Sends()
    own_cols = lambda me: rows(me[3] * 384, 384)
    low, high = pl.ds(0, 2), pl.ds(2, 2)
    first = sends.add(
        ROWS,
        lambda s, me, p: s.at[eighth(64), rows(p[2] * 384, 384)],
        1,
        lambda o, me, p: o.at[me[2], eighth(64), own_cols(me)],
        1,
    )
    sends.add(ROWS, lambda s, me, p: s, 0, lambda o, me, p: o.at[:, rows(me[2] * 512, 512)], 0)
    sends.add(ROWS, lambda s, me, p: s, 2, lambda o, me, p: o.at[me[2]], 2)
    sends.add(ROWS, lambda s, me, p: s, 3, lambda o, me, p: o.at[me[2]], 3)
    sends.append((ONE_WAY, 5, lambda s, me, p: s.at[me[2] // 2], 5, lambda o, me, p: o))
    sends.append((OTHER_WAY, 5, lambda s, me, p: s.at[1 - me[2] // 2], 6, lambda o, me, p: o))
    out_z = sends.add(COLS, lambda o, me: o.at[low, me[3], eighth(16)], 4, needs=[-2])
    out_y = sends.add(LINES, lambda o, me: o.at[high, me[3], eighth(16)], 4, needs=[-2])
    stages = [len(sends)]
    by_z = sends.add(
        COLS, lambda o, me: o.at[low, eighth(64), own_cols(me)], 1, needs=[-1] + first
    )
    by_y = sends.add(LINES, lambda o, me: o.at[high, eighth(64), own_cols(me)], 1, needs=first)
    sends.add(LINES, lambda o, me: o.at[low, eighth(64), own_cols(me)], 1, needs=first)
    sends.add(COLS, lambda o, me: o.at[high, eighth(64), own_cols(me)], 1, needs=first)
    stages.append(len(sends))
    last_z, last_y = {0: [len(sends) - 6 + i for i in range(3)]}, {0: list(range(len(sends) - 3, len(sends)))}
    for d in (1, 3, 2):
        came = by_z[[offset[3] for offset in COLS].index(d)]
        cols = lambda me, d=d: rows((me[3] + 4 - d) % 4 * 384, 384)
        last_z[d] = sends.add(
            LINES,
            lambda o, me, cols=cols: o.at[low, eighth(64), cols(me)],
            1,
            needs=[came],
        )
        came = by_y[[offset[0] for offset in LINES].index(d)]
        span = lambda me, d=d: rows((me[1] * 4 + (me[0] + 4 - d) % 4) * 64, 64)
        last_y[d] = sends.add(
            COLS,
            lambda o, me, span=span: o.at[high, span(me), own_cols(me)],
            1,
            needs=[came],
        )
    out_zy = sends.add(LINES, lambda o, me: o.at[low, :, eighth(16)], 4, needs=out_z)
    out_yz = sends.add(COLS, lambda o, me: o.at[high, me[3], half(64)], 4, needs=out_y)
    stages.append(len(sends))
    pair = [SIBLING]
    sends.add(pair, lambda o, me: o.at[low, eighth(64)], 1, needs=by_z)
    sends.add(pair, lambda o, me: o.at[high, half(256), own_cols(me)], 1, needs=by_y)
    for d in (1, 3, 2):
        line = [offset[0] for offset in LINES].index(d)
        span = lambda me, d=d: rows((me[1] * 4 + (me[0] + 4 - d) % 4) * 64, 64)
        sends.add(
            pair,
            lambda o, me, span=span: o.at[low, span(me)],
            1,
            needs=[numbers[line] for numbers in last_z.values()],
        )
        col = [offset[3] for offset in COLS].index(d)
        cols = lambda me, d=d: rows((me[3] + 4 - d) % 4 * 384, 384)
        sends.add(
            pair,
            lambda o, me, cols=cols: o.at[high, half(256), cols(me)],
            1,
            needs=[numbers[col] for numbers in last_y.values()],
        )
    sends.add(pair, lambda o, me: o.at[low, :, half(64)], 4, needs=out_zy)
    sends.add(pair, lambda o, me: o.at[high, :, half(64)], 4, needs=out_yz)
    kept = [
        (
            1,
            lambda s, me: s.at[eighth(64), rows(me[2] * 384, 384)],
            1,
            lambda o, me: o.at[me[2], eighth(64), own_cols(me)],
            (64, 384),
        ),
        (
            4,
            lambda s, me: s.at[:, eighth(16)],
            4,
            lambda o, me: o.at[:, me[3], eighth(16)],
            (4, 16, 512),
        ),
        (0, lambda s, me: s, 0, lambda o, me: o.at[:, rows(me[2] * 512, 512)], (512, 512)),
        (2, lambda s, me: s, 2, lambda o, me: o.at[me[2]], (4, HEAD)),
        (3, lambda s, me: s, 3, lambda o, me: o.at[me[2]], (4, HEAD)),
    ]
    return exchange(
        [
            tokens,
            w_qkv.reshape(512, 1536),
            small_int,
            small_float,
            w_out.reshape(4, HEAD, 512),
            w_down,
        ],
        outputs,
        sends,
        kept,
        0,
        work=early_kernel,
        work_in=early,
        work_out=[
            shape((WIDTH, 512)),
            shape((WIDTH, 512)),
            shape((EXPERTS, MAIN, 512)),
            shape((EXPERTS, TAIL, 512)),
        ],
        stages=stages,
    )


def to_heads(qkv):
    take = lambda s, me, p: s.at[:, rows(p[3] * 384, 384)]
    put = lambda o, me, p: o.at[rows(me[3] * 512, 512)]
    return exchange(
        [qkv],
        [shape((SEQ, 384))],
        [(offset, 0, take, 0, put) for offset in COLS],
        [(0, lambda s, me: take(s, me, me), 0, lambda o, me: put(o, me, me), (512, 384))],
        1,
    )[0]


def combine_kernel(links, hidden_ref, main_pick, tail_pick, main_ref, tail_ref, out_ref):
    total = hidden_ref[...]
    total = total + lax.dot_general(
        main_pick[...], main_ref[...], FIRST, preferred_element_type=F32
    )
    total = total + lax.dot_general(
        tail_pick[...], tail_ref[...], FIRST, preferred_element_type=F32
    )
    out_ref[...] = total.astype(BF)


def from_heads(grads, combine):
    take = lambda s, me, p: s.at[rows(p[3] * 512, 512)]
    put = lambda o, me, p: o.at[:, rows(me[3] * 384, 384)]
    return exchange(
        [grads],
        [shape((512, 1536))],
        [(offset, 0, take, 0, put) for offset in COLS],
        [(0, lambda s, me: take(s, me, me), 0, lambda o, me: put(o, me, me), (512, 384))],
        2,
        micros=300,
        work=combine_kernel,
        work_in=combine,
        work_out=[shape((512, 512))],
    )


def gather_attended(attended):
    take = lambda s, me, p: s.at[rows(p[3] * 512, 512)]
    put = lambda o, me, p: o.at[:, rows((me[2] * 4 + me[3]) * HEAD, HEAD)]
    return exchange(
        [attended],
        [shape((512, WIDTH))],
        [(offset, 0, take, 0, put) for offset in PLANE],
        [(0, lambda s, me: take(s, me, me), 0, lambda o, me: put(o, me, me), (512, HEAD))],
        3,
    )[0]


def spread_attended_grad(partial, out_part, small_part):
    take = lambda s, me, p: s.at[:, rows((p[2] * 4 + p[3]) * HEAD, HEAD)]
    put = lambda o, me, p: o.at[me[2], rows(me[3] * 512, 512)]
    return exchange(
        [partial, out_part, small_part],
        [shape((4, SEQ, HEAD)), shape((16, 64, 512)), shape(small_part.shape, F32)],
        [(offset, 0, take, 0, put) for offset in PLANE]
        + [
            (SIBLING, 1, lambda s, me, p: s.at[:, rows(p[1] * 64, 64)], 1, lambda o, me, p: o),
            (SIBLING, 2, lambda s, me, p: s, 2, lambda o, me, p: o),
        ],
        [(0, lambda s, me: take(s, me, me), 0, lambda o, me: put(o, me, me), (512, HEAD))],
        4,
    )


def row_stack(operand, call_id):
    take = lambda s, me, p: s
    put = lambda o, me, p: o.at[me[2]]
    return exchange(
        [operand],
        [shape((4,) + operand.shape, operand.dtype)],
        [(offset, 0, take, 0, put) for offset in ROWS],
        [(0, lambda s, me: s, 0, lambda o, me: put(o, me, me), operand.shape)],
        call_id,
    )[0]


def sum_weights_kernel(
    links, first, normed_ref, grad_ref, piece_ref, their_half, came, half, spread
):
    core, y = lax.axis_index("dp") % 2, lax.axis_index("dp") // 2

    def product(start):
        return lax.dot_general(
            normed_ref[:, rows(start, 256)], grad_ref[...], FIRST, preferred_element_type=F32
        )

    for r in range(4):
        their_half[r] = product(r * 512 + (1 - core) * 256).astype(BF)
        links.send(first + r)
    for r in range(4):
        mine = product(r * 512 + core * 256)
        links.arrive(first + r)
        half[r] = (mine + came[r].astype(F32)).astype(BF)
        for line in range(3):
            links.send(first + 4 + 3 * r + line)
        spread[y, r] = half[r, rows(y * 64, 64), :]
    for r in range(4):
        for line in range(3):
            links.arrive(first + 4 + 3 * r + line)
        total = spread[0, r].astype(F32)
        for source in range(1, 4):
            total = total + spread[source, r].astype(F32)
        piece_ref[r] = total.astype(BF)


def spread_features(partial, stats, out_half, small, normed, grads):
    take = lambda s, me, p: s.at[:, rows(p[2] * 512, 512)]
    put = lambda o, me, p: o.at[me[2]]
    whole = lambda s, me, p: s
    take_out = lambda s, me, p: s.at[p[0] * 4 + p[3]]
    put_out = lambda o, me, p: o.at[me[0] * 4 + me[3]]
    keep = lambda i, take, put, dims: (
        i,
        lambda s, me: take(s, me, me),
        i,
        lambda o, me: put(o, me, me),
        dims,
    )
    sends = (
        [(offset, 0, take, 0, put) for offset in ROWS]
        + [(offset, 1, whole, 1, put) for offset in ROWS]
        + [(offset, 2, take_out, 2, put_out) for offset in SOURCES]
        + [(offset, 3, take_out, 3, put_out) for offset in SOURCES]
    )
    first = len(sends)
    for r in range(4):
        view = lambda ref, me, p, r=r: ref.at[r]
        sends.append((SIBLING, ("scratch", 0), view, ("scratch", 1), view))
    for r in range(4):
        for offset in LINES:
            sends.append(
                (
                    offset,
                    ("scratch", 2),
                    lambda s, me, p, r=r: s.at[r, rows(p[0] * 64, 64)],
                    ("scratch", 3),
                    lambda o, me, p, r=r: o.at[me[0], r],
                )
            )
    return exchange(
        [partial, stats, out_half, small],
        [
            shape((4, 512, 512)),
            shape((4,) + stats.shape, F32),
            shape((16, 64, 512)),
            shape((16,) + small.shape[1:], F32),
        ],
        sends,
        [
            keep(0, take, put, (512, 512)),
            keep(1, whole, put, stats.shape),
            keep(2, take_out, put_out, (64, 512)),
            keep(3, take_out, put_out, small.shape[1:]),
        ],
        5,
        work=lambda links, *refs: sum_weights_kernel(links, first, *refs),
        work_in=[normed, grads],
        work_out=[shape((4, 64, 1536))],
        work_scratch=[pltpu.VMEM((4, 256, 1536), BF)] * 3 + [pltpu.VMEM((4, 4, 64, 1536), BF)],
        deferred=range(first, len(sends)),
    )


def expert_at(place):
    return place[0] * 16 + (place[2] // 2) * 8 + place[3] * 2 + place[2] % 2


def to_experts(main, tail, call_id, **work):
    take = lambda s, me, p: s.at[expert_at(p)]
    put_main = lambda o, me, p: o.at[me[0] * 4 + me[3], :, rows(me[2] * 512, 512)]
    put_tail = lambda o, me, p: o.at[me[0] * 4 + me[3], :, rows(me[2] * 512, 512)]
    sends = []
    for offset in CUBE:
        sends.append((offset, 0, take, 0, put_main))
        sends.append((offset, 1, take, 1, put_tail))
    return exchange(
        [main, tail],
        [shape((16, MAIN, WIDTH)), shape((16, TAIL, WIDTH))],
        sends,
        [
            (0, lambda s, me: take(s, me, me), 0, lambda o, me: put_main(o, me, me), (MAIN, 512)),
            (1, lambda s, me: take(s, me, me), 1, lambda o, me: put_tail(o, me, me), (TAIL, 512)),
        ],
        call_id,
        **work,
    )


def from_experts(main, tail, call_id, first_sends=(), **work):
    take_main = lambda s, me, p: s.at[p[0] * 4 + p[3], :, rows(p[2] * 512, 512)]
    take_tail = lambda s, me, p: s.at[p[0] * 4 + p[3], :, rows(p[2] * 512, 512)]
    put = lambda o, me, p: o.at[expert_at(me)]
    sends = list(first_sends)
    for offset in CUBE:
        sends.append((offset, 0, take_main, 0, put))
        sends.append((offset, 1, take_tail, 1, put))
    return exchange(
        [main, tail],
        [shape((EXPERTS, MAIN, 512)), shape((EXPERTS, TAIL, 512))],
        sends,
        [
            (0, lambda s, me: take_main(s, me, me), 0, lambda o, me: put(o, me, me), (MAIN, 512)),
            (1, lambda s, me: take_tail(s, me, me), 1, lambda o, me: put(o, me, me), (TAIL, 512)),
        ],
        call_id,
        **work,
    )


def collect_sums(qkv_piece, out_piece, small_piece, late):
    put_qkv = lambda o, me, p: o.at[me[1], me[0]]
    put_out = lambda o, me, p: o.at[me[0], me[1]]
    put_small = lambda o, me, p: o.at[me[0] * 4 + me[3]]
    put_late = lambda o, me, p: o.at[(me[0] * 2 + me[1]) * 4 + me[3]]
    whole = lambda s, me, p: s
    sends = Sends()
    heads = sends.add(
        PLANE,
        lambda s, me, p: s.at[p[2], :, rows(p[3] * 384, 384)],
        ("scratch", 0),
        lambda o, me, p: o.at[me[3], me[2]],
        ("work", 0),
    )
    out_sent = sends.add(LINES, whole, 0, put_out, 0)
    sends.add([SIBLING], whole, 0, put_out, 0)
    sends.add(SOURCES, whole, 1, put_small, 1)
    sends.add(OTHERS, whole, 2, put_late, 2)
    later = len(sends)
    qkv_sent = sends.add(LINES, whole, ("made", 0), put_qkv, ("scratch", 1))
    sends.add([SIBLING], whole, ("made", 0), put_qkv, ("scratch", 1))
    relays = []
    for index in (1, 2, 0):
        origin = lambda me, d=LINES[index][0]: (me[0] + 4 - d) % 4
        view = lambda ref, me, p, origin=origin: ref.at[origin(me), me[1]]
        relays.append((out_sent[index], len(sends)))
        sends.append((SIBLING, 0, view, 0, view, [out_sent[index]]))
    for index in (1, 2, 0):
        origin = lambda me, d=LINES[index][0]: (me[0] + 4 - d) % 4
        view = lambda ref, me, p, origin=origin: ref.at[me[1], origin(me)]
        relays.append((qkv_sent[index], len(sends)))
        sends.append((SIBLING, ("made", 0), view, ("made", 0), view, [qkv_sent[index]]))

    def work(links, piece_ref, total_ref, spread, mine):
        group, row, col = lax.axis_index("dp"), lax.axis_index("row"), lax.axis_index("col")
        spread[col, row] = piece_ref[row, :, rows(col * 384, 384)]
        for number in heads:
            links.arrive(number)
        for head in range(4):
            total = spread[0, head].astype(F32)
            for source in range(1, 4):
                total = total + spread[source, head].astype(F32)
            mine[:, head * 384 : (head + 1) * 384] = total.astype(BF)
        for number in range(later, later + 4):
            links.send(number)
        total_ref[group % 2, group // 2] = mine[...]
        for came, number in relays:
            links.arrive(came)
            links.send(number)

    return exchange(
        [out_piece, small_piece, late],
        [
            shape((4, 2, 64, 512)),
            shape((16,) + small_piece.shape, F32),
            shape((32,) + late.shape, F32),
        ],
        sends,
        [
            (0, lambda s, me: s, 0, lambda o, me: put_out(o, me, me), (64, 512)),
            (1, lambda s, me: s, 1, lambda o, me: put_small(o, me, me), small_piece.shape),
            (2, lambda s, me: s, 2, lambda o, me: put_late(o, me, me), late.shape),
        ],
        12,
        work=work,
        work_in=[qkv_piece],
        work_out=[shape((2, 4, 64, 1536))],
        work_scratch=[pltpu.VMEM((4, 4, 64, 384), BF), pltpu.VMEM((64, 1536), BF)],
        deferred=range(later, len(sends)),
    )


BLOCK = 256
SCALE = HEAD ** (-0.5)
LAST = (((1,), (1,)), ((), ()))
FIRST = (((0,), (0,)), ((), ()))


def swapped(operand):
    return pltpu.roll(operand, HEAD // 2, 1)


def attend_kernel(
    links,
    qkv_ref,
    position_ref,
    frequency_ref,
    gain_ref,
    out_ref,
    query_ref,
    key_ref,
    lse_ref,
    cos_ref,
    sin_ref,
):
    def prepare(step, carry):
        span = pl.ds(pl.multiple_of(step * BLOCK, BLOCK), BLOCK)
        angles = position_ref[span, :] * frequency_ref[0:1, :]
        cos_ref[span, :] = jnp.cos(angles)
        sin_ref[span, :] = jnp.sin(angles) * frequency_ref[1:2, :]
        for part, target in ((0, query_ref), (1, key_ref)):
            raw = qkv_ref[span, part * HEAD : (part + 1) * HEAD].astype(F32)
            scaled = (
                raw
                * lax.rsqrt(jnp.mean(raw * raw, axis=1, keepdims=True) + EPS)
                * gain_ref[part : part + 1, :]
            )
            target[span, :] = (scaled * cos_ref[span, :] + swapped(scaled) * sin_ref[span, :]).astype(
                BF
            )
        return carry

    lax.fori_loop(0, SEQ // BLOCK, prepare, 0)

    def block(step, carry):
        span = pl.ds(pl.multiple_of(step * BLOCK, BLOCK), BLOCK)
        scores = (
            lax.dot_general(query_ref[span, :], key_ref[...], LAST, preferred_element_type=F32)
            * SCALE
        )
        largest = jnp.max(scores, axis=1, keepdims=True)
        weights = jnp.exp(scores - largest)
        total = jnp.sum(weights, axis=1, keepdims=True)
        mixed = jnp.dot(
            weights.astype(BF), qkv_ref[:, 2 * HEAD :], preferred_element_type=F32
        )
        out_ref[span, :] = (mixed / total).astype(BF)
        lse_ref[span, :] = largest + jnp.log(total)
        return carry

    lax.fori_loop(0, SEQ // BLOCK, block, 0)


def attend(qkv, position, frequency, gains, main, tail):
    return to_experts(
        main,
        tail,
        6,
        work=attend_kernel,
        work_in=[qkv, position, frequency, gains],
        work_out=[
            shape((SEQ, HEAD)),
            shape((SEQ, HEAD)),
            shape((SEQ, HEAD)),
            shape((SEQ, 1), F32),
            shape((SEQ, HEAD), F32),
            shape((SEQ, HEAD), F32),
        ],
    )


def attend_back_kernel(
    links,
    qkv_ref,
    query_ref,
    key_ref,
    lse_ref,
    parts_ref,
    cos_ref,
    sin_ref,
    gain_ref,
    grad_ref,
    gain_grad_ref,
    query_grad,
    key_grad,
    value_grad,
):
    key_grad[...] = jnp.zeros_like(key_grad)
    value_grad[...] = jnp.zeros_like(value_grad)

    def block(step, carry):
        span = pl.ds(pl.multiple_of(step * BLOCK, BLOCK), BLOCK)
        query = query_ref[span, :]
        out_grad = parts_ref[0, span, :].astype(F32)
        for part in range(1, 4):
            out_grad = out_grad + parts_ref[part, span, :].astype(F32)
        out_grad = out_grad.astype(BF)
        scores = (
            lax.dot_general(query, key_ref[...], LAST, preferred_element_type=F32) * SCALE
        )
        soft = jnp.exp(scores - lse_ref[span, :])
        prob_grad = lax.dot_general(
            out_grad, qkv_ref[:, 2 * HEAD :], LAST, preferred_element_type=F32
        )
        inner = jnp.sum(soft * prob_grad, axis=1, keepdims=True)
        score_grad = (soft * (prob_grad - inner)).astype(BF)
        query_grad[span, :] = (
            jnp.dot(score_grad, key_ref[...], preferred_element_type=F32) * SCALE
        )
        key_grad[...] += lax.dot_general(score_grad, query, FIRST, preferred_element_type=F32)
        value_grad[...] += lax.dot_general(
            soft.astype(BF), out_grad, FIRST, preferred_element_type=F32
        )
        return carry

    lax.fori_loop(0, SEQ // BLOCK, block, 0)
    gain_grad_ref[...] = jnp.zeros_like(gain_grad_ref)

    def finish(step, carry):
        span = pl.ds(pl.multiple_of(step * BLOCK, BLOCK), BLOCK)
        for part, source, factor in ((0, query_grad, 1.0), (1, key_grad, SCALE)):
            turned = source[span, :] * factor
            grad = turned * cos_ref[span, :] + swapped(turned * sin_ref[span, :])
            raw = qkv_ref[span, part * HEAD : (part + 1) * HEAD].astype(F32)
            inverse = lax.rsqrt(jnp.mean(raw * raw, axis=1, keepdims=True) + EPS)
            unit = raw * inverse
            gain_grad_ref[part : part + 1, :] += jnp.sum(grad * unit, axis=0, keepdims=True)
            scaled = grad * gain_ref[part : part + 1, :]
            raw_grad = inverse * (scaled - unit * jnp.mean(scaled * unit, axis=1, keepdims=True))
            grad_ref[span, part * HEAD : (part + 1) * HEAD] = raw_grad.astype(BF)
        grad_ref[span, 2 * HEAD :] = value_grad[span, :].astype(BF)
        return carry

    lax.fori_loop(0, SEQ // BLOCK, finish, 0)

def attend_back(operands, main, tail):
    return from_experts(
        main,
        tail,
        13,
        work=attend_back_kernel,
        work_in=operands,
        work_out=[shape((SEQ, 3 * HEAD)), shape((8, HEAD), F32)],
        work_scratch=[pltpu.VMEM((SEQ, HEAD), F32)] * 3,
    )


SLOTS = 16 * (MAIN + TAIL)


def expert_kernel(*refs):
    in_main, in_tail, cot_main, cot_tail, gate_ref = refs[:5]
    weights, refs = refs[5:13], refs[13:]
    x_ref, slot_grad_ref, out_main, out_tail, back_main, back_tail = refs[:6]
    act_ref, grad_ref, gate_grad_ref, inner_ref = refs[6:10]
    cot_ref, up_ref, down_ref, out_sum, back_sum, row_sem, weight_sem = refs[10:]
    whole, first, last = pl.ds(0, SLOTS), pl.ds(0, 16 * MAIN), pl.ds(16 * MAIN, 16 * TAIL)
    loads = [
        pltpu.make_async_copy(source, target.at[span], row_sem.at[index])
        for index, (source, target, span) in enumerate(
            (
                (in_main, x_ref, first),
                (in_tail, x_ref, last),
                (cot_main, cot_ref, first),
                (cot_tail, cot_ref, last),
            )
        )
    ]
    for load in loads:
        load.start()
    weight_loads = []
    for slot in range(4):
        for part, target in ((0, up_ref), (4, down_ref)):
            weight_loads.append(
                pltpu.make_async_copy(
                    weights[part + slot], target.at[slot], weight_sem.at[part + slot]
                )
            )
            weight_loads[-1].start()
    for load in loads:
        load.wait()
    slot_grad_ref[...] = (gate_ref[...] * cot_ref[...].astype(F32)).astype(BF)
    for slot in range(4):
        weight_loads[2 * slot].wait()
        weight_loads[2 * slot + 1].wait()
        gate_up = jnp.dot(x_ref[...], up_ref[slot], preferred_element_type=F32)
        gate_part, up_part = gate_up[:, :256], gate_up[:, 256:]
        sigmoid = 1.0 / (1.0 + jnp.exp(-gate_part))
        silu = gate_part * sigmoid
        act = (silu * up_part).astype(BF)
        act_ref[slot] = act
        act_grad = lax.dot_general(
            slot_grad_ref[...], down_ref[slot], LAST, preferred_element_type=F32
        )
        slope = sigmoid * (1.0 + gate_part * (1.0 - sigmoid))
        grad_ref[slot, :, :256] = (act_grad * up_part * slope).astype(BF)
        grad_ref[slot, :, 256:] = (act_grad * silu).astype(BF)
        out = jnp.dot(act, down_ref[slot], preferred_element_type=F32)
        out_sum[...] = out if slot == 0 else out_sum[...] + out
        in_grad = lax.dot_general(
            grad_ref[slot], up_ref[slot], LAST, preferred_element_type=F32
        )
        back_sum[...] = in_grad if slot == 0 else back_sum[...] + in_grad
    out = out_sum[...].astype(BF)
    gated = (gate_ref[...] * out_sum[...]).astype(BF)
    out_main[...] = gated[: 16 * MAIN]
    out_tail[...] = gated[16 * MAIN :]
    gate_grad_ref[...] = jnp.sum(
        cot_ref[...].astype(F32) * out.astype(F32), axis=1, keepdims=True
    )
    inner_ref[...] = jnp.sum(back_sum[...] * x_ref[...].astype(F32), axis=1, keepdims=True)
    in_grad = back_sum[...].astype(BF)
    back_main[...] = in_grad[: 16 * MAIN]
    back_tail[...] = in_grad[16 * MAIN :]


def run_expert(in_main, in_tail, cot_main, cot_tail, gate, weights):
    main, tail = shape((16 * MAIN, WIDTH)), shape((16 * TAIL, WIDTH))
    return pl.pallas_call(
        expert_kernel,
        out_shape=[
            shape((SLOTS, WIDTH)),
            shape((SLOTS, WIDTH)),
            main,
            tail,
            main,
            tail,
            shape((4, SLOTS, 256)),
            shape((4, SLOTS, 512)),
            shape((SLOTS, 1), F32),
            shape((SLOTS, 1), F32),
        ],
        in_specs=[pl.BlockSpec(memory_space=pl.ANY)] * 4
        + [pl.BlockSpec(memory_space=pltpu.VMEM)]
        + [pl.BlockSpec(memory_space=pl.ANY)] * 8,
        out_specs=[pl.BlockSpec(memory_space=pltpu.VMEM)] * 10,
        scratch_shapes=[
            pltpu.VMEM((SLOTS, WIDTH), BF),
            pltpu.VMEM((4, WIDTH, 512), BF),
            pltpu.VMEM((4, 256, WIDTH), BF),
            pltpu.VMEM((SLOTS, WIDTH), F32),
            pltpu.VMEM((SLOTS, WIDTH), F32),
            pltpu.SemaphoreType.DMA((4,)),
            pltpu.SemaphoreType.DMA((8,)),
        ],
        compiler_params=pltpu.CompilerParams(vmem_limit_bytes=60 * 2**20),
        cost_estimate=pl.CostEstimate(
            flops=2 * SLOTS * WIDTH * 1024 * 6,
            bytes_accessed=100_000_000,
            transcendentals=SLOTS * 1024,
        ),
    )(in_main, in_tail, cot_main, cot_tail, gate, *weights)


def weight_grads_kernel(
    links, x_ref, slot_grad_ref, grad_ref, act_ref, up_1, up_2, down_1, down_2, *theirs
):
    their_x, their_slot_grad, their_grad, their_act = theirs
    for index in range(4):
        links.arrive(index)

    def part(step, carry):
        span = pl.ds(pl.multiple_of(step * 512, 512), 512)
        for slot, up, down in ((0, up_1, down_1), (1, up_2, down_2)):
            up[span, :] = (
                lax.dot_general(
                    x_ref[:, span], grad_ref[slot], FIRST, preferred_element_type=F32
                )
                + lax.dot_general(
                    their_x[:, span], their_grad[slot], FIRST, preferred_element_type=F32
                )
            ).astype(BF)
            down[:, span] = (
                lax.dot_general(
                    act_ref[slot], slot_grad_ref[:, span], FIRST, preferred_element_type=F32
                )
                + lax.dot_general(
                    their_act[slot],
                    their_slot_grad[:, span],
                    FIRST,
                    preferred_element_type=F32,
                )
            ).astype(BF)
        return carry

    lax.fori_loop(0, 4, part, 0)


def return_rows(main, tail, x, slot_grad, grads, acts):
    whole = lambda s, me, p: s
    other = lambda s, me, p: s.at[pl.ds(2, 2)]
    return from_experts(
        main,
        tail,
        9,
        first_sends=[
            (SIBLING, ("work", 0), whole, ("scratch", 0), whole),
            (SIBLING, ("work", 1), whole, ("scratch", 1), whole),
            (SIBLING, ("work", 2), other, ("scratch", 2), whole),
            (SIBLING, ("work", 3), other, ("scratch", 3), whole),
        ],
        work=weight_grads_kernel,
        work_in=[x, slot_grad, grads, acts],
        work_out=[shape((WIDTH, 512))] * 2 + [shape((256, WIDTH))] * 2,
        work_scratch=[
            pltpu.VMEM((SLOTS, WIDTH), BF),
            pltpu.VMEM((SLOTS, WIDTH), BF),
            pltpu.VMEM((2, SLOTS, 512), BF),
            pltpu.VMEM((2, SLOTS, 256), BF),
        ],
    )


def pack_kernel(up_1, up_2, down_1, down_2, up_ref, down_ref):
    upper = lax.axis_index("row") // 2
    for which, up, down in ((upper, up_1, down_1), (1 - upper, up_2, down_2)):
        value = up[...].astype(F32)
        up_ref[which, :, 0, :] = value[:, :256]
        up_ref[which, :, 1, :] = value[:, 256:]
        down_ref[which] = down[...].astype(F32)


def pack_grads(up_1, up_2, down_1, down_2):
    steps = 8
    up, down = (WIDTH // steps, 512), (256 // steps, WIDTH)
    return pl.pallas_call(
        pack_kernel,
        grid=(steps,),
        out_shape=[shape((2, WIDTH, 2, 256), F32), shape((2, 256, WIDTH), F32)],
        in_specs=[pl.BlockSpec(up, lambda i: (i, 0))] * 2
        + [pl.BlockSpec(down, lambda i: (i, 0))] * 2,
        out_specs=[
            pl.BlockSpec((2, up[0], 2, 256), lambda i: (0, i, 0, 0)),
            pl.BlockSpec((2,) + down, lambda i: (0, i, 0)),
        ],
    )(up_1, up_2, down_1, down_2)


def dot(left, right):
    return jnp.dot(left, right, preferred_element_type=F32)


def dot_last(left, right):
    return lax.dot_general(left, right, LAST, preferred_element_type=F32)


def dot_first(left, right):
    return lax.dot_general(left, right, FIRST, preferred_element_type=F32)


def pieces(value):
    high = value.astype(BF)
    rest = value - high.astype(F32)
    middle = rest.astype(BF)
    low = (rest - middle.astype(F32)).astype(BF)
    return [high, middle, low]


def aux_rows(values, count):
    held = [jnp.stack(pieces(value), axis=1) for value in values]
    padded = [jnp.pad(rows_of, ((0, 0), (USED, 1), (0, HEAD - MAIN - TAIL))) for rows_of in held]
    width = 512 - HEAD * len(values)
    padded.append(jnp.zeros((held[0].shape[0], TAIL, width), BF))
    return jnp.concatenate(padded * count, axis=2)


def aux_value(tail, index):
    part = tail[:, USED : USED + 3, index * HEAD : index * HEAD + MAIN + TAIL]
    return jnp.sum(part.astype(F32), axis=1)


def join_values(values):
    return jnp.concatenate([values[:, :MAIN].reshape(-1), values[:, MAIN:].reshape(-1)])


def split_values(values):
    return jnp.concatenate(
        [values[: 16 * MAIN].reshape(16, MAIN), values[16 * MAIN :].reshape(16, TAIL)], axis=1
    )


FIRST_HOP = [
    ((2 * y + k) * 4 + x, (2 * y + 1 - x % 2) * 4 + 2 * k + x // 2)
    for y in range(4)
    for k in range(2)
    for x in range(4)
]
SECOND_HOP = [
    ((2 * y + k) * 4 + x, (2 * y + x % 2) * 4 + 2 * k + 1 - x // 2)
    for y in range(4)
    for k in range(2)
    for x in range(4)
]
PAIR = [(d, d ^ 1) for d in range(8)]


def hop(operand, pairs):
    return lax.ppermute(operand, ("dp", "row"), pairs)


def after(*operands):
    return lax.optimization_barrier(operands)


def inverse_pairs(pairs):
    return [(b, a) for a, b in pairs]


def shards(
    tokens,
    positions,
    routes,
    attention_norm_gain,
    experts_norm_gain,
    w_qkv,
    q_gain,
    k_gain,
    w_out,
    w_router,
    w_gate_up,
    w_down,
    cotangent,
):
    core = lax.axis_index("dp") % 2
    experts = jnp.arange(EXPERTS, dtype=jnp.int32)
    named = jnp.any(routes[:, :, None] == experts[None, None, :], axis=1)
    place = jnp.arange(512, dtype=jnp.int32)
    earlier = (place[None, :] < place[:, None]).astype(BF)
    rank = dot(earlier, named.astype(BF))
    rank = jnp.where(named, rank, -1.0).T
    (
        token_rows,
        w_group,
        position_rows,
        gain_rows,
        w_all,
        down_1,
        down_2,
        send_up_1,
        send_up_2,
        send_cot_main,
        send_cot_tail,
    ) = gather_inputs(
        tokens,
        w_qkv,
        w_out,
        w_down,
        positions.reshape(4, HEAD),
        attention_norm_gain.reshape(4, HEAD),
        [w_gate_up, rank, cotangent],
    )
    w_all = w_all.reshape(WIDTH, 512)
    w_group = w_group.reshape(WIDTH, 1536)
    gain_full = gain_rows.reshape(WIDTH)

    gate_up_1, gate_up_2 = hop(send_up_1, FIRST_HOP), hop(send_up_2, SECOND_HOP)
    sibling = lambda w: lax.ppermute(w, "dp", PAIR)
    frequency = THETA ** (-2.0 * jnp.arange(HEAD // 2, dtype=F32) / HEAD)
    half_signs = jnp.where(jnp.arange(HEAD) < HEAD // 2, -1.0, 1.0).astype(F32)
    frequency = jnp.concatenate(
        [jnp.concatenate([frequency] * 2)[None], half_signs[None], jnp.zeros((6, HEAD), F32)]
    )
    position_column = position_rows.reshape(SEQ, 1).astype(F32)
    gains = jnp.concatenate([q_gain[None], k_gain[None], jnp.zeros((6, HEAD), F32)], axis=0)

    main_pick = (
        (rank[:, None, :] == jnp.arange(MAIN, dtype=F32)[None, :, None])
        .astype(BF)
        .reshape(EXPERTS * MAIN, 512)
    )
    tail_pick = (
        (rank[:, None, :] == jnp.arange(MAIN, MAIN + TAIL, dtype=F32)[None, :, None])
        .astype(BF)
        .reshape(EXPERTS * TAIL, 512)
    )

    def pick_rows(operand):
        return (
            dot(main_pick, operand).astype(BF).reshape(EXPERTS, MAIN, 512),
            dot(tail_pick, operand).astype(BF).reshape(EXPERTS, TAIL, 512),
        )

    def place_rows(main, tail):
        return dot_first(main_pick, main.reshape(EXPERTS * MAIN, 512)) + dot_first(
            tail_pick, tail.reshape(EXPERTS * TAIL, 512)
        )

    def pick_values(values):
        return jnp.concatenate(
            [
                jnp.sum(pick.reshape(EXPERTS, -1, 512).astype(F32) * values[:, None, :], axis=2)
                for pick in (main_pick, tail_pick)
            ],
            axis=1,
        )

    def place_values(values):
        return sum(
            jnp.sum(pick.reshape(EXPERTS, -1, 512).astype(F32) * part[:, :, None], axis=1)
            for pick, part in ((main_pick, values[:, :MAIN]), (tail_pick, values[:, MAIN:]))
        )

    token_full = token_rows.astype(F32)
    inverse_attention = lax.rsqrt(jnp.mean(token_full * token_full, axis=1) + EPS)
    normed_exact = token_full * inverse_attention[:, None] * gain_full[None, :]
    normed = normed_exact.astype(BF)
    qkv = to_heads(dot(normed, w_group).astype(BF))
    cot_main, cot_tail, attended, query, key, lse, cosine, sine = attend(
        qkv, position_column, frequency, gains, send_cot_main, send_cot_tail
    )
    attended, gate_up_1, gate_up_2, down_1, down_2 = after(
        attended, gate_up_1, gate_up_2, down_1, down_2
    )
    up_ws = [gate_up_1, gate_up_2, sibling(gate_up_1), sibling(gate_up_2)]
    down_ws = [down_1, down_2, sibling(down_1), sibling(down_2)]
    attended_rows = gather_attended(attended)

    token_float = tokens.astype(F32)
    hidden = token_float + dot(attended_rows, w_all)
    scaled_hidden = hidden * experts_norm_gain
    partial_stats = jnp.concatenate(
        [
            lax.dot_general(
                w_router.astype(F32),
                scaled_hidden,
                (((0,), (1,)), ((), ())),
                precision=EXACT,
                preferred_element_type=F32,
            ),
            jnp.sum(hidden * hidden, axis=1)[None],
            jnp.zeros((7, 512), F32),
        ],
        axis=0,
    )
    stats = jnp.sum(row_stack(partial_stats, 7), axis=0)
    inverse_experts = lax.rsqrt(stats[EXPERTS] / WIDTH + EPS)
    logits = stats[:EXPERTS] * inverse_experts[None, :]
    unit_experts = hidden * inverse_experts[:, None]
    experts_input = (unit_experts * experts_norm_gain).astype(BF)
    named_t = rank >= 0
    largest = jnp.max(jnp.where(named_t, logits, -jnp.inf), axis=0, keepdims=True)
    shifted = jnp.where(named_t, jnp.exp(jnp.where(named_t, logits - largest, 0.0)), 0.0)
    gates = shifted / jnp.sum(shifted, axis=0, keepdims=True)
    slot_gates = pick_values(gates)

    send_main, send_tail = pick_rows(experts_input)
    in_main, in_tail = to_experts(
        send_main, send_tail + aux_rows([slot_gates], 1), 8
    )
    gate_of = aux_value(in_tail[:, :, :512], 0)
    gate_of = jnp.where(jnp.arange(MAIN + TAIL)[None, :] < CAP, gate_of, 0.0)
    gate_of = join_values(gate_of)[:, None]
    (
        slot_in,
        slot_grad,
        out_main,
        out_tail,
        back_main,
        back_tail,
        acts,
        gate_up_grads,
        slot_gate_grad,
        slot_inner,
    ) = run_expert(
        in_main.reshape(16 * MAIN, WIDTH),
        in_tail.reshape(16 * TAIL, WIDTH),
        cot_main.reshape(16 * MAIN, WIDTH),
        cot_tail.reshape(16 * TAIL, WIDTH),
        gate_of,
        up_ws + down_ws,
    )
    aux = aux_rows([split_values(slot_gate_grad[:, 0]), split_values(slot_inner[:, 0])], 4)
    back_main, back_tail, up_1, up_2, down_1, down_2 = return_rows(
        back_main.reshape(16, MAIN, WIDTH),
        back_tail.reshape(16, TAIL, WIDTH) + aux,
        slot_in,
        slot_grad,
        gate_up_grads,
        acts,
    )
    gate_grad = place_values(aux_value(back_tail, 0))
    inner = jnp.sum(place_values(aux_value(back_tail, 1)), axis=0)
    first_back, second_back = inverse_pairs(FIRST_HOP), inverse_pairs(SECOND_HOP)
    logit_grad = gates * (gate_grad - jnp.sum(gates * gate_grad, axis=0, keepdims=True))
    experts_input_grad = place_rows(back_main, back_tail) + lax.dot_general(
        logit_grad,
        w_router.astype(F32),
        (((0,), (1,)), ((), ())),
        precision=EXACT,
        preferred_element_type=F32,
    )
    mean_experts = (inner + jnp.sum(logit_grad * logits, axis=0)) / WIDTH
    cot_float = cotangent.astype(F32)
    middle_grad = cot_float + inverse_experts[:, None] * (
        experts_input_grad * experts_norm_gain - unit_experts * mean_experts[:, None]
    )
    router_part = lax.dot_general(
        logit_grad,
        experts_input.astype(F32),
        (((1,), (0,)), ((), ())),
        precision=EXACT,
        preferred_element_type=F32,
    )
    experts_gain_part = jnp.sum(experts_input_grad * unit_experts, axis=0)
    attended_grad = middle_grad.astype(BF)
    out_part = dot_first(attended_rows, attended_grad).astype(BF).reshape(16, HEAD, 512)
    small_part = jnp.concatenate(
        [
            router_part.reshape(256, HEAD),
            experts_gain_part.reshape(4, HEAD),
            jnp.zeros((124, HEAD), F32),
        ],
        axis=0,
    )
    grad_parts, out_other, small_other = spread_attended_grad(
        dot_last(attended_grad, w_all).astype(BF), out_part, small_part
    )
    out_half = (
        lax.dynamic_slice_in_dim(out_part, core * 64, 64, 1).astype(F32)
        + out_other.astype(F32)
    ).astype(BF)
    small = (small_part + small_other).reshape(16, 24, HEAD)
    out_main, out_tail, qkv_grad, head_gain_part = attend_back(
        [qkv, query, key, lse, grad_parts, cosine, sine, gains],
        out_main.reshape(16, MAIN, WIDTH),
        out_tail.reshape(16, TAIL, WIDTH),
    )
    qkv_grad, up_1, up_2, down_1, down_2 = after(qkv_grad, up_1, up_2, down_1, down_2)
    up_1, up_2 = hop(up_1, first_back), hop(up_2, second_back)
    down_1, down_2 = hop(down_1, first_back), hop(down_2, second_back)
    qkv_grad, output = from_heads(
        qkv_grad,
        [
            hidden,
            main_pick,
            tail_pick,
            out_main.reshape(EXPERTS * MAIN, 512),
            out_tail.reshape(EXPERTS * TAIL, 512),
        ],
    )
    normed_grad_part = dot_last(qkv_grad, w_group)
    stat_part = jnp.sum(normed_grad_part * normed_exact, axis=1)
    normed_grad, row_stats, out_pieces, small_pieces, qkv_piece = spread_features(
        normed_grad_part.astype(BF),
        jnp.concatenate([stat_part.reshape(4, HEAD), head_gain_part[:4]], axis=0),
        out_half,
        small,
        normed,
        qkv_grad,
    )
    normed_grad = jnp.sum(normed_grad.astype(F32), axis=0)
    row_stats = jnp.sum(row_stats, axis=0)
    mean_attention = row_stats[:4].reshape(512) / WIDTH
    unit_attention = token_float * inverse_attention[:, None]
    token_grad = middle_grad + inverse_attention[:, None] * (
        normed_grad * attention_norm_gain - unit_attention * mean_attention[:, None]
    )
    attention_gain_part = jnp.sum(normed_grad * unit_attention, axis=0)

    out_piece = jnp.sum(out_pieces.astype(F32), axis=0).astype(BF)
    out_total, small_total, late, qkv_total = collect_sums(
        qkv_piece,
        out_piece,
        jnp.sum(small_pieces, axis=0),
        jnp.concatenate([attention_gain_part.reshape(4, HEAD), row_stats[4:]], axis=0),
    )
    small_total = small_total.reshape(384, HEAD)
    late = jnp.sum(late, axis=0)
    grad_gate_up, grad_down = pack_grads(up_1, up_2, down_1, down_2)
    return (
        output,
        token_grad.astype(BF),
        late[:4].reshape(512),
        small_total[256:260].reshape(512),
        qkv_total.astype(F32).reshape(512, 4, 384),
        late[4],
        late[5],
        out_total.astype(F32).reshape(512, 512),
        small_total[:256].reshape(EXPERTS, 512).T,
        grad_gate_up,
        grad_down,
    )


def solution(mesh):
    tokens_like = P(("dp", "col"), "row")
    up_like = P(("dp", "col"), None, None, "row")
    down_like = P(("dp", "col"), "row", None)
    return jax.shard_map(
        shards,
        mesh=mesh,
        in_specs=(
            tokens_like,
            P("dp", "row"),
            P(("dp", "col"), None),
            P("row"),
            P("row"),
            P("row", "col", None),
            P(),
            P(),
            P("col", "row"),
            P("row", None),
            up_like,
            down_like,
            tokens_like,
        ),
        out_specs=(
            tokens_like,
            tokens_like,
            P("row"),
            P("row"),
            P("row", "col", None),
            P(),
            P(),
            P("col", "row"),
            P("row", None),
            up_like,
            down_like,
        ),
        check_vma=False,
    )
```

```python
import jax
import jax.numpy as jnp
from jax import lax
from jax.experimental import pallas as pl
from jax.experimental.pallas import tpu as pltpu
from jax.sharding import PartitionSpec as P

WIDTH = 2048
HEAD = 128
EXPERTS = 64
CAP = 36
ROOM = 40
SEQ = 2048
EPS = 1e-06
THETA = 10000.0
EXACT = lax.Precision.HIGHEST
MESH = pl.DeviceIdType.MESH
SIZES = (4, 2, 4, 4)
BF = jnp.bfloat16
F32 = jnp.float32
ROWS = [(0, 0, d, 0) for d in (2, 1, 3)]
COLS = [(0, 0, 0, d) for d in (2, 1, 3)]
SIBLING = (0, 1, 0, 0)
PLANE = [(0, 0, i, (i + s) % 4) for s in range(4) for i in range(4) if (i, s) != (0, 0)]
CUBE = [
    (i, 0, (i + s) % 4, (g - i) % 4)
    for g in range(4)
    for s in range(4)
    for i in range(4)
    if (g, s, i) != (0, 0, 0)
]
SOURCES = [(i, 0, 0, (i + s) % 4) for s in range(4) for i in range(4) if (i, s) != (0, 0)]
LINES = [(d, 0, 0, 0) for d in (2, 1, 3)]
OTHERS = [
    (a, k, 0, d) for a in range(4) for k in range(2) for d in range(4) if (a, k, d) != (0, 0, 0)
]


def shape(dims, dtype=BF):
    return jax.ShapeDtypeStruct(dims, dtype)


def here():
    group = lax.axis_index("dp")
    return (group // 2, group % 2, lax.axis_index("row"), lax.axis_index("col"))


class Hop:
    def __init__(self, to, origin):
        self.to, self.origin = to, origin


ONE_WAY = Hop(
    lambda p: (p[0], 1 - p[2] % 2, 2 * p[1] + p[2] // 2, p[3]),
    lambda p: (p[0], p[2] // 2, 2 * (p[2] % 2) + 1 - p[1], p[3]),
)
OTHER_WAY = Hop(
    lambda p: (p[0], p[2] % 2, 2 * p[1] + 1 - p[2] // 2, p[3]),
    lambda p: (p[0], p[2] // 2, 2 * (1 - p[2] % 2) + p[1], p[3]),
)


class Links:
    def __init__(self, send, arrive, ins, outs):
        self.send, self.arrive, self.ins, self.outs = send, arrive, ins, outs


def moved(place, offset):
    if isinstance(offset, Hop):
        return offset.to(place)
    return tuple((p + o) % n for p, o, n in zip(place, offset, SIZES))


def device(place):
    return (place[0] * 2 + place[1], place[2], place[3])


def exchange(
    inputs,
    outputs,
    sends,
    kept,
    call_id,
    micros=30,
    work=None,
    work_in=(),
    work_out=(),
    work_scratch=(),
    stages=(),
    deferred=(),
):
    offsets = sorted({s[0] for s in sends if not isinstance(s[0], Hop)})
    hops = {id(s[0]): s[0] for s in sends if isinstance(s[0], Hop)}.values()
    n_in, n_out, n_send = len(inputs), len(outputs), len(sends)
    m_in, m_out = len(work_in), len(work_out)

    def kernel(*refs):
        ins, refs = refs[:n_in], refs[n_in:]
        worked, refs = refs[:m_in], refs[m_in:]
        outs, refs = refs[:n_out], refs[n_out:]
        made, refs = refs[:m_out], refs[m_out:]
        send_sem, recv_sem, kept_sem = refs[:3]
        staged, refs = refs[3 : 3 + len(kept)], refs[3 + len(kept) :]
        special = {"work": worked, "made": made, "scratch": refs}
        me = here()
        barrier = pltpu.get_barrier_semaphore()
        greeted = [moved(me, offset) for offset in offsets]
        for way in hops:
            greeted += [way.to(me), way.origin(me)]
        for peer in greeted:
            pl.semaphore_signal(barrier, inc=1, device_id=device(peer), device_id_type=MESH)
        local = []
        for index, (i, take, o, put, _) in enumerate(kept):
            source, target = take(ins[i], me), put(outs[o], me)
            local.append(
                (
                    pltpu.make_async_copy(source, staged[index], kept_sem.at[index, 0]),
                    pltpu.make_async_copy(staged[index], target, kept_sem.at[index, 1]),
                )
            )
            local[-1][0].start()
        pl.semaphore_wait(barrier, len(greeted))
        copies, arrived = {}, set()

        def arrive(index):
            if index not in arrived:
                arrived.add(index)
                copies[index].wait_recv()

        def named(group, index):
            return special[index[0]][index[1]] if isinstance(index, tuple) else group[index]

        def start(index):
            offset, i, take, o, put = sends[index][:5]
            needs = sends[index][5] if len(sends[index]) > 5 else None
            for need in needs or ():
                if need >= 0:
                    arrive(need)
                elif need not in arrived:
                    arrived.add(need)
                    local[-need - 1][1].wait()
            peer = moved(me, offset)
            copies[index] = pltpu.make_async_remote_copy(
                src_ref=take(named(ins if needs is None else outs, i), me, peer),
                dst_ref=put(named(outs, o), me, peer),
                send_sem=send_sem.at[index],
                recv_sem=recv_sem.at[index],
                device_id=device(peer),
                device_id_type=MESH,
            )
            copies[index].start()

        links = Links(start, arrive, ins, outs)
        parts = work(links, *worked, *made, *refs) if stages else ()
        first = [i for i in range(n_send) if len(sends[i]) < 6 and i not in deferred]
        for index in first:
            start(index)
        for load, store in local:
            load.wait()
            store.start()
        for index in range(n_send):
            if index in first or index in deferred:
                continue
            for part, at in zip(parts, stages):
                if at == index:
                    part()
            start(index)
        if work is not None and not stages:
            work(links, *worked, *made, *refs)
        for index in range(n_send):
            arrive(index)
        for copy in copies.values():
            copy.wait_send()
        for index, copy in enumerate(local):
            if -index - 1 not in arrived:
                copy[1].wait()

    return pl.pallas_call(
        kernel,
        out_shape=list(outputs) + list(work_out),
        in_specs=[pl.BlockSpec(memory_space=pl.ANY)] * n_in
        + [pl.BlockSpec(memory_space=pltpu.VMEM)] * m_in,
        out_specs=[pl.BlockSpec(memory_space=pl.ANY)] * n_out
        + [pl.BlockSpec(memory_space=pltpu.VMEM)] * m_out,
        scratch_shapes=[
            pltpu.SemaphoreType.DMA((n_send,)),
            pltpu.SemaphoreType.DMA((n_send,)),
            pltpu.SemaphoreType.DMA((max(1, len(kept)), 2)),
            *[pltpu.VMEM(k[4], inputs[k[0]].dtype) for k in kept],
            *work_scratch,
        ],
        compiler_params=pltpu.CompilerParams(
            collective_id=call_id,
            has_side_effects=True,
            vmem_limit_bytes=(8 if work is None else 60) * 2**20,
        ),
        cost_estimate=pl.CostEstimate(
            flops=0, bytes_accessed=micros * 3_500_000, transcendentals=0
        ),
    )(*inputs, *work_in)


def rows(start, size):
    return pl.ds(pl.multiple_of(start, size), size)


def eighth(size):
    me = here()
    return rows((me[1] * 4 + me[0]) * size, size)


def half(size):
    return rows(here()[1] * size, size)


class Sends(list):
    def add(self, group, take, o, put=None, i=None, needs=None):
        first = len(self)
        for offset in group:
            if needs is None:
                self.append((offset, i, take, o, put))
            else:
                view = lambda ref, me, p: take(ref, me)
                self.append((offset, o, view, o, view, needs))
        return list(range(first, len(self)))


def early_kernel(links, up_ref, rank_ref, cot_ref, up_1, up_2, rows_ref):
    upper = lax.axis_index("row") // 2

    def unpack(which, target):
        def part(step, carry):
            span = pl.ds(pl.multiple_of(step * 256, 256), 256)
            target[span, :256] = up_ref[which, span, 0, :]
            target[span, 256:] = up_ref[which, span, 1, :]
            return carry

        return lambda: lax.fori_loop(0, WIDTH // 256, part, 0)

    def pick():
        def part(step, carry):
            ranks = rank_ref[pl.ds(pl.multiple_of(step * 8, 8), 8), :]
            slots = lax.broadcasted_iota(jnp.int32, (8, ROOM, 512), 1).astype(F32)
            chosen = (ranks[:, None, :] == slots).astype(F32).reshape(8 * ROOM, 512)
            rows_of = jnp.dot(chosen.astype(BF), cot_ref[...], preferred_element_type=F32)
            rows_ref[pl.ds(pl.multiple_of(step * 8, 8), 8)] = rows_of.reshape(
                8, ROOM, 512
            ).astype(BF)
            return carry

        lax.fori_loop(0, EXPERTS // 8, part, 0)

    return [unpack(upper, up_1), unpack(1 - upper, up_2), pick]


def gather_inputs(tokens, w_qkv, w_out, w_down, small_int, small_float, early):
    outputs = [
        shape((512, WIDTH)),
        shape((4, 512, 1536)),
        shape((4, 4, HEAD), jnp.int32),
        shape((4, 4, HEAD), F32),
        shape((4, 4, HEAD, 512)),
        shape((256, WIDTH)),
        shape((256, WIDTH)),
    ]
    sends = Sends()
    own_cols = lambda me: rows(me[3] * 384, 384)
    low, high = pl.ds(0, 2), pl.ds(2, 2)
    first = sends.add(
        ROWS,
        lambda s, me, p: s.at[eighth(64), rows(p[2] * 384, 384)],
        1,
        lambda o, me, p: o.at[me[2], eighth(64), own_cols(me)],
        1,
    )
    sends.add(ROWS, lambda s, me, p: s, 0, lambda o, me, p: o.at[:, rows(me[2] * 512, 512)], 0)
    sends.add(ROWS, lambda s, me, p: s, 2, lambda o, me, p: o.at[me[2]], 2)
    sends.add(ROWS, lambda s, me, p: s, 3, lambda o, me, p: o.at[me[2]], 3)
    sends.append((ONE_WAY, 5, lambda s, me, p: s.at[me[2] // 2], 5, lambda o, me, p: o))
    sends.append((OTHER_WAY, 5, lambda s, me, p: s.at[1 - me[2] // 2], 6, lambda o, me, p: o))
    out_z = sends.add(COLS, lambda o, me: o.at[low, me[3], eighth(16)], 4, needs=[-2])
    out_y = sends.add(LINES, lambda o, me: o.at[high, me[3], eighth(16)], 4, needs=[-2])
    stages = [len(sends)]
    by_z = sends.add(
        COLS, lambda o, me: o.at[low, eighth(64), own_cols(me)], 1, needs=[-1] + first
    )
    by_y = sends.add(LINES, lambda o, me: o.at[high, eighth(64), own_cols(me)], 1, needs=first)
    sends.add(LINES, lambda o, me: o.at[low, eighth(64), own_cols(me)], 1, needs=first)
    sends.add(COLS, lambda o, me: o.at[high, eighth(64), own_cols(me)], 1, needs=first)
    stages.append(len(sends))
    last_z, last_y = {0: [len(sends) - 6 + i for i in range(3)]}, {0: list(range(len(sends) - 3, len(sends)))}
    for d in (1, 3, 2):
        came = by_z[[offset[3] for offset in COLS].index(d)]
        cols = lambda me, d=d: rows((me[3] + 4 - d) % 4 * 384, 384)
        last_z[d] = sends.add(
            LINES,
            lambda o, me, cols=cols: o.at[low, eighth(64), cols(me)],
            1,
            needs=[came],
        )
        came = by_y[[offset[0] for offset in LINES].index(d)]
        span = lambda me, d=d: rows((me[1] * 4 + (me[0] + 4 - d) % 4) * 64, 64)
        last_y[d] = sends.add(
            COLS,
            lambda o, me, span=span: o.at[high, span(me), own_cols(me)],
            1,
            needs=[came],
        )
    out_zy = sends.add(LINES, lambda o, me: o.at[low, :, eighth(16)], 4, needs=out_z)
    out_yz = sends.add(COLS, lambda o, me: o.at[high, me[3], half(64)], 4, needs=out_y)
    stages.append(len(sends))
    pair = [SIBLING]
    sends.add(pair, lambda o, me: o.at[low, eighth(64)], 1, needs=by_z)
    sends.add(pair, lambda o, me: o.at[high, half(256), own_cols(me)], 1, needs=by_y)
    for d in (1, 3, 2):
        line = [offset[0] for offset in LINES].index(d)
        span = lambda me, d=d: rows((me[1] * 4 + (me[0] + 4 - d) % 4) * 64, 64)
        sends.add(
            pair,
            lambda o, me, span=span: o.at[low, span(me)],
            1,
            needs=[numbers[line] for numbers in last_z.values()],
        )
        col = [offset[3] for offset in COLS].index(d)
        cols = lambda me, d=d: rows((me[3] + 4 - d) % 4 * 384, 384)
        sends.add(
            pair,
            lambda o, me, cols=cols: o.at[high, half(256), cols(me)],
            1,
            needs=[numbers[col] for numbers in last_y.values()],
        )
    sends.add(pair, lambda o, me: o.at[low, :, half(64)], 4, needs=out_zy)
    sends.add(pair, lambda o, me: o.at[high, :, half(64)], 4, needs=out_yz)
    kept = [
        (
            1,
            lambda s, me: s.at[eighth(64), rows(me[2] * 384, 384)],
            1,
            lambda o, me: o.at[me[2], eighth(64), own_cols(me)],
            (64, 384),
        ),
        (
            4,
            lambda s, me: s.at[:, eighth(16)],
            4,
            lambda o, me: o.at[:, me[3], eighth(16)],
            (4, 16, 512),
        ),
        (0, lambda s, me: s, 0, lambda o, me: o.at[:, rows(me[2] * 512, 512)], (512, 512)),
        (2, lambda s, me: s, 2, lambda o, me: o.at[me[2]], (4, HEAD)),
        (3, lambda s, me: s, 3, lambda o, me: o.at[me[2]], (4, HEAD)),
    ]
    return exchange(
        [
            tokens,
            w_qkv.reshape(512, 1536),
            small_int,
            small_float,
            w_out.reshape(4, HEAD, 512),
            w_down,
        ],
        outputs,
        sends,
        kept,
        0,
        work=early_kernel,
        work_in=early,
        work_out=[
            shape((WIDTH, 512)),
            shape((WIDTH, 512)),
            shape((EXPERTS, ROOM, 512)),
        ],
        stages=stages,
    )


def to_heads(qkv):
    take = lambda s, me, p: s.at[:, rows(p[3] * 384, 384)]
    put = lambda o, me, p: o.at[rows(me[3] * 512, 512)]
    return exchange(
        [qkv],
        [shape((SEQ, 384))],
        [(offset, 0, take, 0, put) for offset in COLS],
        [(0, lambda s, me: take(s, me, me), 0, lambda o, me: put(o, me, me), (512, 384))],
        1,
    )[0]


def combine_kernel(links, hidden_ref, pick_ref, rows_ref, out_ref):
    out_ref[...] = (
        hidden_ref[...]
        + lax.dot_general(pick_ref[...], rows_ref[...], FIRST, preferred_element_type=F32)
    ).astype(BF)


def from_heads(grads, out_part, small_part, combine):
    take = lambda s, me, p: s.at[rows(p[3] * 512, 512)]
    put = lambda o, me, p: o.at[:, rows(me[3] * 384, 384)]
    return exchange(
        [grads, out_part, small_part],
        [shape((512, 1536)), shape((16, 64, 512)), shape(small_part.shape, F32)],
        [(offset, 0, take, 0, put) for offset in COLS]
        + [
            (SIBLING, 1, lambda s, me, p: s.at[:, rows(p[1] * 64, 64)], 1, lambda o, me, p: o),
            (SIBLING, 2, lambda s, me, p: s, 2, lambda o, me, p: o),
        ],
        [(0, lambda s, me: take(s, me, me), 0, lambda o, me: put(o, me, me), (512, 384))],
        2,
        micros=300,
        work=combine_kernel,
        work_in=combine,
        work_out=[shape((512, 512))],
    )


def row_stack(operand, call_id):
    take = lambda s, me, p: s
    put = lambda o, me, p: o.at[me[2]]
    return exchange(
        [operand],
        [shape((4,) + operand.shape, operand.dtype)],
        [(offset, 0, take, 0, put) for offset in ROWS],
        [(0, lambda s, me: s, 0, lambda o, me: put(o, me, me), operand.shape)],
        call_id,
    )[0]


def finish_kernel(
    links,
    numbers,
    normed_ref,
    grad_ref,
    weight_ref,
    gain_ref,
    piece_ref,
    feature_ref,
    stat_ref,
    their_half,
    came,
    half,
    spread,
    feature_part,
    stat_part,
):
    me = here()
    y, core, row = me[0], me[1], me[2]
    to_sibling, to_lines, to_rows, stats = numbers

    def product(start):
        return lax.dot_general(
            normed_ref[:, rows(start, 256)], grad_ref[...], FIRST, preferred_element_type=F32
        )

    for r in range(4):
        their_half[r] = product(r * 512 + (1 - core) * 256).astype(BF)
        links.send(to_sibling[r])
    inner = jnp.zeros((512, 1), F32)
    for ahead in (2, 1, 3, 0):
        span = rows(lax.rem(row + ahead, 4) * 512, 512)
        part = lax.dot_general(
            grad_ref[...], weight_ref[span, :], LAST, preferred_element_type=F32
        )
        inner = inner + jnp.sum(part * normed_ref[:, span].astype(F32), axis=1, keepdims=True)
        if ahead:
            feature_part[ahead - 1] = part.astype(BF)
            links.send(to_rows[ahead])
        else:
            feature_ref[row] = part.astype(BF)
    same = (
        lax.broadcasted_iota(jnp.int32, (HEAD, HEAD), 0)
        == lax.broadcasted_iota(jnp.int32, (HEAD, HEAD), 1)
    ).astype(F32)
    for block in range(4):
        stat_part[block : block + 1, :] = jnp.sum(
            same * inner[block * HEAD : (block + 1) * HEAD], axis=0, keepdims=True
        )
    stat_part[4:, :] = gain_ref[:4, :]
    stat_ref[row] = stat_part[...]
    for number in stats:
        links.send(number)
    for r in range(4):
        mine = product(r * 512 + core * 256)
        links.arrive(to_sibling[r])
        half[r] = (mine + came[r].astype(F32)).astype(BF)
        for number in to_lines[r]:
            links.send(number)
        spread[y, r] = half[r, rows(y * 64, 64), :]
    for r in range(4):
        for number in to_lines[r]:
            links.arrive(number)
        total = spread[0, r].astype(F32)
        for source in range(1, 4):
            total = total + spread[source, r].astype(F32)
        piece_ref[r] = total.astype(BF)


def finish(out_half, small, normed, grads, weights, gains):
    take_out = lambda s, me, p: s.at[p[0] * 4 + p[3]]
    put_out = lambda o, me, p: o.at[me[0] * 4 + me[3]]
    whole = lambda s, me, p: s
    own_row = lambda o, me, p: o.at[me[2]]
    keep = lambda i, dims: (
        i,
        lambda s, me: take_out(s, me, me),
        i,
        lambda o, me: put_out(o, me, me),
        dims,
    )
    sends = [(offset, 0, take_out, 0, put_out) for offset in SOURCES]
    sends += [(offset, 1, take_out, 1, put_out) for offset in SOURCES]
    later = len(sends)
    to_sibling, to_lines, to_rows, stats = [], [[], [], [], []], {}, []
    for r in range(4):
        view = lambda ref, me, p, r=r: ref.at[r]
        to_sibling.append(len(sends))
        sends.append((SIBLING, ("scratch", 0), view, ("scratch", 1), view))
    for r in range(4):
        for offset in LINES:
            to_lines[r].append(len(sends))
            sends.append(
                (
                    offset,
                    ("scratch", 2),
                    lambda s, me, p, r=r: s.at[r, rows(p[0] * 64, 64)],
                    ("scratch", 3),
                    lambda o, me, p, r=r: o.at[me[0], r],
                )
            )
    for offset in ROWS:
        ahead = offset[2]
        to_rows[ahead] = len(sends)
        part = lambda s, me, p, ahead=ahead: s.at[ahead - 1]
        sends.append((offset, ("scratch", 4), part, ("made", 1), own_row))
        stats.append(len(sends))
        sends.append((offset, ("scratch", 5), whole, ("made", 2), own_row))
    return exchange(
        [out_half, small],
        [shape((16, 64, 512)), shape((16,) + small.shape[1:], F32)],
        sends,
        [keep(0, (64, 512)), keep(1, small.shape[1:])],
        5,
        work=lambda links, *refs: finish_kernel(
            links, (to_sibling, to_lines, to_rows, stats), *refs
        ),
        work_in=[normed, grads, weights, gains],
        work_out=[shape((4, 64, 1536)), shape((4, 512, 512)), shape((4, 8, HEAD), F32)],
        work_scratch=[pltpu.VMEM((4, 256, 1536), BF)] * 3
        + [
            pltpu.VMEM((4, 4, 64, 1536), BF),
            pltpu.VMEM((3, 512, 512), BF),
            pltpu.VMEM((8, HEAD), F32),
        ],
        deferred=range(later, len(sends)),
    )


def expert_at(place):
    return place[0] * 16 + (place[2] // 2) * 8 + place[3] * 2 + place[2] % 2


def expert_views():
    return (
        lambda s, me, p: s.at[expert_at(p)],
        lambda o, me, p: o.at[me[0] * 4 + me[3], :, rows(me[2] * 512, 512)],
    )


def token_views():
    return (
        lambda s, me, p: s.at[p[0] * 4 + p[3], :, rows(p[2] * 512, 512)],
        lambda o, me, p: o.at[expert_at(me)],
    )


def collect_sums(qkv_piece, out_piece, small_piece, late):
    put_qkv = lambda o, me, p: o.at[me[1], me[0]]
    put_out = lambda o, me, p: o.at[me[0], me[1]]
    put_small = lambda o, me, p: o.at[me[0] * 4 + me[3]]
    put_late = lambda o, me, p: o.at[(me[0] * 2 + me[1]) * 4 + me[3]]
    whole = lambda s, me, p: s
    sends = Sends()
    heads = sends.add(
        PLANE,
        lambda s, me, p: s.at[p[2], :, rows(p[3] * 384, 384)],
        ("scratch", 0),
        lambda o, me, p: o.at[me[3], me[2]],
        ("work", 0),
    )
    out_sent = sends.add(LINES, whole, 0, put_out, 0)
    sends.add([SIBLING], whole, 0, put_out, 0)
    sends.add(SOURCES, whole, 1, put_small, 1)
    sends.add(OTHERS, whole, 2, put_late, 2)
    later = len(sends)
    qkv_sent = sends.add(LINES, whole, ("made", 0), put_qkv, ("scratch", 1))
    sends.add([SIBLING], whole, ("made", 0), put_qkv, ("scratch", 1))
    relays = []
    for index in (1, 2, 0):
        origin = lambda me, d=LINES[index][0]: (me[0] + 4 - d) % 4
        view = lambda ref, me, p, origin=origin: ref.at[origin(me), me[1]]
        relays.append((out_sent[index], len(sends)))
        sends.append((SIBLING, 0, view, 0, view, [out_sent[index]]))
    for index in (1, 2, 0):
        origin = lambda me, d=LINES[index][0]: (me[0] + 4 - d) % 4
        view = lambda ref, me, p, origin=origin: ref.at[me[1], origin(me)]
        relays.append((qkv_sent[index], len(sends)))
        sends.append((SIBLING, ("made", 0), view, ("made", 0), view, [qkv_sent[index]]))

    def work(links, piece_ref, total_ref, spread, mine):
        group, row, col = lax.axis_index("dp"), lax.axis_index("row"), lax.axis_index("col")
        spread[col, row] = piece_ref[row, :, rows(col * 384, 384)]
        for number in heads:
            links.arrive(number)
        for head in range(4):
            total = spread[0, head].astype(F32)
            for source in range(1, 4):
                total = total + spread[source, head].astype(F32)
            mine[:, head * 384 : (head + 1) * 384] = total.astype(BF)
        for number in range(later, later + 4):
            links.send(number)
        total_ref[group % 2, group // 2] = mine[...]
        for came, number in relays:
            links.arrive(came)
            links.send(number)

    return exchange(
        [out_piece, small_piece, late],
        [
            shape((4, 2, 64, 512)),
            shape((16,) + small_piece.shape, F32),
            shape((32,) + late.shape, F32),
        ],
        sends,
        [
            (0, lambda s, me: s, 0, lambda o, me: put_out(o, me, me), (64, 512)),
            (1, lambda s, me: s, 1, lambda o, me: put_small(o, me, me), small_piece.shape),
            (2, lambda s, me: s, 2, lambda o, me: put_late(o, me, me), late.shape),
        ],
        12,
        work=work,
        work_in=[qkv_piece],
        work_out=[shape((2, 4, 64, 1536))],
        work_scratch=[pltpu.VMEM((4, 4, 64, 384), BF), pltpu.VMEM((64, 1536), BF)],
        deferred=range(later, len(sends)),
    )


BLOCK = 256
SCALE = HEAD ** (-0.5)
LAST = (((1,), (1,)), ((), ()))
FIRST = (((0,), (0,)), ((), ()))


def swapped(operand):
    return pltpu.roll(operand, HEAD // 2, 1)


def attend_kernel(
    links,
    ready,
    qkv_ref,
    position_ref,
    frequency_ref,
    gain_ref,
    query_ref,
    key_ref,
    lse_ref,
    cos_ref,
    sin_ref,
    gathered,
    out_ref,
):
    def prepare(step, carry):
        span = pl.ds(pl.multiple_of(step * BLOCK, BLOCK), BLOCK)
        angles = position_ref[span, :] * frequency_ref[0:1, :]
        cos_ref[span, :] = jnp.cos(angles)
        sin_ref[span, :] = jnp.sin(angles) * frequency_ref[1:2, :]
        for part, target in ((0, query_ref), (1, key_ref)):
            raw = qkv_ref[span, part * HEAD : (part + 1) * HEAD].astype(F32)
            scaled = (
                raw
                * lax.rsqrt(jnp.mean(raw * raw, axis=1, keepdims=True) + EPS)
                * gain_ref[part : part + 1, :]
            )
            target[span, :] = (scaled * cos_ref[span, :] + swapped(scaled) * sin_ref[span, :]).astype(
                BF
            )
        return carry

    lax.fori_loop(0, SEQ // BLOCK, prepare, 0)
    row, col = lax.axis_index("row"), lax.axis_index("col")
    for ahead in (2, 1, 3, 0):
        first = lax.rem(col + ahead, 4) * 512

        def block(step, carry, first=first):
            span = pl.ds(pl.multiple_of(first + step * BLOCK, BLOCK), BLOCK)
            scores = (
                lax.dot_general(
                    query_ref[span, :], key_ref[...], LAST, preferred_element_type=F32
                )
                * SCALE
            )
            largest = jnp.max(scores, axis=1, keepdims=True)
            weights = jnp.exp(scores - largest)
            total = jnp.sum(weights, axis=1, keepdims=True)
            mixed = jnp.dot(
                weights.astype(BF), qkv_ref[:, 2 * HEAD :], preferred_element_type=F32
            )
            out_ref[span, :] = (mixed / total).astype(BF)
            lse_ref[span, :] = largest + jnp.log(total)
            return carry

        lax.fori_loop(0, 512 // BLOCK, block, 0)
        for number in ready[ahead]:
            links.send(number)
    gathered[:, rows((row * 4 + col) * HEAD, HEAD)] = out_ref[rows(col * 512, 512), :]


def attend(qkv, position, frequency, gains, blocks):
    take, put = expert_views()
    sends = [(offset, 0, take, 0, put) for offset in CUBE]
    ready = {ahead: [] for ahead in range(4)}
    for offset in PLANE:
        ready[offset[3]].append(len(sends))
        sends.append(
            (
                offset,
                ("scratch", 0),
                lambda s, me, p: s.at[rows(p[3] * 512, 512)],
                ("made", 5),
                lambda o, me, p: o.at[:, rows((me[2] * 4 + me[3]) * HEAD, HEAD)],
            )
        )
    return exchange(
        [blocks],
        [shape((16, ROOM, WIDTH))],
        sends,
        [(0, lambda s, me: take(s, me, me), 0, lambda o, me: put(o, me, me), (ROOM, 512))],
        6,
        work=lambda links, *refs: attend_kernel(links, ready, *refs),
        work_in=[qkv, position, frequency, gains],
        work_out=[
            shape((SEQ, HEAD)),
            shape((SEQ, HEAD)),
            shape((SEQ, 1), F32),
            shape((SEQ, HEAD), F32),
            shape((SEQ, HEAD), F32),
            shape((512, WIDTH)),
        ],
        work_scratch=[pltpu.VMEM((SEQ, HEAD), BF)],
        deferred=range(len(CUBE), len(sends)),
    )


def attend_back_kernel(
    links,
    came,
    later,
    partial_ref,
    qkv_ref,
    query_ref,
    key_ref,
    lse_ref,
    cos_ref,
    sin_ref,
    gain_ref,
    grad_ref,
    gain_grad_ref,
    parts_ref,
    query_grad,
    key_grad,
    value_grad,
):
    key_grad[...] = jnp.zeros_like(key_grad)
    value_grad[...] = jnp.zeros_like(value_grad)
    row, col = lax.axis_index("row"), lax.axis_index("col")
    parts_ref[row, rows(col * 512, 512), :] = partial_ref[:, rows((row * 4 + col) * HEAD, HEAD)]
    for ahead in (0, 1, 3, 2):
        for number in came[ahead]:
            links.arrive(number)
        if ahead == 3:
            for number in later:
                links.send(number)
        first = lax.rem(col + ahead, 4) * 512

        def block(step, carry, first=first):
            span = pl.ds(pl.multiple_of(first + step * BLOCK, BLOCK), BLOCK)
            query = query_ref[span, :]
            out_grad = parts_ref[0, span, :].astype(F32)
            for part in range(1, 4):
                out_grad = out_grad + parts_ref[part, span, :].astype(F32)
            out_grad = out_grad.astype(BF)
            scores = (
                lax.dot_general(query, key_ref[...], LAST, preferred_element_type=F32) * SCALE
            )
            soft = jnp.exp(scores - lse_ref[span, :])
            prob_grad = lax.dot_general(
                out_grad, qkv_ref[:, 2 * HEAD :], LAST, preferred_element_type=F32
            )
            inner = jnp.sum(soft * prob_grad, axis=1, keepdims=True)
            score_grad = (soft * (prob_grad - inner)).astype(BF)
            query_grad[span, :] = (
                jnp.dot(score_grad, key_ref[...], preferred_element_type=F32) * SCALE
            )
            key_grad[...] += lax.dot_general(
                score_grad, query, FIRST, preferred_element_type=F32
            )
            value_grad[...] += lax.dot_general(
                soft.astype(BF), out_grad, FIRST, preferred_element_type=F32
            )
            return carry

        lax.fori_loop(0, 512 // BLOCK, block, 0)
    gain_grad_ref[...] = jnp.zeros_like(gain_grad_ref)

    def finish(step, carry):
        span = pl.ds(pl.multiple_of(step * BLOCK, BLOCK), BLOCK)
        for part, source, factor in ((0, query_grad, 1.0), (1, key_grad, SCALE)):
            turned = source[span, :] * factor
            grad = turned * cos_ref[span, :] + swapped(turned * sin_ref[span, :])
            raw = qkv_ref[span, part * HEAD : (part + 1) * HEAD].astype(F32)
            inverse = lax.rsqrt(jnp.mean(raw * raw, axis=1, keepdims=True) + EPS)
            unit = raw * inverse
            gain_grad_ref[part : part + 1, :] += jnp.sum(grad * unit, axis=0, keepdims=True)
            scaled = grad * gain_ref[part : part + 1, :]
            raw_grad = inverse * (scaled - unit * jnp.mean(scaled * unit, axis=1, keepdims=True))
            grad_ref[span, part * HEAD : (part + 1) * HEAD] = raw_grad.astype(BF)
        grad_ref[span, 2 * HEAD :] = value_grad[span, :].astype(BF)
        return carry

    lax.fori_loop(0, SEQ // BLOCK, finish, 0)


def attend_back(operands, blocks):
    take, put = token_views()
    sends, came = [], {ahead: [] for ahead in range(4)}
    for offset in PLANE:
        came[(4 - offset[3]) % 4].append(len(sends))
        sends.append(
            (
                offset,
                ("work", 0),
                lambda s, me, p: s.at[:, rows((p[2] * 4 + p[3]) * HEAD, HEAD)],
                ("scratch", 0),
                lambda o, me, p: o.at[me[2], rows(me[3] * 512, 512)],
            )
        )
    later = range(len(sends), len(sends) + len(CUBE))
    sends += [(offset, 0, take, 0, put) for offset in CUBE]
    return exchange(
        [blocks],
        [shape((EXPERTS, ROOM, 512))],
        sends,
        [(0, lambda s, me: take(s, me, me), 0, lambda o, me: put(o, me, me), (ROOM, 512))],
        13,
        deferred=later,
        work=lambda links, *refs: attend_back_kernel(links, came, later, *refs),
        work_in=operands,
        work_out=[shape((SEQ, 3 * HEAD)), shape((8, HEAD), F32)],
        work_scratch=[pltpu.VMEM((4, SEQ, HEAD), BF)] + [pltpu.VMEM((SEQ, HEAD), F32)] * 3,
    )


SLOTS = 16 * ROOM
GROUP = 4 * ROOM


def expert_kernel(
    links,
    came,
    returns,
    shares,
    cot_ref,
    gated_ref,
    up_1,
    up_2,
    down_1,
    down_2,
    x_ref,
    back_ref,
    joined,
    slot_grads,
    acts,
    grads,
    their_x,
    their_slot_grads,
    their_acts,
    their_grads,
    up_ref,
    down_ref,
    out_sum,
    back_sum,
    weight_sem,
    own_sem,
):
    me = here()
    loads = []
    for slot in range(4):
        for part, target in ((1, up_ref), (5, down_ref)):
            loads.append(
                pltpu.make_async_copy(
                    links.ins[part + slot], target.at[slot], weight_sem.at[part + slot - 1]
                )
            )
    take, put = expert_views()
    own_in = pltpu.make_async_copy(take(links.ins[0], me, me), put(x_ref, me, me), own_sem.at[0])
    take, put = token_views()
    own_out = pltpu.make_async_copy(
        take(back_ref, me, me), put(links.outs[0], me, me), own_sem.at[1]
    )
    own_in.start()
    for load in loads:
        load.start()
    line = lax.broadcasted_iota(jnp.int32, (ROOM, HEAD), 0)
    lane = lax.broadcasted_iota(jnp.int32, (ROOM, HEAD), 1)
    same = (line == lane).astype(F32)
    for group in range(4):
        if group == 0:
            own_in.wait()
        for number in came[group]:
            links.arrive(number)
        if group == 0:
            for load in loads:
                load.wait()
        blocks = [
            lax.rem(me[0] + 4 - i, 4) * 4 + lax.rem(me[3] + 4 - (group - i) % 4, 4)
            for i in range(4)
        ]
        span = pl.ds(group * GROUP, GROUP)
        received = jnp.concatenate([x_ref[block].astype(F32) for block in blocks], axis=0)
        cot = jnp.concatenate([cot_ref[block].astype(F32) for block in blocks], axis=0)
        gates = []
        for i in range(4):
            aux = jnp.where(line >= CAP, received[i * ROOM : (i + 1) * ROOM, :HEAD], 0.0)
            gates.append(
                jnp.sum(same * jnp.sum(aux, axis=0, keepdims=True), axis=1, keepdims=True)
            )
        gate = jnp.concatenate(gates, axis=0)
        joined[span, :] = received.astype(BF)
        slot_grads[span, :] = (gate * cot).astype(BF)
        out_sum[...] = jnp.zeros_like(out_sum)
        back_sum[...] = jnp.zeros_like(back_sum)

        def quarter(slot, carry, span=span):
            gate_up = jnp.dot(joined[span, :], up_ref[slot], preferred_element_type=F32)
            gate_part, up_part = gate_up[:, :256], gate_up[:, 256:]
            sigmoid = 1.0 / (1.0 + jnp.exp(-gate_part))
            silu = gate_part * sigmoid
            act = (silu * up_part).astype(BF)
            acts[slot, span, :] = act
            act_grad = lax.dot_general(
                slot_grads[span, :], down_ref[slot], LAST, preferred_element_type=F32
            )
            slope = sigmoid * (1.0 + gate_part * (1.0 - sigmoid))
            grads[slot, span, :256] = (act_grad * up_part * slope).astype(BF)
            grads[slot, span, 256:] = (act_grad * silu).astype(BF)
            out_sum[...] += jnp.dot(act, down_ref[slot], preferred_element_type=F32)
            back_sum[...] += lax.dot_general(
                grads[slot, span, :], up_ref[slot], LAST, preferred_element_type=F32
            )
            return carry

        lax.fori_loop(0, 4, quarter, 0)
        out = out_sum[...]
        gated = gate * out
        gate_grad = jnp.sum(cot * out.astype(BF).astype(F32), axis=1, keepdims=True)
        back = back_sum[...]
        inner = jnp.sum(back * joined[span, :].astype(F32), axis=1, keepdims=True)
        for i, block in enumerate(blocks):
            part = slice(i * ROOM, (i + 1) * ROOM)
            gated_ref[block] = gated[part].astype(BF)
            back_ref[block] = back[part].astype(BF)
            for index, value in enumerate((gate_grad, inner)):
                high, middle, low = pieces(jnp.sum(same * value[part], axis=0, keepdims=True))
                aux = jnp.where(line == CAP, high.astype(F32), 0.0)
                aux = aux + jnp.where(line == CAP + 1, middle.astype(F32), 0.0)
                aux = aux + jnp.where(line == CAP + 2, low.astype(F32), 0.0)
                for r in range(4):
                    start = r * 512 + index * HEAD
                    back_ref[block, :, start : start + HEAD] = (
                        back[part, start : start + HEAD] + aux
                    ).astype(BF)
        for number in returns[group]:
            links.send(number)
        if group == 0:
            own_out.start()
        for number in shares[group]:
            links.send(number)
    for numbers in shares:
        for number in numbers:
            links.arrive(number)

    def weight_grads(step, carry):
        span = pl.ds(pl.multiple_of(step * 512, 512), 512)
        for slot, up, down in ((0, up_1, down_1), (1, up_2, down_2)):
            up[span, :] = (
                lax.dot_general(joined[:, span], grads[slot], FIRST, preferred_element_type=F32)
                + lax.dot_general(
                    their_x[:, span], their_grads[slot], FIRST, preferred_element_type=F32
                )
            ).astype(BF)
            down[:, span] = (
                lax.dot_general(
                    acts[slot], slot_grads[:, span], FIRST, preferred_element_type=F32
                )
                + lax.dot_general(
                    their_acts[slot],
                    their_slot_grads[:, span],
                    FIRST,
                    preferred_element_type=F32,
                )
            ).astype(BF)
        return carry

    lax.fori_loop(0, 4, weight_grads, 0)
    own_out.wait()


def run_experts(blocks, cot_slots, weights):
    take, put = expert_views()
    came, returns, shares = ([[], [], [], []] for _ in range(3))
    sends = []
    for offset in CUBE:
        came[(offset[0] + offset[3]) % 4].append(len(sends))
        sends.append((offset, 0, take, ("scratch", 0), put))
    take, put = token_views()
    for offset in CUBE:
        returns[-(offset[0] + offset[3]) % 4].append(len(sends))
        sends.append((offset, ("scratch", 1), take, 0, put))
    for place in range(4):
        span = pl.ds(place * GROUP, GROUP)
        for mine, theirs in ((2, 6), (3, 7)):
            view = lambda ref, me, p, span=span: ref.at[span]
            shares[place].append(len(sends))
            sends.append((SIBLING, ("scratch", mine), view, ("scratch", theirs), view))
        for mine, theirs in ((4, 8), (5, 9)):
            shares[place].append(len(sends))
            sends.append(
                (
                    SIBLING,
                    ("scratch", mine),
                    lambda ref, me, p, span=span: ref.at[pl.ds(2, 2), span],
                    ("scratch", theirs),
                    lambda ref, me, p, span=span: ref.at[:, span],
                )
            )
    return exchange(
        [blocks] + weights,
        [shape((EXPERTS, ROOM, 512))],
        sends,
        [],
        8,
        work=lambda links, *refs: expert_kernel(
            links, came, returns, shares, *refs
        ),
        work_in=[cot_slots],
        work_out=[shape((16, ROOM, WIDTH))]
        + [shape((WIDTH, 512))] * 2
        + [shape((256, WIDTH))] * 2,
        work_scratch=[
            pltpu.VMEM((16, ROOM, WIDTH), BF),
            pltpu.VMEM((16, ROOM, WIDTH), BF),
            pltpu.VMEM((SLOTS, WIDTH), BF),
            pltpu.VMEM((SLOTS, WIDTH), BF),
            pltpu.VMEM((4, SLOTS, 256), BF),
            pltpu.VMEM((4, SLOTS, 512), BF),
            pltpu.VMEM((SLOTS, WIDTH), BF),
            pltpu.VMEM((SLOTS, WIDTH), BF),
            pltpu.VMEM((2, SLOTS, 256), BF),
            pltpu.VMEM((2, SLOTS, 512), BF),
            pltpu.VMEM((4, WIDTH, 512), BF),
            pltpu.VMEM((4, 256, WIDTH), BF),
            pltpu.VMEM((GROUP, WIDTH), F32),
            pltpu.VMEM((GROUP, WIDTH), F32),
            pltpu.SemaphoreType.DMA((8,)),
            pltpu.SemaphoreType.DMA((2,)),
        ],
        deferred=range(len(CUBE), len(sends)),
    )


def pack_kernel(up_1, up_2, down_1, down_2, up_ref, down_ref):
    upper = lax.axis_index("row") // 2
    for which, up, down in ((upper, up_1, down_1), (1 - upper, up_2, down_2)):
        value = up[...].astype(F32)
        up_ref[which, :, 0, :] = value[:, :256]
        up_ref[which, :, 1, :] = value[:, 256:]
        down_ref[which] = down[...].astype(F32)


def pack_grads(up_1, up_2, down_1, down_2):
    steps = 8
    up, down = (WIDTH // steps, 512), (256 // steps, WIDTH)
    return pl.pallas_call(
        pack_kernel,
        grid=(steps,),
        out_shape=[shape((2, WIDTH, 2, 256), F32), shape((2, 256, WIDTH), F32)],
        in_specs=[pl.BlockSpec(up, lambda i: (i, 0))] * 2
        + [pl.BlockSpec(down, lambda i: (i, 0))] * 2,
        out_specs=[
            pl.BlockSpec((2, up[0], 2, 256), lambda i: (0, i, 0, 0)),
            pl.BlockSpec((2,) + down, lambda i: (0, i, 0)),
        ],
    )(up_1, up_2, down_1, down_2)


def dot(left, right):
    return jnp.dot(left, right, preferred_element_type=F32)


def dot_last(left, right):
    return lax.dot_general(left, right, LAST, preferred_element_type=F32)


def dot_first(left, right):
    return lax.dot_general(left, right, FIRST, preferred_element_type=F32)


def pieces(value):
    high = value.astype(BF)
    rest = value - high.astype(F32)
    middle = rest.astype(BF)
    low = (rest - middle.astype(F32)).astype(BF)
    return [high, middle, low]


def aux_rows(value):
    held = jnp.stack(pieces(value), axis=1)
    return jnp.pad(held, ((0, 0), (CAP, ROOM - CAP - 3), (0, 512 - ROOM)))


def aux_value(blocks, index):
    part = blocks[:, CAP : CAP + 3, index * HEAD : index * HEAD + ROOM]
    return jnp.sum(part.astype(F32), axis=1)


FIRST_HOP = [
    ((2 * y + k) * 4 + x, (2 * y + 1 - x % 2) * 4 + 2 * k + x // 2)
    for y in range(4)
    for k in range(2)
    for x in range(4)
]
SECOND_HOP = [
    ((2 * y + k) * 4 + x, (2 * y + x % 2) * 4 + 2 * k + 1 - x // 2)
    for y in range(4)
    for k in range(2)
    for x in range(4)
]
PAIR = [(d, d ^ 1) for d in range(8)]


def hop(operand, pairs):
    return lax.ppermute(operand, ("dp", "row"), pairs)


def after(*operands):
    return lax.optimization_barrier(operands)


def inverse_pairs(pairs):
    return [(b, a) for a, b in pairs]


def shards(
    tokens,
    positions,
    routes,
    attention_norm_gain,
    experts_norm_gain,
    w_qkv,
    q_gain,
    k_gain,
    w_out,
    w_router,
    w_gate_up,
    w_down,
    cotangent,
):
    core = lax.axis_index("dp") % 2
    experts = jnp.arange(EXPERTS, dtype=jnp.int32)
    named = jnp.any(routes[:, :, None] == experts[None, None, :], axis=1)
    place = jnp.arange(512, dtype=jnp.int32)
    earlier = (place[None, :] < place[:, None]).astype(BF)
    rank = dot(earlier, named.astype(BF))
    rank = jnp.where(named, rank, -1.0).T
    (
        token_rows,
        w_group,
        position_rows,
        gain_rows,
        w_all,
        down_1,
        down_2,
        send_up_1,
        send_up_2,
        send_cot,
    ) = gather_inputs(
        tokens,
        w_qkv,
        w_out,
        w_down,
        positions.reshape(4, HEAD),
        attention_norm_gain.reshape(4, HEAD),
        [w_gate_up, rank, cotangent],
    )
    w_all = w_all.reshape(WIDTH, 512)
    w_group = w_group.reshape(WIDTH, 1536)
    gain_full = gain_rows.reshape(WIDTH)

    gate_up_1, gate_up_2 = hop(send_up_1, FIRST_HOP), hop(send_up_2, SECOND_HOP)
    sibling = lambda w: lax.ppermute(w, "dp", PAIR)
    frequency = THETA ** (-2.0 * jnp.arange(HEAD // 2, dtype=F32) / HEAD)
    half_signs = jnp.where(jnp.arange(HEAD) < HEAD // 2, -1.0, 1.0).astype(F32)
    frequency = jnp.concatenate(
        [jnp.concatenate([frequency] * 2)[None], half_signs[None], jnp.zeros((6, HEAD), F32)]
    )
    position_column = position_rows.reshape(SEQ, 1).astype(F32)
    gains = jnp.concatenate([q_gain[None], k_gain[None], jnp.zeros((6, HEAD), F32)], axis=0)

    pick = (rank[:, None, :] == jnp.arange(ROOM, dtype=F32)[None, :, None]).astype(BF)
    flat_pick = pick.reshape(EXPERTS * ROOM, 512)

    token_full = token_rows.astype(F32)
    inverse_attention = lax.rsqrt(jnp.mean(token_full * token_full, axis=1) + EPS)
    normed_exact = token_full * inverse_attention[:, None] * gain_full[None, :]
    normed = normed_exact.astype(BF)
    qkv = to_heads(dot(normed, w_group).astype(BF))
    cot_slots, query, key, lse, cosine, sine, attended_rows = attend(
        qkv, position_column, frequency, gains, send_cot
    )
    attended_rows, gate_up_1, gate_up_2, down_1, down_2 = after(
        attended_rows, gate_up_1, gate_up_2, down_1, down_2
    )
    up_ws = [gate_up_1, gate_up_2, sibling(gate_up_1), sibling(gate_up_2)]
    down_ws = [down_1, down_2, sibling(down_1), sibling(down_2)]

    token_float = tokens.astype(F32)
    hidden = token_float + dot(attended_rows, w_all)
    scaled_hidden = hidden * experts_norm_gain
    partial_stats = jnp.concatenate(
        [
            lax.dot_general(
                w_router.astype(F32),
                scaled_hidden,
                (((0,), (1,)), ((), ())),
                precision=EXACT,
                preferred_element_type=F32,
            ),
            jnp.sum(hidden * hidden, axis=1)[None],
            jnp.zeros((7, 512), F32),
        ],
        axis=0,
    )
    stats = jnp.sum(row_stack(partial_stats, 7), axis=0)
    inverse_experts = lax.rsqrt(stats[EXPERTS] / WIDTH + EPS)
    logits = stats[:EXPERTS] * inverse_experts[None, :]
    unit_experts = hidden * inverse_experts[:, None]
    experts_input = (unit_experts * experts_norm_gain).astype(BF)
    named_t = rank >= 0
    largest = jnp.max(jnp.where(named_t, logits, -jnp.inf), axis=0, keepdims=True)
    shifted = jnp.where(named_t, jnp.exp(jnp.where(named_t, logits - largest, 0.0)), 0.0)
    gates = shifted / jnp.sum(shifted, axis=0, keepdims=True)
    slot_gates = jnp.sum(pick.astype(F32) * gates[:, None, :], axis=2)
    send_rows = dot(flat_pick, experts_input).astype(BF).reshape(EXPERTS, ROOM, 512)
    back_rows, out_rows, up_1, up_2, down_1, down_2 = run_experts(
        send_rows + aux_rows(slot_gates), cot_slots, up_ws + down_ws
    )
    gate_grad = jnp.sum(pick.astype(F32) * aux_value(back_rows, 0)[:, :, None], axis=1)
    inner = jnp.sum(pick.astype(F32) * aux_value(back_rows, 1)[:, :, None], axis=(0, 1))
    first_back, second_back = inverse_pairs(FIRST_HOP), inverse_pairs(SECOND_HOP)
    logit_grad = gates * (gate_grad - jnp.sum(gates * gate_grad, axis=0, keepdims=True))
    experts_input_grad = dot_first(
        flat_pick, back_rows.reshape(EXPERTS * ROOM, 512)
    ) + lax.dot_general(
        logit_grad,
        w_router.astype(F32),
        (((0,), (1,)), ((), ())),
        precision=EXACT,
        preferred_element_type=F32,
    )
    mean_experts = (inner + jnp.sum(logit_grad * logits, axis=0)) / WIDTH
    cot_float = cotangent.astype(F32)
    middle_grad = cot_float + inverse_experts[:, None] * (
        experts_input_grad * experts_norm_gain - unit_experts * mean_experts[:, None]
    )
    router_part = lax.dot_general(
        logit_grad,
        experts_input.astype(F32),
        (((1,), (0,)), ((), ())),
        precision=EXACT,
        preferred_element_type=F32,
    )
    experts_gain_part = jnp.sum(experts_input_grad * unit_experts, axis=0)
    attended_grad = middle_grad.astype(BF)
    out_part = dot_first(attended_rows, attended_grad).astype(BF).reshape(16, HEAD, 512)
    small_part = jnp.concatenate(
        [
            router_part.reshape(256, HEAD),
            experts_gain_part.reshape(4, HEAD),
            jnp.zeros((124, HEAD), F32),
        ],
        axis=0,
    )
    out_rows, qkv_grad, head_gain_part = attend_back(
        [dot_last(attended_grad, w_all).astype(BF), qkv, query, key, lse, cosine, sine, gains],
        out_rows,
    )
    qkv_grad, up_1, up_2, down_1, down_2 = after(qkv_grad, up_1, up_2, down_1, down_2)
    up_1, up_2 = hop(up_1, first_back), hop(up_2, second_back)
    down_1, down_2 = hop(down_1, first_back), hop(down_2, second_back)
    qkv_grad, out_other, small_other, output = from_heads(
        qkv_grad,
        out_part,
        small_part,
        [hidden, flat_pick, out_rows.reshape(EXPERTS * ROOM, 512)],
    )
    out_half = (
        lax.dynamic_slice_in_dim(out_part, core * 64, 64, 1).astype(F32)
        + out_other.astype(F32)
    ).astype(BF)
    small = (small_part + small_other).reshape(16, 24, HEAD)
    out_pieces, small_pieces, qkv_piece, normed_grad, row_stats = finish(
        out_half, small, normed, qkv_grad, w_group, head_gain_part
    )
    normed_grad = jnp.sum(normed_grad.astype(F32), axis=0)
    row_stats = jnp.sum(row_stats, axis=0)
    mean_attention = row_stats[:4].reshape(512) / WIDTH
    unit_attention = token_float * inverse_attention[:, None]
    token_grad = middle_grad + inverse_attention[:, None] * (
        normed_grad * attention_norm_gain - unit_attention * mean_attention[:, None]
    )
    attention_gain_part = jnp.sum(normed_grad * unit_attention, axis=0)

    out_piece = jnp.sum(out_pieces.astype(F32), axis=0).astype(BF)
    out_total, small_total, late, qkv_total = collect_sums(
        qkv_piece,
        out_piece,
        jnp.sum(small_pieces, axis=0),
        jnp.concatenate([attention_gain_part.reshape(4, HEAD), row_stats[4:]], axis=0),
    )
    small_total = small_total.reshape(384, HEAD)
    late = jnp.sum(late, axis=0)
    grad_gate_up, grad_down = pack_grads(up_1, up_2, down_1, down_2)
    return (
        output,
        token_grad.astype(BF),
        late[:4].reshape(512),
        small_total[256:260].reshape(512),
        qkv_total.astype(F32).reshape(512, 4, 384),
        late[4],
        late[5],
        out_total.astype(F32).reshape(512, 512),
        small_total[:256].reshape(EXPERTS, 512).T,
        grad_gate_up,
        grad_down,
    )


def solution(mesh):
    tokens_like = P(("dp", "col"), "row")
    up_like = P(("dp", "col"), None, None, "row")
    down_like = P(("dp", "col"), "row", None)
    return jax.shard_map(
        shards,
        mesh=mesh,
        in_specs=(
            tokens_like,
            P("dp", "row"),
            P(("dp", "col"), None),
            P("row"),
            P("row"),
            P("row", "col", None),
            P(),
            P(),
            P("col", "row"),
            P("row", None),
            up_like,
            down_like,
            tokens_like,
        ),
        out_specs=(
            tokens_like,
            tokens_like,
            P("row"),
            P("row"),
            P("row", "col", None),
            P(),
            P(),
            P("col", "row"),
            P("row", None),
            up_like,
            down_like,
        ),
        check_vma=False,
    )
```

```python
import jax
import jax.numpy as jnp
from jax import lax
from jax.experimental import pallas as pl
from jax.experimental.pallas import tpu as pltpu
from jax.sharding import PartitionSpec as P

WIDTH = 2048
HEAD = 128
EXPERTS = 64
CAP = 36
ROOM = 40
SEQ = 2048
EPS = 1e-06
THETA = 10000.0
EXACT = lax.Precision.HIGHEST
MESH = pl.DeviceIdType.MESH
SIZES = (4, 2, 4, 4)
BF = jnp.bfloat16
F32 = jnp.float32
ROWS = [(0, 0, d, 0) for d in (2, 1, 3)]
COLS = [(0, 0, 0, d) for d in (2, 1, 3)]
SIBLING = (0, 1, 0, 0)
PLANE = [(0, 0, i, (i + s) % 4) for s in range(4) for i in range(4) if (i, s) != (0, 0)]
CUBE = [
    (i, 0, (i + s) % 4, (g - i) % 4)
    for g in range(4)
    for s in range(4)
    for i in range(4)
    if (g, s, i) != (0, 0, 0)
]
SOURCES = [(i, 0, 0, (i + s) % 4) for s in range(4) for i in range(4) if (i, s) != (0, 0)]
SIDES = [(i, 0, (i + s) % 4, 0) for s in range(4) for i in range(4) if (i, s) != (0, 0)]
LINES = [(d, 0, 0, 0) for d in (2, 1, 3)]
OTHERS = [
    (a, k, 0, d) for a in range(4) for k in range(2) for d in range(4) if (a, k, d) != (0, 0, 0)
]


def shape(dims, dtype=BF):
    return jax.ShapeDtypeStruct(dims, dtype)


def here():
    group = lax.axis_index("dp")
    return (group // 2, group % 2, lax.axis_index("row"), lax.axis_index("col"))


class Hop:
    def __init__(self, to, origin):
        self.to, self.origin = to, origin


ONE_WAY = Hop(
    lambda p: (p[0], 1 - p[2] % 2, 2 * p[1] + p[2] // 2, p[3]),
    lambda p: (p[0], p[2] // 2, 2 * (p[2] % 2) + 1 - p[1], p[3]),
)
OTHER_WAY = Hop(
    lambda p: (p[0], p[2] % 2, 2 * p[1] + 1 - p[2] // 2, p[3]),
    lambda p: (p[0], p[2] // 2, 2 * (1 - p[2] % 2) + p[1], p[3]),
)


ONE_BACK, OTHER_BACK = Hop(ONE_WAY.origin, ONE_WAY.to), Hop(OTHER_WAY.origin, OTHER_WAY.to)


class Links:
    def __init__(self, send, arrive, ins, outs):
        self.send, self.arrive, self.ins, self.outs = send, arrive, ins, outs


def moved(place, offset):
    if isinstance(offset, Hop):
        return offset.to(place)
    return tuple((p + o) % n for p, o, n in zip(place, offset, SIZES))


def device(place):
    return (place[0] * 2 + place[1], place[2], place[3])


def exchange(
    inputs,
    outputs,
    sends,
    kept,
    call_id,
    micros=30,
    work=None,
    work_in=(),
    work_out=(),
    work_scratch=(),
    stages=(),
    deferred=(),
):
    offsets = sorted({s[0] for s in sends if not isinstance(s[0], Hop)})
    hops = {id(s[0]): s[0] for s in sends if isinstance(s[0], Hop)}.values()
    n_in, n_out, n_send = len(inputs), len(outputs), len(sends)
    m_in, m_out = len(work_in), len(work_out)

    def kernel(*refs):
        ins, refs = refs[:n_in], refs[n_in:]
        worked, refs = refs[:m_in], refs[m_in:]
        outs, refs = refs[:n_out], refs[n_out:]
        made, refs = refs[:m_out], refs[m_out:]
        send_sem, recv_sem, kept_sem = refs[:3]
        staged, refs = refs[3 : 3 + len(kept)], refs[3 + len(kept) :]
        special = {"work": worked, "made": made, "scratch": refs}
        me = here()
        barrier = pltpu.get_barrier_semaphore()
        greeted = [moved(me, offset) for offset in offsets]
        for way in hops:
            greeted += [way.to(me), way.origin(me)]
        for peer in greeted:
            pl.semaphore_signal(barrier, inc=1, device_id=device(peer), device_id_type=MESH)
        local = []
        for index, (i, take, o, put, _) in enumerate(kept):
            source, target = take(ins[i], me), put(outs[o], me)
            local.append(
                (
                    pltpu.make_async_copy(source, staged[index], kept_sem.at[index, 0]),
                    pltpu.make_async_copy(staged[index], target, kept_sem.at[index, 1]),
                )
            )
            local[-1][0].start()
        pl.semaphore_wait(barrier, len(greeted))
        copies, arrived = {}, set()

        def arrive(index):
            if index not in arrived:
                arrived.add(index)
                copies[index].wait_recv()

        def named(group, index):
            return special[index[0]][index[1]] if isinstance(index, tuple) else group[index]

        def start(index):
            offset, i, take, o, put = sends[index][:5]
            needs = sends[index][5] if len(sends[index]) > 5 else None
            for need in needs or ():
                if need >= 0:
                    arrive(need)
                elif need not in arrived:
                    arrived.add(need)
                    local[-need - 1][1].wait()
            peer = moved(me, offset)
            copies[index] = pltpu.make_async_remote_copy(
                src_ref=take(named(ins if needs is None else outs, i), me, peer),
                dst_ref=put(named(outs, o), me, peer),
                send_sem=send_sem.at[index],
                recv_sem=recv_sem.at[index],
                device_id=device(peer),
                device_id_type=MESH,
            )
            copies[index].start()

        links = Links(start, arrive, ins, outs)
        parts = work(links, *worked, *made, *refs) if stages else ()
        first = [i for i in range(n_send) if len(sends[i]) < 6 and i not in deferred]
        for index in first:
            start(index)
        for load, store in local:
            load.wait()
            store.start()
        for index in range(n_send):
            if index in first or index in deferred:
                continue
            for part, at in zip(parts, stages):
                if at == index:
                    part()
            start(index)
        if work is not None and not stages:
            work(links, *worked, *made, *refs)
        for index in range(n_send):
            arrive(index)
        for copy in copies.values():
            copy.wait_send()
        for index, copy in enumerate(local):
            if -index - 1 not in arrived:
                copy[1].wait()

    return pl.pallas_call(
        kernel,
        out_shape=list(outputs) + list(work_out),
        in_specs=[pl.BlockSpec(memory_space=pl.ANY)] * n_in
        + [pl.BlockSpec(memory_space=pltpu.VMEM)] * m_in,
        out_specs=[pl.BlockSpec(memory_space=pl.ANY)] * n_out
        + [pl.BlockSpec(memory_space=pltpu.VMEM)] * m_out,
        scratch_shapes=[
            pltpu.SemaphoreType.DMA((n_send,)),
            pltpu.SemaphoreType.DMA((n_send,)),
            pltpu.SemaphoreType.DMA((max(1, len(kept)), 2)),
            *[pltpu.VMEM(k[4], inputs[k[0]].dtype) for k in kept],
            *work_scratch,
        ],
        compiler_params=pltpu.CompilerParams(
            collective_id=call_id,
            has_side_effects=True,
            vmem_limit_bytes=(8 if work is None else 60) * 2**20,
        ),
        cost_estimate=pl.CostEstimate(
            flops=0, bytes_accessed=micros * 3_500_000, transcendentals=0
        ),
    )(*inputs, *work_in)


def rows(start, size):
    return pl.ds(pl.multiple_of(start, size), size)


def eighth(size):
    me = here()
    return rows((me[1] * 4 + me[0]) * size, size)


def half(size):
    return rows(here()[1] * size, size)


class Sends(list):
    def add(self, group, take, o, put=None, i=None, needs=None):
        first = len(self)
        for offset in group:
            if needs is None:
                self.append((offset, i, take, o, put))
            else:
                view = lambda ref, me, p: take(ref, me)
                self.append((offset, o, view, o, view, needs))
        return list(range(first, len(self)))


def early_kernel(links, up_ref, rank_ref, cot_ref, up_1, up_2, rows_ref):
    upper = lax.axis_index("row") // 2

    def unpack(which, target, first):
        def part():
            for step in range(4):
                span = pl.ds(first + step * 64, 64)
                target[span, :256] = up_ref[which, span, 0, :]
                target[span, 256:] = up_ref[which, span, 1, :]

        return part

    def pick(step):
        def part():
            ranks = rank_ref[step * 8 : step * 8 + 8, :]
            slots = lax.broadcasted_iota(jnp.int32, (8, ROOM, 512), 1).astype(F32)
            chosen = (ranks[:, None, :] == slots).astype(F32).reshape(8 * ROOM, 512)
            rows_of = jnp.dot(chosen.astype(BF), cot_ref[...], preferred_element_type=F32)
            rows_ref[pl.ds(step * 8, 8)] = rows_of.reshape(8, ROOM, 512).astype(BF)

        return part

    parts = [unpack(upper, up_1, step * 256) for step in range(8)]
    parts += [unpack(1 - upper, up_2, step * 256) for step in range(8)]
    return parts + [pick(step) for step in range(8)]


def gather_inputs(tokens, w_qkv, w_out, w_down, small_int, small_float, early):
    outputs = [
        shape((512, WIDTH)),
        shape((4, 512, 1536)),
        shape((4, 4, HEAD), jnp.int32),
        shape((4, 4, HEAD), F32),
        shape((4, 4, HEAD, 512)),
        shape((256, WIDTH)),
        shape((256, WIDTH)),
    ]
    sends = Sends()
    own_cols = lambda me: rows(me[3] * 384, 384)
    low, high = pl.ds(0, 2), pl.ds(2, 2)
    first = sends.add(
        ROWS,
        lambda s, me, p: s.at[eighth(64), rows(p[2] * 384, 384)],
        1,
        lambda o, me, p: o.at[me[2], eighth(64), own_cols(me)],
        1,
    )
    both = [(0, 0, 1, 0), (0, 0, 3, 0)]
    beside = sends.add(
        both, lambda s, me, p: s, 0, lambda o, me, p: o.at[:, rows(me[2] * 512, 512)], 0
    )
    sends.add(ROWS, lambda s, me, p: s, 2, lambda o, me, p: o.at[me[2]], 2)
    sends.add(ROWS, lambda s, me, p: s, 3, lambda o, me, p: o.at[me[2]], 3)
    sends.append((ONE_WAY, 5, lambda s, me, p: s.at[me[2] // 2], 5, lambda o, me, p: o))
    sends.append((OTHER_WAY, 5, lambda s, me, p: s.at[1 - me[2] // 2], 6, lambda o, me, p: o))
    out_z = sends.add(COLS, lambda o, me: o.at[low, me[3], eighth(16)], 4, needs=[-2])
    out_y = sends.add(LINES, lambda o, me: o.at[high, me[3], eighth(16)], 4, needs=[-2])
    stages = [len(sends)] * 3
    by_z = sends.add(
        COLS, lambda o, me: o.at[low, eighth(64), own_cols(me)], 1, needs=[-1] + first
    )
    by_y = sends.add(LINES, lambda o, me: o.at[high, eighth(64), own_cols(me)], 1, needs=first)
    sends.add(LINES, lambda o, me: o.at[low, eighth(64), own_cols(me)], 1, needs=first)
    sends.add(COLS, lambda o, me: o.at[high, eighth(64), own_cols(me)], 1, needs=first)
    last_z, last_y = {0: [len(sends) - 6 + i for i in range(3)]}, {0: list(range(len(sends) - 3, len(sends)))}
    for d in (1, 3, 2):
        came = by_z[[offset[3] for offset in COLS].index(d)]
        cols = lambda me, d=d: rows((me[3] + 4 - d) % 4 * 384, 384)
        stages += [len(sends)] * (3 if d == 1 else 1)
        last_z[d] = sends.add(
            LINES,
            lambda o, me, cols=cols: o.at[low, eighth(64), cols(me)],
            1,
            needs=[came],
        )
        came = by_y[[offset[0] for offset in LINES].index(d)]
        span = lambda me, d=d: rows((me[1] * 4 + (me[0] + 4 - d) % 4) * 64, 64)
        stages.append(len(sends))
        last_y[d] = sends.add(
            COLS,
            lambda o, me, span=span: o.at[high, span(me), own_cols(me)],
            1,
            needs=[came],
        )
    for index, offset in enumerate(both):
        passed = lambda o, me, index=index, d=offset[2]: o.at[
            pl.ds(index * 256, 256), rows((me[2] + 4 - d) % 4 * 512, 512)
        ]
        sends.add([offset], passed, 0, needs=[beside[index]])
    stages.append(len(sends))
    out_zy = sends.add(LINES, lambda o, me: o.at[low, :, eighth(16)], 4, needs=out_z)
    stages.append(len(sends))
    out_yz = sends.add(COLS, lambda o, me: o.at[high, me[3], half(64)], 4, needs=out_y)
    stages.append(len(sends))
    pair = [SIBLING]
    sends.add(pair, lambda o, me: o.at[low, eighth(64)], 1, needs=by_z)
    sends.add(pair, lambda o, me: o.at[high, half(256), own_cols(me)], 1, needs=by_y)
    for d in (1, 3, 2):
        line = [offset[0] for offset in LINES].index(d)
        stages += [len(sends)] * (4 if d == 1 else 2)
        span = lambda me, d=d: rows((me[1] * 4 + (me[0] + 4 - d) % 4) * 64, 64)
        sends.add(
            pair,
            lambda o, me, span=span: o.at[low, span(me)],
            1,
            needs=[numbers[line] for numbers in last_z.values()],
        )
        col = [offset[3] for offset in COLS].index(d)
        stages += [len(sends)] * (24 - len(stages) if d == 2 else 1)
        cols = lambda me, d=d: rows((me[3] + 4 - d) % 4 * 384, 384)
        sends.add(
            pair,
            lambda o, me, cols=cols: o.at[high, half(256), cols(me)],
            1,
            needs=[numbers[col] for numbers in last_y.values()],
        )
    sends.add(pair, lambda o, me: o.at[low, :, half(64)], 4, needs=out_zy)
    sends.add(pair, lambda o, me: o.at[high, :, half(64)], 4, needs=out_yz)
    kept = [
        (
            1,
            lambda s, me: s.at[eighth(64), rows(me[2] * 384, 384)],
            1,
            lambda o, me: o.at[me[2], eighth(64), own_cols(me)],
            (64, 384),
        ),
        (
            4,
            lambda s, me: s.at[:, eighth(16)],
            4,
            lambda o, me: o.at[:, me[3], eighth(16)],
            (4, 16, 512),
        ),
        (0, lambda s, me: s, 0, lambda o, me: o.at[:, rows(me[2] * 512, 512)], (512, 512)),
        (2, lambda s, me: s, 2, lambda o, me: o.at[me[2]], (4, HEAD)),
        (3, lambda s, me: s, 3, lambda o, me: o.at[me[2]], (4, HEAD)),
    ]
    return exchange(
        [
            tokens,
            w_qkv.reshape(512, 1536),
            small_int,
            small_float,
            w_out.reshape(4, HEAD, 512),
            w_down,
        ],
        outputs,
        sends,
        kept,
        0,
        work=early_kernel,
        work_in=early,
        work_out=[
            shape((WIDTH, 512)),
            shape((WIDTH, 512)),
            shape((EXPERTS, ROOM, 512)),
        ],
        stages=stages,
    )


def to_heads(qkv):
    take = lambda s, me, p: s.at[:, rows(p[3] * 384, 384)]
    put = lambda o, me, p: o.at[rows(me[3] * 512, 512)]
    return exchange(
        [qkv],
        [shape((SEQ, 384))],
        [(offset, 0, take, 0, put) for offset in COLS],
        [(0, lambda s, me: take(s, me, me), 0, lambda o, me: put(o, me, me), (512, 384))],
        1,
    )[0]


def row_stack(operand, call_id):
    take = lambda s, me, p: s
    put = lambda o, me, p: o.at[me[2]]
    return exchange(
        [operand],
        [shape((4,) + operand.shape, operand.dtype)],
        [(offset, 0, take, 0, put) for offset in ROWS],
        [(0, lambda s, me: s, 0, lambda o, me: put(o, me, me), operand.shape)],
        call_id,
    )[0]


def finish_kernel(
    links,
    numbers,
    normed_ref,
    grad_ref,
    weight_ref,
    gain_ref,
    hidden_ref,
    pick_ref,
    rows_ref,
    by_y_ref,
    by_z_ref,
    feature_ref,
    stat_ref,
    out_ref,
    their_half,
    came,
    half,
    spread_y,
    spread_z,
    feature_part,
    stat_part,
    feature_sum,
    passing,
):
    me = here()
    y, core, row, col = me
    to_sibling, to_lines, to_cols, to_rows, last = numbers

    def product(start):
        return lax.dot_general(
            normed_ref[:, rows(start, 256)], grad_ref[...], FIRST, preferred_element_type=F32
        )

    for r in range(4):
        their_half[r] = product(r * 512 + (1 - core) * 256).astype(BF)
        links.send(to_sibling[r])
    inner = jnp.zeros((512, 1), F32)
    for ahead in (2, 1, 3, 0):
        span = rows(lax.rem(row + ahead, 4) * 512, 512)
        part = lax.dot_general(
            grad_ref[...], weight_ref[span, :], LAST, preferred_element_type=F32
        )
        inner = inner + jnp.sum(part * normed_ref[:, span].astype(F32), axis=1, keepdims=True)
        if ahead == 2:
            feature_part[1] = part.astype(BF)
            for number in to_rows[2]:
                links.send(number)
        elif ahead:
            feature_sum[ahead // 2] = part
        else:
            feature_ref[0] = part.astype(BF)
    for index, ahead in enumerate((1, 3)):
        links.arrive(to_rows[2][index])
        part = slice(index * 256, (index + 1) * 256)
        feature_sum[index, part, :] += passing[index].astype(F32)
        feature_part[ahead - 1] = feature_sum[index].astype(BF)
        links.send(to_rows[ahead])
    same = (
        lax.broadcasted_iota(jnp.int32, (HEAD, HEAD), 0)
        == lax.broadcasted_iota(jnp.int32, (HEAD, HEAD), 1)
    ).astype(F32)
    for block in range(4):
        stat_part[block : block + 1, :] = jnp.sum(
            same * inner[block * HEAD : (block + 1) * HEAD], axis=0, keepdims=True
        )
    stat_part[4:, :] = gain_ref[:4, :]
    stat_ref[row] = stat_part[...]
    for number in last:
        links.send(number)
    for r in range(4):
        mine = product(r * 512 + core * 256)
        links.arrive(to_sibling[r])
        half[r] = (mine + came[r].astype(F32)).astype(BF)
        for number in to_lines[r] + to_cols[r]:
            links.send(number)
        spread_y[y, r] = half[r, rows(y * 32, 32), :]
        spread_z[col, r] = half[r, 128:, rows(col * 384, 384)]
    out_ref[...] = (
        hidden_ref[...]
        + lax.dot_general(pick_ref[...], rows_ref[...], FIRST, preferred_element_type=F32)
    ).astype(BF)
    for r in range(4):
        for numbers_of, target, spread in (
            (to_lines, by_y_ref, spread_y),
            (to_cols, by_z_ref, spread_z),
        ):
            for number in numbers_of[r]:
                links.arrive(number)
            total = spread[0, r].astype(F32)
            for source in range(1, 4):
                total = total + spread[source, r].astype(F32)
            target[r] = total.astype(BF)


def finish(out_half, small, down_1, down_2, operands):
    take_out = lambda s, me, p: s.at[p[0] * 4 + p[3]]
    put_out = lambda o, me, p: o.at[me[0] * 4 + me[3]]
    whole = lambda s, me, p: s
    own_row = lambda o, me, p: o.at[me[2]]
    keep = lambda i, dims: (
        i,
        lambda s, me: take_out(s, me, me),
        i,
        lambda o, me: put_out(o, me, me),
        dims,
    )
    sends = [(offset, 0, take_out, 0, put_out) for offset in SOURCES]
    sends += [(offset, 1, take_out, 1, put_out) for offset in SOURCES]
    later = len(sends)
    to_sibling, to_lines, to_cols = [], [[], [], [], []], [[], [], [], []]
    to_rows, last = {}, []
    for r in range(4):
        view = lambda ref, me, p, r=r: ref.at[r]
        to_sibling.append(len(sends))
        sends.append((SIBLING, ("scratch", 0), view, ("scratch", 1), view))
    for r in range(4):
        for offset in LINES:
            to_lines[r].append(len(sends))
            sends.append(
                (
                    offset,
                    ("scratch", 2),
                    lambda s, me, p, r=r: s.at[r, rows(p[0] * 32, 32)],
                    ("scratch", 3),
                    lambda o, me, p, r=r: o.at[me[0], r],
                )
            )
        for offset in COLS:
            to_cols[r].append(len(sends))
            sends.append(
                (
                    offset,
                    ("scratch", 2),
                    lambda s, me, p, r=r: s.at[r, pl.ds(128, 128), rows(p[3] * 384, 384)],
                    ("scratch", 4),
                    lambda o, me, p, r=r: o.at[me[3], r],
                )
            )
    to_rows[2] = [len(sends), len(sends) + 1]
    for index, offset in enumerate(((0, 0, 1, 0), (0, 0, 3, 0))):
        part = lambda s, me, p, index=index: s.at[1, pl.ds(index * 256, 256)]
        slot = lambda o, me, p, index=index: o.at[index]
        sends.append((offset, ("scratch", 5), part, ("scratch", 8), slot))
    for index, offset in enumerate(((0, 0, 1, 0), (0, 0, 3, 0))):
        to_rows[offset[2]] = len(sends)
        part = lambda s, me, p, ahead=offset[2]: s.at[ahead - 1]
        slot = lambda o, me, p, index=index: o.at[1 + index]
        sends.append((offset, ("scratch", 5), part, ("made", 2), slot))
    for offset in ROWS:
        last.append(len(sends))
        sends.append((offset, ("scratch", 6), whole, ("made", 3), own_row))
    for way, index in ((ONE_BACK, 2), (OTHER_BACK, 3)):
        last.append(len(sends))
        sends.append((way, index, whole, index, whole))
    return exchange(
        [out_half, small, down_1, down_2],
        [shape((16, 64, 512)), shape((16,) + small.shape[1:], F32)]
        + [shape(down_1.shape)] * 2,
        sends,
        [keep(0, (64, 512)), keep(1, small.shape[1:])],
        5,
        work=lambda links, *refs: finish_kernel(
            links, (to_sibling, to_lines, to_cols, to_rows, last), *refs
        ),
        work_in=operands,
        work_out=[
            shape((4, 32, 1536)),
            shape((4, 128, 384)),
            shape((3, 512, 512)),
            shape((4, 8, HEAD), F32),
            shape((512, 512)),
        ],
        work_scratch=[pltpu.VMEM((4, 256, 1536), BF)] * 3
        + [
            pltpu.VMEM((4, 4, 32, 1536), BF),
            pltpu.VMEM((4, 4, 128, 384), BF),
            pltpu.VMEM((3, 512, 512), BF),
            pltpu.VMEM((8, HEAD), F32),
            pltpu.VMEM((2, 512, 512), F32),
            pltpu.VMEM((2, 256, 512), BF),
        ],
        deferred=range(later, len(sends)),
    )


def expert_at(place):
    return place[0] * 16 + (place[2] // 2) * 8 + place[3] * 2 + place[2] % 2


def expert_views():
    return (
        lambda s, me, p: s.at[expert_at(p)],
        lambda o, me, p: o.at[me[0] * 4 + me[3], :, rows(me[2] * 512, 512)],
    )


def token_views():
    return (
        lambda s, me, p: s.at[p[0] * 4 + p[3], :, rows(p[2] * 512, 512)],
        lambda o, me, p: o.at[expert_at(me)],
    )


def collect_sums(by_y, by_z, out_piece, small_piece, late, up_grad):
    put_qkv = lambda o, me, p: o.at[me[1], :, me[0]]
    put_out = lambda o, me, p: o.at[me[0], me[1]]
    put_small = lambda o, me, p: o.at[me[0] * 4 + me[3]]
    put_late = lambda o, me, p: o.at[(me[0] * 2 + me[1]) * 4 + me[3]]
    whole = lambda s, me, p: s
    sends = Sends()
    heads = sends.add(
        PLANE,
        lambda s, me, p: s.at[p[2], :, rows(p[3] * 384, 384)],
        ("scratch", 0),
        lambda o, me, p: o.at[me[3], me[2]],
        ("work", 0),
    )
    heads += sends.add(
        SIDES,
        lambda s, me, p: s.at[p[2], rows(p[0] * 32, 32)],
        ("scratch", 1),
        lambda o, me, p: o.at[me[0], me[2]],
        ("work", 1),
    )
    out_sent = sends.add(LINES, whole, 0, put_out, 0)
    sends.add([SIBLING], whole, 0, put_out, 0)
    sends.add(SOURCES, whole, 1, put_small, 1)
    sends.add(OTHERS, whole, 2, put_late, 2)
    sends.add([OTHER_BACK], whole, 3, whole, 3)
    later = len(sends)
    qkv_sent = sends.add(LINES, whole, ("made", 0), put_qkv, ("scratch", 2))
    sends.add([SIBLING], whole, ("made", 0), put_qkv, ("scratch", 2))
    relays = []
    for index in (1, 2, 0):
        origin = lambda me, d=LINES[index][0]: (me[0] + 4 - d) % 4
        view = lambda ref, me, p, origin=origin: ref.at[origin(me), me[1]]
        relays.append((out_sent[index], len(sends)))
        sends.append((SIBLING, 0, view, 0, view, [out_sent[index]]))
    for index in (1, 2, 0):
        origin = lambda me, d=LINES[index][0]: (me[0] + 4 - d) % 4
        view = lambda ref, me, p, origin=origin: ref.at[me[1], :, origin(me)]
        relays.append((qkv_sent[index], len(sends)))
        sends.append((SIBLING, ("made", 0), view, ("made", 0), view, [qkv_sent[index]]))

    def work(links, by_y_ref, by_z_ref, total_ref, spread_z, spread_y, mine):
        me = here()
        spread_z[me[3], me[2]] = by_y_ref[me[2], :, rows(me[3] * 384, 384)]
        spread_y[me[0], me[2]] = by_z_ref[me[2], rows(me[0] * 32, 32), :]
        for number in heads:
            links.arrive(number)
        for part, spread in ((0, spread_z), (1, spread_y)):
            for head in range(4):
                total = spread[0, head].astype(F32)
                for source in range(1, 4):
                    total = total + spread[source, head].astype(F32)
                mine[part, :, head * 384 : (head + 1) * 384] = total.astype(BF)
        for number in range(later, later + 4):
            links.send(number)
        for part in range(2):
            total_ref[me[1], part, me[0]] = mine[part]
        for came, number in relays:
            links.arrive(came)
            links.send(number)

    return exchange(
        [out_piece, small_piece, late, up_grad],
        [
            shape((4, 2, 64, 512)),
            shape((16,) + small_piece.shape, F32),
            shape((32,) + late.shape, F32),
            shape(up_grad.shape),
        ],
        sends,
        [
            (0, lambda s, me: s, 0, lambda o, me: put_out(o, me, me), (64, 512)),
            (1, lambda s, me: s, 1, lambda o, me: put_small(o, me, me), small_piece.shape),
            (2, lambda s, me: s, 2, lambda o, me: put_late(o, me, me), late.shape),
        ],
        12,
        work=work,
        work_in=[by_y, by_z],
        work_out=[shape((2, 2, 4, 32, 1536))],
        work_scratch=[
            pltpu.VMEM((4, 4, 32, 384), BF),
            pltpu.VMEM((4, 4, 32, 384), BF),
            pltpu.VMEM((2, 32, 1536), BF),
        ],
        deferred=range(later, len(sends)),
    )


BLOCK = 256
SCALE = HEAD ** (-0.5)
LAST = (((1,), (1,)), ((), ()))
FIRST = (((0,), (0,)), ((), ()))


def swapped(operand):
    return pltpu.roll(operand, HEAD // 2, 1)


def attend_kernel(
    links,
    ready,
    qkv_ref,
    position_ref,
    frequency_ref,
    gain_ref,
    query_ref,
    key_ref,
    lse_ref,
    cos_ref,
    sin_ref,
    gathered,
    out_ref,
):
    def prepare(step, carry):
        span = pl.ds(pl.multiple_of(step * BLOCK, BLOCK), BLOCK)
        angles = position_ref[span, :] * frequency_ref[0:1, :]
        cos_ref[span, :] = jnp.cos(angles)
        sin_ref[span, :] = jnp.sin(angles) * frequency_ref[1:2, :]
        for part, target in ((0, query_ref), (1, key_ref)):
            raw = qkv_ref[span, part * HEAD : (part + 1) * HEAD].astype(F32)
            scaled = (
                raw
                * lax.rsqrt(jnp.mean(raw * raw, axis=1, keepdims=True) + EPS)
                * gain_ref[part : part + 1, :]
            )
            target[span, :] = (scaled * cos_ref[span, :] + swapped(scaled) * sin_ref[span, :]).astype(
                BF
            )
        return carry

    lax.fori_loop(0, SEQ // BLOCK, prepare, 0)
    row, col = lax.axis_index("row"), lax.axis_index("col")
    for ahead in (1, 3, 2, 0):
        first = lax.rem(col + ahead, 4) * 512

        def block(step, carry, first=first):
            span = pl.ds(pl.multiple_of(first + step * BLOCK, BLOCK), BLOCK)
            scores = (
                lax.dot_general(
                    query_ref[span, :], key_ref[...], LAST, preferred_element_type=F32
                )
                * SCALE
            )
            largest = jnp.max(scores, axis=1, keepdims=True)
            weights = jnp.exp(scores - largest)
            total = jnp.sum(weights, axis=1, keepdims=True)
            mixed = jnp.dot(
                weights.astype(BF), qkv_ref[:, 2 * HEAD :], preferred_element_type=F32
            )
            out_ref[span, :] = (mixed / total).astype(BF)
            lse_ref[span, :] = largest + jnp.log(total)
            return carry

        lax.fori_loop(0, 512 // BLOCK, block, 0)
        for number in ready[ahead]:
            links.send(number)
    gathered[:, rows((row * 4 + col) * HEAD, HEAD)] = out_ref[rows(col * 512, 512), :]


def attend(qkv, position, frequency, gains, blocks):
    take, put = expert_views()
    sends = [(offset, 0, take, 0, put) for offset in CUBE]
    ready = {ahead: [] for ahead in range(4)}
    for offset in PLANE:
        ready[offset[3]].append(len(sends))
        sends.append(
            (
                offset,
                ("scratch", 0),
                lambda s, me, p: s.at[rows(p[3] * 512, 512)],
                ("made", 5),
                lambda o, me, p: o.at[:, rows((me[2] * 4 + me[3]) * HEAD, HEAD)],
            )
        )
    return exchange(
        [blocks],
        [shape((16, ROOM, WIDTH))],
        sends,
        [(0, lambda s, me: take(s, me, me), 0, lambda o, me: put(o, me, me), (ROOM, 512))],
        6,
        work=lambda links, *refs: attend_kernel(links, ready, *refs),
        work_in=[qkv, position, frequency, gains],
        work_out=[
            shape((SEQ, HEAD)),
            shape((SEQ, HEAD)),
            shape((SEQ, 1), F32),
            shape((SEQ, HEAD), F32),
            shape((SEQ, HEAD), F32),
            shape((512, WIDTH)),
        ],
        work_scratch=[pltpu.VMEM((SEQ, HEAD), BF)],
        deferred=range(len(CUBE), len(sends)),
    )


NEAR_FIRST = (1, 3, 2, 0)


def attend_back_kernel(
    links,
    numbers,
    partial_ref,
    qkv_ref,
    query_ref,
    key_ref,
    lse_ref,
    cos_ref,
    sin_ref,
    gain_ref,
    qkv_grad_ref,
    gain_grad_ref,
    cross,
    mixed,
    out_grads,
    grad_ref,
    query_grad,
    key_grad,
    value_grad,
):
    to_rows, to_cols, back_query, back_to_cols, last = numbers
    row, col = lax.axis_index("row"), lax.axis_index("col")
    for ahead in NEAR_FIRST:
        for number in to_rows[ahead]:
            links.send(number)
    key_grad[...] = jnp.zeros_like(key_grad)
    value_grad[...] = jnp.zeros_like(value_grad)

    def mix(ahead):
        head = lax.rem(col + ahead, 4)
        for number in to_rows[ahead]:
            links.arrive(number)
        total = partial_ref[:, rows((row * 4 + head) * HEAD, HEAD)].astype(F32)
        for part in range(3):
            total = total + cross[part, ahead].astype(F32)
        if ahead:
            mixed[ahead] = total.astype(BF)
            links.send(to_cols[ahead])
        else:
            out_grads[rows(col * 512, 512), :] = total.astype(BF)

    def attend_block(ahead):
        if ahead:
            links.arrive(to_cols[ahead])
        first = lax.rem(col + 4 - ahead, 4) * 512

        def block(step, carry):
            span = pl.ds(pl.multiple_of(first + step * BLOCK, BLOCK), BLOCK)
            query, out_grad = query_ref[span, :], out_grads[span, :]
            scores = (
                lax.dot_general(query, key_ref[...], LAST, preferred_element_type=F32) * SCALE
            )
            soft = jnp.exp(scores - lse_ref[span, :])
            prob_grad = lax.dot_general(
                out_grad, qkv_ref[:, 2 * HEAD :], LAST, preferred_element_type=F32
            )
            inner = jnp.sum(soft * prob_grad, axis=1, keepdims=True)
            score_grad = (soft * (prob_grad - inner)).astype(BF)
            query_grad[span, :] = (
                jnp.dot(score_grad, key_ref[...], preferred_element_type=F32) * SCALE
            )
            key_grad[...] += lax.dot_general(
                score_grad, query, FIRST, preferred_element_type=F32
            )
            value_grad[...] += lax.dot_general(
                soft.astype(BF), out_grad, FIRST, preferred_element_type=F32
            )
            return carry

        lax.fori_loop(0, 512 // BLOCK, block, 0)
        finish_part(first, ((0, query_grad, 1.0),))
        if ahead:
            links.send(back_query[(4 - ahead) % 4])

    def finish_part(first, sources):
        def finish_block(step, carry):
            span = pl.ds(pl.multiple_of(first + step * BLOCK, BLOCK), BLOCK)
            for part, source, factor in sources:
                turned = source[span, :] * factor
                grad = turned * cos_ref[span, :] + swapped(turned * sin_ref[span, :])
                raw = qkv_ref[span, part * HEAD : (part + 1) * HEAD].astype(F32)
                inverse = lax.rsqrt(jnp.mean(raw * raw, axis=1, keepdims=True) + EPS)
                unit = raw * inverse
                gain_grad_ref[part : part + 1, :] += jnp.sum(grad * unit, axis=0, keepdims=True)
                scaled = grad * gain_ref[part : part + 1, :]
                raw_grad = inverse * (
                    scaled - unit * jnp.mean(scaled * unit, axis=1, keepdims=True)
                )
                grad_ref[span, part * HEAD : (part + 1) * HEAD] = raw_grad.astype(BF)
                if part:
                    grad_ref[span, 2 * HEAD :] = value_grad[span, :].astype(BF)
            return carry

        lax.fori_loop(0, 512 // BLOCK, finish_block, 0)

    gain_grad_ref[...] = jnp.zeros_like(gain_grad_ref)
    mix(1)
    mix(3)
    attend_block(1)
    mix(2)
    attend_block(3)
    mix(0)
    for number in last:
        links.send(number)
    attend_block(2)
    attend_block(0)
    for ahead in NEAR_FIRST:
        finish_part(lax.rem(col + ahead, 4) * 512, ((1, key_grad, SCALE),))
        if ahead:
            links.send(back_to_cols[ahead])
    qkv_grad_ref[:, rows(col * 384, 384)] = grad_ref[rows(col * 512, 512), :]


def attend_back(operands, out_part, small_part, up_grad):
    whole = lambda s, me, p: s
    sends = [
        (SIBLING, 0, lambda s, me, p: s.at[:, rows(p[1] * 64, 64)], 0, whole),
        (SIBLING, 1, whole, 1, whole),
    ]
    later = len(sends)
    to_rows, to_cols, back_query, back_to_cols = {}, {}, {}, {}
    for ahead in NEAR_FIRST:
        to_rows[ahead] = []
        for part, offset in enumerate(ROWS):
            to_rows[ahead].append(len(sends))
            head = lambda me, p, ahead=ahead: p[2] * 4 + (me[3] + ahead) % 4
            sends.append(
                (
                    offset,
                    ("work", 0),
                    lambda s, me, p, head=head: s.at[:, rows(head(me, p) * HEAD, HEAD)],
                    ("scratch", 0),
                    lambda o, me, p, part=part, ahead=ahead: o.at[part, ahead],
                )
            )
    for offset in COLS:
        ahead = offset[3]
        to_cols[ahead] = len(sends)
        sends.append(
            (
                offset,
                ("scratch", 1),
                lambda s, me, p, ahead=ahead: s.at[ahead],
                ("scratch", 2),
                lambda o, me, p: o.at[rows(me[3] * 512, 512)],
            )
        )
        for numbers, skip, size in ((back_query, 0, HEAD), (back_to_cols, HEAD, 2 * HEAD)):
            numbers[ahead] = len(sends)
            sends.append(
                (
                    offset,
                    ("scratch", 3),
                    lambda s, me, p, skip=skip, size=size: s.at[
                        rows(p[3] * 512, 512), pl.ds(skip, size)
                    ],
                    ("made", 0),
                    lambda o, me, p, skip=skip, size=size: o.at[
                        :, pl.ds(pl.multiple_of(me[3] * 384 + skip, HEAD), size)
                    ],
                )
            )
    last = [len(sends)]
    sends.append((ONE_BACK, 2, whole, 2, whole))
    return exchange(
        [out_part, small_part, up_grad],
        [
            shape((16, 64, 512)),
            shape(small_part.shape, F32),
            shape(up_grad.shape),
        ],
        sends,
        [],
        13,
        deferred=range(later, len(sends)),
        work=lambda links, *refs: attend_back_kernel(
            links, (to_rows, to_cols, back_query, back_to_cols, last), *refs
        ),
        work_in=operands,
        work_out=[shape((512, 1536)), shape((8, HEAD), F32)],
        work_scratch=[
            pltpu.VMEM((3, 4, 512, HEAD), BF),
            pltpu.VMEM((4, 512, HEAD), BF),
            pltpu.VMEM((SEQ, HEAD), BF),
            pltpu.VMEM((SEQ, 3 * HEAD), BF),
        ]
        + [pltpu.VMEM((SEQ, HEAD), F32)] * 3,
    )


SLOTS = 16 * ROOM
GROUP = 4 * ROOM


def expert_kernel(
    links,
    came,
    returns,
    results,
    shares,
    cot_ref,
    gated_ref,
    up_1,
    up_2,
    down_1,
    down_2,
    x_ref,
    back_ref,
    joined,
    slot_grads,
    acts,
    grads,
    their_x,
    their_slot_grads,
    their_acts,
    their_grads,
    up_ref,
    down_ref,
    out_sum,
    back_sum,
    weight_sem,
    own_sem,
):
    me = here()
    loads = []
    for slot in range(4):
        for part, target in ((1, up_ref), (5, down_ref)):
            loads.append(
                pltpu.make_async_copy(
                    links.ins[part + slot], target.at[slot], weight_sem.at[part + slot - 1]
                )
            )
    take, put = expert_views()
    own_in = pltpu.make_async_copy(take(links.ins[0], me, me), put(x_ref, me, me), own_sem.at[0])
    take, put = token_views()
    own_out = pltpu.make_async_copy(
        take(back_ref, me, me), put(links.outs[0], me, me), own_sem.at[1]
    )
    own_result = pltpu.make_async_copy(
        take(gated_ref, me, me), put(links.outs[1], me, me), own_sem.at[2]
    )
    own_in.start()
    for load in loads:
        load.start()
    line = lax.broadcasted_iota(jnp.int32, (ROOM, HEAD), 0)
    lane = lax.broadcasted_iota(jnp.int32, (ROOM, HEAD), 1)
    same = (line == lane).astype(F32)
    for group in range(4):
        if group == 0:
            own_in.wait()
        for number in came[group]:
            links.arrive(number)
        if group == 0:
            for load in loads:
                load.wait()
        blocks = [
            lax.rem(me[0] + 4 - i, 4) * 4 + lax.rem(me[3] + 4 - (group - i) % 4, 4)
            for i in range(4)
        ]
        span = pl.ds(group * GROUP, GROUP)
        received = jnp.concatenate([x_ref[block].astype(F32) for block in blocks], axis=0)
        cot = jnp.concatenate([cot_ref[block].astype(F32) for block in blocks], axis=0)
        gates = []
        for i in range(4):
            aux = jnp.where(line >= CAP, received[i * ROOM : (i + 1) * ROOM, :HEAD], 0.0)
            gates.append(
                jnp.sum(same * jnp.sum(aux, axis=0, keepdims=True), axis=1, keepdims=True)
            )
        gate = jnp.concatenate(gates, axis=0)
        joined[span, :] = received.astype(BF)
        slot_grads[span, :] = (gate * cot).astype(BF)
        out_sum[...] = jnp.zeros_like(out_sum)
        back_sum[...] = jnp.zeros_like(back_sum)

        def quarter(slot, carry, span=span):
            gate_up = jnp.dot(joined[span, :], up_ref[slot], preferred_element_type=F32)
            gate_part, up_part = gate_up[:, :256], gate_up[:, 256:]
            sigmoid = 1.0 / (1.0 + jnp.exp(-gate_part))
            silu = gate_part * sigmoid
            act = (silu * up_part).astype(BF)
            acts[slot, span, :] = act
            act_grad = lax.dot_general(
                slot_grads[span, :], down_ref[slot], LAST, preferred_element_type=F32
            )
            slope = sigmoid * (1.0 + gate_part * (1.0 - sigmoid))
            grads[slot, span, :256] = (act_grad * up_part * slope).astype(BF)
            grads[slot, span, 256:] = (act_grad * silu).astype(BF)
            out_sum[...] += jnp.dot(act, down_ref[slot], preferred_element_type=F32)
            back_sum[...] += lax.dot_general(
                grads[slot, span, :], up_ref[slot], LAST, preferred_element_type=F32
            )
            return carry

        lax.fori_loop(0, 4, quarter, 0)
        out = out_sum[...]
        gated = gate * out
        gate_grad = jnp.sum(cot * out.astype(BF).astype(F32), axis=1, keepdims=True)
        back = back_sum[...]
        inner = jnp.sum(back * joined[span, :].astype(F32), axis=1, keepdims=True)
        for i, block in enumerate(blocks):
            part = slice(i * ROOM, (i + 1) * ROOM)
            gated_ref[block] = gated[part].astype(BF)
            back_ref[block] = back[part].astype(BF)
            for index, value in enumerate((gate_grad, inner)):
                high, middle, low = pieces(jnp.sum(same * value[part], axis=0, keepdims=True))
                aux = jnp.where(line == CAP, high.astype(F32), 0.0)
                aux = aux + jnp.where(line == CAP + 1, middle.astype(F32), 0.0)
                aux = aux + jnp.where(line == CAP + 2, low.astype(F32), 0.0)
                for r in range(4):
                    start = r * 512 + index * HEAD
                    back_ref[block, :, start : start + HEAD] = (
                        back[part, start : start + HEAD] + aux
                    ).astype(BF)
        for number in returns[group]:
            links.send(number)
        if group == 0:
            own_out.start()
            own_result.start()
        for number in shares[group] + results[group]:
            links.send(number)
    for numbers in shares:
        for number in numbers:
            links.arrive(number)

    def weight_grads(step, carry):
        span = pl.ds(pl.multiple_of(step * 512, 512), 512)
        for slot, up, down in ((0, up_1, down_1), (1, up_2, down_2)):
            up[span, :] = (
                lax.dot_general(joined[:, span], grads[slot], FIRST, preferred_element_type=F32)
                + lax.dot_general(
                    their_x[:, span], their_grads[slot], FIRST, preferred_element_type=F32
                )
            ).astype(BF)
            down[:, span] = (
                lax.dot_general(
                    acts[slot], slot_grads[:, span], FIRST, preferred_element_type=F32
                )
                + lax.dot_general(
                    their_acts[slot],
                    their_slot_grads[:, span],
                    FIRST,
                    preferred_element_type=F32,
                )
            ).astype(BF)
        return carry

    lax.fori_loop(0, 4, weight_grads, 0)
    own_out.wait()
    own_result.wait()


def run_experts(blocks, cot_slots, weights):
    take, put = expert_views()
    came, returns, results, shares = ([[], [], [], []] for _ in range(4))
    sends = []
    for offset in CUBE:
        came[(offset[0] + offset[3]) % 4].append(len(sends))
        sends.append((offset, 0, take, ("scratch", 0), put))
    take, put = token_views()
    for offset in CUBE:
        returns[-(offset[0] + offset[3]) % 4].append(len(sends))
        sends.append((offset, ("scratch", 1), take, 0, put))
    for offset in CUBE:
        results[-(offset[0] + offset[3]) % 4].append(len(sends))
        sends.append((offset, ("made", 0), take, 1, put))
    for place in range(4):
        span = pl.ds(place * GROUP, GROUP)
        for mine, theirs in ((2, 6), (3, 7)):
            view = lambda ref, me, p, span=span: ref.at[span]
            shares[place].append(len(sends))
            sends.append((SIBLING, ("scratch", mine), view, ("scratch", theirs), view))
        for mine, theirs in ((4, 8), (5, 9)):
            shares[place].append(len(sends))
            sends.append(
                (
                    SIBLING,
                    ("scratch", mine),
                    lambda ref, me, p, span=span: ref.at[pl.ds(2, 2), span],
                    ("scratch", theirs),
                    lambda ref, me, p, span=span: ref.at[:, span],
                )
            )
    return exchange(
        [blocks] + weights,
        [shape((EXPERTS, ROOM, 512))] * 2,
        sends,
        [],
        8,
        work=lambda links, *refs: expert_kernel(
            links, came, returns, results, shares, *refs
        ),
        work_in=[cot_slots],
        work_out=[shape((16, ROOM, WIDTH))]
        + [shape((WIDTH, 512))] * 2
        + [shape((256, WIDTH))] * 2,
        work_scratch=[
            pltpu.VMEM((16, ROOM, WIDTH), BF),
            pltpu.VMEM((16, ROOM, WIDTH), BF),
            pltpu.VMEM((SLOTS, WIDTH), BF),
            pltpu.VMEM((SLOTS, WIDTH), BF),
            pltpu.VMEM((4, SLOTS, 256), BF),
            pltpu.VMEM((4, SLOTS, 512), BF),
            pltpu.VMEM((SLOTS, WIDTH), BF),
            pltpu.VMEM((SLOTS, WIDTH), BF),
            pltpu.VMEM((2, SLOTS, 256), BF),
            pltpu.VMEM((2, SLOTS, 512), BF),
            pltpu.VMEM((4, WIDTH, 512), BF),
            pltpu.VMEM((4, 256, WIDTH), BF),
            pltpu.VMEM((GROUP, WIDTH), F32),
            pltpu.VMEM((GROUP, WIDTH), F32),
            pltpu.SemaphoreType.DMA((8,)),
            pltpu.SemaphoreType.DMA((3,)),
        ],
        deferred=range(len(CUBE), len(sends)),
    )


def pack_kernel(up_1, up_2, down_1, down_2, qkv, up_ref, down_ref, qkv_ref):
    upper = lax.axis_index("row") // 2
    for which, up, down in ((upper, up_1, down_1), (1 - upper, up_2, down_2)):
        value = up[...].astype(F32)
        up_ref[which, :, 0, :] = value[:, :256]
        up_ref[which, :, 1, :] = value[:, 256:]
        down_ref[which] = down[...].astype(F32)
    for head in range(4):
        qkv_ref[:, head, :] = qkv[:, head * 384 : (head + 1) * 384].astype(F32)


def pack_grads(up_1, up_2, down_1, down_2, qkv):
    steps = 8
    up, down = (WIDTH // steps, 512), (256 // steps, WIDTH)
    return pl.pallas_call(
        pack_kernel,
        grid=(steps,),
        out_shape=[
            shape((2, WIDTH, 2, 256), F32),
            shape((2, 256, WIDTH), F32),
            shape((512, 4, 384), F32),
        ],
        in_specs=[pl.BlockSpec(up, lambda i: (i, 0))] * 2
        + [pl.BlockSpec(down, lambda i: (i, 0))] * 2
        + [pl.BlockSpec((512 // steps, 1536), lambda i: (i, 0))],
        out_specs=[
            pl.BlockSpec((2, up[0], 2, 256), lambda i: (0, i, 0, 0)),
            pl.BlockSpec((2,) + down, lambda i: (0, i, 0)),
            pl.BlockSpec((512 // steps, 4, 384), lambda i: (i, 0, 0)),
        ],
    )(up_1, up_2, down_1, down_2, qkv)


def dot(left, right):
    return jnp.dot(left, right, preferred_element_type=F32)


def dot_last(left, right):
    return lax.dot_general(left, right, LAST, preferred_element_type=F32)


def dot_first(left, right):
    return lax.dot_general(left, right, FIRST, preferred_element_type=F32)


def pieces(value):
    high = value.astype(BF)
    rest = value - high.astype(F32)
    middle = rest.astype(BF)
    low = (rest - middle.astype(F32)).astype(BF)
    return [high, middle, low]


def aux_rows(value):
    held = jnp.stack(pieces(value), axis=1)
    return jnp.pad(held, ((0, 0), (CAP, ROOM - CAP - 3), (0, 512 - ROOM)))


def aux_value(blocks, index):
    part = blocks[:, CAP : CAP + 3, index * HEAD : index * HEAD + ROOM]
    return jnp.sum(part.astype(F32), axis=1)


FIRST_HOP = [
    ((2 * y + k) * 4 + x, (2 * y + 1 - x % 2) * 4 + 2 * k + x // 2)
    for y in range(4)
    for k in range(2)
    for x in range(4)
]
SECOND_HOP = [
    ((2 * y + k) * 4 + x, (2 * y + x % 2) * 4 + 2 * k + 1 - x // 2)
    for y in range(4)
    for k in range(2)
    for x in range(4)
]
PAIR = [(d, d ^ 1) for d in range(8)]


def hop(operand, pairs):
    return lax.ppermute(operand, ("dp", "row"), pairs)


def after(*operands):
    return lax.optimization_barrier(operands)


def shards(
    tokens,
    positions,
    routes,
    attention_norm_gain,
    experts_norm_gain,
    w_qkv,
    q_gain,
    k_gain,
    w_out,
    w_router,
    w_gate_up,
    w_down,
    cotangent,
):
    core = lax.axis_index("dp") % 2
    experts = jnp.arange(EXPERTS, dtype=jnp.int32)
    named = jnp.any(routes[:, :, None] == experts[None, None, :], axis=1)
    place = jnp.arange(512, dtype=jnp.int32)
    earlier = (place[None, :] < place[:, None]).astype(BF)
    rank = dot(earlier, named.astype(BF))
    rank = jnp.where(named, rank, -1.0).T
    (
        token_rows,
        w_group,
        position_rows,
        gain_rows,
        w_all,
        down_1,
        down_2,
        send_up_1,
        send_up_2,
        send_cot,
    ) = gather_inputs(
        tokens,
        w_qkv,
        w_out,
        w_down,
        positions.reshape(4, HEAD),
        attention_norm_gain.reshape(4, HEAD),
        [w_gate_up, rank, cotangent],
    )
    w_all = w_all.reshape(WIDTH, 512)
    w_group = w_group.reshape(WIDTH, 1536)
    gain_full = gain_rows.reshape(WIDTH)

    gate_up_1, gate_up_2 = hop(send_up_1, FIRST_HOP), hop(send_up_2, SECOND_HOP)
    sibling = lambda w: lax.ppermute(w, "dp", PAIR)
    frequency = THETA ** (-2.0 * jnp.arange(HEAD // 2, dtype=F32) / HEAD)
    half_signs = jnp.where(jnp.arange(HEAD) < HEAD // 2, -1.0, 1.0).astype(F32)
    frequency = jnp.concatenate(
        [jnp.concatenate([frequency] * 2)[None], half_signs[None], jnp.zeros((6, HEAD), F32)]
    )
    position_column = position_rows.reshape(SEQ, 1).astype(F32)
    gains = jnp.concatenate([q_gain[None], k_gain[None], jnp.zeros((6, HEAD), F32)], axis=0)

    pick = (rank[:, None, :] == jnp.arange(ROOM, dtype=F32)[None, :, None]).astype(BF)
    flat_pick = pick.reshape(EXPERTS * ROOM, 512)

    token_full = token_rows.astype(F32)
    inverse_attention = lax.rsqrt(jnp.mean(token_full * token_full, axis=1) + EPS)
    normed_exact = token_full * inverse_attention[:, None] * gain_full[None, :]
    normed = normed_exact.astype(BF)
    qkv = to_heads(dot(normed, w_group).astype(BF))
    cot_slots, query, key, lse, cosine, sine, attended_rows = attend(
        qkv, position_column, frequency, gains, send_cot
    )
    attended_rows, gate_up_1, gate_up_2, down_1, down_2 = after(
        attended_rows, gate_up_1, gate_up_2, down_1, down_2
    )
    up_ws = [gate_up_1, gate_up_2, sibling(gate_up_1), sibling(gate_up_2)]
    down_ws = [down_1, down_2, sibling(down_1), sibling(down_2)]

    token_float = tokens.astype(F32)
    hidden = token_float + dot(attended_rows, w_all)
    scaled_hidden = hidden * experts_norm_gain
    partial_stats = jnp.concatenate(
        [
            lax.dot_general(
                w_router.astype(F32),
                scaled_hidden,
                (((0,), (1,)), ((), ())),
                precision=EXACT,
                preferred_element_type=F32,
            ),
            jnp.sum(hidden * hidden, axis=1)[None],
            jnp.zeros((7, 512), F32),
        ],
        axis=0,
    )
    stats = jnp.sum(row_stack(partial_stats, 7), axis=0)
    inverse_experts = lax.rsqrt(stats[EXPERTS] / WIDTH + EPS)
    logits = stats[:EXPERTS] * inverse_experts[None, :]
    unit_experts = hidden * inverse_experts[:, None]
    experts_input = (unit_experts * experts_norm_gain).astype(BF)
    named_t = rank >= 0
    largest = jnp.max(jnp.where(named_t, logits, -jnp.inf), axis=0, keepdims=True)
    shifted = jnp.where(named_t, jnp.exp(jnp.where(named_t, logits - largest, 0.0)), 0.0)
    gates = shifted / jnp.sum(shifted, axis=0, keepdims=True)
    slot_gates = jnp.sum(pick.astype(F32) * gates[:, None, :], axis=2)
    send_rows = dot(flat_pick, experts_input).astype(BF).reshape(EXPERTS, ROOM, 512)
    back_rows, out_rows, _, up_1, up_2, down_1, down_2 = run_experts(
        send_rows + aux_rows(slot_gates), cot_slots, up_ws + down_ws
    )
    gate_grad = jnp.sum(pick.astype(F32) * aux_value(back_rows, 0)[:, :, None], axis=1)
    inner = jnp.sum(pick.astype(F32) * aux_value(back_rows, 1)[:, :, None], axis=(0, 1))
    logit_grad = gates * (gate_grad - jnp.sum(gates * gate_grad, axis=0, keepdims=True))
    experts_input_grad = dot_first(
        flat_pick, back_rows.reshape(EXPERTS * ROOM, 512)
    ) + lax.dot_general(
        logit_grad,
        w_router.astype(F32),
        (((0,), (1,)), ((), ())),
        precision=EXACT,
        preferred_element_type=F32,
    )
    mean_experts = (inner + jnp.sum(logit_grad * logits, axis=0)) / WIDTH
    cot_float = cotangent.astype(F32)
    middle_grad = cot_float + inverse_experts[:, None] * (
        experts_input_grad * experts_norm_gain - unit_experts * mean_experts[:, None]
    )
    router_part = lax.dot_general(
        logit_grad,
        experts_input.astype(F32),
        (((1,), (0,)), ((), ())),
        precision=EXACT,
        preferred_element_type=F32,
    )
    experts_gain_part = jnp.sum(experts_input_grad * unit_experts, axis=0)
    attended_grad = middle_grad.astype(BF)
    out_part = dot_first(attended_rows, attended_grad).astype(BF).reshape(16, HEAD, 512)
    small_part = jnp.concatenate(
        [
            router_part.reshape(256, HEAD),
            experts_gain_part.reshape(4, HEAD),
            jnp.zeros((124, HEAD), F32),
        ],
        axis=0,
    )
    out_other, small_other, up_1, qkv_grad, head_gain_part = attend_back(
        [dot_last(attended_grad, w_all).astype(BF), qkv, query, key, lse, cosine, sine, gains],
        out_part,
        small_part,
        up_1,
    )
    out_half = (
        lax.dynamic_slice_in_dim(out_part, core * 64, 64, 1).astype(F32)
        + out_other.astype(F32)
    ).astype(BF)
    small = (small_part + small_other).reshape(16, 24, HEAD)
    out_pieces, small_pieces, down_1, down_2, by_y, by_z, normed_grad, row_stats, output = finish(
        out_half,
        small,
        down_1,
        down_2,
        [
            normed,
            qkv_grad,
            w_group,
            head_gain_part,
            hidden,
            flat_pick,
            out_rows.reshape(EXPERTS * ROOM, 512),
        ],
    )
    normed_grad = jnp.sum(normed_grad.astype(F32), axis=0)
    row_stats = jnp.sum(row_stats, axis=0)
    mean_attention = row_stats[:4].reshape(512) / WIDTH
    unit_attention = token_float * inverse_attention[:, None]
    token_grad = middle_grad + inverse_attention[:, None] * (
        normed_grad * attention_norm_gain - unit_attention * mean_attention[:, None]
    )
    attention_gain_part = jnp.sum(normed_grad * unit_attention, axis=0)

    out_piece = jnp.sum(out_pieces.astype(F32), axis=0).astype(BF)
    out_total, small_total, late, up_2, qkv_total = collect_sums(
        by_y,
        by_z,
        out_piece,
        jnp.sum(small_pieces, axis=0),
        jnp.concatenate([attention_gain_part.reshape(4, HEAD), row_stats[4:]], axis=0),
        up_2,
    )
    small_total = small_total.reshape(384, HEAD)
    late = jnp.sum(late, axis=0)
    grad_gate_up, grad_down, grad_qkv = pack_grads(
        up_1, up_2, down_1, down_2, qkv_total.reshape(512, 1536)
    )
    return (
        output,
        token_grad.astype(BF),
        late[:4].reshape(512),
        small_total[256:260].reshape(512),
        grad_qkv,
        late[4],
        late[5],
        out_total.astype(F32).reshape(512, 512),
        small_total[:256].reshape(EXPERTS, 512).T,
        grad_gate_up,
        grad_down,
    )


def solution(mesh):
    tokens_like = P(("dp", "col"), "row")
    up_like = P(("dp", "col"), None, None, "row")
    down_like = P(("dp", "col"), "row", None)
    return jax.shard_map(
        shards,
        mesh=mesh,
        in_specs=(
            tokens_like,
            P("dp", "row"),
            P(("dp", "col"), None),
            P("row"),
            P("row"),
            P("row", "col", None),
            P(),
            P(),
            P("col", "row"),
            P("row", None),
            up_like,
            down_like,
            tokens_like,
        ),
        out_specs=(
            tokens_like,
            tokens_like,
            P("row"),
            P("row"),
            P("row", "col", None),
            P(),
            P(),
            P("col", "row"),
            P("row", None),
            up_like,
            down_like,
        ),
        check_vma=False,
    )
```

```python
import jax
import jax.numpy as jnp
from jax import lax
from jax.experimental import pallas as pl
from jax.experimental.pallas import tpu as pltpu
from jax.sharding import PartitionSpec as P

WIDTH = 2048
HEAD = 128
EXPERTS = 64
CAP = 36
ROOM = 40
SEQ = 2048
EPS = 1e-06
THETA = 10000.0
EXACT = lax.Precision.HIGHEST
MESH = pl.DeviceIdType.MESH
SIZES = (4, 2, 4, 4)
BF = jnp.bfloat16
F32 = jnp.float32
ROWS = [(0, 0, d, 0) for d in (2, 1, 3)]
COLS = [(0, 0, 0, d) for d in (2, 1, 3)]
SIBLING = (0, 1, 0, 0)
PLANE = [(0, 0, i, (i + s) % 4) for s in range(4) for i in range(4) if (i, s) != (0, 0)]
CUBE = [
    (i, 0, (i + s) % 4, (g - i) % 4)
    for g in range(4)
    for s in range(4)
    for i in range(4)
    if (g, s, i) != (0, 0, 0)
]
SOURCES = [(i, 0, 0, (i + s) % 4) for s in range(4) for i in range(4) if (i, s) != (0, 0)]
SIDES = [(i, 0, (i + s) % 4, 0) for s in range(4) for i in range(4) if (i, s) != (0, 0)]
LINES = [(d, 0, 0, 0) for d in (2, 1, 3)]
OTHERS = [
    (a, k, 0, d) for a in range(4) for k in range(2) for d in range(4) if (a, k, d) != (0, 0, 0)
]


def shape(dims, dtype=BF):
    return jax.ShapeDtypeStruct(dims, dtype)


def here():
    group = lax.axis_index("dp")
    return (group // 2, group % 2, lax.axis_index("row"), lax.axis_index("col"))


class Hop:
    def __init__(self, to, origin):
        self.to, self.origin = to, origin


ONE_WAY = Hop(
    lambda p: (p[0], 1 - p[2] % 2, 2 * p[1] + p[2] // 2, p[3]),
    lambda p: (p[0], p[2] // 2, 2 * (p[2] % 2) + 1 - p[1], p[3]),
)
OTHER_WAY = Hop(
    lambda p: (p[0], p[2] % 2, 2 * p[1] + 1 - p[2] // 2, p[3]),
    lambda p: (p[0], p[2] // 2, 2 * (1 - p[2] % 2) + p[1], p[3]),
)


ONE_BACK, OTHER_BACK = Hop(ONE_WAY.origin, ONE_WAY.to), Hop(OTHER_WAY.origin, OTHER_WAY.to)


class Links:
    def __init__(self, send, arrive, ins, outs):
        self.send, self.arrive, self.ins, self.outs = send, arrive, ins, outs


def moved(place, offset):
    if isinstance(offset, Hop):
        return offset.to(place)
    return tuple((p + o) % n for p, o, n in zip(place, offset, SIZES))


def device(place):
    return (place[0] * 2 + place[1], place[2], place[3])


def exchange(
    inputs,
    outputs,
    sends,
    kept,
    call_id,
    micros=30,
    work=None,
    work_in=(),
    work_out=(),
    work_scratch=(),
    stages=(),
    deferred=(),
):
    offsets = sorted({s[0] for s in sends if not isinstance(s[0], Hop)})
    hops = {id(s[0]): s[0] for s in sends if isinstance(s[0], Hop)}.values()
    n_in, n_out, n_send = len(inputs), len(outputs), len(sends)
    m_in, m_out = len(work_in), len(work_out)

    def kernel(*refs):
        ins, refs = refs[:n_in], refs[n_in:]
        worked, refs = refs[:m_in], refs[m_in:]
        outs, refs = refs[:n_out], refs[n_out:]
        made, refs = refs[:m_out], refs[m_out:]
        send_sem, recv_sem, kept_sem = refs[:3]
        staged, refs = refs[3 : 3 + len(kept)], refs[3 + len(kept) :]
        special = {"work": worked, "made": made, "scratch": refs}
        me = here()
        barrier = pltpu.get_barrier_semaphore()
        greeted = [moved(me, offset) for offset in offsets]
        for way in hops:
            greeted += [way.to(me), way.origin(me)]
        for peer in greeted:
            pl.semaphore_signal(barrier, inc=1, device_id=device(peer), device_id_type=MESH)
        local = []
        for index, (i, take, o, put, _) in enumerate(kept):
            source, target = take(ins[i], me), put(outs[o], me)
            local.append(
                (
                    pltpu.make_async_copy(source, staged[index], kept_sem.at[index, 0]),
                    pltpu.make_async_copy(staged[index], target, kept_sem.at[index, 1]),
                )
            )
            local[-1][0].start()
        pl.semaphore_wait(barrier, len(greeted))
        copies, arrived = {}, set()

        def arrive(index):
            if index not in arrived:
                arrived.add(index)
                copies[index].wait_recv()

        def named(group, index):
            return special[index[0]][index[1]] if isinstance(index, tuple) else group[index]

        def start(index):
            offset, i, take, o, put = sends[index][:5]
            needs = sends[index][5] if len(sends[index]) > 5 else None
            for need in needs or ():
                if need >= 0:
                    arrive(need)
                elif need not in arrived:
                    arrived.add(need)
                    local[-need - 1][1].wait()
            peer = moved(me, offset)
            copies[index] = pltpu.make_async_remote_copy(
                src_ref=take(named(ins if needs is None else outs, i), me, peer),
                dst_ref=put(named(outs, o), me, peer),
                send_sem=send_sem.at[index],
                recv_sem=recv_sem.at[index],
                device_id=device(peer),
                device_id_type=MESH,
            )
            copies[index].start()

        links = Links(start, arrive, ins, outs)
        parts = work(links, *worked, *made, *refs) if stages else ()
        first = [i for i in range(n_send) if len(sends[i]) < 6 and i not in deferred]
        for index in first:
            start(index)
        for load, store in local:
            load.wait()
            store.start()
        for index in range(n_send):
            if index in first or index in deferred:
                continue
            for part, at in zip(parts, stages):
                if at == index:
                    part()
            start(index)
        if work is not None and not stages:
            work(links, *worked, *made, *refs)
        for index in range(n_send):
            arrive(index)
        for copy in copies.values():
            copy.wait_send()
        for index, copy in enumerate(local):
            if -index - 1 not in arrived:
                copy[1].wait()

    return pl.pallas_call(
        kernel,
        out_shape=list(outputs) + list(work_out),
        in_specs=[pl.BlockSpec(memory_space=pl.ANY)] * n_in
        + [pl.BlockSpec(memory_space=pltpu.VMEM)] * m_in,
        out_specs=[pl.BlockSpec(memory_space=pl.ANY)] * n_out
        + [pl.BlockSpec(memory_space=pltpu.VMEM)] * m_out,
        scratch_shapes=[
            pltpu.SemaphoreType.DMA((n_send,)),
            pltpu.SemaphoreType.DMA((n_send,)),
            pltpu.SemaphoreType.DMA((max(1, len(kept)), 2)),
            *[pltpu.VMEM(k[4], inputs[k[0]].dtype) for k in kept],
            *work_scratch,
        ],
        compiler_params=pltpu.CompilerParams(
            collective_id=call_id,
            has_side_effects=True,
            vmem_limit_bytes=(8 if work is None else 60) * 2**20,
        ),
        cost_estimate=pl.CostEstimate(
            flops=0, bytes_accessed=micros * 3_500_000, transcendentals=0
        ),
    )(*inputs, *work_in)


def rows(start, size):
    return pl.ds(pl.multiple_of(start, size), size)


def eighth(size):
    me = here()
    return rows((me[1] * 4 + me[0]) * size, size)


def half(size):
    return rows(here()[1] * size, size)


class Sends(list):
    def add(self, group, take, o, put=None, i=None, needs=None):
        first = len(self)
        for offset in group:
            if needs is None:
                self.append((offset, i, take, o, put))
            else:
                view = lambda ref, me, p: take(ref, me)
                self.append((offset, o, view, o, view, needs))
        return list(range(first, len(self)))


def early_kernel(links, up_ref, rank_ref, cot_ref, up_1, up_2, rows_ref):
    upper = lax.axis_index("row") // 2

    def unpack(which, target, first):
        def part():
            for step in range(4):
                span = pl.ds(first + step * 64, 64)
                target[span, :256] = up_ref[which, span, 0, :]
                target[span, 256:] = up_ref[which, span, 1, :]

        return part

    def pick(step):
        def part():
            ranks = rank_ref[step * 8 : step * 8 + 8, :]
            slots = lax.broadcasted_iota(jnp.int32, (8, ROOM, 512), 1).astype(F32)
            chosen = (ranks[:, None, :] == slots).astype(F32).reshape(8 * ROOM, 512)
            rows_of = jnp.dot(chosen.astype(BF), cot_ref[...], preferred_element_type=F32)
            rows_ref[pl.ds(step * 8, 8)] = rows_of.reshape(8, ROOM, 512).astype(BF)

        return part

    parts = [unpack(upper, up_1, step * 256) for step in range(8)]
    parts += [unpack(1 - upper, up_2, step * 256) for step in range(8)]
    return parts + [pick(step) for step in range(8)]


def gather_inputs(tokens, w_qkv, w_out, w_down, small_int, small_float, early):
    outputs = [
        shape((512, WIDTH)),
        shape((4, 512, 1536)),
        shape((4, 4, HEAD), jnp.int32),
        shape((4, 4, HEAD), F32),
        shape((4, 4, HEAD, 512)),
        shape((256, WIDTH)),
        shape((256, WIDTH)),
    ]
    sends = Sends()
    own_cols = lambda me: rows(me[3] * 384, 384)
    low, high = pl.ds(0, 2), pl.ds(2, 2)
    first = sends.add(
        ROWS,
        lambda s, me, p: s.at[eighth(64), rows(p[2] * 384, 384)],
        1,
        lambda o, me, p: o.at[me[2], eighth(64), own_cols(me)],
        1,
    )
    both = [(0, 0, 1, 0), (0, 0, 3, 0)]
    beside = sends.add(
        both, lambda s, me, p: s, 0, lambda o, me, p: o.at[:, rows(me[2] * 512, 512)], 0
    )
    sends.add(ROWS, lambda s, me, p: s, 2, lambda o, me, p: o.at[me[2]], 2)
    sends.add(ROWS, lambda s, me, p: s, 3, lambda o, me, p: o.at[me[2]], 3)
    sends.append((ONE_WAY, 5, lambda s, me, p: s.at[me[2] // 2], 5, lambda o, me, p: o))
    sends.append((OTHER_WAY, 5, lambda s, me, p: s.at[1 - me[2] // 2], 6, lambda o, me, p: o))
    out_z = sends.add(COLS, lambda o, me: o.at[low, me[3], eighth(16)], 4, needs=[-2])
    out_y = sends.add(LINES, lambda o, me: o.at[high, me[3], eighth(16)], 4, needs=[-2])
    stages = [len(sends)] * 3
    by_z = sends.add(
        COLS, lambda o, me: o.at[low, eighth(64), own_cols(me)], 1, needs=[-1] + first
    )
    by_y = sends.add(LINES, lambda o, me: o.at[high, eighth(64), own_cols(me)], 1, needs=first)
    sends.add(LINES, lambda o, me: o.at[low, eighth(64), own_cols(me)], 1, needs=first)
    sends.add(COLS, lambda o, me: o.at[high, eighth(64), own_cols(me)], 1, needs=first)
    last_z, last_y = {0: [len(sends) - 6 + i for i in range(3)]}, {0: list(range(len(sends) - 3, len(sends)))}
    for d in (1, 3, 2):
        came = by_z[[offset[3] for offset in COLS].index(d)]
        cols = lambda me, d=d: rows((me[3] + 4 - d) % 4 * 384, 384)
        stages += [len(sends)] * (3 if d == 1 else 1)
        last_z[d] = sends.add(
            LINES,
            lambda o, me, cols=cols: o.at[low, eighth(64), cols(me)],
            1,
            needs=[came],
        )
        came = by_y[[offset[0] for offset in LINES].index(d)]
        span = lambda me, d=d: rows((me[1] * 4 + (me[0] + 4 - d) % 4) * 64, 64)
        stages.append(len(sends))
        last_y[d] = sends.add(
            COLS,
            lambda o, me, span=span: o.at[high, span(me), own_cols(me)],
            1,
            needs=[came],
        )
    for index, offset in enumerate(both):
        passed = lambda o, me, index=index, d=offset[2]: o.at[
            pl.ds(index * 256, 256), rows((me[2] + 4 - d) % 4 * 512, 512)
        ]
        sends.add([offset], passed, 0, needs=[beside[index]])
    stages.append(len(sends))
    out_zy = sends.add(LINES, lambda o, me: o.at[low, :, eighth(16)], 4, needs=out_z)
    stages.append(len(sends))
    out_yz = sends.add(COLS, lambda o, me: o.at[high, me[3], half(64)], 4, needs=out_y)
    stages.append(len(sends))
    pair = [SIBLING]
    sends.add(pair, lambda o, me: o.at[low, eighth(64)], 1, needs=by_z)
    sends.add(pair, lambda o, me: o.at[high, half(256), own_cols(me)], 1, needs=by_y)
    for d in (1, 3, 2):
        line = [offset[0] for offset in LINES].index(d)
        stages += [len(sends)] * (4 if d == 1 else 2)
        span = lambda me, d=d: rows((me[1] * 4 + (me[0] + 4 - d) % 4) * 64, 64)
        sends.add(
            pair,
            lambda o, me, span=span: o.at[low, span(me)],
            1,
            needs=[numbers[line] for numbers in last_z.values()],
        )
        col = [offset[3] for offset in COLS].index(d)
        stages += [len(sends)] * (24 - len(stages) if d == 2 else 1)
        cols = lambda me, d=d: rows((me[3] + 4 - d) % 4 * 384, 384)
        sends.add(
            pair,
            lambda o, me, cols=cols: o.at[high, half(256), cols(me)],
            1,
            needs=[numbers[col] for numbers in last_y.values()],
        )
    sends.add(pair, lambda o, me: o.at[low, :, half(64)], 4, needs=out_zy)
    sends.add(pair, lambda o, me: o.at[high, :, half(64)], 4, needs=out_yz)
    kept = [
        (
            1,
            lambda s, me: s.at[eighth(64), rows(me[2] * 384, 384)],
            1,
            lambda o, me: o.at[me[2], eighth(64), own_cols(me)],
            (64, 384),
        ),
        (
            4,
            lambda s, me: s.at[:, eighth(16)],
            4,
            lambda o, me: o.at[:, me[3], eighth(16)],
            (4, 16, 512),
        ),
        (0, lambda s, me: s, 0, lambda o, me: o.at[:, rows(me[2] * 512, 512)], (512, 512)),
        (2, lambda s, me: s, 2, lambda o, me: o.at[me[2]], (4, HEAD)),
        (3, lambda s, me: s, 3, lambda o, me: o.at[me[2]], (4, HEAD)),
    ]
    return exchange(
        [
            tokens,
            w_qkv.reshape(512, 1536),
            small_int,
            small_float,
            w_out.reshape(4, HEAD, 512),
            w_down,
        ],
        outputs,
        sends,
        kept,
        0,
        work=early_kernel,
        work_in=early,
        work_out=[
            shape((WIDTH, 512)),
            shape((WIDTH, 512)),
            shape((EXPERTS, ROOM, 512)),
        ],
        stages=stages,
    )


def to_heads(qkv):
    take = lambda s, me, p: s.at[:, rows(p[3] * 384, 384)]
    put = lambda o, me, p: o.at[rows(me[3] * 512, 512)]
    return exchange(
        [qkv],
        [shape((SEQ, 384))],
        [(offset, 0, take, 0, put) for offset in COLS],
        [(0, lambda s, me: take(s, me, me), 0, lambda o, me: put(o, me, me), (512, 384))],
        1,
    )[0]


def row_stack(operand, call_id):
    take = lambda s, me, p: s
    put = lambda o, me, p: o.at[me[2]]
    return exchange(
        [operand],
        [shape((4,) + operand.shape, operand.dtype)],
        [(offset, 0, take, 0, put) for offset in ROWS],
        [(0, lambda s, me: s, 0, lambda o, me: put(o, me, me), operand.shape)],
        call_id,
    )[0]


def finish_kernel(
    links,
    numbers,
    normed_ref,
    grad_ref,
    weight_ref,
    gain_ref,
    hidden_ref,
    pick_ref,
    rows_ref,
    out_part_ref,
    out_other_ref,
    small_part_ref,
    small_other_ref,
    middle_ref,
    tokens_ref,
    inverse_ref,
    norm_gain_ref,
    by_y_ref,
    by_z_ref,
    feature_ref,
    stat_ref,
    out_ref,
    out_piece_ref,
    small_piece_ref,
    token_grad_ref,
    late_ref,
    their_half,
    came,
    half,
    spread_y,
    spread_z,
    feature_part,
    stat_part,
    feature_sum,
    passing,
    out_half,
    out_came,
    small_sum,
    small_came,
):
    me = here()
    y, core, row, col = me
    to_sibling, to_lines, to_cols, to_rows, stats, last, spread_out = numbers
    own = y * 4 + col

    def product(start):
        return lax.dot_general(
            normed_ref[:, rows(start, 256)], grad_ref[...], FIRST, preferred_element_type=F32
        )

    for r in range(4):
        their_half[r] = product(r * 512 + (1 - core) * 256).astype(BF)
        links.send(to_sibling[r])
    for block in range(16):
        out_half[block] = (
            out_part_ref[block, rows(core * 64, 64), :].astype(F32)
            + out_other_ref[block].astype(F32)
        ).astype(BF)
        span = slice(block * 24, (block + 1) * 24)
        small_sum[block] = small_part_ref[span, :] + small_other_ref[span, :]
    for number in spread_out:
        links.send(number)
    out_came[own] = out_half[own]
    small_came[own] = small_sum[own]
    inner = jnp.zeros((512, 1), F32)
    for ahead in (2, 1, 3, 0):
        span = rows(lax.rem(row + ahead, 4) * 512, 512)
        part = lax.dot_general(
            grad_ref[...], weight_ref[span, :], LAST, preferred_element_type=F32
        )
        inner = inner + jnp.sum(part * normed_ref[:, span].astype(F32), axis=1, keepdims=True)
        if ahead == 2:
            feature_part[1] = part.astype(BF)
            for number in to_rows[2]:
                links.send(number)
        elif ahead:
            feature_sum[ahead // 2] = part
        else:
            feature_sum[2] = part
    for index, ahead in enumerate((1, 3)):
        links.arrive(to_rows[2][index])
        part = slice(index * 256, (index + 1) * 256)
        feature_sum[index, part, :] += passing[index].astype(F32)
        feature_part[ahead - 1] = feature_sum[index].astype(BF)
        links.send(to_rows[ahead])
    same = (
        lax.broadcasted_iota(jnp.int32, (HEAD, HEAD), 0)
        == lax.broadcasted_iota(jnp.int32, (HEAD, HEAD), 1)
    ).astype(F32)
    for block in range(4):
        stat_part[block : block + 1, :] = jnp.sum(
            same * inner[block * HEAD : (block + 1) * HEAD], axis=0, keepdims=True
        )
    stat_part[4:, :] = gain_ref[:4, :]
    stat_ref[row] = stat_part[...]
    for number in stats + last:
        links.send(number)
    for r in range(4):
        mine = product(r * 512 + core * 256)
        links.arrive(to_sibling[r])
        half[r] = (mine + came[r].astype(F32)).astype(BF)
        for number in to_lines[r] + to_cols[r]:
            links.send(number)
        spread_y[y, r] = half[r, rows(y * 32, 32), :]
        spread_z[col, r] = half[r, 128:, rows(col * 384, 384)]
    out_ref[...] = (
        hidden_ref[...]
        + lax.dot_general(pick_ref[...], rows_ref[...], FIRST, preferred_element_type=F32)
    ).astype(BF)
    for r in range(4):
        for numbers_of, target, spread in (
            (to_lines, by_y_ref, spread_y),
            (to_cols, by_z_ref, spread_z),
        ):
            for number in numbers_of[r]:
                links.arrive(number)
            total = spread[0, r].astype(F32)
            for source in range(1, 4):
                total = total + spread[source, r].astype(F32)
            target[r] = total.astype(BF)
    for number in (to_rows[1], to_rows[3], *stats):
        links.arrive(number)
    row_stats = stat_ref[0] + stat_ref[1] + stat_ref[2] + stat_ref[3]
    late_ref[4:, :] = row_stats[4:, :]
    for block in range(4):
        span = pl.ds(block * HEAD, HEAD)
        mean = jnp.sum(same * row_stats[block : block + 1, :], axis=1, keepdims=True) / WIDTH
        features = feature_sum[2, span, :]
        for part in range(2):
            features = features + feature_ref[part, span, :].astype(F32)
        inverse = inverse_ref[span, :]
        unit = tokens_ref[span, :].astype(F32) * inverse
        token_grad_ref[span, :] = (
            middle_ref[span, :] + inverse * (features * norm_gain_ref[0:1, :] - unit * mean)
        ).astype(BF)
        share = jnp.sum(features * unit, axis=0, keepdims=True)
        for part in range(4):
            lanes = share[:, part * HEAD : (part + 1) * HEAD]
            if block == 0:
                late_ref[part : part + 1, :] = lanes
            else:
                late_ref[part : part + 1, :] += lanes
    for number in spread_out:
        links.arrive(number)
    out_total, small_total = out_came[0].astype(F32), small_came[0]
    for source in range(1, 16):
        out_total = out_total + out_came[source].astype(F32)
        small_total = small_total + small_came[source]
    out_piece_ref[...] = out_total.astype(BF)
    small_piece_ref[...] = small_total


def finish(down_1, down_2, operands):
    take_out = lambda s, me, p: s.at[p[0] * 4 + p[3]]
    put_out = lambda o, me, p: o.at[me[0] * 4 + me[3]]
    whole = lambda s, me, p: s
    own_row = lambda o, me, p: o.at[me[2]]
    sends = []
    to_sibling, to_lines, to_cols = [], [[], [], [], []], [[], [], [], []]
    to_rows, stats, last, spread_out = {}, [], [], []
    for offset in SOURCES:
        for mine, theirs in ((9, 10), (11, 12)):
            spread_out.append(len(sends))
            sends.append((offset, ("scratch", mine), take_out, ("scratch", theirs), put_out))
    for r in range(4):
        view = lambda ref, me, p, r=r: ref.at[r]
        to_sibling.append(len(sends))
        sends.append((SIBLING, ("scratch", 0), view, ("scratch", 1), view))
    for r in range(4):
        for offset in LINES:
            to_lines[r].append(len(sends))
            sends.append(
                (
                    offset,
                    ("scratch", 2),
                    lambda s, me, p, r=r: s.at[r, rows(p[0] * 32, 32)],
                    ("scratch", 3),
                    lambda o, me, p, r=r: o.at[me[0], r],
                )
            )
        for offset in COLS:
            to_cols[r].append(len(sends))
            sends.append(
                (
                    offset,
                    ("scratch", 2),
                    lambda s, me, p, r=r: s.at[r, pl.ds(128, 128), rows(p[3] * 384, 384)],
                    ("scratch", 4),
                    lambda o, me, p, r=r: o.at[me[3], r],
                )
            )
    to_rows[2] = [len(sends), len(sends) + 1]
    for index, offset in enumerate(((0, 0, 1, 0), (0, 0, 3, 0))):
        part = lambda s, me, p, index=index: s.at[1, pl.ds(index * 256, 256)]
        slot = lambda o, me, p, index=index: o.at[index]
        sends.append((offset, ("scratch", 5), part, ("scratch", 8), slot))
    for index, offset in enumerate(((0, 0, 1, 0), (0, 0, 3, 0))):
        to_rows[offset[2]] = len(sends)
        part = lambda s, me, p, ahead=offset[2]: s.at[ahead - 1]
        slot = lambda o, me, p, index=index: o.at[index]
        sends.append((offset, ("scratch", 5), part, ("made", 2), slot))
    for offset in ROWS:
        stats.append(len(sends))
        sends.append((offset, ("scratch", 6), whole, ("made", 3), own_row))
    for way, index in ((ONE_BACK, 0), (OTHER_BACK, 1)):
        last.append(len(sends))
        sends.append((way, index, whole, index, whole))
    return exchange(
        [down_1, down_2],
        [shape(down_1.shape)] * 2,
        sends,
        [],
        5,
        work=lambda links, *refs: finish_kernel(
            links, (to_sibling, to_lines, to_cols, to_rows, stats, last, spread_out), *refs
        ),
        work_in=operands,
        work_out=[
            shape((4, 32, 1536)),
            shape((4, 128, 384)),
            shape((2, 512, 512)),
            shape((4, 8, HEAD), F32),
            shape((512, 512)),
            shape((64, 512)),
            shape((24, HEAD), F32),
            shape((512, 512)),
            shape((8, HEAD), F32),
        ],
        work_scratch=[pltpu.VMEM((4, 256, 1536), BF)] * 3
        + [
            pltpu.VMEM((4, 4, 32, 1536), BF),
            pltpu.VMEM((4, 4, 128, 384), BF),
            pltpu.VMEM((3, 512, 512), BF),
            pltpu.VMEM((8, HEAD), F32),
            pltpu.VMEM((3, 512, 512), F32),
            pltpu.VMEM((2, 256, 512), BF),
            pltpu.VMEM((16, 64, 512), BF),
            pltpu.VMEM((16, 64, 512), BF),
            pltpu.VMEM((16, 24, HEAD), F32),
            pltpu.VMEM((16, 24, HEAD), F32),
        ],
        deferred=range(len(sends)),
    )


def expert_at(place):
    return place[0] * 16 + (place[2] // 2) * 8 + place[3] * 2 + place[2] % 2


def expert_views():
    return (
        lambda s, me, p: s.at[expert_at(p)],
        lambda o, me, p: o.at[me[0] * 4 + me[3], :, rows(me[2] * 512, 512)],
    )


def token_views():
    return (
        lambda s, me, p: s.at[p[0] * 4 + p[3], :, rows(p[2] * 512, 512)],
        lambda o, me, p: o.at[expert_at(me)],
    )


def collect_sums(by_y, by_z, out_piece, small_piece, late, up_grad):
    put_qkv = lambda o, me, p: o.at[me[1], :, me[0]]
    put_out = lambda o, me, p: o.at[me[0], me[1]]
    put_small = lambda o, me, p: o.at[me[0] * 4 + me[3]]
    put_late = lambda o, me, p: o.at[(me[0] * 2 + me[1]) * 4 + me[3]]
    whole = lambda s, me, p: s
    sends = Sends()
    heads = sends.add(
        PLANE,
        lambda s, me, p: s.at[p[2], :, rows(p[3] * 384, 384)],
        ("scratch", 0),
        lambda o, me, p: o.at[me[3], me[2]],
        ("work", 0),
    )
    heads += sends.add(
        SIDES,
        lambda s, me, p: s.at[p[2], rows(p[0] * 32, 32)],
        ("scratch", 1),
        lambda o, me, p: o.at[me[0], me[2]],
        ("work", 1),
    )
    out_sent = sends.add(LINES, whole, 0, put_out, 0)
    sends.add([SIBLING], whole, 0, put_out, 0)
    sends.add(SOURCES, whole, 1, put_small, 1)
    sends.add(OTHERS, whole, 2, put_late, 2)
    sends.add([OTHER_BACK], whole, 3, whole, 3)
    later = len(sends)
    qkv_sent = sends.add(LINES, whole, ("made", 0), put_qkv, ("scratch", 2))
    sends.add([SIBLING], whole, ("made", 0), put_qkv, ("scratch", 2))
    relays = []
    for index in (1, 2, 0):
        origin = lambda me, d=LINES[index][0]: (me[0] + 4 - d) % 4
        view = lambda ref, me, p, origin=origin: ref.at[origin(me), me[1]]
        relays.append((out_sent[index], len(sends)))
        sends.append((SIBLING, 0, view, 0, view, [out_sent[index]]))
    for index in (1, 2, 0):
        origin = lambda me, d=LINES[index][0]: (me[0] + 4 - d) % 4
        view = lambda ref, me, p, origin=origin: ref.at[me[1], :, origin(me)]
        relays.append((qkv_sent[index], len(sends)))
        sends.append((SIBLING, ("made", 0), view, ("made", 0), view, [qkv_sent[index]]))

    def work(links, by_y_ref, by_z_ref, total_ref, spread_z, spread_y, mine):
        me = here()
        spread_z[me[3], me[2]] = by_y_ref[me[2], :, rows(me[3] * 384, 384)]
        spread_y[me[0], me[2]] = by_z_ref[me[2], rows(me[0] * 32, 32), :]
        for number in heads:
            links.arrive(number)
        for part, spread in ((0, spread_z), (1, spread_y)):
            for head in range(4):
                total = spread[0, head].astype(F32)
                for source in range(1, 4):
                    total = total + spread[source, head].astype(F32)
                mine[part, :, head * 384 : (head + 1) * 384] = total.astype(BF)
        for number in range(later, later + 4):
            links.send(number)
        for part in range(2):
            total_ref[me[1], part, me[0]] = mine[part]
        for came, number in relays:
            links.arrive(came)
            links.send(number)

    return exchange(
        [out_piece, small_piece, late, up_grad],
        [
            shape((4, 2, 64, 512)),
            shape((16,) + small_piece.shape, F32),
            shape((32,) + late.shape, F32),
            shape(up_grad.shape),
        ],
        sends,
        [
            (0, lambda s, me: s, 0, lambda o, me: put_out(o, me, me), (64, 512)),
            (1, lambda s, me: s, 1, lambda o, me: put_small(o, me, me), small_piece.shape),
            (2, lambda s, me: s, 2, lambda o, me: put_late(o, me, me), late.shape),
        ],
        12,
        work=work,
        work_in=[by_y, by_z],
        work_out=[shape((2, 2, 4, 32, 1536))],
        work_scratch=[
            pltpu.VMEM((4, 4, 32, 384), BF),
            pltpu.VMEM((4, 4, 32, 384), BF),
            pltpu.VMEM((2, 32, 1536), BF),
        ],
        deferred=range(later, len(sends)),
    )


BLOCK = 256
SCALE = HEAD ** (-0.5)
LAST = (((1,), (1,)), ((), ()))
FIRST = (((0,), (0,)), ((), ()))


def swapped(operand):
    return pltpu.roll(operand, HEAD // 2, 1)


def attend_kernel(
    links,
    ready,
    qkv_ref,
    position_ref,
    frequency_ref,
    gain_ref,
    query_ref,
    key_ref,
    lse_ref,
    cos_ref,
    sin_ref,
    gathered,
    out_ref,
):
    def prepare(step, carry):
        span = pl.ds(pl.multiple_of(step * BLOCK, BLOCK), BLOCK)
        angles = position_ref[span, :] * frequency_ref[0:1, :]
        cos_ref[span, :] = jnp.cos(angles)
        sin_ref[span, :] = jnp.sin(angles) * frequency_ref[1:2, :]
        for part, target in ((0, query_ref), (1, key_ref)):
            raw = qkv_ref[span, part * HEAD : (part + 1) * HEAD].astype(F32)
            scaled = (
                raw
                * lax.rsqrt(jnp.mean(raw * raw, axis=1, keepdims=True) + EPS)
                * gain_ref[part : part + 1, :]
            )
            target[span, :] = (scaled * cos_ref[span, :] + swapped(scaled) * sin_ref[span, :]).astype(
                BF
            )
        return carry

    lax.fori_loop(0, SEQ // BLOCK, prepare, 0)
    row, col = lax.axis_index("row"), lax.axis_index("col")
    for ahead in (1, 3, 2, 0):
        first = lax.rem(col + ahead, 4) * 512

        def block(step, carry, first=first):
            span = pl.ds(pl.multiple_of(first + step * BLOCK, BLOCK), BLOCK)
            scores = (
                lax.dot_general(
                    query_ref[span, :], key_ref[...], LAST, preferred_element_type=F32
                )
                * SCALE
            )
            largest = jnp.max(scores, axis=1, keepdims=True)
            weights = jnp.exp(scores - largest)
            total = jnp.sum(weights, axis=1, keepdims=True)
            mixed = jnp.dot(
                weights.astype(BF), qkv_ref[:, 2 * HEAD :], preferred_element_type=F32
            )
            out_ref[span, :] = (mixed / total).astype(BF)
            lse_ref[span, :] = largest + jnp.log(total)
            return carry

        lax.fori_loop(0, 512 // BLOCK, block, 0)
        for number in ready[ahead]:
            links.send(number)
    gathered[:, rows((row * 4 + col) * HEAD, HEAD)] = out_ref[rows(col * 512, 512), :]


def attend(qkv, position, frequency, gains, blocks):
    take, put = expert_views()
    sends = [(offset, 0, take, 0, put) for offset in CUBE]
    ready = {ahead: [] for ahead in range(4)}
    for offset in PLANE:
        ready[offset[3]].append(len(sends))
        sends.append(
            (
                offset,
                ("scratch", 0),
                lambda s, me, p: s.at[rows(p[3] * 512, 512)],
                ("made", 5),
                lambda o, me, p: o.at[:, rows((me[2] * 4 + me[3]) * HEAD, HEAD)],
            )
        )
    return exchange(
        [blocks],
        [shape((16, ROOM, WIDTH))],
        sends,
        [(0, lambda s, me: take(s, me, me), 0, lambda o, me: put(o, me, me), (ROOM, 512))],
        6,
        work=lambda links, *refs: attend_kernel(links, ready, *refs),
        work_in=[qkv, position, frequency, gains],
        work_out=[
            shape((SEQ, HEAD)),
            shape((SEQ, HEAD)),
            shape((SEQ, 1), F32),
            shape((SEQ, HEAD), F32),
            shape((SEQ, HEAD), F32),
            shape((512, WIDTH)),
        ],
        work_scratch=[pltpu.VMEM((SEQ, HEAD), BF)],
        deferred=range(len(CUBE), len(sends)),
    )


NEAR_FIRST = (1, 3, 2, 0)


def attend_back_kernel(
    links,
    numbers,
    partial_ref,
    qkv_ref,
    query_ref,
    key_ref,
    lse_ref,
    cos_ref,
    sin_ref,
    gain_ref,
    qkv_grad_ref,
    gain_grad_ref,
    cross,
    mixed,
    out_grads,
    grad_ref,
    query_grad,
    key_grad,
    value_grad,
):
    to_rows, to_cols, back_query, back_to_cols, last = numbers
    row, col = lax.axis_index("row"), lax.axis_index("col")
    for ahead in NEAR_FIRST:
        for number in to_rows[ahead]:
            links.send(number)
    key_grad[...] = jnp.zeros_like(key_grad)
    value_grad[...] = jnp.zeros_like(value_grad)

    def mix(ahead):
        head = lax.rem(col + ahead, 4)
        for number in to_rows[ahead]:
            links.arrive(number)
        total = partial_ref[:, rows((row * 4 + head) * HEAD, HEAD)].astype(F32)
        for part in range(3):
            total = total + cross[part, ahead].astype(F32)
        if ahead:
            mixed[ahead] = total.astype(BF)
            links.send(to_cols[ahead])
        else:
            out_grads[rows(col * 512, 512), :] = total.astype(BF)

    def attend_block(ahead):
        if ahead:
            links.arrive(to_cols[ahead])
        first = lax.rem(col + 4 - ahead, 4) * 512

        def block(step, carry):
            span = pl.ds(pl.multiple_of(first + step * BLOCK, BLOCK), BLOCK)
            query, out_grad = query_ref[span, :], out_grads[span, :]
            scores = (
                lax.dot_general(query, key_ref[...], LAST, preferred_element_type=F32) * SCALE
            )
            soft = jnp.exp(scores - lse_ref[span, :])
            prob_grad = lax.dot_general(
                out_grad, qkv_ref[:, 2 * HEAD :], LAST, preferred_element_type=F32
            )
            inner = jnp.sum(soft * prob_grad, axis=1, keepdims=True)
            score_grad = (soft * (prob_grad - inner)).astype(BF)
            query_grad[span, :] = (
                jnp.dot(score_grad, key_ref[...], preferred_element_type=F32) * SCALE
            )
            key_grad[...] += lax.dot_general(
                score_grad, query, FIRST, preferred_element_type=F32
            )
            value_grad[...] += lax.dot_general(
                soft.astype(BF), out_grad, FIRST, preferred_element_type=F32
            )
            return carry

        lax.fori_loop(0, 512 // BLOCK, block, 0)
        finish_part(first, ((0, query_grad, 1.0),))
        if ahead:
            links.send(back_query[(4 - ahead) % 4])

    def finish_part(first, sources):
        def finish_block(step, carry):
            span = pl.ds(pl.multiple_of(first + step * BLOCK, BLOCK), BLOCK)
            for part, source, factor in sources:
                turned = source[span, :] * factor
                grad = turned * cos_ref[span, :] + swapped(turned * sin_ref[span, :])
                raw = qkv_ref[span, part * HEAD : (part + 1) * HEAD].astype(F32)
                inverse = lax.rsqrt(jnp.mean(raw * raw, axis=1, keepdims=True) + EPS)
                unit = raw * inverse
                gain_grad_ref[part : part + 1, :] += jnp.sum(grad * unit, axis=0, keepdims=True)
                scaled = grad * gain_ref[part : part + 1, :]
                raw_grad = inverse * (
                    scaled - unit * jnp.mean(scaled * unit, axis=1, keepdims=True)
                )
                grad_ref[span, part * HEAD : (part + 1) * HEAD] = raw_grad.astype(BF)
                if part:
                    grad_ref[span, 2 * HEAD :] = value_grad[span, :].astype(BF)
            return carry

        lax.fori_loop(0, 512 // BLOCK, finish_block, 0)

    gain_grad_ref[...] = jnp.zeros_like(gain_grad_ref)
    mix(1)
    mix(3)
    attend_block(1)
    mix(2)
    attend_block(3)
    mix(0)
    for number in last:
        links.send(number)
    attend_block(2)
    attend_block(0)
    for ahead in NEAR_FIRST:
        finish_part(lax.rem(col + ahead, 4) * 512, ((1, key_grad, SCALE),))
        if ahead:
            links.send(back_to_cols[ahead])
    qkv_grad_ref[:, rows(col * 384, 384)] = grad_ref[rows(col * 512, 512), :]


def attend_back(operands, out_part, small_part, up_grad):
    whole = lambda s, me, p: s
    sends = [
        (SIBLING, 0, lambda s, me, p: s.at[:, rows(p[1] * 64, 64)], 0, whole),
        (SIBLING, 1, whole, 1, whole),
    ]
    later = len(sends)
    to_rows, to_cols, back_query, back_to_cols = {}, {}, {}, {}
    for ahead in NEAR_FIRST:
        to_rows[ahead] = []
        for part, offset in enumerate(ROWS):
            to_rows[ahead].append(len(sends))
            head = lambda me, p, ahead=ahead: p[2] * 4 + (me[3] + ahead) % 4
            sends.append(
                (
                    offset,
                    ("work", 0),
                    lambda s, me, p, head=head: s.at[:, rows(head(me, p) * HEAD, HEAD)],
                    ("scratch", 0),
                    lambda o, me, p, part=part, ahead=ahead: o.at[part, ahead],
                )
            )
    for offset in COLS:
        ahead = offset[3]
        to_cols[ahead] = len(sends)
        sends.append(
            (
                offset,
                ("scratch", 1),
                lambda s, me, p, ahead=ahead: s.at[ahead],
                ("scratch", 2),
                lambda o, me, p: o.at[rows(me[3] * 512, 512)],
            )
        )
        for numbers, skip, size in ((back_query, 0, HEAD), (back_to_cols, HEAD, 2 * HEAD)):
            numbers[ahead] = len(sends)
            sends.append(
                (
                    offset,
                    ("scratch", 3),
                    lambda s, me, p, skip=skip, size=size: s.at[
                        rows(p[3] * 512, 512), pl.ds(skip, size)
                    ],
                    ("made", 0),
                    lambda o, me, p, skip=skip, size=size: o.at[
                        :, pl.ds(pl.multiple_of(me[3] * 384 + skip, HEAD), size)
                    ],
                )
            )
    last = [len(sends)]
    sends.append((ONE_BACK, 2, whole, 2, whole))
    return exchange(
        [out_part, small_part, up_grad],
        [
            shape((16, 64, 512)),
            shape(small_part.shape, F32),
            shape(up_grad.shape),
        ],
        sends,
        [],
        13,
        deferred=range(later, len(sends)),
        work=lambda links, *refs: attend_back_kernel(
            links, (to_rows, to_cols, back_query, back_to_cols, last), *refs
        ),
        work_in=operands,
        work_out=[shape((512, 1536)), shape((8, HEAD), F32)],
        work_scratch=[
            pltpu.VMEM((3, 4, 512, HEAD), BF),
            pltpu.VMEM((4, 512, HEAD), BF),
            pltpu.VMEM((SEQ, HEAD), BF),
            pltpu.VMEM((SEQ, 3 * HEAD), BF),
        ]
        + [pltpu.VMEM((SEQ, HEAD), F32)] * 3,
    )


SLOTS = 16 * ROOM
GROUP = 4 * ROOM


def expert_kernel(
    links,
    came,
    returns,
    results,
    shares,
    cot_ref,
    gated_ref,
    up_1,
    up_2,
    down_1,
    down_2,
    x_ref,
    back_ref,
    joined,
    slot_grads,
    acts,
    grads,
    their_x,
    their_slot_grads,
    their_acts,
    their_grads,
    up_ref,
    down_ref,
    out_sum,
    back_sum,
    weight_sem,
    own_sem,
):
    me = here()
    loads = []
    for slot in range(4):
        for part, target in ((1, up_ref), (5, down_ref)):
            loads.append(
                pltpu.make_async_copy(
                    links.ins[part + slot], target.at[slot], weight_sem.at[part + slot - 1]
                )
            )
    take, put = expert_views()
    own_in = pltpu.make_async_copy(take(links.ins[0], me, me), put(x_ref, me, me), own_sem.at[0])
    take, put = token_views()
    own_out = pltpu.make_async_copy(
        take(back_ref, me, me), put(links.outs[0], me, me), own_sem.at[1]
    )
    own_result = pltpu.make_async_copy(
        take(gated_ref, me, me), put(links.outs[1], me, me), own_sem.at[2]
    )
    own_in.start()
    for load in loads:
        load.start()
    line = lax.broadcasted_iota(jnp.int32, (ROOM, HEAD), 0)
    lane = lax.broadcasted_iota(jnp.int32, (ROOM, HEAD), 1)
    same = (line == lane).astype(F32)
    for group in range(4):
        if group == 0:
            own_in.wait()
        for number in came[group]:
            links.arrive(number)
        if group == 0:
            for load in loads:
                load.wait()
        blocks = [
            lax.rem(me[0] + 4 - i, 4) * 4 + lax.rem(me[3] + 4 - (group - i) % 4, 4)
            for i in range(4)
        ]
        span = pl.ds(group * GROUP, GROUP)
        received = jnp.concatenate([x_ref[block].astype(F32) for block in blocks], axis=0)
        cot = jnp.concatenate([cot_ref[block].astype(F32) for block in blocks], axis=0)
        gates = []
        for i in range(4):
            aux = jnp.where(line >= CAP, received[i * ROOM : (i + 1) * ROOM, :HEAD], 0.0)
            gates.append(
                jnp.sum(same * jnp.sum(aux, axis=0, keepdims=True), axis=1, keepdims=True)
            )
        gate = jnp.concatenate(gates, axis=0)
        joined[span, :] = received.astype(BF)
        slot_grads[span, :] = (gate * cot).astype(BF)
        out_sum[...] = jnp.zeros_like(out_sum)
        back_sum[...] = jnp.zeros_like(back_sum)

        def quarter(slot, carry, span=span):
            gate_up = jnp.dot(joined[span, :], up_ref[slot], preferred_element_type=F32)
            gate_part, up_part = gate_up[:, :256], gate_up[:, 256:]
            sigmoid = 1.0 / (1.0 + jnp.exp(-gate_part))
            silu = gate_part * sigmoid
            act = (silu * up_part).astype(BF)
            acts[slot, span, :] = act
            act_grad = lax.dot_general(
                slot_grads[span, :], down_ref[slot], LAST, preferred_element_type=F32
            )
            slope = sigmoid * (1.0 + gate_part * (1.0 - sigmoid))
            grads[slot, span, :256] = (act_grad * up_part * slope).astype(BF)
            grads[slot, span, 256:] = (act_grad * silu).astype(BF)
            out_sum[...] += jnp.dot(act, down_ref[slot], preferred_element_type=F32)
            back_sum[...] += lax.dot_general(
                grads[slot, span, :], up_ref[slot], LAST, preferred_element_type=F32
            )
            return carry

        lax.fori_loop(0, 4, quarter, 0)
        out = out_sum[...]
        gated = gate * out
        gate_grad = jnp.sum(cot * out.astype(BF).astype(F32), axis=1, keepdims=True)
        back = back_sum[...]
        inner = jnp.sum(back * joined[span, :].astype(F32), axis=1, keepdims=True)
        for i, block in enumerate(blocks):
            part = slice(i * ROOM, (i + 1) * ROOM)
            gated_ref[block] = gated[part].astype(BF)
            back_ref[block] = back[part].astype(BF)
            for index, value in enumerate((gate_grad, inner)):
                high, middle, low = pieces(jnp.sum(same * value[part], axis=0, keepdims=True))
                aux = jnp.where(line == CAP, high.astype(F32), 0.0)
                aux = aux + jnp.where(line == CAP + 1, middle.astype(F32), 0.0)
                aux = aux + jnp.where(line == CAP + 2, low.astype(F32), 0.0)
                for r in range(4):
                    start = r * 512 + index * HEAD
                    back_ref[block, :, start : start + HEAD] = (
                        back[part, start : start + HEAD] + aux
                    ).astype(BF)
        for number in returns[group]:
            links.send(number)
        if group == 0:
            own_out.start()
            own_result.start()
        for number in shares[group] + results[group]:
            links.send(number)
    for numbers in shares:
        for number in numbers:
            links.arrive(number)

    def weight_grads(step, carry):
        span = pl.ds(pl.multiple_of(step * 512, 512), 512)
        for slot, up, down in ((0, up_1, down_1), (1, up_2, down_2)):
            up[span, :] = (
                lax.dot_general(joined[:, span], grads[slot], FIRST, preferred_element_type=F32)
                + lax.dot_general(
                    their_x[:, span], their_grads[slot], FIRST, preferred_element_type=F32
                )
            ).astype(BF)
            down[:, span] = (
                lax.dot_general(
                    acts[slot], slot_grads[:, span], FIRST, preferred_element_type=F32
                )
                + lax.dot_general(
                    their_acts[slot],
                    their_slot_grads[:, span],
                    FIRST,
                    preferred_element_type=F32,
                )
            ).astype(BF)
        return carry

    lax.fori_loop(0, 4, weight_grads, 0)
    own_out.wait()
    own_result.wait()


def run_experts(blocks, cot_slots, weights):
    take, put = expert_views()
    came, returns, results, shares = ([[], [], [], []] for _ in range(4))
    sends = []
    for offset in CUBE:
        came[(offset[0] + offset[3]) % 4].append(len(sends))
        sends.append((offset, 0, take, ("scratch", 0), put))
    take, put = token_views()
    for offset in CUBE:
        returns[-(offset[0] + offset[3]) % 4].append(len(sends))
        sends.append((offset, ("scratch", 1), take, 0, put))
    for offset in CUBE:
        results[-(offset[0] + offset[3]) % 4].append(len(sends))
        sends.append((offset, ("made", 0), take, 1, put))
    for place in range(4):
        span = pl.ds(place * GROUP, GROUP)
        for mine, theirs in ((2, 6), (3, 7)):
            view = lambda ref, me, p, span=span: ref.at[span]
            shares[place].append(len(sends))
            sends.append((SIBLING, ("scratch", mine), view, ("scratch", theirs), view))
        for mine, theirs in ((4, 8), (5, 9)):
            shares[place].append(len(sends))
            sends.append(
                (
                    SIBLING,
                    ("scratch", mine),
                    lambda ref, me, p, span=span: ref.at[pl.ds(2, 2), span],
                    ("scratch", theirs),
                    lambda ref, me, p, span=span: ref.at[:, span],
                )
            )
    return exchange(
        [blocks] + weights,
        [shape((EXPERTS, ROOM, 512))] * 2,
        sends,
        [],
        8,
        work=lambda links, *refs: expert_kernel(
            links, came, returns, results, shares, *refs
        ),
        work_in=[cot_slots],
        work_out=[shape((16, ROOM, WIDTH))]
        + [shape((WIDTH, 512))] * 2
        + [shape((256, WIDTH))] * 2,
        work_scratch=[
            pltpu.VMEM((16, ROOM, WIDTH), BF),
            pltpu.VMEM((16, ROOM, WIDTH), BF),
            pltpu.VMEM((SLOTS, WIDTH), BF),
            pltpu.VMEM((SLOTS, WIDTH), BF),
            pltpu.VMEM((4, SLOTS, 256), BF),
            pltpu.VMEM((4, SLOTS, 512), BF),
            pltpu.VMEM((SLOTS, WIDTH), BF),
            pltpu.VMEM((SLOTS, WIDTH), BF),
            pltpu.VMEM((2, SLOTS, 256), BF),
            pltpu.VMEM((2, SLOTS, 512), BF),
            pltpu.VMEM((4, WIDTH, 512), BF),
            pltpu.VMEM((4, 256, WIDTH), BF),
            pltpu.VMEM((GROUP, WIDTH), F32),
            pltpu.VMEM((GROUP, WIDTH), F32),
            pltpu.SemaphoreType.DMA((8,)),
            pltpu.SemaphoreType.DMA((3,)),
        ],
        deferred=range(len(CUBE), len(sends)),
    )


def pack_kernel(up_1, up_2, down_1, down_2, qkv, out, up_ref, down_ref, qkv_ref, out_ref):
    upper = lax.axis_index("row") // 2
    for which, up, down in ((upper, up_1, down_1), (1 - upper, up_2, down_2)):
        value = up[...].astype(F32)
        up_ref[which, :, 0, :] = value[:, :256]
        up_ref[which, :, 1, :] = value[:, 256:]
        down_ref[which] = down[...].astype(F32)
    out_ref[...] = out[...].astype(F32)
    for head in range(4):
        qkv_ref[:, head, :] = qkv[:, head * 384 : (head + 1) * 384].astype(F32)


def pack_grads(up_1, up_2, down_1, down_2, qkv, out):
    steps = 8
    up, down = (WIDTH // steps, 512), (256 // steps, WIDTH)
    return pl.pallas_call(
        pack_kernel,
        grid=(steps,),
        out_shape=[
            shape((2, WIDTH, 2, 256), F32),
            shape((2, 256, WIDTH), F32),
            shape((512, 4, 384), F32),
            shape((512, 512), F32),
        ],
        in_specs=[pl.BlockSpec(up, lambda i: (i, 0))] * 2
        + [pl.BlockSpec(down, lambda i: (i, 0))] * 2
        + [pl.BlockSpec((512 // steps, 1536), lambda i: (i, 0))]
        + [pl.BlockSpec((512 // steps, 512), lambda i: (i, 0))],
        out_specs=[
            pl.BlockSpec((2, up[0], 2, 256), lambda i: (0, i, 0, 0)),
            pl.BlockSpec((2,) + down, lambda i: (0, i, 0)),
            pl.BlockSpec((512 // steps, 4, 384), lambda i: (i, 0, 0)),
            pl.BlockSpec((512 // steps, 512), lambda i: (i, 0)),
        ],
    )(up_1, up_2, down_1, down_2, qkv, out)


def dot(left, right):
    return jnp.dot(left, right, preferred_element_type=F32)


def dot_last(left, right):
    return lax.dot_general(left, right, LAST, preferred_element_type=F32)


def dot_first(left, right):
    return lax.dot_general(left, right, FIRST, preferred_element_type=F32)


def pieces(value):
    high = value.astype(BF)
    rest = value - high.astype(F32)
    middle = rest.astype(BF)
    low = (rest - middle.astype(F32)).astype(BF)
    return [high, middle, low]


def aux_rows(value):
    held = jnp.stack(pieces(value), axis=1)
    return jnp.pad(held, ((0, 0), (CAP, ROOM - CAP - 3), (0, 512 - ROOM)))


def aux_value(blocks, index):
    part = blocks[:, CAP : CAP + 3, index * HEAD : index * HEAD + ROOM]
    return jnp.sum(part.astype(F32), axis=1)


FIRST_HOP = [
    ((2 * y + k) * 4 + x, (2 * y + 1 - x % 2) * 4 + 2 * k + x // 2)
    for y in range(4)
    for k in range(2)
    for x in range(4)
]
SECOND_HOP = [
    ((2 * y + k) * 4 + x, (2 * y + x % 2) * 4 + 2 * k + 1 - x // 2)
    for y in range(4)
    for k in range(2)
    for x in range(4)
]
PAIR = [(d, d ^ 1) for d in range(8)]


def hop(operand, pairs):
    return lax.ppermute(operand, ("dp", "row"), pairs)


def after(*operands):
    return lax.optimization_barrier(operands)


def shards(
    tokens,
    positions,
    routes,
    attention_norm_gain,
    experts_norm_gain,
    w_qkv,
    q_gain,
    k_gain,
    w_out,
    w_router,
    w_gate_up,
    w_down,
    cotangent,
):
    core = lax.axis_index("dp") % 2
    experts = jnp.arange(EXPERTS, dtype=jnp.int32)
    named = jnp.any(routes[:, :, None] == experts[None, None, :], axis=1)
    place = jnp.arange(512, dtype=jnp.int32)
    earlier = (place[None, :] < place[:, None]).astype(BF)
    rank = dot(earlier, named.astype(BF))
    rank = jnp.where(named, rank, -1.0).T
    (
        token_rows,
        w_group,
        position_rows,
        gain_rows,
        w_all,
        down_1,
        down_2,
        send_up_1,
        send_up_2,
        send_cot,
    ) = gather_inputs(
        tokens,
        w_qkv,
        w_out,
        w_down,
        positions.reshape(4, HEAD),
        attention_norm_gain.reshape(4, HEAD),
        [w_gate_up, rank, cotangent],
    )
    w_all = w_all.reshape(WIDTH, 512)
    w_group = w_group.reshape(WIDTH, 1536)
    gain_full = gain_rows.reshape(WIDTH)

    gate_up_1, gate_up_2 = hop(send_up_1, FIRST_HOP), hop(send_up_2, SECOND_HOP)
    sibling = lambda w: lax.ppermute(w, "dp", PAIR)
    frequency = THETA ** (-2.0 * jnp.arange(HEAD // 2, dtype=F32) / HEAD)
    half_signs = jnp.where(jnp.arange(HEAD) < HEAD // 2, -1.0, 1.0).astype(F32)
    frequency = jnp.concatenate(
        [jnp.concatenate([frequency] * 2)[None], half_signs[None], jnp.zeros((6, HEAD), F32)]
    )
    position_column = position_rows.reshape(SEQ, 1).astype(F32)
    gains = jnp.concatenate([q_gain[None], k_gain[None], jnp.zeros((6, HEAD), F32)], axis=0)

    pick = (rank[:, None, :] == jnp.arange(ROOM, dtype=F32)[None, :, None]).astype(BF)
    flat_pick = pick.reshape(EXPERTS * ROOM, 512)

    token_full = token_rows.astype(F32)
    inverse_attention = lax.rsqrt(jnp.mean(token_full * token_full, axis=1) + EPS)
    normed_exact = token_full * inverse_attention[:, None] * gain_full[None, :]
    normed = normed_exact.astype(BF)
    qkv = to_heads(dot(normed, w_group).astype(BF))
    cot_slots, query, key, lse, cosine, sine, attended_rows = attend(
        qkv, position_column, frequency, gains, send_cot
    )
    attended_rows, gate_up_1, gate_up_2, down_1, down_2 = after(
        attended_rows, gate_up_1, gate_up_2, down_1, down_2
    )
    up_ws = [gate_up_1, gate_up_2, sibling(gate_up_1), sibling(gate_up_2)]
    down_ws = [down_1, down_2, sibling(down_1), sibling(down_2)]

    token_float = tokens.astype(F32)
    hidden = token_float + dot(attended_rows, w_all)
    scaled_hidden = hidden * experts_norm_gain
    partial_stats = jnp.concatenate(
        [
            lax.dot_general(
                w_router.astype(F32),
                scaled_hidden,
                (((0,), (1,)), ((), ())),
                precision=EXACT,
                preferred_element_type=F32,
            ),
            jnp.sum(hidden * hidden, axis=1)[None],
            jnp.zeros((7, 512), F32),
        ],
        axis=0,
    )
    stats = jnp.sum(row_stack(partial_stats, 7), axis=0)
    inverse_experts = lax.rsqrt(stats[EXPERTS] / WIDTH + EPS)
    logits = stats[:EXPERTS] * inverse_experts[None, :]
    unit_experts = hidden * inverse_experts[:, None]
    experts_input = (unit_experts * experts_norm_gain).astype(BF)
    named_t = rank >= 0
    largest = jnp.max(jnp.where(named_t, logits, -jnp.inf), axis=0, keepdims=True)
    shifted = jnp.where(named_t, jnp.exp(jnp.where(named_t, logits - largest, 0.0)), 0.0)
    gates = shifted / jnp.sum(shifted, axis=0, keepdims=True)
    slot_gates = jnp.sum(pick.astype(F32) * gates[:, None, :], axis=2)
    send_rows = dot(flat_pick, experts_input).astype(BF).reshape(EXPERTS, ROOM, 512)
    back_rows, out_rows, _, up_1, up_2, down_1, down_2 = run_experts(
        send_rows + aux_rows(slot_gates), cot_slots, up_ws + down_ws
    )
    gate_grad = jnp.sum(pick.astype(F32) * aux_value(back_rows, 0)[:, :, None], axis=1)
    inner = jnp.sum(pick.astype(F32) * aux_value(back_rows, 1)[:, :, None], axis=(0, 1))
    logit_grad = gates * (gate_grad - jnp.sum(gates * gate_grad, axis=0, keepdims=True))
    experts_input_grad = dot_first(
        flat_pick, back_rows.reshape(EXPERTS * ROOM, 512)
    ) + lax.dot_general(
        logit_grad,
        w_router.astype(F32),
        (((0,), (1,)), ((), ())),
        precision=EXACT,
        preferred_element_type=F32,
    )
    mean_experts = (inner + jnp.sum(logit_grad * logits, axis=0)) / WIDTH
    cot_float = cotangent.astype(F32)
    middle_grad = cot_float + inverse_experts[:, None] * (
        experts_input_grad * experts_norm_gain - unit_experts * mean_experts[:, None]
    )
    router_part = lax.dot_general(
        logit_grad,
        experts_input.astype(F32),
        (((1,), (0,)), ((), ())),
        precision=EXACT,
        preferred_element_type=F32,
    )
    experts_gain_part = jnp.sum(experts_input_grad * unit_experts, axis=0)
    attended_grad = middle_grad.astype(BF)
    out_part = dot_first(attended_rows, attended_grad).astype(BF).reshape(16, HEAD, 512)
    small_part = jnp.concatenate(
        [
            router_part.reshape(256, HEAD),
            experts_gain_part.reshape(4, HEAD),
            jnp.zeros((124, HEAD), F32),
        ],
        axis=0,
    )
    out_other, small_other, up_1, qkv_grad, head_gain_part = attend_back(
        [dot_last(attended_grad, w_all).astype(BF), qkv, query, key, lse, cosine, sine, gains],
        out_part,
        small_part,
        up_1,
    )
    down_1, down_2, by_y, by_z, _, _, output, out_piece, small_piece, token_grad, late = finish(
        down_1,
        down_2,
        [
            normed,
            qkv_grad,
            w_group,
            head_gain_part,
            hidden,
            flat_pick,
            out_rows.reshape(EXPERTS * ROOM, 512),
            out_part,
            out_other,
            small_part,
            small_other,
            middle_grad,
            tokens,
            inverse_attention[:, None],
            jnp.broadcast_to(attention_norm_gain[None], (8, 512)),
        ],
    )
    out_total, small_total, late, up_2, qkv_total = collect_sums(
        by_y, by_z, out_piece, small_piece, late, up_2
    )
    small_total = small_total.reshape(384, HEAD)
    late = jnp.sum(late, axis=0)
    grad_gate_up, grad_down, grad_qkv, grad_out = pack_grads(
        up_1,
        up_2,
        down_1,
        down_2,
        qkv_total.reshape(512, 1536),
        out_total.reshape(512, 512),
    )
    return (
        output,
        token_grad,
        late[:4].reshape(512),
        small_total[256:260].reshape(512),
        grad_qkv,
        late[4],
        late[5],
        grad_out,
        small_total[:256].reshape(EXPERTS, 512).T,
        grad_gate_up,
        grad_down,
    )


def solution(mesh):
    tokens_like = P(("dp", "col"), "row")
    up_like = P(("dp", "col"), None, None, "row")
    down_like = P(("dp", "col"), "row", None)
    return jax.shard_map(
        shards,
        mesh=mesh,
        in_specs=(
            tokens_like,
            P("dp", "row"),
            P(("dp", "col"), None),
            P("row"),
            P("row"),
            P("row", "col", None),
            P(),
            P(),
            P("col", "row"),
            P("row", None),
            up_like,
            down_like,
            tokens_like,
        ),
        out_specs=(
            tokens_like,
            tokens_like,
            P("row"),
            P("row"),
            P("row", "col", None),
            P(),
            P(),
            P("col", "row"),
            P("row", None),
            up_like,
            down_like,
        ),
        check_vma=False,
    )
```

```python
import jax
import jax.numpy as jnp
from jax import lax
from jax.experimental import pallas as pl
from jax.experimental.pallas import tpu as pltpu
from jax.sharding import PartitionSpec as P

WIDTH = 2048
HEAD = 128
EXPERTS = 64
CAP = 36
ROOM = 40
SEQ = 2048
EPS = 1e-06
THETA = 10000.0
EXACT = lax.Precision.HIGHEST
MESH = pl.DeviceIdType.MESH
SIZES = (4, 2, 4, 4)
BF = jnp.bfloat16
F32 = jnp.float32
ROWS = [(0, 0, d, 0) for d in (2, 1, 3)]
COLS = [(0, 0, 0, d) for d in (2, 1, 3)]
SIBLING = (0, 1, 0, 0)
PLANE = [(0, 0, i, (i + s) % 4) for s in range(4) for i in range(4) if (i, s) != (0, 0)]
CUBE = [
    (i, 0, (i + s) % 4, (g - i) % 4)
    for g in range(4)
    for s in range(4)
    for i in range(4)
    if (g, s, i) != (0, 0, 0)
]
SOURCES = [(i, 0, 0, (i + s) % 4) for s in range(4) for i in range(4) if (i, s) != (0, 0)]
SIDES = [(i, 0, (i + s) % 4, 0) for s in range(4) for i in range(4) if (i, s) != (0, 0)]
LINES = [(d, 0, 0, 0) for d in (2, 1, 3)]
OTHERS = [
    (a, k, 0, d) for a in range(4) for k in range(2) for d in range(4) if (a, k, d) != (0, 0, 0)
]


def shape(dims, dtype=BF):
    return jax.ShapeDtypeStruct(dims, dtype)


def here():
    group = lax.axis_index("dp")
    return (group // 2, group % 2, lax.axis_index("row"), lax.axis_index("col"))


class Hop:
    def __init__(self, to, origin):
        self.to, self.origin = to, origin


ONE_WAY = Hop(
    lambda p: (p[0], 1 - p[2] % 2, 2 * p[1] + p[2] // 2, p[3]),
    lambda p: (p[0], p[2] // 2, 2 * (p[2] % 2) + 1 - p[1], p[3]),
)
OTHER_WAY = Hop(
    lambda p: (p[0], p[2] % 2, 2 * p[1] + 1 - p[2] // 2, p[3]),
    lambda p: (p[0], p[2] // 2, 2 * (1 - p[2] % 2) + p[1], p[3]),
)


ONE_BACK, OTHER_BACK = Hop(ONE_WAY.origin, ONE_WAY.to), Hop(OTHER_WAY.origin, OTHER_WAY.to)


class Links:
    def __init__(self, send, arrive, ins, outs):
        self.send, self.arrive, self.ins, self.outs = send, arrive, ins, outs


def moved(place, offset):
    if isinstance(offset, Hop):
        return offset.to(place)
    return tuple((p + o) % n for p, o, n in zip(place, offset, SIZES))


def device(place):
    return (place[0] * 2 + place[1], place[2], place[3])


def exchange(
    inputs,
    outputs,
    sends,
    kept,
    call_id,
    micros=30,
    work=None,
    work_in=(),
    work_out=(),
    work_scratch=(),
    stages=(),
    deferred=(),
):
    offsets = sorted({s[0] for s in sends if not isinstance(s[0], Hop)})
    hops = {id(s[0]): s[0] for s in sends if isinstance(s[0], Hop)}.values()
    n_in, n_out, n_send = len(inputs), len(outputs), len(sends)
    m_in, m_out = len(work_in), len(work_out)

    def kernel(*refs):
        ins, refs = refs[:n_in], refs[n_in:]
        worked, refs = refs[:m_in], refs[m_in:]
        outs, refs = refs[:n_out], refs[n_out:]
        made, refs = refs[:m_out], refs[m_out:]
        send_sem, recv_sem, kept_sem = refs[:3]
        staged, refs = refs[3 : 3 + len(kept)], refs[3 + len(kept) :]
        special = {"work": worked, "made": made, "scratch": refs}
        me = here()
        barrier = pltpu.get_barrier_semaphore()
        greeted = [moved(me, offset) for offset in offsets]
        for way in hops:
            greeted += [way.to(me), way.origin(me)]
        for peer in greeted:
            pl.semaphore_signal(barrier, inc=1, device_id=device(peer), device_id_type=MESH)
        local = []
        for index, (i, take, o, put, _) in enumerate(kept):
            source, target = take(ins[i], me), put(outs[o], me)
            local.append(
                (
                    pltpu.make_async_copy(source, staged[index], kept_sem.at[index, 0]),
                    pltpu.make_async_copy(staged[index], target, kept_sem.at[index, 1]),
                )
            )
            local[-1][0].start()
        pl.semaphore_wait(barrier, len(greeted))
        copies, arrived = {}, set()

        def arrive(index):
            if index not in arrived:
                arrived.add(index)
                copies[index].wait_recv()

        def named(group, index):
            return special[index[0]][index[1]] if isinstance(index, tuple) else group[index]

        def start(index):
            offset, i, take, o, put = sends[index][:5]
            needs = sends[index][5] if len(sends[index]) > 5 else None
            for need in needs or ():
                if need >= 0:
                    arrive(need)
                elif need not in arrived:
                    arrived.add(need)
                    local[-need - 1][1].wait()
            peer = moved(me, offset)
            copies[index] = pltpu.make_async_remote_copy(
                src_ref=take(named(ins if needs is None else outs, i), me, peer),
                dst_ref=put(named(outs, o), me, peer),
                send_sem=send_sem.at[index],
                recv_sem=recv_sem.at[index],
                device_id=device(peer),
                device_id_type=MESH,
            )
            copies[index].start()

        links = Links(start, arrive, ins, outs)
        parts = work(links, *worked, *made, *refs) if stages else ()
        first = [i for i in range(n_send) if len(sends[i]) < 6 and i not in deferred]
        for index in first:
            start(index)
        for load, store in local:
            load.wait()
            store.start()
        for index in range(n_send):
            if index in first or index in deferred:
                continue
            for part, at in zip(parts, stages):
                if at == index:
                    part()
            start(index)
        if work is not None and not stages:
            work(links, *worked, *made, *refs)
        for index in range(n_send):
            arrive(index)
        for copy in copies.values():
            copy.wait_send()
        for index, copy in enumerate(local):
            if -index - 1 not in arrived:
                copy[1].wait()

    return pl.pallas_call(
        kernel,
        out_shape=list(outputs) + list(work_out),
        in_specs=[pl.BlockSpec(memory_space=pl.ANY)] * n_in
        + [pl.BlockSpec(memory_space=pltpu.VMEM)] * m_in,
        out_specs=[pl.BlockSpec(memory_space=pl.ANY)] * n_out
        + [pl.BlockSpec(memory_space=pltpu.VMEM)] * m_out,
        scratch_shapes=[
            pltpu.SemaphoreType.DMA((n_send,)),
            pltpu.SemaphoreType.DMA((n_send,)),
            pltpu.SemaphoreType.DMA((max(1, len(kept)), 2)),
            *[pltpu.VMEM(k[4], inputs[k[0]].dtype) for k in kept],
            *work_scratch,
        ],
        compiler_params=pltpu.CompilerParams(
            collective_id=call_id,
            has_side_effects=True,
            vmem_limit_bytes=(8 if work is None else 60) * 2**20,
        ),
        cost_estimate=pl.CostEstimate(
            flops=0, bytes_accessed=micros * 3_500_000, transcendentals=0
        ),
    )(*inputs, *work_in)


def rows(start, size):
    return pl.ds(pl.multiple_of(start, size), size)


def eighth(size):
    me = here()
    return rows((me[1] * 4 + me[0]) * size, size)


def half(size):
    return rows(here()[1] * size, size)


class Sends(list):
    def add(self, group, take, o, put=None, i=None, needs=None):
        first = len(self)
        for offset in group:
            if needs is None:
                self.append((offset, i, take, o, put))
            else:
                view = lambda ref, me, p: take(ref, me)
                self.append((offset, o, view, o, view, needs))
        return list(range(first, len(self)))


def early_kernel(links, up_ref, rank_ref, cot_ref, up_1, up_2, rows_ref):
    upper = lax.axis_index("row") // 2

    def unpack(which, target, first):
        def part():
            for step in range(4):
                span = pl.ds(first + step * 64, 64)
                target[span, :256] = up_ref[which, span, 0, :]
                target[span, 256:] = up_ref[which, span, 1, :]

        return part

    def pick(step):
        def part():
            ranks = rank_ref[step * 8 : step * 8 + 8, :]
            slots = lax.broadcasted_iota(jnp.int32, (8, ROOM, 512), 1).astype(F32)
            chosen = (ranks[:, None, :] == slots).astype(F32).reshape(8 * ROOM, 512)
            rows_of = jnp.dot(chosen.astype(BF), cot_ref[...], preferred_element_type=F32)
            rows_ref[pl.ds(step * 8, 8)] = rows_of.reshape(8, ROOM, 512).astype(BF)

        return part

    parts = [unpack(upper, up_1, step * 256) for step in range(8)]
    parts += [unpack(1 - upper, up_2, step * 256) for step in range(8)]
    return parts + [pick(step) for step in range(8)]


def gather_inputs(tokens, w_qkv, w_out, w_down, small_int, small_float, early):
    outputs = [
        shape((512, WIDTH)),
        shape((4, 512, 1536)),
        shape((4, 4, HEAD), jnp.int32),
        shape((4, 4, HEAD), F32),
        shape((4, 4, HEAD, 512)),
        shape((256, WIDTH)),
        shape((256, WIDTH)),
    ]
    sends = Sends()
    own_cols = lambda me: rows(me[3] * 384, 384)
    low, high = pl.ds(0, 2), pl.ds(2, 2)
    first = sends.add(
        ROWS,
        lambda s, me, p: s.at[eighth(64), rows(p[2] * 384, 384)],
        1,
        lambda o, me, p: o.at[me[2], eighth(64), own_cols(me)],
        1,
    )
    both = [(0, 0, 1, 0), (0, 0, 3, 0)]
    beside = sends.add(
        both, lambda s, me, p: s, 0, lambda o, me, p: o.at[:, rows(me[2] * 512, 512)], 0
    )
    sends.add(ROWS, lambda s, me, p: s, 2, lambda o, me, p: o.at[me[2]], 2)
    sends.add(ROWS, lambda s, me, p: s, 3, lambda o, me, p: o.at[me[2]], 3)
    sends.append((ONE_WAY, 5, lambda s, me, p: s.at[me[2] // 2], 5, lambda o, me, p: o))
    sends.append((OTHER_WAY, 5, lambda s, me, p: s.at[1 - me[2] // 2], 6, lambda o, me, p: o))
    out_z = sends.add(COLS, lambda o, me: o.at[low, me[3], eighth(16)], 4, needs=[-2])
    out_y = sends.add(LINES, lambda o, me: o.at[high, me[3], eighth(16)], 4, needs=[-2])
    stages = [len(sends)] * 3
    by_z = sends.add(
        COLS, lambda o, me: o.at[low, eighth(64), own_cols(me)], 1, needs=[-1] + first
    )
    by_y = sends.add(LINES, lambda o, me: o.at[high, eighth(64), own_cols(me)], 1, needs=first)
    sends.add(LINES, lambda o, me: o.at[low, eighth(64), own_cols(me)], 1, needs=first)
    sends.add(COLS, lambda o, me: o.at[high, eighth(64), own_cols(me)], 1, needs=first)
    last_z, last_y = {0: [len(sends) - 6 + i for i in range(3)]}, {0: list(range(len(sends) - 3, len(sends)))}
    for d in (1, 3, 2):
        came = by_z[[offset[3] for offset in COLS].index(d)]
        cols = lambda me, d=d: rows((me[3] + 4 - d) % 4 * 384, 384)
        stages += [len(sends)] * (3 if d == 1 else 1)
        last_z[d] = sends.add(
            LINES,
            lambda o, me, cols=cols: o.at[low, eighth(64), cols(me)],
            1,
            needs=[came],
        )
        came = by_y[[offset[0] for offset in LINES].index(d)]
        span = lambda me, d=d: rows((me[1] * 4 + (me[0] + 4 - d) % 4) * 64, 64)
        stages.append(len(sends))
        last_y[d] = sends.add(
            COLS,
            lambda o, me, span=span: o.at[high, span(me), own_cols(me)],
            1,
            needs=[came],
        )
    for index, offset in enumerate(both):
        passed = lambda o, me, index=index, d=offset[2]: o.at[
            pl.ds(index * 256, 256), rows((me[2] + 4 - d) % 4 * 512, 512)
        ]
        sends.add([offset], passed, 0, needs=[beside[index]])
    stages.append(len(sends))
    out_zy = sends.add(LINES, lambda o, me: o.at[low, :, eighth(16)], 4, needs=out_z)
    stages.append(len(sends))
    out_yz = sends.add(COLS, lambda o, me: o.at[high, me[3], half(64)], 4, needs=out_y)
    stages.append(len(sends))
    pair = [SIBLING]
    sends.add(pair, lambda o, me: o.at[low, eighth(64)], 1, needs=by_z)
    sends.add(pair, lambda o, me: o.at[high, half(256), own_cols(me)], 1, needs=by_y)
    for d in (1, 3, 2):
        line = [offset[0] for offset in LINES].index(d)
        stages += [len(sends)] * (4 if d == 1 else 2)
        span = lambda me, d=d: rows((me[1] * 4 + (me[0] + 4 - d) % 4) * 64, 64)
        sends.add(
            pair,
            lambda o, me, span=span: o.at[low, span(me)],
            1,
            needs=[numbers[line] for numbers in last_z.values()],
        )
        col = [offset[3] for offset in COLS].index(d)
        stages += [len(sends)] * (24 - len(stages) if d == 2 else 1)
        cols = lambda me, d=d: rows((me[3] + 4 - d) % 4 * 384, 384)
        sends.add(
            pair,
            lambda o, me, cols=cols: o.at[high, half(256), cols(me)],
            1,
            needs=[numbers[col] for numbers in last_y.values()],
        )
    sends.add(pair, lambda o, me: o.at[low, :, half(64)], 4, needs=out_zy)
    sends.add(pair, lambda o, me: o.at[high, :, half(64)], 4, needs=out_yz)
    kept = [
        (
            1,
            lambda s, me: s.at[eighth(64), rows(me[2] * 384, 384)],
            1,
            lambda o, me: o.at[me[2], eighth(64), own_cols(me)],
            (64, 384),
        ),
        (
            4,
            lambda s, me: s.at[:, eighth(16)],
            4,
            lambda o, me: o.at[:, me[3], eighth(16)],
            (4, 16, 512),
        ),
        (0, lambda s, me: s, 0, lambda o, me: o.at[:, rows(me[2] * 512, 512)], (512, 512)),
        (2, lambda s, me: s, 2, lambda o, me: o.at[me[2]], (4, HEAD)),
        (3, lambda s, me: s, 3, lambda o, me: o.at[me[2]], (4, HEAD)),
    ]
    return exchange(
        [
            tokens,
            w_qkv.reshape(512, 1536),
            small_int,
            small_float,
            w_out.reshape(4, HEAD, 512),
            w_down,
        ],
        outputs,
        sends,
        kept,
        0,
        work=early_kernel,
        work_in=early,
        work_out=[
            shape((WIDTH, 512)),
            shape((WIDTH, 512)),
            shape((EXPERTS, ROOM, 512)),
        ],
        stages=stages,
    )


def to_heads(qkv):
    take = lambda s, me, p: s.at[:, rows(p[3] * 384, 384)]
    put = lambda o, me, p: o.at[rows(me[3] * 512, 512)]
    return exchange(
        [qkv],
        [shape((SEQ, 384))],
        [(offset, 0, take, 0, put) for offset in COLS],
        [(0, lambda s, me: take(s, me, me), 0, lambda o, me: put(o, me, me), (512, 384))],
        1,
    )[0]


def row_stack(operand, call_id):
    take = lambda s, me, p: s
    put = lambda o, me, p: o.at[me[2]]
    return exchange(
        [operand],
        [shape((4,) + operand.shape, operand.dtype)],
        [(offset, 0, take, 0, put) for offset in ROWS],
        [(0, lambda s, me: s, 0, lambda o, me: put(o, me, me), operand.shape)],
        call_id,
    )[0]


def finish_kernel(
    links,
    numbers,
    normed_ref,
    grad_ref,
    weight_ref,
    gain_ref,
    hidden_ref,
    pick_ref,
    rows_ref,
    out_part_ref,
    out_other_ref,
    small_part_ref,
    small_other_ref,
    middle_ref,
    tokens_ref,
    inverse_ref,
    norm_gain_ref,
    by_y_ref,
    by_z_ref,
    feature_ref,
    stat_ref,
    out_ref,
    out_piece_ref,
    small_piece_ref,
    token_grad_ref,
    late_ref,
    their_half,
    came,
    half,
    spread_y,
    spread_z,
    feature_part,
    stat_part,
    feature_sum,
    passing,
    out_half,
    out_came,
    small_sum,
    small_came,
):
    me = here()
    y, core, row, col = me
    to_sibling, to_lines, to_cols, to_rows, stats, last, spread_out = numbers
    own = y * 4 + col

    def product(start):
        return lax.dot_general(
            normed_ref[:, rows(start, 256)], grad_ref[...], FIRST, preferred_element_type=F32
        )

    for r in range(4):
        their_half[r] = product(r * 512 + (1 - core) * 256).astype(BF)
        links.send(to_sibling[r])
    for block in range(16):
        out_half[block] = (
            out_part_ref[block, rows(core * 64, 64), :].astype(F32)
            + out_other_ref[block].astype(F32)
        ).astype(BF)
        span = slice(block * 24, (block + 1) * 24)
        small_sum[block] = small_part_ref[span, :] + small_other_ref[span, :]
    for number in spread_out:
        links.send(number)
    out_came[own] = out_half[own]
    small_came[own] = small_sum[own]
    inner = jnp.zeros((512, 1), F32)
    for ahead in (2, 1, 3, 0):
        span = rows(lax.rem(row + ahead, 4) * 512, 512)
        part = lax.dot_general(
            grad_ref[...], weight_ref[span, :], LAST, preferred_element_type=F32
        )
        inner = inner + jnp.sum(part * normed_ref[:, span].astype(F32), axis=1, keepdims=True)
        if ahead == 2:
            feature_part[1] = part.astype(BF)
            for number in to_rows[2]:
                links.send(number)
        elif ahead:
            feature_sum[ahead // 2] = part
        else:
            feature_sum[2] = part
    for index, ahead in enumerate((1, 3)):
        links.arrive(to_rows[2][index])
        part = slice(index * 256, (index + 1) * 256)
        feature_sum[index, part, :] += passing[index].astype(F32)
        feature_part[ahead - 1] = feature_sum[index].astype(BF)
        links.send(to_rows[ahead])
    same = (
        lax.broadcasted_iota(jnp.int32, (HEAD, HEAD), 0)
        == lax.broadcasted_iota(jnp.int32, (HEAD, HEAD), 1)
    ).astype(F32)
    for block in range(4):
        stat_part[block : block + 1, :] = jnp.sum(
            same * inner[block * HEAD : (block + 1) * HEAD], axis=0, keepdims=True
        )
    stat_part[4:, :] = gain_ref[:4, :]
    stat_ref[row] = stat_part[...]
    for number in stats + last:
        links.send(number)
    for r in range(4):
        mine = product(r * 512 + core * 256)
        links.arrive(to_sibling[r])
        half[r] = (mine + came[r].astype(F32)).astype(BF)
        for number in to_lines[r] + to_cols[r]:
            links.send(number)
        spread_y[y, r] = half[r, rows(y * 32, 32), :]
        spread_z[col, r] = half[r, 128:, rows(col * 384, 384)]
    out_ref[...] = (
        hidden_ref[...]
        + lax.dot_general(pick_ref[...], rows_ref[...], FIRST, preferred_element_type=F32)
    ).astype(BF)
    for r in range(4):
        for numbers_of, target, spread in (
            (to_lines, by_y_ref, spread_y),
            (to_cols, by_z_ref, spread_z),
        ):
            for number in numbers_of[r]:
                links.arrive(number)
            total = spread[0, r].astype(F32)
            for source in range(1, 4):
                total = total + spread[source, r].astype(F32)
            target[r] = total.astype(BF)
    for number in (to_rows[1], to_rows[3], *stats):
        links.arrive(number)
    row_stats = stat_ref[0] + stat_ref[1] + stat_ref[2] + stat_ref[3]
    late_ref[4:, :] = row_stats[4:, :]
    for block in range(4):
        span = pl.ds(block * HEAD, HEAD)
        mean = jnp.sum(same * row_stats[block : block + 1, :], axis=1, keepdims=True) / WIDTH
        features = feature_sum[2, span, :]
        for part in range(2):
            features = features + feature_ref[part, span, :].astype(F32)
        inverse = inverse_ref[span, :]
        unit = tokens_ref[span, :].astype(F32) * inverse
        token_grad_ref[span, :] = (
            middle_ref[span, :] + inverse * (features * norm_gain_ref[0:1, :] - unit * mean)
        ).astype(BF)
        share = jnp.sum(features * unit, axis=0, keepdims=True)
        for part in range(4):
            lanes = share[:, part * HEAD : (part + 1) * HEAD]
            if block == 0:
                late_ref[part : part + 1, :] = lanes
            else:
                late_ref[part : part + 1, :] += lanes
    for number in spread_out:
        links.arrive(number)
    out_total, small_total = out_came[0].astype(F32), small_came[0]
    for source in range(1, 16):
        out_total = out_total + out_came[source].astype(F32)
        small_total = small_total + small_came[source]
    out_piece_ref[...] = out_total.astype(BF)
    small_piece_ref[...] = small_total


def finish(down_1, down_2, operands):
    take_out = lambda s, me, p: s.at[p[0] * 4 + p[3]]
    put_out = lambda o, me, p: o.at[me[0] * 4 + me[3]]
    whole = lambda s, me, p: s
    own_row = lambda o, me, p: o.at[me[2]]
    sends = []
    to_sibling, to_lines, to_cols = [], [[], [], [], []], [[], [], [], []]
    to_rows, stats, last, spread_out = {}, [], [], []
    for offset in SOURCES:
        for mine, theirs in ((9, 10), (11, 12)):
            spread_out.append(len(sends))
            sends.append((offset, ("scratch", mine), take_out, ("scratch", theirs), put_out))
    for r in range(4):
        view = lambda ref, me, p, r=r: ref.at[r]
        to_sibling.append(len(sends))
        sends.append((SIBLING, ("scratch", 0), view, ("scratch", 1), view))
    for r in range(4):
        for offset in LINES:
            to_lines[r].append(len(sends))
            sends.append(
                (
                    offset,
                    ("scratch", 2),
                    lambda s, me, p, r=r: s.at[r, rows(p[0] * 32, 32)],
                    ("scratch", 3),
                    lambda o, me, p, r=r: o.at[me[0], r],
                )
            )
        for offset in COLS:
            to_cols[r].append(len(sends))
            sends.append(
                (
                    offset,
                    ("scratch", 2),
                    lambda s, me, p, r=r: s.at[r, pl.ds(128, 128), rows(p[3] * 384, 384)],
                    ("scratch", 4),
                    lambda o, me, p, r=r: o.at[me[3], r],
                )
            )
    to_rows[2] = [len(sends), len(sends) + 1]
    for index, offset in enumerate(((0, 0, 1, 0), (0, 0, 3, 0))):
        part = lambda s, me, p, index=index: s.at[1, pl.ds(index * 256, 256)]
        slot = lambda o, me, p, index=index: o.at[index]
        sends.append((offset, ("scratch", 5), part, ("scratch", 8), slot))
    for index, offset in enumerate(((0, 0, 1, 0), (0, 0, 3, 0))):
        to_rows[offset[2]] = len(sends)
        part = lambda s, me, p, ahead=offset[2]: s.at[ahead - 1]
        slot = lambda o, me, p, index=index: o.at[index]
        sends.append((offset, ("scratch", 5), part, ("made", 2), slot))
    for offset in ROWS:
        stats.append(len(sends))
        sends.append((offset, ("scratch", 6), whole, ("made", 3), own_row))
    for way, index in ((ONE_BACK, 0), (OTHER_BACK, 1)):
        last.append(len(sends))
        sends.append((way, index, whole, index, whole))
    return exchange(
        [down_1, down_2],
        [shape(down_1.shape)] * 2,
        sends,
        [],
        5,
        work=lambda links, *refs: finish_kernel(
            links, (to_sibling, to_lines, to_cols, to_rows, stats, last, spread_out), *refs
        ),
        work_in=operands,
        work_out=[
            shape((4, 32, 1536)),
            shape((4, 128, 384)),
            shape((2, 512, 512)),
            shape((4, 8, HEAD), F32),
            shape((512, 512)),
            shape((64, 512)),
            shape((24, HEAD), F32),
            shape((512, 512)),
            shape((8, HEAD), F32),
        ],
        work_scratch=[pltpu.VMEM((4, 256, 1536), BF)] * 3
        + [
            pltpu.VMEM((4, 4, 32, 1536), BF),
            pltpu.VMEM((4, 4, 128, 384), BF),
            pltpu.VMEM((3, 512, 512), BF),
            pltpu.VMEM((8, HEAD), F32),
            pltpu.VMEM((3, 512, 512), F32),
            pltpu.VMEM((2, 256, 512), BF),
            pltpu.VMEM((16, 64, 512), BF),
            pltpu.VMEM((16, 64, 512), BF),
            pltpu.VMEM((16, 24, HEAD), F32),
            pltpu.VMEM((16, 24, HEAD), F32),
        ],
        deferred=range(len(sends)),
    )


def expert_at(place):
    return place[0] * 16 + (place[2] // 2) * 8 + place[3] * 2 + place[2] % 2


def expert_views():
    return (
        lambda s, me, p: s.at[expert_at(p)],
        lambda o, me, p: o.at[me[0] * 4 + me[3], :, rows(me[2] * 512, 512)],
    )


def token_views():
    return (
        lambda s, me, p: s.at[p[0] * 4 + p[3], :, rows(p[2] * 512, 512)],
        lambda o, me, p: o.at[expert_at(me)],
    )


def collect_sums(by_y, by_z, out_piece, small_piece, late, up_grad):
    put_qkv = lambda o, me, p: o.at[me[1], :, me[0]]
    put_out = lambda o, me, p: o.at[me[0], me[1]]
    put_small = lambda o, me, p: o.at[me[0] * 4 + me[3]]
    put_late = lambda o, me, p: o.at[(me[0] * 2 + me[1]) * 4 + me[3]]
    whole = lambda s, me, p: s
    sends = Sends()
    heads = sends.add(
        PLANE,
        lambda s, me, p: s.at[p[2], :, rows(p[3] * 384, 384)],
        ("scratch", 0),
        lambda o, me, p: o.at[me[3], me[2]],
        ("work", 0),
    )
    heads += sends.add(
        SIDES,
        lambda s, me, p: s.at[p[2], rows(p[0] * 32, 32)],
        ("scratch", 1),
        lambda o, me, p: o.at[me[0], me[2]],
        ("work", 1),
    )
    out_sent = sends.add(LINES, whole, 0, put_out, 0)
    sends.add([SIBLING], whole, 0, put_out, 0)
    sends.add(SOURCES, whole, 1, put_small, 1)
    sends.add(OTHERS, whole, 2, put_late, 2)
    sends.add([OTHER_BACK], whole, 3, whole, 3)
    later = len(sends)
    qkv_sent = sends.add(LINES, whole, ("made", 0), put_qkv, ("scratch", 2))
    sends.add([SIBLING], whole, ("made", 0), put_qkv, ("scratch", 2))
    relays = []
    for index in (1, 2, 0):
        origin = lambda me, d=LINES[index][0]: (me[0] + 4 - d) % 4
        view = lambda ref, me, p, origin=origin: ref.at[origin(me), me[1]]
        relays.append((out_sent[index], len(sends)))
        sends.append((SIBLING, 0, view, 0, view, [out_sent[index]]))
    for index in (1, 2, 0):
        origin = lambda me, d=LINES[index][0]: (me[0] + 4 - d) % 4
        view = lambda ref, me, p, origin=origin: ref.at[me[1], :, origin(me)]
        relays.append((qkv_sent[index], len(sends)))
        sends.append((SIBLING, ("made", 0), view, ("made", 0), view, [qkv_sent[index]]))

    def work(links, by_y_ref, by_z_ref, total_ref, spread_z, spread_y, mine):
        me = here()
        spread_z[me[3], me[2]] = by_y_ref[me[2], :, rows(me[3] * 384, 384)]
        spread_y[me[0], me[2]] = by_z_ref[me[2], rows(me[0] * 32, 32), :]
        for number in heads:
            links.arrive(number)
        for part, spread in ((0, spread_z), (1, spread_y)):
            for head in range(4):
                total = spread[0, head].astype(F32)
                for source in range(1, 4):
                    total = total + spread[source, head].astype(F32)
                mine[part, :, head * 384 : (head + 1) * 384] = total.astype(BF)
        for number in range(later, later + 4):
            links.send(number)
        for part in range(2):
            total_ref[me[1], part, me[0]] = mine[part]
        for came, number in relays:
            links.arrive(came)
            links.send(number)

    return exchange(
        [out_piece, small_piece, late, up_grad],
        [
            shape((4, 2, 64, 512)),
            shape((16,) + small_piece.shape, F32),
            shape((32,) + late.shape, F32),
            shape(up_grad.shape),
        ],
        sends,
        [
            (0, lambda s, me: s, 0, lambda o, me: put_out(o, me, me), (64, 512)),
            (1, lambda s, me: s, 1, lambda o, me: put_small(o, me, me), small_piece.shape),
            (2, lambda s, me: s, 2, lambda o, me: put_late(o, me, me), late.shape),
        ],
        12,
        work=work,
        work_in=[by_y, by_z],
        work_out=[shape((2, 2, 4, 32, 1536))],
        work_scratch=[
            pltpu.VMEM((4, 4, 32, 384), BF),
            pltpu.VMEM((4, 4, 32, 384), BF),
            pltpu.VMEM((2, 32, 1536), BF),
        ],
        deferred=range(later, len(sends)),
    )


BLOCK = 256
SCALE = HEAD ** (-0.5)
LAST = (((1,), (1,)), ((), ()))
FIRST = (((0,), (0,)), ((), ()))


def swapped(operand):
    return pltpu.roll(operand, HEAD // 2, 1)


def attend_kernel(
    links,
    numbers,
    qkv_ref,
    position_ref,
    frequency_ref,
    gain_ref,
    query_ref,
    key_ref,
    lse_ref,
    cos_ref,
    sin_ref,
    gathered,
    out_ref,
):
    def prepare(step, carry):
        span = pl.ds(pl.multiple_of(step * BLOCK, BLOCK), BLOCK)
        angles = position_ref[span, :] * frequency_ref[0:1, :]
        cos_ref[span, :] = jnp.cos(angles)
        sin_ref[span, :] = jnp.sin(angles) * frequency_ref[1:2, :]
        for part, target in ((0, query_ref), (1, key_ref)):
            raw = qkv_ref[span, part * HEAD : (part + 1) * HEAD].astype(F32)
            scaled = (
                raw
                * lax.rsqrt(jnp.mean(raw * raw, axis=1, keepdims=True) + EPS)
                * gain_ref[part : part + 1, :]
            )
            target[span, :] = (scaled * cos_ref[span, :] + swapped(scaled) * sin_ref[span, :]).astype(
                BF
            )
        return carry

    lax.fori_loop(0, SEQ // BLOCK, prepare, 0)
    to_cols, beside, passed = numbers
    row, col = lax.axis_index("row"), lax.axis_index("col")
    for ahead in (1, 3, 2, 0):
        first = lax.rem(col + ahead, 4) * 512

        def block(step, carry, first=first):
            span = pl.ds(pl.multiple_of(first + step * BLOCK, BLOCK), BLOCK)
            scores = (
                lax.dot_general(
                    query_ref[span, :], key_ref[...], LAST, preferred_element_type=F32
                )
                * SCALE
            )
            largest = jnp.max(scores, axis=1, keepdims=True)
            weights = jnp.exp(scores - largest)
            total = jnp.sum(weights, axis=1, keepdims=True)
            mixed = jnp.dot(
                weights.astype(BF), qkv_ref[:, 2 * HEAD :], preferred_element_type=F32
            )
            out_ref[span, :] = (mixed / total).astype(BF)
            lse_ref[span, :] = largest + jnp.log(total)
            return carry

        lax.fori_loop(0, 512 // BLOCK, block, 0)
        if ahead:
            links.send(to_cols[ahead])
    gathered[:, rows((row * 4 + col) * HEAD, HEAD)] = out_ref[rows(col * 512, 512), :]
    for ahead in (0, 1, 3, 2):
        if ahead:
            links.arrive(to_cols[ahead])
        for number in beside[ahead]:
            links.send(number)
    for ahead in (0, 1, 3, 2):
        for number, onward in zip(beside[ahead], passed[ahead]):
            links.arrive(number)
            links.send(onward)


def attend(qkv, position, frequency, gains, blocks):
    take, put = expert_views()
    sends = [(offset, 0, take, 0, put) for offset in CUBE]
    to_cols, beside, passed = {}, {}, {}
    for offset in COLS:
        to_cols[offset[3]] = len(sends)
        sends.append(
            (
                offset,
                ("scratch", 0),
                lambda s, me, p: s.at[rows(p[3] * 512, 512)],
                ("made", 5),
                lambda o, me, p: o.at[:, rows((me[2] * 4 + me[3]) * HEAD, HEAD)],
            )
        )
    sides = ((0, 0, 1, 0), (0, 0, 3, 0))
    head_of = lambda row, me, ahead: rows((row * 4 + (me[3] + 4 - ahead) % 4) * HEAD, HEAD)
    for ahead in range(4):
        beside[ahead], passed[ahead] = [], []
        for offset in sides:
            view = lambda ref, me, p, ahead=ahead: ref.at[:, head_of(me[2], me, ahead)]
            beside[ahead].append(len(sends))
            sends.append((offset, ("made", 5), view, ("made", 5), view))
        for index, offset in enumerate(sides):
            view = lambda ref, me, p, ahead=ahead, index=index, d=offset[2]: ref.at[
                pl.ds(index * 256, 256), head_of((me[2] + 4 - d) % 4, me, ahead)
            ]
            passed[ahead].append(len(sends))
            sends.append((offset, ("made", 5), view, ("made", 5), view))
    return exchange(
        [blocks],
        [shape((16, ROOM, WIDTH))],
        sends,
        [(0, lambda s, me: take(s, me, me), 0, lambda o, me: put(o, me, me), (ROOM, 512))],
        6,
        work=lambda links, *refs: attend_kernel(links, (to_cols, beside, passed), *refs),
        work_in=[qkv, position, frequency, gains],
        work_out=[
            shape((SEQ, HEAD)),
            shape((SEQ, HEAD)),
            shape((SEQ, 1), F32),
            shape((SEQ, HEAD), F32),
            shape((SEQ, HEAD), F32),
            shape((512, WIDTH)),
        ],
        work_scratch=[pltpu.VMEM((SEQ, HEAD), BF)],
        deferred=range(len(CUBE), len(sends)),
    )


NEAR_FIRST = (1, 3, 2, 0)


def attend_back_kernel(
    links,
    numbers,
    partial_ref,
    qkv_ref,
    query_ref,
    key_ref,
    lse_ref,
    cos_ref,
    sin_ref,
    gain_ref,
    qkv_grad_ref,
    gain_grad_ref,
    cross,
    mixed,
    out_grads,
    grad_ref,
    query_grad,
    key_grad,
    value_grad,
):
    to_rows, to_cols, back_query, back_to_cols, last = numbers
    row, col = lax.axis_index("row"), lax.axis_index("col")
    for ahead in NEAR_FIRST:
        for number in to_rows[ahead]:
            links.send(number)
    key_grad[...] = jnp.zeros_like(key_grad)
    value_grad[...] = jnp.zeros_like(value_grad)

    def mix(ahead):
        head = lax.rem(col + ahead, 4)
        for number in to_rows[ahead]:
            links.arrive(number)
        total = partial_ref[:, rows((row * 4 + head) * HEAD, HEAD)].astype(F32)
        for part in range(3):
            total = total + cross[part, ahead].astype(F32)
        if ahead:
            mixed[ahead] = total.astype(BF)
            links.send(to_cols[ahead])
        else:
            out_grads[rows(col * 512, 512), :] = total.astype(BF)

    def attend_block(ahead):
        if ahead:
            links.arrive(to_cols[ahead])
        first = lax.rem(col + 4 - ahead, 4) * 512

        def block(step, carry):
            span = pl.ds(pl.multiple_of(first + step * BLOCK, BLOCK), BLOCK)
            query, out_grad = query_ref[span, :], out_grads[span, :]
            scores = (
                lax.dot_general(query, key_ref[...], LAST, preferred_element_type=F32) * SCALE
            )
            soft = jnp.exp(scores - lse_ref[span, :])
            prob_grad = lax.dot_general(
                out_grad, qkv_ref[:, 2 * HEAD :], LAST, preferred_element_type=F32
            )
            inner = jnp.sum(soft * prob_grad, axis=1, keepdims=True)
            score_grad = (soft * (prob_grad - inner)).astype(BF)
            query_grad[span, :] = (
                jnp.dot(score_grad, key_ref[...], preferred_element_type=F32) * SCALE
            )
            key_grad[...] += lax.dot_general(
                score_grad, query, FIRST, preferred_element_type=F32
            )
            value_grad[...] += lax.dot_general(
                soft.astype(BF), out_grad, FIRST, preferred_element_type=F32
            )
            return carry

        lax.fori_loop(0, 512 // BLOCK, block, 0)
        finish_part(first, ((0, query_grad, 1.0),))
        if ahead:
            links.send(back_query[(4 - ahead) % 4])

    def finish_part(first, sources):
        def finish_block(step, carry):
            span = pl.ds(pl.multiple_of(first + step * BLOCK, BLOCK), BLOCK)
            for part, source, factor in sources:
                turned = source[span, :] * factor
                grad = turned * cos_ref[span, :] + swapped(turned * sin_ref[span, :])
                raw = qkv_ref[span, part * HEAD : (part + 1) * HEAD].astype(F32)
                inverse = lax.rsqrt(jnp.mean(raw * raw, axis=1, keepdims=True) + EPS)
                unit = raw * inverse
                gain_grad_ref[part : part + 1, :] += jnp.sum(grad * unit, axis=0, keepdims=True)
                scaled = grad * gain_ref[part : part + 1, :]
                raw_grad = inverse * (
                    scaled - unit * jnp.mean(scaled * unit, axis=1, keepdims=True)
                )
                grad_ref[span, part * HEAD : (part + 1) * HEAD] = raw_grad.astype(BF)
                if part:
                    grad_ref[span, 2 * HEAD :] = value_grad[span, :].astype(BF)
            return carry

        lax.fori_loop(0, 512 // BLOCK, finish_block, 0)

    gain_grad_ref[...] = jnp.zeros_like(gain_grad_ref)
    mix(1)
    mix(3)
    attend_block(1)
    mix(2)
    attend_block(3)
    mix(0)
    for number in last:
        links.send(number)
    attend_block(2)
    attend_block(0)
    for ahead in NEAR_FIRST:
        finish_part(lax.rem(col + ahead, 4) * 512, ((1, key_grad, SCALE),))
        if ahead:
            links.send(back_to_cols[ahead])
    qkv_grad_ref[:, rows(col * 384, 384)] = grad_ref[rows(col * 512, 512), :]


def attend_back(operands, out_part, small_part, up_grad):
    whole = lambda s, me, p: s
    sends = [
        (SIBLING, 0, lambda s, me, p: s.at[:, rows(p[1] * 64, 64)], 0, whole),
        (SIBLING, 1, whole, 1, whole),
    ]
    later = len(sends)
    to_rows, to_cols, back_query, back_to_cols = {}, {}, {}, {}
    for ahead in NEAR_FIRST:
        to_rows[ahead] = []
        for part, offset in enumerate(ROWS):
            to_rows[ahead].append(len(sends))
            head = lambda me, p, ahead=ahead: p[2] * 4 + (me[3] + ahead) % 4
            sends.append(
                (
                    offset,
                    ("work", 0),
                    lambda s, me, p, head=head: s.at[:, rows(head(me, p) * HEAD, HEAD)],
                    ("scratch", 0),
                    lambda o, me, p, part=part, ahead=ahead: o.at[part, ahead],
                )
            )
    for offset in COLS:
        ahead = offset[3]
        to_cols[ahead] = len(sends)
        sends.append(
            (
                offset,
                ("scratch", 1),
                lambda s, me, p, ahead=ahead: s.at[ahead],
                ("scratch", 2),
                lambda o, me, p: o.at[rows(me[3] * 512, 512)],
            )
        )
        for numbers, skip, size in ((back_query, 0, HEAD), (back_to_cols, HEAD, 2 * HEAD)):
            numbers[ahead] = len(sends)
            sends.append(
                (
                    offset,
                    ("scratch", 3),
                    lambda s, me, p, skip=skip, size=size: s.at[
                        rows(p[3] * 512, 512), pl.ds(skip, size)
                    ],
                    ("made", 0),
                    lambda o, me, p, skip=skip, size=size: o.at[
                        :, pl.ds(pl.multiple_of(me[3] * 384 + skip, HEAD), size)
                    ],
                )
            )
    last = [len(sends)]
    sends.append((ONE_BACK, 2, whole, 2, whole))
    return exchange(
        [out_part, small_part, up_grad],
        [
            shape((16, 64, 512)),
            shape(small_part.shape, F32),
            shape(up_grad.shape),
        ],
        sends,
        [],
        13,
        deferred=range(later, len(sends)),
        work=lambda links, *refs: attend_back_kernel(
            links, (to_rows, to_cols, back_query, back_to_cols, last), *refs
        ),
        work_in=operands,
        work_out=[shape((512, 1536)), shape((8, HEAD), F32)],
        work_scratch=[
            pltpu.VMEM((3, 4, 512, HEAD), BF),
            pltpu.VMEM((4, 512, HEAD), BF),
            pltpu.VMEM((SEQ, HEAD), BF),
            pltpu.VMEM((SEQ, 3 * HEAD), BF),
        ]
        + [pltpu.VMEM((SEQ, HEAD), F32)] * 3,
    )


SLOTS = 16 * ROOM
GROUP = 4 * ROOM


def expert_kernel(
    links,
    came,
    returns,
    results,
    shares,
    cot_ref,
    gated_ref,
    up_1,
    up_2,
    down_1,
    down_2,
    x_ref,
    back_ref,
    joined,
    slot_grads,
    acts,
    grads,
    their_x,
    their_slot_grads,
    their_acts,
    their_grads,
    up_ref,
    down_ref,
    out_sum,
    back_sum,
    weight_sem,
    own_sem,
):
    me = here()
    loads = []
    for slot in range(4):
        for part, target in ((1, up_ref), (5, down_ref)):
            loads.append(
                pltpu.make_async_copy(
                    links.ins[part + slot], target.at[slot], weight_sem.at[part + slot - 1]
                )
            )
    take, put = expert_views()
    own_in = pltpu.make_async_copy(take(links.ins[0], me, me), put(x_ref, me, me), own_sem.at[0])
    take, put = token_views()
    own_out = pltpu.make_async_copy(
        take(back_ref, me, me), put(links.outs[0], me, me), own_sem.at[1]
    )
    own_result = pltpu.make_async_copy(
        take(gated_ref, me, me), put(links.outs[1], me, me), own_sem.at[2]
    )
    own_in.start()
    for load in loads:
        load.start()
    line = lax.broadcasted_iota(jnp.int32, (ROOM, HEAD), 0)
    lane = lax.broadcasted_iota(jnp.int32, (ROOM, HEAD), 1)
    same = (line == lane).astype(F32)
    for group in range(4):
        if group == 0:
            own_in.wait()
        for number in came[group]:
            links.arrive(number)
        if group == 0:
            for load in loads:
                load.wait()
        blocks = [
            lax.rem(me[0] + 4 - i, 4) * 4 + lax.rem(me[3] + 4 - (group - i) % 4, 4)
            for i in range(4)
        ]
        span = pl.ds(group * GROUP, GROUP)
        received = jnp.concatenate([x_ref[block].astype(F32) for block in blocks], axis=0)
        cot = jnp.concatenate([cot_ref[block].astype(F32) for block in blocks], axis=0)
        gates = []
        for i in range(4):
            aux = jnp.where(line >= CAP, received[i * ROOM : (i + 1) * ROOM, :HEAD], 0.0)
            gates.append(
                jnp.sum(same * jnp.sum(aux, axis=0, keepdims=True), axis=1, keepdims=True)
            )
        gate = jnp.concatenate(gates, axis=0)
        joined[span, :] = received.astype(BF)
        slot_grads[span, :] = (gate * cot).astype(BF)
        out_sum[...] = jnp.zeros_like(out_sum)
        back_sum[...] = jnp.zeros_like(back_sum)

        def quarter(slot, carry, span=span):
            gate_up = jnp.dot(joined[span, :], up_ref[slot], preferred_element_type=F32)
            gate_part, up_part = gate_up[:, :256], gate_up[:, 256:]
            sigmoid = 1.0 / (1.0 + jnp.exp(-gate_part))
            silu = gate_part * sigmoid
            act = (silu * up_part).astype(BF)
            acts[slot, span, :] = act
            act_grad = lax.dot_general(
                slot_grads[span, :], down_ref[slot], LAST, preferred_element_type=F32
            )
            slope = sigmoid * (1.0 + gate_part * (1.0 - sigmoid))
            grads[slot, span, :256] = (act_grad * up_part * slope).astype(BF)
            grads[slot, span, 256:] = (act_grad * silu).astype(BF)
            out_sum[...] += jnp.dot(act, down_ref[slot], preferred_element_type=F32)
            back_sum[...] += lax.dot_general(
                grads[slot, span, :], up_ref[slot], LAST, preferred_element_type=F32
            )
            return carry

        lax.fori_loop(0, 4, quarter, 0)
        out = out_sum[...]
        gated = gate * out
        gate_grad = jnp.sum(cot * out.astype(BF).astype(F32), axis=1, keepdims=True)
        back = back_sum[...]
        inner = jnp.sum(back * joined[span, :].astype(F32), axis=1, keepdims=True)
        for i, block in enumerate(blocks):
            part = slice(i * ROOM, (i + 1) * ROOM)
            gated_ref[block] = gated[part].astype(BF)
            back_ref[block] = back[part].astype(BF)
            for index, value in enumerate((gate_grad, inner)):
                high, middle, low = pieces(jnp.sum(same * value[part], axis=0, keepdims=True))
                aux = jnp.where(line == CAP, high.astype(F32), 0.0)
                aux = aux + jnp.where(line == CAP + 1, middle.astype(F32), 0.0)
                aux = aux + jnp.where(line == CAP + 2, low.astype(F32), 0.0)
                for r in range(4):
                    start = r * 512 + index * HEAD
                    back_ref[block, :, start : start + HEAD] = (
                        back[part, start : start + HEAD] + aux
                    ).astype(BF)
        for number in returns[group]:
            links.send(number)
        if group == 0:
            own_out.start()
            own_result.start()
        for number in shares[group] + results[group]:
            links.send(number)
    for numbers in shares:
        for number in numbers:
            links.arrive(number)

    def weight_grads(step, carry):
        span = pl.ds(pl.multiple_of(step * 512, 512), 512)
        for slot, up, down in ((0, up_1, down_1), (1, up_2, down_2)):
            up[span, :] = (
                lax.dot_general(joined[:, span], grads[slot], FIRST, preferred_element_type=F32)
                + lax.dot_general(
                    their_x[:, span], their_grads[slot], FIRST, preferred_element_type=F32
                )
            ).astype(BF)
            down[:, span] = (
                lax.dot_general(
                    acts[slot], slot_grads[:, span], FIRST, preferred_element_type=F32
                )
                + lax.dot_general(
                    their_acts[slot],
                    their_slot_grads[:, span],
                    FIRST,
                    preferred_element_type=F32,
                )
            ).astype(BF)
        return carry

    lax.fori_loop(0, 4, weight_grads, 0)
    own_out.wait()
    own_result.wait()


def run_experts(blocks, cot_slots, weights):
    take, put = expert_views()
    came, returns, results, shares = ([[], [], [], []] for _ in range(4))
    sends = []
    for offset in CUBE:
        came[(offset[0] + offset[3]) % 4].append(len(sends))
        sends.append((offset, 0, take, ("scratch", 0), put))
    take, put = token_views()
    for offset in CUBE:
        returns[-(offset[0] + offset[3]) % 4].append(len(sends))
        sends.append((offset, ("scratch", 1), take, 0, put))
    for offset in CUBE:
        results[-(offset[0] + offset[3]) % 4].append(len(sends))
        sends.append((offset, ("made", 0), take, 1, put))
    for place in range(4):
        span = pl.ds(place * GROUP, GROUP)
        for mine, theirs in ((2, 6), (3, 7)):
            view = lambda ref, me, p, span=span: ref.at[span]
            shares[place].append(len(sends))
            sends.append((SIBLING, ("scratch", mine), view, ("scratch", theirs), view))
        for mine, theirs in ((4, 8), (5, 9)):
            shares[place].append(len(sends))
            sends.append(
                (
                    SIBLING,
                    ("scratch", mine),
                    lambda ref, me, p, span=span: ref.at[pl.ds(2, 2), span],
                    ("scratch", theirs),
                    lambda ref, me, p, span=span: ref.at[:, span],
                )
            )
    return exchange(
        [blocks] + weights,
        [shape((EXPERTS, ROOM, 512))] * 2,
        sends,
        [],
        8,
        work=lambda links, *refs: expert_kernel(
            links, came, returns, results, shares, *refs
        ),
        work_in=[cot_slots],
        work_out=[shape((16, ROOM, WIDTH))]
        + [shape((WIDTH, 512))] * 2
        + [shape((256, WIDTH))] * 2,
        work_scratch=[
            pltpu.VMEM((16, ROOM, WIDTH), BF),
            pltpu.VMEM((16, ROOM, WIDTH), BF),
            pltpu.VMEM((SLOTS, WIDTH), BF),
            pltpu.VMEM((SLOTS, WIDTH), BF),
            pltpu.VMEM((4, SLOTS, 256), BF),
            pltpu.VMEM((4, SLOTS, 512), BF),
            pltpu.VMEM((SLOTS, WIDTH), BF),
            pltpu.VMEM((SLOTS, WIDTH), BF),
            pltpu.VMEM((2, SLOTS, 256), BF),
            pltpu.VMEM((2, SLOTS, 512), BF),
            pltpu.VMEM((4, WIDTH, 512), BF),
            pltpu.VMEM((4, 256, WIDTH), BF),
            pltpu.VMEM((GROUP, WIDTH), F32),
            pltpu.VMEM((GROUP, WIDTH), F32),
            pltpu.SemaphoreType.DMA((8,)),
            pltpu.SemaphoreType.DMA((3,)),
        ],
        deferred=range(len(CUBE), len(sends)),
    )


def pack_kernel(up_1, up_2, down_1, down_2, qkv, out, up_ref, down_ref, qkv_ref, out_ref):
    upper = lax.axis_index("row") // 2
    for which, up, down in ((upper, up_1, down_1), (1 - upper, up_2, down_2)):
        value = up[...].astype(F32)
        up_ref[which, :, 0, :] = value[:, :256]
        up_ref[which, :, 1, :] = value[:, 256:]
        down_ref[which] = down[...].astype(F32)
    out_ref[...] = out[...].astype(F32)
    for head in range(4):
        qkv_ref[:, head, :] = qkv[:, head * 384 : (head + 1) * 384].astype(F32)


def pack_grads(up_1, up_2, down_1, down_2, qkv, out):
    steps = 8
    up, down = (WIDTH // steps, 512), (256 // steps, WIDTH)
    return pl.pallas_call(
        pack_kernel,
        grid=(steps,),
        out_shape=[
            shape((2, WIDTH, 2, 256), F32),
            shape((2, 256, WIDTH), F32),
            shape((512, 4, 384), F32),
            shape((512, 512), F32),
        ],
        in_specs=[pl.BlockSpec(up, lambda i: (i, 0))] * 2
        + [pl.BlockSpec(down, lambda i: (i, 0))] * 2
        + [pl.BlockSpec((512 // steps, 1536), lambda i: (i, 0))]
        + [pl.BlockSpec((512 // steps, 512), lambda i: (i, 0))],
        out_specs=[
            pl.BlockSpec((2, up[0], 2, 256), lambda i: (0, i, 0, 0)),
            pl.BlockSpec((2,) + down, lambda i: (0, i, 0)),
            pl.BlockSpec((512 // steps, 4, 384), lambda i: (i, 0, 0)),
            pl.BlockSpec((512 // steps, 512), lambda i: (i, 0)),
        ],
    )(up_1, up_2, down_1, down_2, qkv, out)


def dot(left, right):
    return jnp.dot(left, right, preferred_element_type=F32)


def dot_last(left, right):
    return lax.dot_general(left, right, LAST, preferred_element_type=F32)


def dot_first(left, right):
    return lax.dot_general(left, right, FIRST, preferred_element_type=F32)


def pieces(value):
    high = value.astype(BF)
    rest = value - high.astype(F32)
    middle = rest.astype(BF)
    low = (rest - middle.astype(F32)).astype(BF)
    return [high, middle, low]


def aux_rows(value):
    held = jnp.stack(pieces(value), axis=1)
    return jnp.pad(held, ((0, 0), (CAP, ROOM - CAP - 3), (0, 512 - ROOM)))


def aux_value(blocks, index):
    part = blocks[:, CAP : CAP + 3, index * HEAD : index * HEAD + ROOM]
    return jnp.sum(part.astype(F32), axis=1)


FIRST_HOP = [
    ((2 * y + k) * 4 + x, (2 * y + 1 - x % 2) * 4 + 2 * k + x // 2)
    for y in range(4)
    for k in range(2)
    for x in range(4)
]
SECOND_HOP = [
    ((2 * y + k) * 4 + x, (2 * y + x % 2) * 4 + 2 * k + 1 - x // 2)
    for y in range(4)
    for k in range(2)
    for x in range(4)
]
PAIR = [(d, d ^ 1) for d in range(8)]


def hop(operand, pairs):
    return lax.ppermute(operand, ("dp", "row"), pairs)


def after(*operands):
    return lax.optimization_barrier(operands)


def shards(
    tokens,
    positions,
    routes,
    attention_norm_gain,
    experts_norm_gain,
    w_qkv,
    q_gain,
    k_gain,
    w_out,
    w_router,
    w_gate_up,
    w_down,
    cotangent,
):
    core = lax.axis_index("dp") % 2
    experts = jnp.arange(EXPERTS, dtype=jnp.int32)
    named = jnp.any(routes[:, :, None] == experts[None, None, :], axis=1)
    place = jnp.arange(512, dtype=jnp.int32)
    earlier = (place[None, :] < place[:, None]).astype(BF)
    rank = dot(earlier, named.astype(BF))
    rank = jnp.where(named, rank, -1.0).T
    (
        token_rows,
        w_group,
        position_rows,
        gain_rows,
        w_all,
        down_1,
        down_2,
        send_up_1,
        send_up_2,
        send_cot,
    ) = gather_inputs(
        tokens,
        w_qkv,
        w_out,
        w_down,
        positions.reshape(4, HEAD),
        attention_norm_gain.reshape(4, HEAD),
        [w_gate_up, rank, cotangent],
    )
    w_all = w_all.reshape(WIDTH, 512)
    w_group = w_group.reshape(WIDTH, 1536)
    gain_full = gain_rows.reshape(WIDTH)

    gate_up_1, gate_up_2 = hop(send_up_1, FIRST_HOP), hop(send_up_2, SECOND_HOP)
    sibling = lambda w: lax.ppermute(w, "dp", PAIR)
    frequency = THETA ** (-2.0 * jnp.arange(HEAD // 2, dtype=F32) / HEAD)
    half_signs = jnp.where(jnp.arange(HEAD) < HEAD // 2, -1.0, 1.0).astype(F32)
    frequency = jnp.concatenate(
        [jnp.concatenate([frequency] * 2)[None], half_signs[None], jnp.zeros((6, HEAD), F32)]
    )
    position_column = position_rows.reshape(SEQ, 1).astype(F32)
    gains = jnp.concatenate([q_gain[None], k_gain[None], jnp.zeros((6, HEAD), F32)], axis=0)

    pick = (rank[:, None, :] == jnp.arange(ROOM, dtype=F32)[None, :, None]).astype(BF)
    flat_pick = pick.reshape(EXPERTS * ROOM, 512)

    token_full = token_rows.astype(F32)
    inverse_attention = lax.rsqrt(jnp.mean(token_full * token_full, axis=1) + EPS)
    normed_exact = token_full * inverse_attention[:, None] * gain_full[None, :]
    normed = normed_exact.astype(BF)
    qkv = to_heads(dot(normed, w_group).astype(BF))
    cot_slots, query, key, lse, cosine, sine, attended_rows = attend(
        qkv, position_column, frequency, gains, send_cot
    )
    attended_rows, gate_up_1, gate_up_2, down_1, down_2 = after(
        attended_rows, gate_up_1, gate_up_2, down_1, down_2
    )
    up_ws = [gate_up_1, gate_up_2, sibling(gate_up_1), sibling(gate_up_2)]
    down_ws = [down_1, down_2, sibling(down_1), sibling(down_2)]

    token_float = tokens.astype(F32)
    hidden = token_float + dot(attended_rows, w_all)
    scaled_hidden = hidden * experts_norm_gain
    partial_stats = jnp.concatenate(
        [
            lax.dot_general(
                w_router.astype(F32),
                scaled_hidden,
                (((0,), (1,)), ((), ())),
                precision=EXACT,
                preferred_element_type=F32,
            ),
            jnp.sum(hidden * hidden, axis=1)[None],
            jnp.zeros((7, 512), F32),
        ],
        axis=0,
    )
    stats = jnp.sum(row_stack(partial_stats, 7), axis=0)
    inverse_experts = lax.rsqrt(stats[EXPERTS] / WIDTH + EPS)
    logits = stats[:EXPERTS] * inverse_experts[None, :]
    unit_experts = hidden * inverse_experts[:, None]
    experts_input = (unit_experts * experts_norm_gain).astype(BF)
    named_t = rank >= 0
    largest = jnp.max(jnp.where(named_t, logits, -jnp.inf), axis=0, keepdims=True)
    shifted = jnp.where(named_t, jnp.exp(jnp.where(named_t, logits - largest, 0.0)), 0.0)
    gates = shifted / jnp.sum(shifted, axis=0, keepdims=True)
    slot_gates = jnp.sum(pick.astype(F32) * gates[:, None, :], axis=2)
    send_rows = dot(flat_pick, experts_input).astype(BF).reshape(EXPERTS, ROOM, 512)
    back_rows, out_rows, _, up_1, up_2, down_1, down_2 = run_experts(
        send_rows + aux_rows(slot_gates), cot_slots, up_ws + down_ws
    )
    gate_grad = jnp.sum(pick.astype(F32) * aux_value(back_rows, 0)[:, :, None], axis=1)
    inner = jnp.sum(pick.astype(F32) * aux_value(back_rows, 1)[:, :, None], axis=(0, 1))
    logit_grad = gates * (gate_grad - jnp.sum(gates * gate_grad, axis=0, keepdims=True))
    experts_input_grad = dot_first(
        flat_pick, back_rows.reshape(EXPERTS * ROOM, 512)
    ) + lax.dot_general(
        logit_grad,
        w_router.astype(F32),
        (((0,), (1,)), ((), ())),
        precision=EXACT,
        preferred_element_type=F32,
    )
    mean_experts = (inner + jnp.sum(logit_grad * logits, axis=0)) / WIDTH
    cot_float = cotangent.astype(F32)
    middle_grad = cot_float + inverse_experts[:, None] * (
        experts_input_grad * experts_norm_gain - unit_experts * mean_experts[:, None]
    )
    router_part = lax.dot_general(
        logit_grad,
        experts_input.astype(F32),
        (((1,), (0,)), ((), ())),
        precision=EXACT,
        preferred_element_type=F32,
    )
    experts_gain_part = jnp.sum(experts_input_grad * unit_experts, axis=0)
    attended_grad = middle_grad.astype(BF)
    out_part = dot_first(attended_rows, attended_grad).astype(BF).reshape(16, HEAD, 512)
    small_part = jnp.concatenate(
        [
            router_part.reshape(256, HEAD),
            experts_gain_part.reshape(4, HEAD),
            jnp.zeros((124, HEAD), F32),
        ],
        axis=0,
    )
    out_other, small_other, up_1, qkv_grad, head_gain_part = attend_back(
        [dot_last(attended_grad, w_all).astype(BF), qkv, query, key, lse, cosine, sine, gains],
        out_part,
        small_part,
        up_1,
    )
    down_1, down_2, by_y, by_z, _, _, output, out_piece, small_piece, token_grad, late = finish(
        down_1,
        down_2,
        [
            normed,
            qkv_grad,
            w_group,
            head_gain_part,
            hidden,
            flat_pick,
            out_rows.reshape(EXPERTS * ROOM, 512),
            out_part,
            out_other,
            small_part,
            small_other,
            middle_grad,
            tokens,
            inverse_attention[:, None],
            jnp.broadcast_to(attention_norm_gain[None], (8, 512)),
        ],
    )
    out_total, small_total, late, up_2, qkv_total = collect_sums(
        by_y, by_z, out_piece, small_piece, late, up_2
    )
    small_total = small_total.reshape(384, HEAD)
    late = jnp.sum(late, axis=0)
    grad_gate_up, grad_down, grad_qkv, grad_out = pack_grads(
        up_1,
        up_2,
        down_1,
        down_2,
        qkv_total.reshape(512, 1536),
        out_total.reshape(512, 512),
    )
    return (
        output,
        token_grad,
        late[:4].reshape(512),
        small_total[256:260].reshape(512),
        grad_qkv,
        late[4],
        late[5],
        grad_out,
        small_total[:256].reshape(EXPERTS, 512).T,
        grad_gate_up,
        grad_down,
    )


def solution(mesh):
    tokens_like = P(("dp", "col"), "row")
    up_like = P(("dp", "col"), None, None, "row")
    down_like = P(("dp", "col"), "row", None)
    return jax.shard_map(
        shards,
        mesh=mesh,
        in_specs=(
            tokens_like,
            P("dp", "row"),
            P(("dp", "col"), None),
            P("row"),
            P("row"),
            P("row", "col", None),
            P(),
            P(),
            P("col", "row"),
            P("row", None),
            up_like,
            down_like,
            tokens_like,
        ),
        out_specs=(
            tokens_like,
            tokens_like,
            P("row"),
            P("row"),
            P("row", "col", None),
            P(),
            P(),
            P("col", "row"),
            P("row", None),
            up_like,
            down_like,
        ),
        check_vma=False,
    )
```

```python
import jax
import jax.numpy as jnp
from jax import lax
from jax.experimental import pallas as pl
from jax.experimental.pallas import tpu as pltpu
from jax.sharding import PartitionSpec as P

WIDTH = 2048
HEAD = 128
EXPERTS = 64
CAP = 36
ROOM = 40
SEQ = 2048
EPS = 1e-06
THETA = 10000.0
EXACT = lax.Precision.HIGHEST
MESH = pl.DeviceIdType.MESH
SIZES = (4, 2, 4, 4)
BF = jnp.bfloat16
F32 = jnp.float32
ROWS = [(0, 0, d, 0) for d in (2, 1, 3)]
COLS = [(0, 0, 0, d) for d in (2, 1, 3)]
SIBLING = (0, 1, 0, 0)
PLANE = [(0, 0, i, (i + s) % 4) for s in range(4) for i in range(4) if (i, s) != (0, 0)]
CUBE = [
    (i, 0, (i + s) % 4, (g - i) % 4)
    for g in range(4)
    for s in range(4)
    for i in range(4)
    if (g, s, i) != (0, 0, 0)
]
SOURCES = [(i, 0, 0, (i + s) % 4) for s in range(4) for i in range(4) if (i, s) != (0, 0)]
SIDES = [(i, 0, (i + s) % 4, 0) for s in range(4) for i in range(4) if (i, s) != (0, 0)]
LINES = [(d, 0, 0, 0) for d in (2, 1, 3)]
OTHERS = [
    (a, k, 0, d) for a in range(4) for k in range(2) for d in range(4) if (a, k, d) != (0, 0, 0)
]


def shape(dims, dtype=BF):
    return jax.ShapeDtypeStruct(dims, dtype)


def here():
    group = lax.axis_index("dp")
    return (group // 2, group % 2, lax.axis_index("row"), lax.axis_index("col"))


class Hop:
    def __init__(self, to, origin):
        self.to, self.origin = to, origin


ONE_WAY = Hop(
    lambda p: (p[0], 1 - p[2] % 2, 2 * p[1] + p[2] // 2, p[3]),
    lambda p: (p[0], p[2] // 2, 2 * (p[2] % 2) + 1 - p[1], p[3]),
)
OTHER_WAY = Hop(
    lambda p: (p[0], p[2] % 2, 2 * p[1] + 1 - p[2] // 2, p[3]),
    lambda p: (p[0], p[2] // 2, 2 * (1 - p[2] % 2) + p[1], p[3]),
)


ONE_BACK, OTHER_BACK = Hop(ONE_WAY.origin, ONE_WAY.to), Hop(OTHER_WAY.origin, OTHER_WAY.to)


class Links:
    def __init__(self, send, arrive, ins, outs):
        self.send, self.arrive, self.ins, self.outs = send, arrive, ins, outs


def moved(place, offset):
    if isinstance(offset, Hop):
        return offset.to(place)
    return tuple((p + o) % n for p, o, n in zip(place, offset, SIZES))


def device(place):
    return (place[0] * 2 + place[1], place[2], place[3])


def exchange(
    inputs,
    outputs,
    sends,
    kept,
    call_id,
    micros=30,
    work=None,
    work_in=(),
    work_out=(),
    work_scratch=(),
    stages=(),
    deferred=(),
):
    offsets = sorted({s[0] for s in sends if not isinstance(s[0], Hop)})
    hops = {id(s[0]): s[0] for s in sends if isinstance(s[0], Hop)}.values()
    n_in, n_out, n_send = len(inputs), len(outputs), len(sends)
    m_in, m_out = len(work_in), len(work_out)

    def kernel(*refs):
        ins, refs = refs[:n_in], refs[n_in:]
        worked, refs = refs[:m_in], refs[m_in:]
        outs, refs = refs[:n_out], refs[n_out:]
        made, refs = refs[:m_out], refs[m_out:]
        send_sem, recv_sem, kept_sem = refs[:3]
        staged, refs = refs[3 : 3 + len(kept)], refs[3 + len(kept) :]
        special = {"work": worked, "made": made, "scratch": refs}
        me = here()
        barrier = pltpu.get_barrier_semaphore()
        greeted = [moved(me, offset) for offset in offsets]
        for way in hops:
            greeted += [way.to(me), way.origin(me)]
        for peer in greeted:
            pl.semaphore_signal(barrier, inc=1, device_id=device(peer), device_id_type=MESH)
        local = []
        for index, (i, take, o, put, _) in enumerate(kept):
            source, target = take(ins[i], me), put(outs[o], me)
            local.append(
                (
                    pltpu.make_async_copy(source, staged[index], kept_sem.at[index, 0]),
                    pltpu.make_async_copy(staged[index], target, kept_sem.at[index, 1]),
                )
            )
            local[-1][0].start()
        pl.semaphore_wait(barrier, len(greeted))
        copies, arrived = {}, set()

        def arrive(index):
            if index not in arrived:
                arrived.add(index)
                copies[index].wait_recv()

        def named(group, index):
            return special[index[0]][index[1]] if isinstance(index, tuple) else group[index]

        def start(index):
            offset, i, take, o, put = sends[index][:5]
            needs = sends[index][5] if len(sends[index]) > 5 else None
            for need in needs or ():
                if need >= 0:
                    arrive(need)
                elif need not in arrived:
                    arrived.add(need)
                    local[-need - 1][1].wait()
            peer = moved(me, offset)
            copies[index] = pltpu.make_async_remote_copy(
                src_ref=take(named(ins if needs is None else outs, i), me, peer),
                dst_ref=put(named(outs, o), me, peer),
                send_sem=send_sem.at[index],
                recv_sem=recv_sem.at[index],
                device_id=device(peer),
                device_id_type=MESH,
            )
            copies[index].start()

        links = Links(start, arrive, ins, outs)
        parts = work(links, *worked, *made, *refs) if stages else ()
        first = [i for i in range(n_send) if len(sends[i]) < 6 and i not in deferred]
        for index in first:
            start(index)
        for load, store in local:
            load.wait()
            store.start()
        for index in range(n_send):
            if index in first or index in deferred:
                continue
            for part, at in zip(parts, stages):
                if at == index:
                    part()
            start(index)
        if work is not None and not stages:
            work(links, *worked, *made, *refs)
        for index in range(n_send):
            arrive(index)
        for copy in copies.values():
            copy.wait_send()
        for index, copy in enumerate(local):
            if -index - 1 not in arrived:
                copy[1].wait()

    return pl.pallas_call(
        kernel,
        out_shape=list(outputs) + list(work_out),
        in_specs=[pl.BlockSpec(memory_space=pl.ANY)] * n_in
        + [pl.BlockSpec(memory_space=pltpu.VMEM)] * m_in,
        out_specs=[pl.BlockSpec(memory_space=pl.ANY)] * n_out
        + [pl.BlockSpec(memory_space=pltpu.VMEM)] * m_out,
        scratch_shapes=[
            pltpu.SemaphoreType.DMA((n_send,)),
            pltpu.SemaphoreType.DMA((n_send,)),
            pltpu.SemaphoreType.DMA((max(1, len(kept)), 2)),
            *[pltpu.VMEM(k[4], inputs[k[0]].dtype) for k in kept],
            *work_scratch,
        ],
        compiler_params=pltpu.CompilerParams(
            collective_id=call_id,
            has_side_effects=True,
            vmem_limit_bytes=(8 if work is None else 60) * 2**20,
        ),
        cost_estimate=pl.CostEstimate(
            flops=0, bytes_accessed=micros * 3_500_000, transcendentals=0
        ),
    )(*inputs, *work_in)


def rows(start, size):
    return pl.ds(pl.multiple_of(start, size), size)


def eighth(size):
    me = here()
    return rows((me[1] * 4 + me[0]) * size, size)


def half(size):
    return rows(here()[1] * size, size)


class Sends(list):
    def add(self, group, take, o, put=None, i=None, needs=None):
        first = len(self)
        for offset in group:
            if needs is None:
                self.append((offset, i, take, o, put))
            else:
                view = lambda ref, me, p: take(ref, me)
                self.append((offset, o, view, o, view, needs))
        return list(range(first, len(self)))


def early_kernel(links, up_ref, rank_ref, cot_ref, up_1, up_2, rows_ref):
    upper = lax.axis_index("row") // 2

    def unpack(which, target, first):
        def part():
            for step in range(4):
                span = pl.ds(first + step * 64, 64)
                target[span, :256] = up_ref[which, span, 0, :]
                target[span, 256:] = up_ref[which, span, 1, :]

        return part

    def pick(step):
        def part():
            ranks = rank_ref[step * 8 : step * 8 + 8, :]
            slots = lax.broadcasted_iota(jnp.int32, (8, ROOM, 512), 1).astype(F32)
            chosen = (ranks[:, None, :] == slots).astype(F32).reshape(8 * ROOM, 512)
            rows_of = jnp.dot(chosen.astype(BF), cot_ref[...], preferred_element_type=F32)
            rows_ref[pl.ds(step * 8, 8)] = rows_of.reshape(8, ROOM, 512).astype(BF)

        return part

    parts = [unpack(upper, up_1, step * 256) for step in range(8)]
    parts += [unpack(1 - upper, up_2, step * 256) for step in range(8)]
    return parts + [pick(step) for step in range(8)]


def gather_inputs(tokens, w_qkv, w_out, w_down, small_int, small_float, early):
    outputs = [
        shape((512, WIDTH)),
        shape((4, 512, 1536)),
        shape((4, 4, HEAD), jnp.int32),
        shape((4, 4, HEAD), F32),
        shape((4, 4, HEAD, 512)),
        shape((256, WIDTH)),
        shape((256, WIDTH)),
    ]
    sends = Sends()
    own_cols = lambda me: rows(me[3] * 384, 384)
    low, high = pl.ds(0, 2), pl.ds(2, 2)
    first = sends.add(
        ROWS,
        lambda s, me, p: s.at[eighth(64), rows(p[2] * 384, 384)],
        1,
        lambda o, me, p: o.at[me[2], eighth(64), own_cols(me)],
        1,
    )
    both = [(0, 0, 1, 0), (0, 0, 3, 0)]
    beside = sends.add(
        both, lambda s, me, p: s, 0, lambda o, me, p: o.at[:, rows(me[2] * 512, 512)], 0
    )
    sends.add(ROWS, lambda s, me, p: s, 2, lambda o, me, p: o.at[me[2]], 2)
    sends.add(ROWS, lambda s, me, p: s, 3, lambda o, me, p: o.at[me[2]], 3)
    sends.append((ONE_WAY, 5, lambda s, me, p: s.at[me[2] // 2], 5, lambda o, me, p: o))
    sends.append((OTHER_WAY, 5, lambda s, me, p: s.at[1 - me[2] // 2], 6, lambda o, me, p: o))
    out_z = sends.add(COLS, lambda o, me: o.at[low, me[3], eighth(16)], 4, needs=[-2])
    out_y = sends.add(LINES, lambda o, me: o.at[high, me[3], eighth(16)], 4, needs=[-2])
    stages = [len(sends)] * 3
    by_z = sends.add(
        COLS, lambda o, me: o.at[low, eighth(64), own_cols(me)], 1, needs=[-1] + first
    )
    by_y = sends.add(LINES, lambda o, me: o.at[high, eighth(64), own_cols(me)], 1, needs=first)
    sends.add(LINES, lambda o, me: o.at[low, eighth(64), own_cols(me)], 1, needs=first)
    sends.add(COLS, lambda o, me: o.at[high, eighth(64), own_cols(me)], 1, needs=first)
    last_z, last_y = {0: [len(sends) - 6 + i for i in range(3)]}, {0: list(range(len(sends) - 3, len(sends)))}
    for d in (1, 3, 2):
        came = by_z[[offset[3] for offset in COLS].index(d)]
        cols = lambda me, d=d: rows((me[3] + 4 - d) % 4 * 384, 384)
        stages += [len(sends)] * (3 if d == 1 else 1)
        last_z[d] = sends.add(
            LINES,
            lambda o, me, cols=cols: o.at[low, eighth(64), cols(me)],
            1,
            needs=[came],
        )
        came = by_y[[offset[0] for offset in LINES].index(d)]
        span = lambda me, d=d: rows((me[1] * 4 + (me[0] + 4 - d) % 4) * 64, 64)
        stages.append(len(sends))
        last_y[d] = sends.add(
            COLS,
            lambda o, me, span=span: o.at[high, span(me), own_cols(me)],
            1,
            needs=[came],
        )
    for index, offset in enumerate(both):
        passed = lambda o, me, index=index, d=offset[2]: o.at[
            pl.ds(index * 256, 256), rows((me[2] + 4 - d) % 4 * 512, 512)
        ]
        sends.add([offset], passed, 0, needs=[beside[index]])
    stages.append(len(sends))
    out_zy = sends.add(LINES, lambda o, me: o.at[low, :, eighth(16)], 4, needs=out_z)
    stages.append(len(sends))
    out_yz = sends.add(COLS, lambda o, me: o.at[high, me[3], half(64)], 4, needs=out_y)
    stages.append(len(sends))
    pair = [SIBLING]
    sends.add(pair, lambda o, me: o.at[low, eighth(64)], 1, needs=by_z)
    sends.add(pair, lambda o, me: o.at[high, half(256), own_cols(me)], 1, needs=by_y)
    for d in (1, 3, 2):
        line = [offset[0] for offset in LINES].index(d)
        stages += [len(sends)] * (4 if d == 1 else 2)
        span = lambda me, d=d: rows((me[1] * 4 + (me[0] + 4 - d) % 4) * 64, 64)
        sends.add(
            pair,
            lambda o, me, span=span: o.at[low, span(me)],
            1,
            needs=[numbers[line] for numbers in last_z.values()],
        )
        col = [offset[3] for offset in COLS].index(d)
        stages += [len(sends)] * (24 - len(stages) if d == 2 else 1)
        cols = lambda me, d=d: rows((me[3] + 4 - d) % 4 * 384, 384)
        sends.add(
            pair,
            lambda o, me, cols=cols: o.at[high, half(256), cols(me)],
            1,
            needs=[numbers[col] for numbers in last_y.values()],
        )
    sends.add(pair, lambda o, me: o.at[low, :, half(64)], 4, needs=out_zy)
    sends.add(pair, lambda o, me: o.at[high, :, half(64)], 4, needs=out_yz)
    kept = [
        (
            1,
            lambda s, me: s.at[eighth(64), rows(me[2] * 384, 384)],
            1,
            lambda o, me: o.at[me[2], eighth(64), own_cols(me)],
            (64, 384),
        ),
        (
            4,
            lambda s, me: s.at[:, eighth(16)],
            4,
            lambda o, me: o.at[:, me[3], eighth(16)],
            (4, 16, 512),
        ),
        (0, lambda s, me: s, 0, lambda o, me: o.at[:, rows(me[2] * 512, 512)], (512, 512)),
        (2, lambda s, me: s, 2, lambda o, me: o.at[me[2]], (4, HEAD)),
        (3, lambda s, me: s, 3, lambda o, me: o.at[me[2]], (4, HEAD)),
    ]
    return exchange(
        [
            tokens,
            w_qkv.reshape(512, 1536),
            small_int,
            small_float,
            w_out.reshape(4, HEAD, 512),
            w_down,
        ],
        outputs,
        sends,
        kept,
        0,
        work=early_kernel,
        work_in=early,
        work_out=[
            shape((WIDTH, 512)),
            shape((WIDTH, 512)),
            shape((EXPERTS, ROOM, 512)),
        ],
        stages=stages,
    )


def to_heads(qkv):
    take = lambda s, me, p: s.at[:, rows(p[3] * 384, 384)]
    put = lambda o, me, p: o.at[rows(me[3] * 512, 512)]
    return exchange(
        [qkv],
        [shape((SEQ, 384))],
        [(offset, 0, take, 0, put) for offset in COLS],
        [(0, lambda s, me: take(s, me, me), 0, lambda o, me: put(o, me, me), (512, 384))],
        1,
    )[0]


def row_stack(operand, call_id):
    take = lambda s, me, p: s
    put = lambda o, me, p: o.at[me[2]]
    return exchange(
        [operand],
        [shape((4,) + operand.shape, operand.dtype)],
        [(offset, 0, take, 0, put) for offset in ROWS],
        [(0, lambda s, me: s, 0, lambda o, me: put(o, me, me), operand.shape)],
        call_id,
    )[0]


def finish_kernel(
    links,
    numbers,
    normed_ref,
    grad_ref,
    weight_ref,
    gain_ref,
    hidden_ref,
    pick_ref,
    rows_ref,
    out_part_ref,
    out_other_ref,
    small_part_ref,
    small_other_ref,
    middle_ref,
    tokens_ref,
    inverse_ref,
    norm_gain_ref,
    by_y_ref,
    by_z_ref,
    feature_ref,
    stat_ref,
    out_ref,
    out_piece_ref,
    small_piece_ref,
    token_grad_ref,
    late_ref,
    their_half,
    came,
    half,
    spread_y,
    spread_z,
    feature_part,
    stat_part,
    feature_sum,
    passing,
    out_half,
    out_came,
    small_sum,
    small_came,
):
    me = here()
    y, core, row, col = me
    to_sibling, to_lines, to_cols, to_rows, stats, last, spread_out = numbers
    own = y * 4 + col

    def product(start):
        return lax.dot_general(
            normed_ref[:, rows(start, 256)], grad_ref[...], FIRST, preferred_element_type=F32
        )

    for r in range(4):
        their_half[r] = product(r * 512 + (1 - core) * 256).astype(BF)
        links.send(to_sibling[r])
    for block in range(16):
        out_half[block] = (
            out_part_ref[block, rows(core * 64, 64), :].astype(F32)
            + out_other_ref[block].astype(F32)
        ).astype(BF)
        span = slice(block * 24, (block + 1) * 24)
        small_sum[block] = small_part_ref[span, :] + small_other_ref[span, :]
    for number in spread_out:
        links.send(number)
    out_came[own] = out_half[own]
    small_came[own] = small_sum[own]
    inner = jnp.zeros((512, 1), F32)
    for ahead in (2, 1, 3, 0):
        span = rows(lax.rem(row + ahead, 4) * 512, 512)
        part = lax.dot_general(
            grad_ref[...], weight_ref[span, :], LAST, preferred_element_type=F32
        )
        inner = inner + jnp.sum(part * normed_ref[:, span].astype(F32), axis=1, keepdims=True)
        if ahead == 2:
            feature_part[1] = part.astype(BF)
            for number in to_rows[2]:
                links.send(number)
        elif ahead:
            feature_sum[ahead // 2] = part
        else:
            feature_sum[2] = part
    for index, ahead in enumerate((1, 3)):
        links.arrive(to_rows[2][index])
        part = slice(index * 256, (index + 1) * 256)
        feature_sum[index, part, :] += passing[index].astype(F32)
        feature_part[ahead - 1] = feature_sum[index].astype(BF)
        links.send(to_rows[ahead])
    same = (
        lax.broadcasted_iota(jnp.int32, (HEAD, HEAD), 0)
        == lax.broadcasted_iota(jnp.int32, (HEAD, HEAD), 1)
    ).astype(F32)
    for block in range(4):
        stat_part[block : block + 1, :] = jnp.sum(
            same * inner[block * HEAD : (block + 1) * HEAD], axis=0, keepdims=True
        )
    stat_part[4:, :] = gain_ref[:4, :]
    stat_ref[row] = stat_part[...]
    for number in stats + last:
        links.send(number)
    for r in range(4):
        mine = product(r * 512 + core * 256)
        links.arrive(to_sibling[r])
        half[r] = (mine + came[r].astype(F32)).astype(BF)
        for number in to_lines[r] + to_cols[r]:
            links.send(number)
        spread_y[y, r] = half[r, rows(y * 32, 32), :]
        spread_z[col, r] = half[r, 128:, rows(col * 384, 384)]
    out_ref[...] = (
        hidden_ref[...]
        + lax.dot_general(pick_ref[...], rows_ref[...], FIRST, preferred_element_type=F32)
    ).astype(BF)
    for r in range(4):
        for numbers_of, target, spread in (
            (to_lines, by_y_ref, spread_y),
            (to_cols, by_z_ref, spread_z),
        ):
            for number in numbers_of[r]:
                links.arrive(number)
            total = spread[0, r].astype(F32)
            for source in range(1, 4):
                total = total + spread[source, r].astype(F32)
            target[r] = total.astype(BF)
    for number in (to_rows[1], to_rows[3], *stats):
        links.arrive(number)
    row_stats = stat_ref[0] + stat_ref[1] + stat_ref[2] + stat_ref[3]
    late_ref[4:, :] = row_stats[4:, :]
    for block in range(4):
        span = pl.ds(block * HEAD, HEAD)
        mean = jnp.sum(same * row_stats[block : block + 1, :], axis=1, keepdims=True) / WIDTH
        features = feature_sum[2, span, :]
        for part in range(2):
            features = features + feature_ref[part, span, :].astype(F32)
        inverse = inverse_ref[span, :]
        unit = tokens_ref[span, :].astype(F32) * inverse
        token_grad_ref[span, :] = (
            middle_ref[span, :] + inverse * (features * norm_gain_ref[0:1, :] - unit * mean)
        ).astype(BF)
        share = jnp.sum(features * unit, axis=0, keepdims=True)
        for part in range(4):
            lanes = share[:, part * HEAD : (part + 1) * HEAD]
            if block == 0:
                late_ref[part : part + 1, :] = lanes
            else:
                late_ref[part : part + 1, :] += lanes
    for number in spread_out:
        links.arrive(number)
    out_total, small_total = out_came[0].astype(F32), small_came[0]
    for source in range(1, 16):
        out_total = out_total + out_came[source].astype(F32)
        small_total = small_total + small_came[source]
    out_piece_ref[...] = out_total.astype(BF)
    small_piece_ref[...] = small_total


def finish(down_1, down_2, operands):
    take_out = lambda s, me, p: s.at[p[0] * 4 + p[3]]
    put_out = lambda o, me, p: o.at[me[0] * 4 + me[3]]
    whole = lambda s, me, p: s
    own_row = lambda o, me, p: o.at[me[2]]
    sends = []
    to_sibling, to_lines, to_cols = [], [[], [], [], []], [[], [], [], []]
    to_rows, stats, last, spread_out = {}, [], [], []
    for offset in SOURCES:
        for mine, theirs in ((9, 10), (11, 12)):
            spread_out.append(len(sends))
            sends.append((offset, ("scratch", mine), take_out, ("scratch", theirs), put_out))
    for r in range(4):
        view = lambda ref, me, p, r=r: ref.at[r]
        to_sibling.append(len(sends))
        sends.append((SIBLING, ("scratch", 0), view, ("scratch", 1), view))
    for r in range(4):
        for offset in LINES:
            to_lines[r].append(len(sends))
            sends.append(
                (
                    offset,
                    ("scratch", 2),
                    lambda s, me, p, r=r: s.at[r, rows(p[0] * 32, 32)],
                    ("scratch", 3),
                    lambda o, me, p, r=r: o.at[me[0], r],
                )
            )
        for offset in COLS:
            to_cols[r].append(len(sends))
            sends.append(
                (
                    offset,
                    ("scratch", 2),
                    lambda s, me, p, r=r: s.at[r, pl.ds(128, 128), rows(p[3] * 384, 384)],
                    ("scratch", 4),
                    lambda o, me, p, r=r: o.at[me[3], r],
                )
            )
    to_rows[2] = [len(sends), len(sends) + 1]
    for index, offset in enumerate(((0, 0, 1, 0), (0, 0, 3, 0))):
        part = lambda s, me, p, index=index: s.at[1, pl.ds(index * 256, 256)]
        slot = lambda o, me, p, index=index: o.at[index]
        sends.append((offset, ("scratch", 5), part, ("scratch", 8), slot))
    for index, offset in enumerate(((0, 0, 1, 0), (0, 0, 3, 0))):
        to_rows[offset[2]] = len(sends)
        part = lambda s, me, p, ahead=offset[2]: s.at[ahead - 1]
        slot = lambda o, me, p, index=index: o.at[index]
        sends.append((offset, ("scratch", 5), part, ("made", 2), slot))
    for offset in ROWS:
        stats.append(len(sends))
        sends.append((offset, ("scratch", 6), whole, ("made", 3), own_row))
    for way, index in ((ONE_BACK, 0), (OTHER_BACK, 1)):
        last.append(len(sends))
        sends.append((way, index, whole, index, whole))
    return exchange(
        [down_1, down_2],
        [shape(down_1.shape)] * 2,
        sends,
        [],
        5,
        work=lambda links, *refs: finish_kernel(
            links, (to_sibling, to_lines, to_cols, to_rows, stats, last, spread_out), *refs
        ),
        work_in=operands,
        work_out=[
            shape((4, 32, 1536)),
            shape((4, 128, 384)),
            shape((2, 512, 512)),
            shape((4, 8, HEAD), F32),
            shape((512, 512)),
            shape((64, 512)),
            shape((24, HEAD), F32),
            shape((512, 512)),
            shape((8, HEAD), F32),
        ],
        work_scratch=[pltpu.VMEM((4, 256, 1536), BF)] * 3
        + [
            pltpu.VMEM((4, 4, 32, 1536), BF),
            pltpu.VMEM((4, 4, 128, 384), BF),
            pltpu.VMEM((3, 512, 512), BF),
            pltpu.VMEM((8, HEAD), F32),
            pltpu.VMEM((3, 512, 512), F32),
            pltpu.VMEM((2, 256, 512), BF),
            pltpu.VMEM((16, 64, 512), BF),
            pltpu.VMEM((16, 64, 512), BF),
            pltpu.VMEM((16, 24, HEAD), F32),
            pltpu.VMEM((16, 24, HEAD), F32),
        ],
        deferred=range(len(sends)),
    )


def expert_at(place):
    return place[0] * 16 + (place[2] // 2) * 8 + place[3] * 2 + place[2] % 2


def expert_views():
    return (
        lambda s, me, p: s.at[expert_at(p)],
        lambda o, me, p: o.at[me[0] * 4 + me[3], :, rows(me[2] * 512, 512)],
    )


def token_views():
    return (
        lambda s, me, p: s.at[p[0] * 4 + p[3], :, rows(p[2] * 512, 512)],
        lambda o, me, p: o.at[expert_at(me)],
    )


def collect_sums(by_y, by_z, out_piece, small_piece, late, up_grad):
    put_qkv = lambda o, me, p: o.at[me[1], :, me[0]]
    put_out = lambda o, me, p: o.at[me[0], me[1]]
    put_small = lambda o, me, p: o.at[me[0] * 4 + me[3]]
    put_late = lambda o, me, p: o.at[(me[0] * 2 + me[1]) * 4 + me[3]]
    whole = lambda s, me, p: s
    sends = Sends()
    heads = sends.add(
        PLANE,
        lambda s, me, p: s.at[p[2], :, rows(p[3] * 384, 384)],
        ("scratch", 0),
        lambda o, me, p: o.at[me[3], me[2]],
        ("work", 0),
    )
    heads += sends.add(
        SIDES,
        lambda s, me, p: s.at[p[2], rows(p[0] * 32, 32)],
        ("scratch", 1),
        lambda o, me, p: o.at[me[0], me[2]],
        ("work", 1),
    )
    sends.add([OTHER_BACK], whole, 3, whole, 3)
    out_sent = sends.add(LINES, whole, 0, put_out, 0)
    sends.add([SIBLING], whole, 0, put_out, 0)
    sends.add(SOURCES, whole, 1, put_small, 1)
    sends.add(OTHERS, whole, 2, put_late, 2)
    later = len(sends)
    qkv_sent = sends.add(LINES, whole, ("made", 0), put_qkv, ("scratch", 2))
    sends.add([SIBLING], whole, ("made", 0), put_qkv, ("scratch", 2))
    relays = []
    for index in (1, 2, 0):
        origin = lambda me, d=LINES[index][0]: (me[0] + 4 - d) % 4
        view = lambda ref, me, p, origin=origin: ref.at[origin(me), me[1]]
        relays.append((out_sent[index], len(sends)))
        sends.append((SIBLING, 0, view, 0, view, [out_sent[index]]))
    for index in (1, 2, 0):
        origin = lambda me, d=LINES[index][0]: (me[0] + 4 - d) % 4
        view = lambda ref, me, p, origin=origin: ref.at[me[1], :, origin(me)]
        relays.append((qkv_sent[index], len(sends)))
        sends.append((SIBLING, ("made", 0), view, ("made", 0), view, [qkv_sent[index]]))

    def work(links, by_y_ref, by_z_ref, total_ref, spread_z, spread_y, mine):
        me = here()
        spread_z[me[3], me[2]] = by_y_ref[me[2], :, rows(me[3] * 384, 384)]
        spread_y[me[0], me[2]] = by_z_ref[me[2], rows(me[0] * 32, 32), :]
        for number in heads:
            links.arrive(number)
        for part, spread in ((0, spread_z), (1, spread_y)):
            for head in range(4):
                total = spread[0, head].astype(F32)
                for source in range(1, 4):
                    total = total + spread[source, head].astype(F32)
                mine[part, :, head * 384 : (head + 1) * 384] = total.astype(BF)
        for number in range(later, later + 4):
            links.send(number)
        for part in range(2):
            total_ref[me[1], part, me[0]] = mine[part]
        for came, number in relays:
            links.arrive(came)
            links.send(number)

    return exchange(
        [out_piece, small_piece, late, up_grad],
        [
            shape((4, 2, 64, 512)),
            shape((16,) + small_piece.shape, F32),
            shape((32,) + late.shape, F32),
            shape(up_grad.shape),
        ],
        sends,
        [
            (0, lambda s, me: s, 0, lambda o, me: put_out(o, me, me), (64, 512)),
            (1, lambda s, me: s, 1, lambda o, me: put_small(o, me, me), small_piece.shape),
            (2, lambda s, me: s, 2, lambda o, me: put_late(o, me, me), late.shape),
        ],
        12,
        work=work,
        work_in=[by_y, by_z],
        work_out=[shape((2, 2, 4, 32, 1536))],
        work_scratch=[
            pltpu.VMEM((4, 4, 32, 384), BF),
            pltpu.VMEM((4, 4, 32, 384), BF),
            pltpu.VMEM((2, 32, 1536), BF),
        ],
        deferred=range(later, len(sends)),
    )


BLOCK = 256
SCALE = HEAD ** (-0.5)
LAST = (((1,), (1,)), ((), ()))
FIRST = (((0,), (0,)), ((), ()))


def swapped(operand):
    return pltpu.roll(operand, HEAD // 2, 1)


def attend_kernel(
    links,
    numbers,
    qkv_ref,
    position_ref,
    frequency_ref,
    gain_ref,
    query_ref,
    key_ref,
    lse_ref,
    cos_ref,
    sin_ref,
    gathered,
    out_ref,
):
    def prepare(step, carry):
        span = pl.ds(pl.multiple_of(step * BLOCK, BLOCK), BLOCK)
        angles = position_ref[span, :] * frequency_ref[0:1, :]
        cos_ref[span, :] = jnp.cos(angles)
        sin_ref[span, :] = jnp.sin(angles) * frequency_ref[1:2, :]
        for part, target in ((0, query_ref), (1, key_ref)):
            raw = qkv_ref[span, part * HEAD : (part + 1) * HEAD].astype(F32)
            scaled = (
                raw
                * lax.rsqrt(jnp.mean(raw * raw, axis=1, keepdims=True) + EPS)
                * gain_ref[part : part + 1, :]
            )
            target[span, :] = (scaled * cos_ref[span, :] + swapped(scaled) * sin_ref[span, :]).astype(
                BF
            )
        return carry

    lax.fori_loop(0, SEQ // BLOCK, prepare, 0)
    to_cols, beside, passed = numbers
    row, col = lax.axis_index("row"), lax.axis_index("col")
    for ahead in (1, 3, 2, 0):
        first = lax.rem(col + ahead, 4) * 512

        def block(step, carry, first=first):
            span = pl.ds(pl.multiple_of(first + step * BLOCK, BLOCK), BLOCK)
            scores = (
                lax.dot_general(
                    query_ref[span, :], key_ref[...], LAST, preferred_element_type=F32
                )
                * SCALE
            )
            largest = jnp.max(scores, axis=1, keepdims=True)
            weights = jnp.exp(scores - largest)
            total = jnp.sum(weights, axis=1, keepdims=True)
            mixed = jnp.dot(
                weights.astype(BF), qkv_ref[:, 2 * HEAD :], preferred_element_type=F32
            )
            out_ref[span, :] = (mixed / total).astype(BF)
            lse_ref[span, :] = largest + jnp.log(total)
            return carry

        lax.fori_loop(0, 512 // BLOCK, block, 0)
        if ahead:
            links.send(to_cols[ahead])
    gathered[:, rows((row * 4 + col) * HEAD, HEAD)] = out_ref[rows(col * 512, 512), :]
    for ahead in (0, 1, 3, 2):
        if ahead:
            links.arrive(to_cols[ahead])
        for number in beside[ahead]:
            links.send(number)
    for ahead in (0, 1, 3, 2):
        for number, onward in zip(beside[ahead], passed[ahead]):
            links.arrive(number)
            links.send(onward)


def attend(qkv, position, frequency, gains, blocks):
    take, put = expert_views()
    sends = [(offset, 0, take, 0, put) for offset in CUBE]
    to_cols, beside, passed = {}, {}, {}
    for offset in COLS:
        to_cols[offset[3]] = len(sends)
        sends.append(
            (
                offset,
                ("scratch", 0),
                lambda s, me, p: s.at[rows(p[3] * 512, 512)],
                ("made", 5),
                lambda o, me, p: o.at[:, rows((me[2] * 4 + me[3]) * HEAD, HEAD)],
            )
        )
    sides = ((0, 0, 1, 0), (0, 0, 3, 0))
    head_of = lambda row, me, ahead: rows((row * 4 + (me[3] + 4 - ahead) % 4) * HEAD, HEAD)
    for ahead in range(4):
        beside[ahead], passed[ahead] = [], []
        for offset in sides:
            view = lambda ref, me, p, ahead=ahead: ref.at[:, head_of(me[2], me, ahead)]
            beside[ahead].append(len(sends))
            sends.append((offset, ("made", 5), view, ("made", 5), view))
        for index, offset in enumerate(sides):
            view = lambda ref, me, p, ahead=ahead, index=index, d=offset[2]: ref.at[
                pl.ds(index * 256, 256), head_of((me[2] + 4 - d) % 4, me, ahead)
            ]
            passed[ahead].append(len(sends))
            sends.append((offset, ("made", 5), view, ("made", 5), view))
    return exchange(
        [blocks],
        [shape((16, ROOM, WIDTH))],
        sends,
        [(0, lambda s, me: take(s, me, me), 0, lambda o, me: put(o, me, me), (ROOM, 512))],
        6,
        work=lambda links, *refs: attend_kernel(links, (to_cols, beside, passed), *refs),
        work_in=[qkv, position, frequency, gains],
        work_out=[
            shape((SEQ, HEAD)),
            shape((SEQ, HEAD)),
            shape((SEQ, 1), F32),
            shape((SEQ, HEAD), F32),
            shape((SEQ, HEAD), F32),
            shape((512, WIDTH)),
        ],
        work_scratch=[pltpu.VMEM((SEQ, HEAD), BF)],
        deferred=range(len(CUBE), len(sends)),
    )


NEAR_FIRST = (1, 3, 2, 0)


def attend_back_kernel(
    links,
    numbers,
    partial_ref,
    qkv_ref,
    query_ref,
    key_ref,
    lse_ref,
    cos_ref,
    sin_ref,
    gain_ref,
    qkv_grad_ref,
    gain_grad_ref,
    cross,
    mixed,
    out_grads,
    grad_ref,
    query_grad,
    key_grad,
    value_grad,
):
    to_rows, to_cols, back_query, back_to_cols, last = numbers
    row, col = lax.axis_index("row"), lax.axis_index("col")
    for ahead in NEAR_FIRST:
        for number in to_rows[ahead]:
            links.send(number)
    key_grad[...] = jnp.zeros_like(key_grad)
    value_grad[...] = jnp.zeros_like(value_grad)

    def mix(ahead):
        head = lax.rem(col + ahead, 4)
        for number in to_rows[ahead]:
            links.arrive(number)
        total = partial_ref[:, rows((row * 4 + head) * HEAD, HEAD)].astype(F32)
        for part in range(3):
            total = total + cross[part, ahead].astype(F32)
        if ahead:
            mixed[ahead] = total.astype(BF)
            links.send(to_cols[ahead])
        else:
            out_grads[rows(col * 512, 512), :] = total.astype(BF)

    def attend_block(ahead):
        if ahead:
            links.arrive(to_cols[ahead])
        first = lax.rem(col + 4 - ahead, 4) * 512

        def block(step, carry):
            span = pl.ds(pl.multiple_of(first + step * BLOCK, BLOCK), BLOCK)
            query, out_grad = query_ref[span, :], out_grads[span, :]
            scores = (
                lax.dot_general(query, key_ref[...], LAST, preferred_element_type=F32) * SCALE
            )
            soft = jnp.exp(scores - lse_ref[span, :])
            prob_grad = lax.dot_general(
                out_grad, qkv_ref[:, 2 * HEAD :], LAST, preferred_element_type=F32
            )
            inner = jnp.sum(soft * prob_grad, axis=1, keepdims=True)
            score_grad = (soft * (prob_grad - inner)).astype(BF)
            query_grad[span, :] = (
                jnp.dot(score_grad, key_ref[...], preferred_element_type=F32) * SCALE
            )
            key_grad[...] += lax.dot_general(
                score_grad, query, FIRST, preferred_element_type=F32
            )
            value_grad[...] += lax.dot_general(
                soft.astype(BF), out_grad, FIRST, preferred_element_type=F32
            )
            return carry

        lax.fori_loop(0, 512 // BLOCK, block, 0)
        finish_part(first, ((0, query_grad, 1.0),))
        if ahead:
            links.send(back_query[(4 - ahead) % 4])

    def finish_part(first, sources):
        def finish_block(step, carry):
            span = pl.ds(pl.multiple_of(first + step * BLOCK, BLOCK), BLOCK)
            for part, source, factor in sources:
                turned = source[span, :] * factor
                grad = turned * cos_ref[span, :] + swapped(turned * sin_ref[span, :])
                raw = qkv_ref[span, part * HEAD : (part + 1) * HEAD].astype(F32)
                inverse = lax.rsqrt(jnp.mean(raw * raw, axis=1, keepdims=True) + EPS)
                unit = raw * inverse
                gain_grad_ref[part : part + 1, :] += jnp.sum(grad * unit, axis=0, keepdims=True)
                scaled = grad * gain_ref[part : part + 1, :]
                raw_grad = inverse * (
                    scaled - unit * jnp.mean(scaled * unit, axis=1, keepdims=True)
                )
                grad_ref[span, part * HEAD : (part + 1) * HEAD] = raw_grad.astype(BF)
                if part:
                    grad_ref[span, 2 * HEAD :] = value_grad[span, :].astype(BF)
            return carry

        lax.fori_loop(0, 512 // BLOCK, finish_block, 0)

    gain_grad_ref[...] = jnp.zeros_like(gain_grad_ref)
    mix(1)
    mix(3)
    attend_block(1)
    mix(2)
    attend_block(3)
    mix(0)
    for number in last:
        links.send(number)
    attend_block(2)
    attend_block(0)
    for ahead in NEAR_FIRST:
        finish_part(lax.rem(col + ahead, 4) * 512, ((1, key_grad, SCALE),))
        if ahead:
            links.send(back_to_cols[ahead])
    qkv_grad_ref[:, rows(col * 384, 384)] = grad_ref[rows(col * 512, 512), :]


def attend_back(operands, out_part, small_part, up_grad):
    whole = lambda s, me, p: s
    sends = [
        (SIBLING, 0, lambda s, me, p: s.at[:, rows(p[1] * 64, 64)], 0, whole),
        (SIBLING, 1, whole, 1, whole),
    ]
    later = len(sends)
    to_rows, to_cols, back_query, back_to_cols = {}, {}, {}, {}
    for ahead in NEAR_FIRST:
        to_rows[ahead] = []
        for part, offset in enumerate(ROWS):
            to_rows[ahead].append(len(sends))
            head = lambda me, p, ahead=ahead: p[2] * 4 + (me[3] + ahead) % 4
            sends.append(
                (
                    offset,
                    ("work", 0),
                    lambda s, me, p, head=head: s.at[:, rows(head(me, p) * HEAD, HEAD)],
                    ("scratch", 0),
                    lambda o, me, p, part=part, ahead=ahead: o.at[part, ahead],
                )
            )
    for offset in COLS:
        ahead = offset[3]
        to_cols[ahead] = len(sends)
        sends.append(
            (
                offset,
                ("scratch", 1),
                lambda s, me, p, ahead=ahead: s.at[ahead],
                ("scratch", 2),
                lambda o, me, p: o.at[rows(me[3] * 512, 512)],
            )
        )
        for numbers, skip, size in ((back_query, 0, HEAD), (back_to_cols, HEAD, 2 * HEAD)):
            numbers[ahead] = len(sends)
            sends.append(
                (
                    offset,
                    ("scratch", 3),
                    lambda s, me, p, skip=skip, size=size: s.at[
                        rows(p[3] * 512, 512), pl.ds(skip, size)
                    ],
                    ("made", 0),
                    lambda o, me, p, skip=skip, size=size: o.at[
                        :, pl.ds(pl.multiple_of(me[3] * 384 + skip, HEAD), size)
                    ],
                )
            )
    last = [len(sends)]
    sends.append((ONE_BACK, 2, whole, 2, whole))
    return exchange(
        [out_part, small_part, up_grad],
        [
            shape((16, 64, 512)),
            shape(small_part.shape, F32),
            shape(up_grad.shape),
        ],
        sends,
        [],
        13,
        deferred=range(later, len(sends)),
        work=lambda links, *refs: attend_back_kernel(
            links, (to_rows, to_cols, back_query, back_to_cols, last), *refs
        ),
        work_in=operands,
        work_out=[shape((512, 1536)), shape((8, HEAD), F32)],
        work_scratch=[
            pltpu.VMEM((3, 4, 512, HEAD), BF),
            pltpu.VMEM((4, 512, HEAD), BF),
            pltpu.VMEM((SEQ, HEAD), BF),
            pltpu.VMEM((SEQ, 3 * HEAD), BF),
        ]
        + [pltpu.VMEM((SEQ, HEAD), F32)] * 3,
    )


SLOTS = 16 * ROOM
GROUP = 4 * ROOM


def expert_kernel(
    links,
    came,
    returns,
    results,
    shares,
    cot_ref,
    gated_ref,
    up_1,
    up_2,
    down_1,
    down_2,
    x_ref,
    back_ref,
    joined,
    slot_grads,
    acts,
    grads,
    their_x,
    their_slot_grads,
    their_acts,
    their_grads,
    up_ref,
    down_ref,
    out_sum,
    back_sum,
    weight_sem,
    own_sem,
):
    me = here()
    loads = []
    for slot in range(4):
        for part, target in ((1, up_ref), (5, down_ref)):
            loads.append(
                pltpu.make_async_copy(
                    links.ins[part + slot], target.at[slot], weight_sem.at[part + slot - 1]
                )
            )
    take, put = expert_views()
    own_in = pltpu.make_async_copy(take(links.ins[0], me, me), put(x_ref, me, me), own_sem.at[0])
    take, put = token_views()
    own_out = pltpu.make_async_copy(
        take(back_ref, me, me), put(links.outs[0], me, me), own_sem.at[1]
    )
    own_result = pltpu.make_async_copy(
        take(gated_ref, me, me), put(links.outs[1], me, me), own_sem.at[2]
    )
    own_in.start()
    for load in loads:
        load.start()
    line = lax.broadcasted_iota(jnp.int32, (ROOM, HEAD), 0)
    lane = lax.broadcasted_iota(jnp.int32, (ROOM, HEAD), 1)
    same = (line == lane).astype(F32)
    for group in range(4):
        if group == 0:
            own_in.wait()
        for number in came[group]:
            links.arrive(number)
        if group == 0:
            for load in loads:
                load.wait()
        blocks = [
            lax.rem(me[0] + 4 - i, 4) * 4 + lax.rem(me[3] + 4 - (group - i) % 4, 4)
            for i in range(4)
        ]
        span = pl.ds(group * GROUP, GROUP)
        received = jnp.concatenate([x_ref[block].astype(F32) for block in blocks], axis=0)
        cot = jnp.concatenate([cot_ref[block].astype(F32) for block in blocks], axis=0)
        gates = []
        for i in range(4):
            aux = jnp.where(line >= CAP, received[i * ROOM : (i + 1) * ROOM, :HEAD], 0.0)
            gates.append(
                jnp.sum(same * jnp.sum(aux, axis=0, keepdims=True), axis=1, keepdims=True)
            )
        gate = jnp.concatenate(gates, axis=0)
        joined[span, :] = received.astype(BF)
        slot_grads[span, :] = (gate * cot).astype(BF)
        out_sum[...] = jnp.zeros_like(out_sum)
        back_sum[...] = jnp.zeros_like(back_sum)

        def quarter(slot, carry, span=span):
            gate_up = jnp.dot(joined[span, :], up_ref[slot], preferred_element_type=F32)
            gate_part, up_part = gate_up[:, :256], gate_up[:, 256:]
            sigmoid = 1.0 / (1.0 + jnp.exp(-gate_part))
            silu = gate_part * sigmoid
            act = (silu * up_part).astype(BF)
            acts[slot, span, :] = act
            act_grad = lax.dot_general(
                slot_grads[span, :], down_ref[slot], LAST, preferred_element_type=F32
            )
            slope = sigmoid * (1.0 + gate_part * (1.0 - sigmoid))
            grads[slot, span, :256] = (act_grad * up_part * slope).astype(BF)
            grads[slot, span, 256:] = (act_grad * silu).astype(BF)
            out_sum[...] += jnp.dot(act, down_ref[slot], preferred_element_type=F32)
            back_sum[...] += lax.dot_general(
                grads[slot, span, :], up_ref[slot], LAST, preferred_element_type=F32
            )
            return carry

        lax.fori_loop(0, 4, quarter, 0)
        out = out_sum[...]
        gated = gate * out
        gate_grad = jnp.sum(cot * out.astype(BF).astype(F32), axis=1, keepdims=True)
        back = back_sum[...]
        inner = jnp.sum(back * joined[span, :].astype(F32), axis=1, keepdims=True)
        for i, block in enumerate(blocks):
            part = slice(i * ROOM, (i + 1) * ROOM)
            gated_ref[block] = gated[part].astype(BF)
            back_ref[block] = back[part].astype(BF)
            for index, value in enumerate((gate_grad, inner)):
                high, middle, low = pieces(jnp.sum(same * value[part], axis=0, keepdims=True))
                aux = jnp.where(line == CAP, high.astype(F32), 0.0)
                aux = aux + jnp.where(line == CAP + 1, middle.astype(F32), 0.0)
                aux = aux + jnp.where(line == CAP + 2, low.astype(F32), 0.0)
                for r in range(4):
                    start = r * 512 + index * HEAD
                    back_ref[block, :, start : start + HEAD] = (
                        back[part, start : start + HEAD] + aux
                    ).astype(BF)
        for number in returns[group]:
            links.send(number)
        if group == 0:
            own_out.start()
            own_result.start()
        for number in shares[group] + results[group]:
            links.send(number)
    for numbers in shares:
        for number in numbers:
            links.arrive(number)

    def weight_grads(step, carry):
        span = pl.ds(pl.multiple_of(step * 512, 512), 512)
        for slot, up, down in ((0, up_1, down_1), (1, up_2, down_2)):
            up[span, :] = (
                lax.dot_general(joined[:, span], grads[slot], FIRST, preferred_element_type=F32)
                + lax.dot_general(
                    their_x[:, span], their_grads[slot], FIRST, preferred_element_type=F32
                )
            ).astype(BF)
            down[:, span] = (
                lax.dot_general(
                    acts[slot], slot_grads[:, span], FIRST, preferred_element_type=F32
                )
                + lax.dot_general(
                    their_acts[slot],
                    their_slot_grads[:, span],
                    FIRST,
                    preferred_element_type=F32,
                )
            ).astype(BF)
        return carry

    lax.fori_loop(0, 4, weight_grads, 0)
    own_out.wait()
    own_result.wait()


def run_experts(blocks, cot_slots, weights):
    take, put = expert_views()
    came, returns, results, shares = ([[], [], [], []] for _ in range(4))
    sends = []
    for offset in CUBE:
        came[(offset[0] + offset[3]) % 4].append(len(sends))
        sends.append((offset, 0, take, ("scratch", 0), put))
    take, put = token_views()
    for offset in CUBE:
        returns[-(offset[0] + offset[3]) % 4].append(len(sends))
        sends.append((offset, ("scratch", 1), take, 0, put))
    for offset in CUBE:
        results[-(offset[0] + offset[3]) % 4].append(len(sends))
        sends.append((offset, ("made", 0), take, 1, put))
    for place in range(4):
        span = pl.ds(place * GROUP, GROUP)
        for mine, theirs in ((2, 6), (3, 7)):
            view = lambda ref, me, p, span=span: ref.at[span]
            shares[place].append(len(sends))
            sends.append((SIBLING, ("scratch", mine), view, ("scratch", theirs), view))
        for mine, theirs in ((4, 8), (5, 9)):
            shares[place].append(len(sends))
            sends.append(
                (
                    SIBLING,
                    ("scratch", mine),
                    lambda ref, me, p, span=span: ref.at[pl.ds(2, 2), span],
                    ("scratch", theirs),
                    lambda ref, me, p, span=span: ref.at[:, span],
                )
            )
    return exchange(
        [blocks] + weights,
        [shape((EXPERTS, ROOM, 512))] * 2,
        sends,
        [],
        8,
        work=lambda links, *refs: expert_kernel(
            links, came, returns, results, shares, *refs
        ),
        work_in=[cot_slots],
        work_out=[shape((16, ROOM, WIDTH))]
        + [shape((WIDTH, 512))] * 2
        + [shape((256, WIDTH))] * 2,
        work_scratch=[
            pltpu.VMEM((16, ROOM, WIDTH), BF),
            pltpu.VMEM((16, ROOM, WIDTH), BF),
            pltpu.VMEM((SLOTS, WIDTH), BF),
            pltpu.VMEM((SLOTS, WIDTH), BF),
            pltpu.VMEM((4, SLOTS, 256), BF),
            pltpu.VMEM((4, SLOTS, 512), BF),
            pltpu.VMEM((SLOTS, WIDTH), BF),
            pltpu.VMEM((SLOTS, WIDTH), BF),
            pltpu.VMEM((2, SLOTS, 256), BF),
            pltpu.VMEM((2, SLOTS, 512), BF),
            pltpu.VMEM((4, WIDTH, 512), BF),
            pltpu.VMEM((4, 256, WIDTH), BF),
            pltpu.VMEM((GROUP, WIDTH), F32),
            pltpu.VMEM((GROUP, WIDTH), F32),
            pltpu.SemaphoreType.DMA((8,)),
            pltpu.SemaphoreType.DMA((3,)),
        ],
        deferred=range(len(CUBE), len(sends)),
    )


def pack_kernel(up_1, up_2, down_1, down_2, qkv, out, up_ref, down_ref, qkv_ref, out_ref):
    upper = lax.axis_index("row") // 2
    for which, up, down in ((upper, up_1, down_1), (1 - upper, up_2, down_2)):
        value = up[...].astype(F32)
        up_ref[which, :, 0, :] = value[:, :256]
        up_ref[which, :, 1, :] = value[:, 256:]
        down_ref[which] = down[...].astype(F32)
    out_ref[...] = out[...].astype(F32)
    for head in range(4):
        qkv_ref[:, head, :] = qkv[:, head * 384 : (head + 1) * 384].astype(F32)


def pack_grads(up_1, up_2, down_1, down_2, qkv, out):
    steps = 8
    up, down = (WIDTH // steps, 512), (256 // steps, WIDTH)
    return pl.pallas_call(
        pack_kernel,
        grid=(steps,),
        out_shape=[
            shape((2, WIDTH, 2, 256), F32),
            shape((2, 256, WIDTH), F32),
            shape((512, 4, 384), F32),
            shape((512, 512), F32),
        ],
        in_specs=[pl.BlockSpec(up, lambda i: (i, 0))] * 2
        + [pl.BlockSpec(down, lambda i: (i, 0))] * 2
        + [pl.BlockSpec((512 // steps, 1536), lambda i: (i, 0))]
        + [pl.BlockSpec((512 // steps, 512), lambda i: (i, 0))],
        out_specs=[
            pl.BlockSpec((2, up[0], 2, 256), lambda i: (0, i, 0, 0)),
            pl.BlockSpec((2,) + down, lambda i: (0, i, 0)),
            pl.BlockSpec((512 // steps, 4, 384), lambda i: (i, 0, 0)),
            pl.BlockSpec((512 // steps, 512), lambda i: (i, 0)),
        ],
    )(up_1, up_2, down_1, down_2, qkv, out)


def dot(left, right):
    return jnp.dot(left, right, preferred_element_type=F32)


def dot_last(left, right):
    return lax.dot_general(left, right, LAST, preferred_element_type=F32)


def dot_first(left, right):
    return lax.dot_general(left, right, FIRST, preferred_element_type=F32)


def pieces(value):
    high = value.astype(BF)
    rest = value - high.astype(F32)
    middle = rest.astype(BF)
    low = (rest - middle.astype(F32)).astype(BF)
    return [high, middle, low]


def aux_rows(value):
    held = jnp.stack(pieces(value), axis=1)
    return jnp.pad(held, ((0, 0), (CAP, ROOM - CAP - 3), (0, 512 - ROOM)))


def aux_value(blocks, index):
    part = blocks[:, CAP : CAP + 3, index * HEAD : index * HEAD + ROOM]
    return jnp.sum(part.astype(F32), axis=1)


FIRST_HOP = [
    ((2 * y + k) * 4 + x, (2 * y + 1 - x % 2) * 4 + 2 * k + x // 2)
    for y in range(4)
    for k in range(2)
    for x in range(4)
]
SECOND_HOP = [
    ((2 * y + k) * 4 + x, (2 * y + x % 2) * 4 + 2 * k + 1 - x // 2)
    for y in range(4)
    for k in range(2)
    for x in range(4)
]
PAIR = [(d, d ^ 1) for d in range(8)]


def hop(operand, pairs):
    return lax.ppermute(operand, ("dp", "row"), pairs)


def after(*operands):
    return lax.optimization_barrier(operands)


def shards(
    tokens,
    positions,
    routes,
    attention_norm_gain,
    experts_norm_gain,
    w_qkv,
    q_gain,
    k_gain,
    w_out,
    w_router,
    w_gate_up,
    w_down,
    cotangent,
):
    core = lax.axis_index("dp") % 2
    experts = jnp.arange(EXPERTS, dtype=jnp.int32)
    named = jnp.any(routes[:, :, None] == experts[None, None, :], axis=1)
    place = jnp.arange(512, dtype=jnp.int32)
    earlier = (place[None, :] < place[:, None]).astype(BF)
    rank = dot(earlier, named.astype(BF))
    rank = jnp.where(named, rank, -1.0).T
    (
        token_rows,
        w_group,
        position_rows,
        gain_rows,
        w_all,
        down_1,
        down_2,
        send_up_1,
        send_up_2,
        send_cot,
    ) = gather_inputs(
        tokens,
        w_qkv,
        w_out,
        w_down,
        positions.reshape(4, HEAD),
        attention_norm_gain.reshape(4, HEAD),
        [w_gate_up, rank, cotangent],
    )
    w_all = w_all.reshape(WIDTH, 512)
    w_group = w_group.reshape(WIDTH, 1536)
    gain_full = gain_rows.reshape(WIDTH)

    gate_up_1, gate_up_2 = hop(send_up_1, FIRST_HOP), hop(send_up_2, SECOND_HOP)
    sibling = lambda w: lax.ppermute(w, "dp", PAIR)
    frequency = THETA ** (-2.0 * jnp.arange(HEAD // 2, dtype=F32) / HEAD)
    half_signs = jnp.where(jnp.arange(HEAD) < HEAD // 2, -1.0, 1.0).astype(F32)
    frequency = jnp.concatenate(
        [jnp.concatenate([frequency] * 2)[None], half_signs[None], jnp.zeros((6, HEAD), F32)]
    )
    position_column = position_rows.reshape(SEQ, 1).astype(F32)
    gains = jnp.concatenate([q_gain[None], k_gain[None], jnp.zeros((6, HEAD), F32)], axis=0)

    pick = (rank[:, None, :] == jnp.arange(ROOM, dtype=F32)[None, :, None]).astype(BF)
    flat_pick = pick.reshape(EXPERTS * ROOM, 512)

    token_full = token_rows.astype(F32)
    inverse_attention = lax.rsqrt(jnp.mean(token_full * token_full, axis=1) + EPS)
    normed_exact = token_full * inverse_attention[:, None] * gain_full[None, :]
    normed = normed_exact.astype(BF)
    qkv = to_heads(dot(normed, w_group).astype(BF))
    cot_slots, query, key, lse, cosine, sine, attended_rows = attend(
        qkv, position_column, frequency, gains, send_cot
    )
    attended_rows, gate_up_1, gate_up_2, down_1, down_2 = after(
        attended_rows, gate_up_1, gate_up_2, down_1, down_2
    )
    up_ws = [gate_up_1, gate_up_2, sibling(gate_up_1), sibling(gate_up_2)]
    down_ws = [down_1, down_2, sibling(down_1), sibling(down_2)]

    token_float = tokens.astype(F32)
    hidden = token_float + dot(attended_rows, w_all)
    scaled_hidden = hidden * experts_norm_gain
    partial_stats = jnp.concatenate(
        [
            lax.dot_general(
                w_router.astype(F32),
                scaled_hidden,
                (((0,), (1,)), ((), ())),
                precision=EXACT,
                preferred_element_type=F32,
            ),
            jnp.sum(hidden * hidden, axis=1)[None],
            jnp.zeros((7, 512), F32),
        ],
        axis=0,
    )
    stats = jnp.sum(row_stack(partial_stats, 7), axis=0)
    inverse_experts = lax.rsqrt(stats[EXPERTS] / WIDTH + EPS)
    logits = stats[:EXPERTS] * inverse_experts[None, :]
    unit_experts = hidden * inverse_experts[:, None]
    experts_input = (unit_experts * experts_norm_gain).astype(BF)
    named_t = rank >= 0
    largest = jnp.max(jnp.where(named_t, logits, -jnp.inf), axis=0, keepdims=True)
    shifted = jnp.where(named_t, jnp.exp(jnp.where(named_t, logits - largest, 0.0)), 0.0)
    gates = shifted / jnp.sum(shifted, axis=0, keepdims=True)
    slot_gates = jnp.sum(pick.astype(F32) * gates[:, None, :], axis=2)
    send_rows = dot(flat_pick, experts_input).astype(BF).reshape(EXPERTS, ROOM, 512)
    back_rows, out_rows, _, up_1, up_2, down_1, down_2 = run_experts(
        send_rows + aux_rows(slot_gates), cot_slots, up_ws + down_ws
    )
    gate_grad = jnp.sum(pick.astype(F32) * aux_value(back_rows, 0)[:, :, None], axis=1)
    inner = jnp.sum(pick.astype(F32) * aux_value(back_rows, 1)[:, :, None], axis=(0, 1))
    logit_grad = gates * (gate_grad - jnp.sum(gates * gate_grad, axis=0, keepdims=True))
    experts_input_grad = dot_first(
        flat_pick, back_rows.reshape(EXPERTS * ROOM, 512)
    ) + lax.dot_general(
        logit_grad,
        w_router.astype(F32),
        (((0,), (1,)), ((), ())),
        precision=EXACT,
        preferred_element_type=F32,
    )
    mean_experts = (inner + jnp.sum(logit_grad * logits, axis=0)) / WIDTH
    cot_float = cotangent.astype(F32)
    middle_grad = cot_float + inverse_experts[:, None] * (
        experts_input_grad * experts_norm_gain - unit_experts * mean_experts[:, None]
    )
    router_part = lax.dot_general(
        logit_grad,
        experts_input.astype(F32),
        (((1,), (0,)), ((), ())),
        precision=EXACT,
        preferred_element_type=F32,
    )
    experts_gain_part = jnp.sum(experts_input_grad * unit_experts, axis=0)
    attended_grad = middle_grad.astype(BF)
    out_part = dot_first(attended_rows, attended_grad).astype(BF).reshape(16, HEAD, 512)
    small_part = jnp.concatenate(
        [
            router_part.reshape(256, HEAD),
            experts_gain_part.reshape(4, HEAD),
            jnp.zeros((124, HEAD), F32),
        ],
        axis=0,
    )
    out_other, small_other, up_1, qkv_grad, head_gain_part = attend_back(
        [dot_last(attended_grad, w_all).astype(BF), qkv, query, key, lse, cosine, sine, gains],
        out_part,
        small_part,
        up_1,
    )
    down_1, down_2, by_y, by_z, _, _, output, out_piece, small_piece, token_grad, late = finish(
        down_1,
        down_2,
        [
            normed,
            qkv_grad,
            w_group,
            head_gain_part,
            hidden,
            flat_pick,
            out_rows.reshape(EXPERTS * ROOM, 512),
            out_part,
            out_other,
            small_part,
            small_other,
            middle_grad,
            tokens,
            inverse_attention[:, None],
            jnp.broadcast_to(attention_norm_gain[None], (8, 512)),
        ],
    )
    out_total, small_total, late, up_2, qkv_total = collect_sums(
        by_y, by_z, out_piece, small_piece, late, up_2
    )
    small_total = small_total.reshape(384, HEAD)
    late = jnp.sum(late, axis=0)
    grad_gate_up, grad_down, grad_qkv, grad_out = pack_grads(
        up_1,
        up_2,
        down_1,
        down_2,
        qkv_total.reshape(512, 1536),
        out_total.reshape(512, 512),
    )
    return (
        output,
        token_grad,
        late[:4].reshape(512),
        small_total[256:260].reshape(512),
        grad_qkv,
        late[4],
        late[5],
        grad_out,
        small_total[:256].reshape(EXPERTS, 512).T,
        grad_gate_up,
        grad_down,
    )


def solution(mesh):
    tokens_like = P(("dp", "col"), "row")
    up_like = P(("dp", "col"), None, None, "row")
    down_like = P(("dp", "col"), "row", None)
    return jax.shard_map(
        shards,
        mesh=mesh,
        in_specs=(
            tokens_like,
            P("dp", "row"),
            P(("dp", "col"), None),
            P("row"),
            P("row"),
            P("row", "col", None),
            P(),
            P(),
            P("col", "row"),
            P("row", None),
            up_like,
            down_like,
            tokens_like,
        ),
        out_specs=(
            tokens_like,
            tokens_like,
            P("row"),
            P("row"),
            P("row", "col", None),
            P(),
            P(),
            P("col", "row"),
            P("row", None),
            up_like,
            down_like,
        ),
        check_vma=False,
    )
```
